32 devices in a mesh: ctx: 8 (over z, y), chan: 4 (over x, core).
Axes of the slice: x: 2, y: 2, z: 4, core: 2. Of those that a mesh axis runs over, the one named last changes fastest.
Arguments:
- query_proj: bfloat16 [1024, 8192], P('ctx', 'chan'), may hold values from -6 to 6
- key_proj: bfloat16 [1024, 8192], P('ctx', 'chan'), may hold values from -6 to 6
- value_proj: bfloat16 [1024, 8192], P('ctx', 'chan'), may hold values from -6 to 6
- filters: bfloat16 [8192, 128], P('chan'), may hold values from -0.5 to 0.5
- out_weight: bfloat16 [8192, 8192], P('chan'), may hold values from -0.0625 to 0.0625
- cotangent: bfloat16 [1024, 8192], P('ctx', 'chan'), may hold values from -6 to 6
Outputs:
- mixed: bfloat16 [1024, 8192], P('ctx', 'chan')
- grad_query: bfloat16 [1024, 8192], P('ctx', 'chan')
- grad_key: bfloat16 [1024, 8192], P('ctx', 'chan')
- grad_value: bfloat16 [1024, 8192], P('ctx', 'chan')
- grad_filters: float32 [8192, 128], P('chan')
- grad_weight: bfloat16 [8192, 8192], P('chan', 'ctx')
The draws below stay inside these ranges and needn't reach their ends.
All inputs are finite; a program needn't handle non-finite values.
Results may differ from the reference program's by a relative error of at most 0.019.
Values may be sent and summed in bfloat16 or wider, within the bound.
No kernel may reach another device: no remote copies, remote signals or barrier semaphores. Data moves between devices by JAX's collectives and lax.ppermute only.
A program may use at most 128 MiB of HBM per device.

```python
import jax
import jax.numpy as jnp
from jax import lax

D = 8192
TAPS = 128
TOK_DEV = 128
TOKENS = 1024
N_CTX = 8


def with_spikes(drawn, own_key, source, target, shards_of, factor):
    def block_of(dim):
        return (jnp.arange(drawn.shape[dim]) // (drawn.shape[dim] // shards_of)).reshape((-1,) + (1,) * (drawn.ndim - 1 - dim))

    one_side = jax.random.permutation(own_key, shards_of)[block_of(target)]
    second = (block_of(target) + shards_of // 2) % shards_of
    return jnp.where((block_of(source) == one_side) | (block_of(source) == second), factor * drawn, drawn)


def steps_of(stream_key, shape, pieces, smallest, largest):
    def one(position, parts):
        heights = jax.random.uniform(jax.random.fold_in(jax.random.fold_in(stream_key, 6), position), (parts,), jnp.float32, smallest / len(pieces), largest / len(pieces))
        return jnp.repeat(jnp.exp(heights), shape[position] // parts).reshape((-1,) + (1,) * (len(shape) - position - 1))

    factor_of = one(*pieces[0])
    for cut in pieces[1:]:
        factor_of = factor_of * one(*cut)
    return factor_of


def scatter_about(rng, dims, width, limit, pieces=(), held_as=jnp.bfloat16):
    values = width * jax.random.normal(rng, dims, jnp.float32)
    if pieces:
        values = values * steps_of(rng, dims, pieces, -0.22, 0.18)
    return jnp.clip(values, -limit, limit).astype(held_as)


def bell_draw_with(rng, extent, scale, limit, pieces, heavy, kind=jnp.bfloat16):
    values = scale * jax.random.normal(rng, extent, jnp.float32)
    if pieces:
        values = values * steps_of(rng, extent, pieces, -0.22, 0.18)
    return jnp.clip(with_spikes(values, jax.random.fold_in(rng, 3), *heavy), -limit, limit).astype(kind)


def setup_inputs(seed: int = 0) -> dict:
    streams_of = jax.random.split(jax.random.key(seed), 7)
    query_proj = scatter_about(streams_of[0], (TOKENS, D), 1.0, 6.0, ((0, 8), (1, 4)))
    key_proj = scatter_about(streams_of[1], (TOKENS, D), 1.0, 6.0, ((0, 8), (1, 4)))
    value_proj = scatter_about(streams_of[2], (TOKENS, D), 1.0, 6.0, ((0, 8), (1, 4)))
    filters = scatter_about(streams_of[3], (D, TAPS), TAPS ** -0.5, 0.5, ((0, 4),))
    out_weight = scatter_about(streams_of[4], (D, D), D ** -0.5, 0.0625, ((0, 4),))
    cotangent = bell_draw_with(streams_of[5], (TOKENS, D), 1.0, 6.0, ((0, 8), (1, 4)), (0, 1, 8, 2.0))
    return dict(query_proj=query_proj, key_proj=key_proj, value_proj=value_proj, filters=filters, out_weight=out_weight, cotangent=cotangent)


def reference(query_proj, key_proj, value_proj, filters, out_weight, cotangent):
    taps_t = filters.astype(jnp.float32).T
    product = (key_proj.astype(jnp.float32) * value_proj.astype(jnp.float32)).astype(jnp.bfloat16)
    padded = jnp.concatenate([jnp.zeros((TAPS - 1, D), jnp.float32), product.astype(jnp.float32)], axis=0)

    def add_tap(offset, running):
        start = (TAPS - 1 - offset).astype(jnp.int32)
        return running + lax.dynamic_slice_in_dim(padded, start, TOKENS, 0) * taps_t[offset]

    filtered = lax.fori_loop(0, TAPS, add_tap, jnp.zeros((TOKENS, D), jnp.float32))
    gated_rows = (query_proj.astype(jnp.float32) * filtered).astype(jnp.bfloat16)
    mixed = jnp.dot(gated_rows, out_weight, preferred_element_type=jnp.float32).astype(jnp.bfloat16)
    grad_gated = jnp.dot(cotangent, out_weight.T, preferred_element_type=jnp.float32)
    grad_query = (grad_gated * filtered).astype(jnp.bfloat16)
    grad_filtered = (grad_gated * query_proj.astype(jnp.float32)).astype(jnp.bfloat16)
    after = jnp.concatenate([grad_filtered.astype(jnp.float32), jnp.zeros((TAPS - 1, D), jnp.float32)], axis=0)

    def add_back(offset, running):
        start = offset.astype(jnp.int32)
        return running + lax.dynamic_slice_in_dim(after, start, TOKENS, 0) * taps_t[offset]

    grad_product = lax.fori_loop(0, TAPS, add_back, jnp.zeros((TOKENS, D), jnp.float32))
    grad_key = (grad_product * value_proj.astype(jnp.float32)).astype(jnp.bfloat16)
    grad_value = (grad_product * key_proj.astype(jnp.float32)).astype(jnp.bfloat16)
    grad_float = grad_filtered.astype(jnp.float32)

    def one_tap(offset):
        start = (TAPS - 1 - offset).astype(jnp.int32)
        return jnp.sum(grad_float * lax.dynamic_slice_in_dim(padded, start, TOKENS, 0), axis=0)

    grad_filters = lax.map(one_tap, jnp.arange(TAPS, dtype=jnp.int32)).T
    gated_blocks = gated_rows.reshape(N_CTX, TOK_DEV, D)
    cot_blocks = cotangent.reshape(N_CTX, TOK_DEV, D)

    def add_block(running, pair):
        block_term = jnp.dot(pair[0].T, pair[1], preferred_element_type=jnp.float32)
        rounded = lax.optimization_barrier(block_term.astype(jnp.bfloat16)).astype(jnp.float32)
        return running + rounded, None

    weight_sum, unused = lax.scan(add_block, jnp.zeros((D, D), jnp.float32), (gated_blocks, cot_blocks))
    grad_weight = weight_sum.astype(jnp.bfloat16)
    return (mixed, grad_query, grad_key, grad_value, grad_filters, grad_weight)
```

```python
import functools

import jax
import jax.numpy as jnp
import numpy as np
from jax import lax
from jax.experimental import pallas as pl
from jax.experimental.pallas import tpu as pltpu
from jax.sharding import PartitionSpec as P

F32 = jnp.float32
BF16 = jnp.bfloat16
VMEM_BYTES = 40 * 2**20
NT = (((1,), (1,)), ((), ()))
TN = (((0,), (0,)), ((), ()))


def halves(matrix):
    high = matrix.astype(BF16)
    low = (matrix - high.astype(np.float64)).astype(BF16)
    return np.stack([high, low])


def transforms(taps):
    points = 2 * taps
    angle = np.pi * (2 * np.arange(taps)[:, None] + 1) * np.arange(points)[None, :] / points
    forward = np.concatenate([np.cos(angle), -np.sin(angle)], axis=0)
    inverse = forward.T * (2.0 / points)
    late = inverse[taps:]
    early = inverse[:taps]
    lags = inverse[taps - np.arange(taps)]
    return halves(forward), halves(late), halves(early), halves(lags)


def mm(a, b, dims=(((1,), (0,)), ((), ()))):
    return lax.dot_general(a, b, dims, preferred_element_type=F32)


def spectrum(f_ref, rows):
    return mm(f_ref[0], rows) + mm(f_ref[1], rows)


def tap_spectrum(f_ref, filters, taps):
    return mm(f_ref[0, :, :taps], filters, NT) + mm(f_ref[1, :, :taps], filters, NT)


def back(g_ref, real, imag):
    both = jnp.concatenate([real, imag], axis=0)
    high = both.astype(BF16)
    low = (both - high.astype(F32)).astype(BF16)
    return mm(g_ref[0], high) + mm(g_ref[0], low) + mm(g_ref[1], high)


def forward_kernel(taps, q_ref, k_ref, v_ref, earlier_ref, filt_ref, f_ref, g_ref, gated_ref, filtered_ref):
    product = (k_ref[...].astype(F32) * v_ref[...].astype(F32)).astype(BF16)
    x = spectrum(f_ref, jnp.concatenate([earlier_ref[...], product], axis=0))
    h = tap_spectrum(f_ref, filt_ref[...], taps)
    xr, xi, hr, hi = x[:taps], x[taps:], h[:taps], h[taps:]
    filtered = back(g_ref, xr * hr - xi * hi, xr * hi + xi * hr)
    filtered_ref[...] = filtered
    gated_ref[...] = (q_ref[...].astype(F32) * filtered).astype(BF16)


def tap_grad_kernel(taps, k_ref, v_ref, earlier_ref, gf_ref, f_ref, g_ref, out_ref):
    product = (k_ref[...].astype(F32) * v_ref[...].astype(F32)).astype(BF16)
    x = spectrum(f_ref, jnp.concatenate([earlier_ref[...], product], axis=0))
    rows = gf_ref[...]
    g = mm(f_ref[0, :, :taps], rows) + mm(f_ref[1, :, :taps], rows)
    xr, xi, gr, gi = x[:taps], x[taps:], g[:taps], g[taps:]
    tap_rows = back(g_ref, xr * gr + xi * gi, xi * gr - xr * gi)
    out_ref[...] = tap_rows.T.astype(BF16)


def backward_kernel(taps, k_ref, v_ref, gf_ref, following_ref, filt_ref, f_ref, g_ref, gk_ref, gv_ref):
    g = spectrum(f_ref, jnp.concatenate([gf_ref[...], following_ref[...]], axis=0))
    h = tap_spectrum(f_ref, filt_ref[...], taps)
    gr, gi, hr, hi = g[:taps], g[taps:], h[:taps], h[taps:]
    grad_product = back(g_ref, hr * gr + hi * gi, hr * gi - hi * gr)
    gk_ref[...] = (grad_product * v_ref[...].astype(F32)).astype(BF16)
    gv_ref[...] = (grad_product * k_ref[...].astype(F32)).astype(BF16)


def by_channel(kernel, arrays, kinds, outs, name, flops):
    width = 256
    length, channels = arrays[0].shape
    specs = {
        "t": pl.BlockSpec((length, width), lambda i: (0, i)),
        "c": pl.BlockSpec((width, length), lambda i: (i, 0)),
    }

    def spec_of(kind, shape):
        if kind == "w":
            return pl.BlockSpec(shape, lambda i: (0,) * len(shape))
        return specs[kind]

    return pl.pallas_call(
        functools.partial(kernel, length),
        grid=(channels // width,),
        in_specs=[spec_of(kind, a.shape) for kind, a in zip(kinds, arrays)],
        out_specs=[specs[kind] for kind, unused in outs],
        out_shape=[
            jax.ShapeDtypeStruct((length, channels) if kind == "t" else (channels, length), dtype)
            for kind, dtype in outs
        ],
        compiler_params=pltpu.CompilerParams(vmem_limit_bytes=VMEM_BYTES),
        cost_estimate=pl.CostEstimate(flops=flops, bytes_accessed=sum(a.nbytes for a in arrays), transcendentals=0),
        name=name,
    )(*arrays)


def grad_gated_kernel(has_sum, ids_ref, cot_ref, w_ref, *refs):
    total = mm(cot_ref[...], w_ref[...], NT)
    if has_sum:
        total = total + refs[0][...]
    refs[-1][...] = total


def grad_gated_part(cot, weight, block, running):
    length, width = cot.shape
    channels = weight.shape[0]
    tile = 256
    arrays = [cot, weight]
    in_specs = [
        pl.BlockSpec((length, width), lambda i, ids: (0, 0)),
        pl.BlockSpec((tile, width), lambda i, ids: (i, ids[0])),
    ]
    if running is not None:
        arrays.append(running)
        in_specs.append(pl.BlockSpec((length, tile), lambda i, ids: (0, i)))
    return pl.pallas_call(
        functools.partial(grad_gated_kernel, running is not None),
        grid_spec=pltpu.PrefetchScalarGridSpec(
            num_scalar_prefetch=1,
            grid=(channels // tile,),
            in_specs=in_specs,
            out_specs=pl.BlockSpec((length, tile), lambda i, ids: (0, i)),
        ),
        out_shape=jax.ShapeDtypeStruct((length, channels), F32),
        compiler_params=pltpu.CompilerParams(vmem_limit_bytes=VMEM_BYTES),
        cost_estimate=pl.CostEstimate(
            flops=2 * length * width * channels, bytes_accessed=2 * width * channels, transcendentals=0
        ),
        name="grad_gated_part",
    )(jnp.reshape(block, (1,)), *arrays)


def mixed_kernel(adds, ids_ref, gated_ref, w_ref, *refs):
    total = mm(gated_ref[...], w_ref[...])
    for ref in refs[:adds]:
        total = total + ref[...].astype(F32)
    refs[-1][...] = total.astype(refs[-1].dtype)


def mixed_part(gated, weight, blocks, received, kind):
    length, channels = gated.shape
    width = channels
    tile = 512
    steps = width // tile
    ids = jnp.stack([jnp.stack(blocks)] + [jnp.asarray(at, jnp.int32) for unused, at in received])
    in_specs = [
        pl.BlockSpec((length, channels), lambda b, t, ids: (0, 0)),
        pl.BlockSpec((channels, tile), lambda b, t, ids: (0, ids[0, b] * steps + t)),
    ]
    for place in range(len(received)):
        in_specs.append(
            pl.BlockSpec((length, tile), lambda b, t, ids, place=place: (0, ids[place + 1, b] * steps + t))
        )
    return pl.pallas_call(
        functools.partial(mixed_kernel, len(received)),
        grid_spec=pltpu.PrefetchScalarGridSpec(
            num_scalar_prefetch=1,
            grid=(len(blocks), steps),
            in_specs=in_specs,
            out_specs=pl.BlockSpec((length, tile), lambda b, t, ids: (0, b * steps + t)),
        ),
        out_shape=jax.ShapeDtypeStruct((length, width * len(blocks)), kind),
        compiler_params=pltpu.CompilerParams(vmem_limit_bytes=VMEM_BYTES),
        cost_estimate=pl.CostEstimate(
            flops=2 * length * channels * width * len(blocks),
            bytes_accessed=2 * channels * width * len(blocks),
            transcendentals=0,
        ),
        name="mixed_part",
    )(ids, gated, weight, *[array for array, unused in received])


def weight_kernel(slots, parts, half, ids_ref, *refs):
    gated_refs = refs[: slots - 1]
    far_low, far_high = refs[slots - 1 : slots + 1]
    cot_refs = refs[slots + 1 : slots + 1 + parts]
    out_ref = refs[-1]
    length = far_low.shape[0]
    piece = cot_refs[0].shape[1]
    far = jnp.where(pl.program_id(0) < half, far_low[...], far_high[...])
    columns = jnp.concatenate([ref[...] for ref in gated_refs] + [far], axis=0)
    for part in range(parts):
        rows = [
            cot_refs[part][pl.ds(pl.multiple_of(ids_ref[part, slot] * length, length), length), :]
            for slot in range(slots)
        ]
        total = mm(columns, jnp.concatenate(rows, axis=0), TN)
        place = pl.multiple_of(ids_ref[part, slots] * piece, piece)
        out_ref[:, pl.ds(place, piece)] = total.astype(BF16)


def grad_weight_of(blocks, far_low, far_high, cots, ids):
    length, channels = blocks[0].shape
    rows, piece = cots[0].shape
    tile = 256
    half = channels // tile // 2
    slots, parts = len(blocks) + 1, len(cots)
    in_specs = [pl.BlockSpec((length, tile), lambda i, ids: (0, i)) for unused in blocks]
    in_specs.append(pl.BlockSpec((length, tile), lambda i, ids: (0, jnp.minimum(i, half - 1))))
    in_specs.append(pl.BlockSpec((length, tile), lambda i, ids: (0, jnp.maximum(i - half, 0))))
    in_specs += [pl.BlockSpec((rows, piece), lambda i, ids: (0, 0)) for unused in cots]
    return pl.pallas_call(
        functools.partial(weight_kernel, slots, parts, half),
        grid_spec=pltpu.PrefetchScalarGridSpec(
            num_scalar_prefetch=1,
            grid=(channels // tile,),
            in_specs=in_specs,
            out_specs=pl.BlockSpec((tile, piece * parts), lambda i, ids: (i, 0)),
        ),
        out_shape=jax.ShapeDtypeStruct((channels, piece * parts), BF16),
        compiler_params=pltpu.CompilerParams(vmem_limit_bytes=VMEM_BYTES),
        cost_estimate=pl.CostEstimate(
            flops=2 * rows * channels * piece * parts, bytes_accessed=4 * rows * channels, transcendentals=0
        ),
        name="grad_weight",
    )(ids, *blocks, far_low, far_high, *cots)


def in_one_piece(columns, ids, length):
    slots, piece = ids.shape[1] - 1, columns[0].shape[1]
    whole = jnp.zeros((slots * length, piece * len(columns)), columns[0].dtype)
    for part, column in enumerate(columns):
        rows = [lax.dynamic_slice_in_dim(column, ids[part, slot] * length, length, 0) for slot in range(slots)]
        whole = lax.dynamic_update_slice_in_dim(whole, jnp.concatenate(rows, axis=0), ids[part, slots] * piece, 1)
    return [whole], jnp.asarray([list(range(slots)) + [0]], jnp.int32)


def cycle_of(count):
    across = 1 << ((count.bit_length() - 1) // 2)
    order = []
    for column in range(across):
        line = [row * across + column for row in range(count // across)]
        order += line if column % 2 == 0 else line[::-1]
    return order


def swap(block, axis, bit):
    size = lax.axis_size(axis)
    return lax.ppermute(block, axis, [(i, i ^ bit) for i in range(size)])


def bits_of(size):
    return [1 << place for place in range(size.bit_length() - 1)]


def gather_by_swaps(block):
    held = {0: block}
    for bit in reversed(bits_of(lax.axis_size("chan"))):
        held.update({off ^ bit: swap(held[off], "chan", bit) for off in list(held)})
    return held


def sum_over_ctx(local):
    me = lax.axis_index("ctx")
    bits = bits_of(lax.axis_size("ctx"))
    part = local
    for bit in bits:
        middle = part.shape[0] // 2
        mine = (me & bit) != 0
        keep = jnp.where(mine, part[middle:], part[:middle])
        give = jnp.where(mine, part[:middle], part[middle:])
        part = (keep.astype(F32) + swap(give, "ctx", bit).astype(F32)).astype(BF16)
    for bit in reversed(bits):
        mine = (me & bit) != 0
        other = swap(part, "ctx", bit)
        part = jnp.concatenate([jnp.where(mine, other, part), jnp.where(mine, part, other)], axis=0)
    return part.astype(F32)


def per_device(query_proj, key_proj, value_proj, filters, out_weight, cotangent):
    length, channels = query_proj.shape
    taps = filters.shape[1]
    n_ctx, n_chan = lax.axis_size("ctx"), lax.axis_size("chan")
    ctx, chan = lax.axis_index("ctx"), lax.axis_index("chan")
    per_chan = n_ctx // n_chan
    forward, late, early, lags = [jnp.asarray(m) for m in transforms(taps)]

    product = (key_proj.astype(F32) * value_proj.astype(F32)).astype(BF16)
    earlier = lax.ppermute(product, "ctx", [(i, i + 1) for i in range(n_ctx - 1)])

    cots = gather_by_swaps(cotangent)

    piece = channels // n_ctx
    turned = lax.dynamic_slice_in_dim(jnp.concatenate([cotangent, cotangent], axis=1), ctx * piece, channels, 1)
    pieces = []
    for step in range(n_ctx):
        route = []
        for c in range(n_ctx):
            for h in range(n_chan):
                place = (c + step) % n_ctx
                target = (h * per_chan + place // n_chan) * n_chan + place % n_chan
                route.append((c * n_chan + h, target))
        pieces.append(lax.ppermute(turned[:, step * piece : (step + 1) * piece], ("ctx", "chan"), route))
    column_cots = gather_by_swaps(jnp.concatenate(pieces, axis=0))

    grad_gated = None
    for off in sorted(cots):
        grad_gated = grad_gated_part(cots[off], out_weight, chan ^ off, grad_gated)

    gated, filtered = by_channel(
        forward_kernel,
        [query_proj, key_proj, value_proj, earlier, filters, forward, late],
        "ttttcww",
        [("t", BF16), ("t", F32)],
        "forward_filter",
        6 * 10**9,
    )

    order = cycle_of(n_ctx)
    ahead = [(order[i], order[(i + 1) % n_ctx]) for i in range(n_ctx)]
    behind = [(b, a) for a, b in ahead]
    half = channels // 2
    from_behind, from_ahead = gated, gated
    blocks = [gated]
    for step in range(n_ctx // 2 - 1):
        from_behind = lax.ppermute(from_behind, "ctx", ahead)
        from_ahead = lax.ppermute(from_ahead, "ctx", behind)
        blocks += [from_behind, from_ahead]
    far_low = lax.ppermute(from_behind[:, :half], "ctx", ahead)
    far_high = lax.ppermute(from_ahead[:, half:], "ctx", behind)

    grad_query = (grad_gated * filtered).astype(BF16)
    grad_filtered = (grad_gated * query_proj.astype(F32)).astype(BF16)
    following = lax.ppermute(grad_filtered, "ctx", [(i + 1, i) for i in range(n_ctx - 1)])

    received = []
    left = list(range(n_chan))
    for bit in bits_of(n_chan):
        give = [off for off in left if off & bit]
        left = [off for off in left if not off & bit]
        sums = [(array, [offs.index(off) for off in give]) for array, offs in received]
        part = mixed_part(gated, out_weight, [chan ^ off for off in give], sums, BF16)
        received.append((swap(part, "chan", bit), [off ^ bit for off in give]))
    last = received.pop()[0]
    own = mixed_part(
        gated, out_weight, [chan], [(array, [offs.index(0)]) for array, offs in received], F32
    )
    mixed = (own + last.astype(F32)).astype(BF16)

    tap_grad = by_channel(
        tap_grad_kernel,
        [key_proj, value_proj, earlier, grad_filtered, forward, lags],
        "ttttww",
        [("c", BF16)],
        "tap_grad",
        6 * 10**9,
    )[0]
    grad_filters = sum_over_ctx(tap_grad)
    grad_key, grad_value = by_channel(
        backward_kernel,
        [key_proj, value_proj, grad_filtered, following, filters, forward, early],
        "ttttcww",
        [("t", BF16), ("t", BF16)],
        "backward_filter",
        6 * 10**9,
    )

    ring = jnp.asarray(order, jnp.int32)
    spot = jnp.asarray(np.argsort(order), jnp.int32)[ctx]
    owners = [spot]
    for step in range(1, n_ctx // 2):
        owners += [spot - step, spot + step]
    owners.append(spot + n_ctx // 2)
    tokens = ring[jnp.mod(jnp.stack(owners), n_ctx)]
    rows = []
    for off in sorted(column_cots):
        column = chan ^ off
        base = (ctx % per_chan) * n_chan + column
        rows.append(jnp.concatenate([jnp.mod(base - tokens, n_ctx), column[None]]))
    ids = jnp.stack(rows).astype(jnp.int32)
    columns = [column_cots[off] for off in sorted(column_cots)]
    if piece % 128:
        columns, ids = in_one_piece(columns, ids, length)
    grad_weight = grad_weight_of(blocks, far_low, far_high, columns, ids)
    return (mixed, grad_query, grad_key, grad_value, grad_filters, grad_weight)


def solution(mesh):
    placed = (
        P("ctx", "chan"),
        P("ctx", "chan"),
        P("ctx", "chan"),
        P("chan", None),
        P("chan", None),
        P("ctx", "chan"),
    )
    return jax.shard_map(
        per_device,
        mesh=mesh,
        in_specs=placed,
        out_specs=(
            P("ctx", "chan"),
            P("ctx", "chan"),
            P("ctx", "chan"),
            P("ctx", "chan"),
            P("chan", None),
            P("chan", "ctx"),
        ),
        check_vma=False,
    )
```

```python
import functools

import jax
import jax.numpy as jnp
import numpy as np
from jax import lax
from jax.experimental import pallas as pl
from jax.experimental.pallas import tpu as pltpu
from jax.sharding import PartitionSpec as P

F32 = jnp.float32
BF16 = jnp.bfloat16
VMEM_BYTES = 40 * 2**20
NT = (((1,), (1,)), ((), ()))
TN = (((0,), (0,)), ((), ()))


def halves(matrix):
    high = matrix.astype(BF16)
    low = (matrix - high.astype(np.float64)).astype(BF16)
    return np.stack([high, low])


def transforms(taps):
    points = 2 * taps
    angle = np.pi * (2 * np.arange(taps)[:, None] + 1) * np.arange(points)[None, :] / points
    forward = np.concatenate([np.cos(angle), -np.sin(angle)], axis=0)
    inverse = forward.T * (2.0 / points)
    late = inverse[taps:]
    early = inverse[:taps]
    lags = inverse[taps - np.arange(taps)]
    return halves(forward), halves(late), halves(early), halves(lags)


def mm(a, b, dims=(((1,), (0,)), ((), ()))):
    return lax.dot_general(a, b, dims, preferred_element_type=F32)


def spectrum(f_ref, rows):
    return mm(f_ref[0], rows) + mm(f_ref[1], rows)


def tap_spectrum(f_ref, filters, taps):
    return mm(f_ref[0, :, :taps], filters, NT) + mm(f_ref[1, :, :taps], filters, NT)


def back(g_ref, real, imag):
    both = jnp.concatenate([real, imag], axis=0)
    high = both.astype(BF16)
    low = (both - high.astype(F32)).astype(BF16)
    return mm(g_ref[0], high) + mm(g_ref[0], low) + mm(g_ref[1], high)


def forward_kernel(taps, q_ref, k_ref, v_ref, earlier_ref, filt_ref, f_ref, g_ref, gated_ref, filtered_ref):
    product = (k_ref[...].astype(F32) * v_ref[...].astype(F32)).astype(BF16)
    x = spectrum(f_ref, jnp.concatenate([earlier_ref[...], product], axis=0))
    h = tap_spectrum(f_ref, filt_ref[...], taps)
    xr, xi, hr, hi = x[:taps], x[taps:], h[:taps], h[taps:]
    filtered = back(g_ref, xr * hr - xi * hi, xr * hi + xi * hr)
    filtered_ref[...] = filtered
    gated_ref[...] = (q_ref[...].astype(F32) * filtered).astype(BF16)


def tap_grad_kernel(taps, k_ref, v_ref, earlier_ref, gf_ref, f_ref, g_ref, out_ref):
    product = (k_ref[...].astype(F32) * v_ref[...].astype(F32)).astype(BF16)
    x = spectrum(f_ref, jnp.concatenate([earlier_ref[...], product], axis=0))
    rows = gf_ref[...]
    g = mm(f_ref[0, :, :taps], rows) + mm(f_ref[1, :, :taps], rows)
    xr, xi, gr, gi = x[:taps], x[taps:], g[:taps], g[taps:]
    tap_rows = back(g_ref, xr * gr + xi * gi, xi * gr - xr * gi)
    out_ref[...] = tap_rows.T.astype(BF16)


def backward_kernel(taps, k_ref, v_ref, gf_ref, following_ref, filt_ref, f_ref, g_ref, gk_ref, gv_ref):
    g = spectrum(f_ref, jnp.concatenate([gf_ref[...], following_ref[...]], axis=0))
    h = tap_spectrum(f_ref, filt_ref[...], taps)
    gr, gi, hr, hi = g[:taps], g[taps:], h[:taps], h[taps:]
    grad_product = back(g_ref, hr * gr + hi * gi, hr * gi - hi * gr)
    gk_ref[...] = (grad_product * v_ref[...].astype(F32)).astype(BF16)
    gv_ref[...] = (grad_product * k_ref[...].astype(F32)).astype(BF16)


def estimate(flops, bytes_accessed):
    return pl.CostEstimate(flops=flops, bytes_accessed=bytes_accessed, transcendentals=0)


def by_channel(kernel, arrays, kinds, outs, name, me=None):
    length, channels = arrays[0].shape
    width = min(512, channels) if me is None else 256
    specs = {
        "t": pl.BlockSpec((length, width), lambda i, *ids: (0, i)),
        "c": pl.BlockSpec((width, length), lambda i, *ids: (i, 0)),
        "x": pl.BlockSpec((width, length), lambda i, *ids: (i ^ ids[0][0], 0)),
    }

    def spec_of(kind, shape):
        if kind == "w":
            return pl.BlockSpec(shape, lambda i, *ids: (0,) * len(shape))
        return specs[kind]

    body = functools.partial(kernel, length)
    return pl.pallas_call(
        body if me is None else lambda ids_ref, *refs: body(*refs),
        grid_spec=pltpu.PrefetchScalarGridSpec(
            num_scalar_prefetch=0 if me is None else 1,
            grid=(channels // width,),
            in_specs=[spec_of(kind, a.shape) for kind, a in zip(kinds, arrays)],
            out_specs=[specs[kind] for kind, unused in outs],
        ),
        out_shape=[
            jax.ShapeDtypeStruct((length, channels) if kind == "t" else (channels, length), dtype)
            for kind, dtype in outs
        ],
        compiler_params=pltpu.CompilerParams(vmem_limit_bytes=VMEM_BYTES),
        cost_estimate=estimate(10**9, 4 * 2**20),
        name=name,
    )(*([] if me is None else [me]), *arrays)


def grad_gated_kernel(kind, me_ref, cot_ref, w_ref, *refs):
    total = mm(w_ref[...], cot_ref[...], NT).T
    if kind == "first":
        refs[-1][...] = total
        return
    total = total + refs[0][...]
    if kind == "middle":
        refs[-1][...] = total
        return
    q_ref, filtered_ref, gq_ref, gf_ref = refs[1:]
    gq_ref[...] = (total * filtered_ref[...]).astype(BF16)
    gf_ref[...] = (total * q_ref[...].astype(F32)).astype(BF16)


def grad_gated_part(kind, me, cot, weight, off, arrays):
    length, width = cot.shape
    channels = weight.shape[0]
    tile = 512
    row_spec = pl.BlockSpec((length, tile), lambda i, me: (0, i))
    kinds = [BF16, BF16] if kind == "last" else [F32]
    return pl.pallas_call(
        functools.partial(grad_gated_kernel, kind),
        grid_spec=pltpu.PrefetchScalarGridSpec(
            num_scalar_prefetch=1,
            grid=(channels // tile,),
            in_specs=[
                pl.BlockSpec((length, width), lambda i, me: (0, 0)),
                pl.BlockSpec((tile, width), lambda i, me: (i, me[1] ^ off)),
            ]
            + [row_spec] * len(arrays),
            out_specs=[row_spec] * len(kinds),
        ),
        out_shape=[jax.ShapeDtypeStruct((length, channels), dtype) for dtype in kinds],
        compiler_params=pltpu.CompilerParams(vmem_limit_bytes=VMEM_BYTES),
        cost_estimate=estimate(2 * length * width * channels, 2 * width * channels),
        name="grad_gated_" + kind,
    )(me, cot, weight, *arrays)


def mixed_kernel(adds, me_ref, gated_ref, w_ref, *refs):
    total = mm(gated_ref[...], w_ref[...])
    for ref in refs[:adds]:
        total = total + ref[...].astype(F32)
    refs[-1][...] = total.astype(refs[-1].dtype)


def mixed_part(me, gated, weight, offs, received, kind):
    length, channels = gated.shape
    tile = 512
    steps = channels // tile

    def column(b):
        return offs[0] + b * (offs[1] - offs[0] if len(offs) > 1 else 0)

    in_specs = [
        pl.BlockSpec((length, channels), lambda b, t, me: (0, 0)),
        pl.BlockSpec((channels, tile), lambda b, t, me: (0, (me[1] ^ column(b)) * steps + t)),
    ]
    for unused, (start, stride) in received:
        in_specs.append(
            pl.BlockSpec(
                (length, tile), lambda b, t, me, start=start, stride=stride: (0, (start + b * stride) * steps + t)
            )
        )
    return pl.pallas_call(
        functools.partial(mixed_kernel, len(received)),
        grid_spec=pltpu.PrefetchScalarGridSpec(
            num_scalar_prefetch=1,
            grid=(len(offs), steps),
            in_specs=in_specs,
            out_specs=pl.BlockSpec((length, tile), lambda b, t, me: (0, b * steps + t)),
        ),
        out_shape=jax.ShapeDtypeStruct((length, channels * len(offs)), kind),
        compiler_params=pltpu.CompilerParams(vmem_limit_bytes=VMEM_BYTES),
        cost_estimate=estimate(2 * length * channels * channels * len(offs), 2 * channels * channels * len(offs)),
        name="mixed_part",
    )(me, gated, weight, *[array for array, unused in received])


def pieces_kernel(per_chan, me_ref, *refs):
    out_ref = refs[-1]
    length, width = refs[0].shape
    span = width // per_chan
    count = len(refs) - 1
    piece = span // count
    for off in range(count):
        for part in range(per_chan):
            target = (me_ref[1] ^ off) * per_chan + part
            start = pl.multiple_of(part * span + me_ref[1] * piece, 128)
            block = refs[off][:, pl.ds(start, piece)]
            out_ref[target ^ me_ref[0]] = jnp.concatenate(
                [block[:, at : at + 128] for at in range(0, piece, 128)], axis=0
            )


def pieces_of(me, cots, n_ctx):
    length, width = cots[0].shape
    piece = width // n_ctx
    rows = length * piece // 128
    if piece % 128:
        return pieces_by_slices(me, cots, n_ctx)
    return pl.pallas_call(
        functools.partial(pieces_kernel, n_ctx // len(cots)),
        grid_spec=pltpu.PrefetchScalarGridSpec(
            num_scalar_prefetch=1,
            grid=(1,),
            in_specs=[pl.BlockSpec((length, width), lambda i, me: (0, 0))] * len(cots),
            out_specs=pl.BlockSpec((n_ctx, rows, 128), lambda i, me: (0, 0, 0)),
        ),
        out_shape=jax.ShapeDtypeStruct((n_ctx, rows, 128), BF16),
        compiler_params=pltpu.CompilerParams(vmem_limit_bytes=VMEM_BYTES),
        cost_estimate=estimate(10**6, 2**20),
        name="pieces",
    )(me, *cots)


def pieces_by_slices(me, cots, n_ctx):
    length, width = cots[0].shape
    count = len(cots)
    piece = width // n_ctx
    table = jnp.stack(cots).reshape(count, length, n_ctx // count, count, piece)
    mine = lax.dynamic_index_in_dim(table, me[1], 3, False)
    parts = mine.transpose(0, 2, 1, 3).reshape(n_ctx, length * piece // 128, 128)
    order = jnp.arange(n_ctx, dtype=jnp.int32) ^ me[0]
    per_chan = n_ctx // count
    return parts[(order // per_chan ^ me[1]) * per_chan + order % per_chan]


def weight_kernel(slots, parts, half, me_ref, owner_ref, *refs):
    gated_refs = refs[: slots - 1]
    far_low, far_high = refs[slots - 1 : slots + 1]
    cot_refs = refs[slots + 1 : slots + 1 + parts]
    out_ref = refs[-1]
    length = far_low.shape[0]
    far = jnp.where(pl.program_id(0) < half, far_low[...], far_high[...])
    columns = jnp.concatenate([ref[...] for ref in gated_refs] + [far], axis=0)
    for part in range(parts):
        rows = []
        for slot in range(slots):
            block = cot_refs[part][owner_ref[me_ref[0], slot]]
            rows.append(
                jnp.concatenate([block[at : at + length] for at in range(0, block.shape[0], length)], axis=1)
            )
        total = mm(columns, jnp.concatenate(rows, axis=0), TN)
        piece = total.shape[1]
        place = pl.multiple_of((me_ref[1] ^ part) * piece, piece) if parts > 1 else 0
        out_ref[:, pl.ds(place, piece)] = total.astype(BF16)


def grad_weight_of(me, owners, blocks, far_low, far_high, cots):
    length, channels = blocks[0].shape
    rows = cots[0].shape[1]
    piece = rows * 128 // length
    tile = 256
    half = channels // tile // 2
    slots, parts = len(blocks) + 1, len(cots)
    in_specs = [pl.BlockSpec((length, tile), lambda i, *ids: (0, i)) for unused in blocks]
    in_specs.append(pl.BlockSpec((length, tile), lambda i, *ids: (0, jnp.minimum(i, half - 1))))
    in_specs.append(pl.BlockSpec((length, tile), lambda i, *ids: (0, jnp.maximum(i - half, 0))))
    in_specs += [pl.BlockSpec(cot.shape, lambda i, *ids: (0, 0, 0)) for cot in cots]
    return pl.pallas_call(
        functools.partial(weight_kernel, slots, parts, half),
        grid_spec=pltpu.PrefetchScalarGridSpec(
            num_scalar_prefetch=2,
            grid=(channels // tile,),
            in_specs=in_specs,
            out_specs=pl.BlockSpec((tile, piece * parts), lambda i, *ids: (i, 0)),
        ),
        out_shape=jax.ShapeDtypeStruct((channels, piece * parts), BF16),
        compiler_params=pltpu.CompilerParams(vmem_limit_bytes=VMEM_BYTES),
        cost_estimate=estimate(2 * slots * length * channels * piece * parts, 12 * 2**20),
        name="grad_weight",
    )(me, owners, *blocks, far_low, far_high, *cots)


def place_kernel(me_ref, in_ref, out_ref):
    out_ref[...] = in_ref[...].astype(out_ref.dtype)


def placed_blocks(me, blocks):
    count, rows, width = blocks.shape
    return pl.pallas_call(
        place_kernel,
        grid_spec=pltpu.PrefetchScalarGridSpec(
            num_scalar_prefetch=1,
            grid=(count,),
            in_specs=[pl.BlockSpec((None, rows, width), lambda i, me: (i ^ me[0], 0, 0))],
            out_specs=pl.BlockSpec((rows, width), lambda i, me: (i, 0)),
        ),
        out_shape=jax.ShapeDtypeStruct((count * rows, width), F32),
        compiler_params=pltpu.CompilerParams(vmem_limit_bytes=VMEM_BYTES),
        cost_estimate=estimate(10**6, 2 * 2**20),
        name="placed_blocks",
    )(me, blocks)


def in_one_piece(me, columns, length):
    count, rows, unused = columns[0].shape
    table = jnp.stack(columns)[jnp.arange(len(columns), dtype=jnp.int32) ^ me[1]]
    piece = rows * 128 // length
    flat = table.reshape(len(columns), count, length, piece).transpose(1, 2, 0, 3)
    flat = flat.reshape(count, length, piece * len(columns) // 128, 128).transpose(0, 2, 1, 3)
    return [flat.reshape(count, -1, 128)]


def cycle_of(count):
    across = 1 << ((count.bit_length() - 1) // 2)
    order = []
    for column in range(across):
        line = [row * across + column for row in range(count // across)]
        order += line if column % 2 == 0 else line[::-1]
    return order


def swap(block, axis, bit):
    size = lax.axis_size(axis)
    return lax.ppermute(block, axis, [(i, i ^ bit) for i in range(size)])


def bits_of(size):
    return [1 << place for place in range(size.bit_length() - 1)]


def gather_by_swaps(block):
    held = {0: block}
    for bit in reversed(bits_of(lax.axis_size("chan"))):
        held.update({off ^ bit: swap(held[off], "chan", bit) for off in list(held)})
    return held


def sum_and_exchange(partial, pieces):
    count = pieces.shape[0]
    sums, held, sources = partial, pieces[None], [0]
    for bit in bits_of(count):
        give = held[:, 1::2].reshape((-1,) + pieces.shape[1:])
        if partial.shape[1:] == pieces.shape[1:]:
            came = swap(jnp.concatenate([sums[1::2], give], axis=0), "ctx", bit)
            others, came = came[: sums.shape[0] // 2], came[sums.shape[0] // 2 :]
        else:
            others, came = swap(sums[1::2], "ctx", bit), swap(give, "ctx", bit)
        sums = (sums[::2].astype(F32) + others.astype(F32)).astype(BF16)
        held = jnp.concatenate([held[:, ::2], came.reshape((len(sources), -1) + pieces.shape[1:])], axis=0)
        sources += [source ^ bit for source in sources]
    return sums, held[:, 0], sources


def doubled(block, axis):
    held = block
    for bit in reversed(bits_of(lax.axis_size(axis))):
        held = jnp.stack([held, swap(held, axis, bit)], axis=1).reshape((-1,) + block.shape[1:])
    return held


def per_device(query_proj, key_proj, value_proj, filters, out_weight, cotangent):
    length, channels = query_proj.shape
    taps = filters.shape[1]
    n_ctx, n_chan = lax.axis_size("ctx"), lax.axis_size("chan")
    me = jnp.stack([lax.axis_index("ctx"), lax.axis_index("chan")]).astype(jnp.int32)
    forward, late, early, lags = [jnp.asarray(m) for m in transforms(taps)]

    product = (key_proj.astype(F32) * value_proj.astype(F32)).astype(BF16)
    earlier = lax.ppermute(product, "ctx", [(i, i + 1) for i in range(n_ctx - 1)])

    cots = gather_by_swaps(cotangent)
    grad_gated = []
    for off in range(n_chan - 1):
        grad_gated = grad_gated_part("middle" if off else "first", me, cots[off], out_weight, off, grad_gated)
        grad_gated = list(grad_gated)

    gated, filtered = by_channel(
        forward_kernel,
        [query_proj, key_proj, value_proj, earlier, filters, forward, late],
        "ttttcww",
        [("t", BF16), ("t", F32)],
        "forward_filter",
    )

    order = cycle_of(n_ctx)
    ahead = [(order[i], order[(i + 1) % n_ctx]) for i in range(n_ctx)]
    behind = [(b, a) for a, b in ahead]
    half = channels // 2
    from_behind, from_ahead = gated, gated
    blocks = [gated]
    for step in range(n_ctx // 2 - 1):
        from_behind = lax.ppermute(from_behind, "ctx", ahead)
        from_ahead = lax.ppermute(from_ahead, "ctx", behind)
        blocks += [from_behind, from_ahead]
    far_low = lax.ppermute(from_behind[:, :half], "ctx", ahead)
    far_high = lax.ppermute(from_ahead[:, half:], "ctx", behind)

    grad_query, grad_filtered = grad_gated_part(
        "last", me, cots[n_chan - 1], out_weight, n_chan - 1, grad_gated + [query_proj, filtered]
    )
    following = lax.ppermute(grad_filtered, "ctx", [(i + 1, i) for i in range(n_ctx - 1)])

    received = []
    left = list(range(n_chan))
    for bit in bits_of(n_chan):
        give = left[1::2]
        left = left[::2]
        stride = give[1] - give[0] if len(give) > 1 else 1
        sums = [(array, ((give[0] - offs[0]) // step, stride // step)) for array, offs, step in received]
        part = mixed_part(me, gated, out_weight, give, sums, BF16)
        received.append((swap(part, "chan", bit), [off ^ bit for off in give], stride))
    last = received.pop()[0]
    own = mixed_part(me, gated, out_weight, [0], [(array, (0, 1)) for array, offs, step in received], F32)
    mixed = (own + last.astype(F32)).astype(BF16)

    direct = channels // n_ctx == 256
    tap_grad = by_channel(
        tap_grad_kernel,
        [key_proj, value_proj, earlier, grad_filtered, forward, lags],
        "ttttww",
        [("x" if direct else "c", BF16)],
        "tap_grad",
        me,
    )[0].reshape(n_ctx, -1, taps)
    if not direct:
        tap_grad = tap_grad[jnp.arange(n_ctx, dtype=jnp.int32) ^ me[0]]
    pieces = pieces_of(me, [cots[off] for off in range(n_chan)], n_ctx)
    tap_sum, held, sources = sum_and_exchange(tap_grad, pieces)
    grad_filters = placed_blocks(me, doubled(tap_sum, "ctx"))
    grad_key, grad_value = by_channel(
        backward_kernel,
        [key_proj, value_proj, grad_filtered, following, filters, forward, early],
        "ttttcww",
        [("t", BF16), ("t", BF16)],
        "backward_filter",
    )

    columns = gather_by_swaps(held)
    columns = [columns[off] for off in range(n_chan)]
    if (channels // n_ctx) % 128:
        columns = in_one_piece(me, columns, length)
    owners = []
    for c in range(n_ctx):
        spot = order.index(c)
        steps = [0] + [sign * step for step in range(1, n_ctx // 2) for sign in (-1, 1)] + [n_ctx // 2]
        owners.append([sources.index(order[(spot + step) % n_ctx] ^ c) for step in steps])
    grad_weight = grad_weight_of(me, jnp.asarray(owners, jnp.int32), blocks, far_low, far_high, columns)
    return (mixed, grad_query, grad_key, grad_value, grad_filters, grad_weight)


def solution(mesh):
    placed = (
        P("ctx", "chan"),
        P("ctx", "chan"),
        P("ctx", "chan"),
        P("chan", None),
        P("chan", None),
        P("ctx", "chan"),
    )
    return jax.shard_map(
        per_device,
        mesh=mesh,
        in_specs=placed,
        out_specs=(
            P("ctx", "chan"),
            P("ctx", "chan"),
            P("ctx", "chan"),
            P("ctx", "chan"),
            P("chan", None),
            P("chan", "ctx"),
        ),
        check_vma=False,
    )
```

```python
import functools

import jax
import jax.numpy as jnp
import numpy as np
from jax import lax
from jax.experimental import pallas as pl
from jax.experimental.pallas import tpu as pltpu
from jax.sharding import PartitionSpec as P

F32 = jnp.float32
BF16 = jnp.bfloat16
VMEM_BYTES = 40 * 2**20
STREAMS = 4
NT = (((1,), (1,)), ((), ()))
TN = (((0,), (0,)), ((), ()))


def halves(matrix):
    high = matrix.astype(BF16)
    low = (matrix - high.astype(np.float64)).astype(BF16)
    return np.stack([high, low])


def transforms(taps):
    points = 2 * taps
    angle = np.pi * (2 * np.arange(taps)[:, None] + 1) * np.arange(points)[None, :] / points
    forward = np.concatenate([np.cos(angle), -np.sin(angle)], axis=0)
    inverse = forward.T * (2.0 / points)
    late = inverse[taps:]
    early = inverse[:taps]
    lags = inverse[taps - np.arange(taps)]
    return halves(forward), halves(late), halves(early), halves(lags)


def mm(a, b, dims=(((1,), (0,)), ((), ()))):
    return lax.dot_general(a, b, dims, preferred_element_type=F32)


def spectrum(f_ref, rows):
    return mm(f_ref[0], rows) + mm(f_ref[1], rows)


def tap_spectrum(f_ref, filters, taps):
    return mm(f_ref[0, :, :taps], filters, NT) + mm(f_ref[1, :, :taps], filters, NT)


def back(g_ref, real, imag):
    both = jnp.concatenate([real, imag], axis=0)
    high = both.astype(BF16)
    low = (both - high.astype(F32)).astype(BF16)
    return mm(g_ref[0], high) + mm(g_ref[0], low) + mm(g_ref[1], high)


def forward_kernel(taps, q_ref, k_ref, v_ref, earlier_ref, filt_ref, f_ref, g_ref, gated_ref, filtered_ref):
    product = (k_ref[...].astype(F32) * v_ref[...].astype(F32)).astype(BF16)
    x = spectrum(f_ref, jnp.concatenate([earlier_ref[...], product], axis=0))
    h = tap_spectrum(f_ref, filt_ref[...], taps)
    xr, xi, hr, hi = x[:taps], x[taps:], h[:taps], h[taps:]
    filtered = back(g_ref, xr * hr - xi * hi, xr * hi + xi * hr)
    filtered_ref[...] = filtered
    gated_ref[...] = (q_ref[...].astype(F32) * filtered).astype(BF16)


def tap_grad_kernel(taps, k_ref, v_ref, earlier_ref, gf_ref, f_ref, g_ref, out_ref):
    product = (k_ref[...].astype(F32) * v_ref[...].astype(F32)).astype(BF16)
    x = spectrum(f_ref, jnp.concatenate([earlier_ref[...], product], axis=0))
    rows = gf_ref[...]
    g = mm(f_ref[0, :, :taps], rows) + mm(f_ref[1, :, :taps], rows)
    xr, xi, gr, gi = x[:taps], x[taps:], g[:taps], g[taps:]
    tap_rows = back(g_ref, xr * gr + xi * gi, xi * gr - xr * gi)
    out_ref[...] = tap_rows.T.astype(BF16)


def backward_kernel(taps, k_ref, v_ref, gf_ref, following_ref, filt_ref, f_ref, g_ref, gk_ref, gv_ref):
    g = spectrum(f_ref, jnp.concatenate([gf_ref[...], following_ref[...]], axis=0))
    h = tap_spectrum(f_ref, filt_ref[...], taps)
    gr, gi, hr, hi = g[:taps], g[taps:], h[:taps], h[taps:]
    grad_product = back(g_ref, hr * gr + hi * gi, hr * gi - hi * gr)
    gk_ref[...] = (grad_product * v_ref[...].astype(F32)).astype(BF16)
    gv_ref[...] = (grad_product * k_ref[...].astype(F32)).astype(BF16)


def estimate(flops, bytes_accessed):
    return pl.CostEstimate(flops=flops // 16, bytes_accessed=bytes_accessed // 16, transcendentals=0)


def ignoring(body, count, skip):
    def kernel(*refs):
        return body(*refs[:skip], *refs[skip + count :])

    return kernel


def by_channel(kernel, arrays, kinds, outs, name, me=None, after=()):
    length, channels = arrays[0].shape
    width = min(512, channels) if me is None else 256
    specs = {
        "t": pl.BlockSpec((length, width), lambda i, *ids: (0, i)),
        "c": pl.BlockSpec((width, length), lambda i, *ids: (i, 0)),
        "x": pl.BlockSpec((width, length), lambda i, *ids: (i ^ ids[0][0], 0)),
    }

    def spec_of(kind, shape):
        if kind == "w":
            return pl.BlockSpec(shape, lambda i, *ids: (0,) * len(shape))
        return specs[kind]

    body = ignoring(functools.partial(kernel, length), len(after), len(arrays))
    return pl.pallas_call(
        body if me is None else lambda ids_ref, *refs: body(*refs),
        grid_spec=pltpu.PrefetchScalarGridSpec(
            num_scalar_prefetch=0 if me is None else 1,
            grid=(channels // width,),
            in_specs=[spec_of(kind, a.shape) for kind, a in zip(kinds, arrays)]
            + [pl.BlockSpec(memory_space=pl.ANY)] * len(after),
            out_specs=[specs[kind] for kind, unused in outs],
        ),
        out_shape=[
            jax.ShapeDtypeStruct((length, channels) if kind == "t" else (channels, length), dtype)
            for kind, dtype in outs
        ],
        compiler_params=pltpu.CompilerParams(vmem_limit_bytes=VMEM_BYTES),
        cost_estimate=estimate(10**9, 4 * 2**20),
        name=name,
    )(*([] if me is None else [me]), *arrays, *after)


def grad_gated_kernel(kind, me_ref, cot_ref, *refs):
    width = cot_ref.shape[1] // STREAMS
    total = mm(refs[0][...], cot_ref[:, :width], NT)
    for stream in range(1, STREAMS):
        total = total + mm(refs[stream][...], cot_ref[:, stream * width : (stream + 1) * width], NT)
    total = total.T
    refs = refs[STREAMS:]
    if kind == "first":
        refs[-1][...] = total
        return
    total = total + refs[0][...]
    if kind == "middle":
        refs[-1][...] = total
        return
    q_ref, filtered_ref, gq_ref, gf_ref = refs[1:]
    gq_ref[...] = (total * filtered_ref[...]).astype(BF16)
    gf_ref[...] = (total * q_ref[...].astype(F32)).astype(BF16)


def grad_gated_part(kind, me, cot, weight, off, arrays, after=()):
    length, width = cot.shape
    channels = weight.shape[0]
    tile = 512
    row_spec = pl.BlockSpec((length, tile), lambda i, me: (0, i))
    kinds = [BF16, BF16] if kind == "last" else [F32]
    return pl.pallas_call(
        ignoring(functools.partial(grad_gated_kernel, kind), len(after), 2 + STREAMS + len(arrays)),
        grid_spec=pltpu.PrefetchScalarGridSpec(
            num_scalar_prefetch=1,
            grid=(channels // tile,),
            in_specs=[
                pl.BlockSpec((length, width), lambda i, me: (0, 0)),
            ]
            + [
                pl.BlockSpec(
                    (tile, width // STREAMS), lambda i, me, stream=stream: (i, (me[1] ^ off) * STREAMS + stream)
                )
                for stream in range(STREAMS)
            ]
            + [row_spec] * len(arrays)
            + [pl.BlockSpec(memory_space=pl.ANY)] * len(after),
            out_specs=[row_spec] * len(kinds),
        ),
        out_shape=[jax.ShapeDtypeStruct((length, channels), dtype) for dtype in kinds],
        compiler_params=pltpu.CompilerParams(vmem_limit_bytes=VMEM_BYTES),
        cost_estimate=estimate(2 * length * width * channels, 2 * width * channels),
        name="grad_gated_" + kind,
    )(me, cot, *[weight] * STREAMS, *arrays, *after)


def mixed_kernel(adds, me_ref, gated_ref, *refs):
    depth = gated_ref.shape[1] // STREAMS
    total = mm(gated_ref[:, :depth], refs[0][...])
    for stream in range(1, STREAMS):
        total = total + mm(gated_ref[:, stream * depth : (stream + 1) * depth], refs[stream][...])
    for ref in refs[STREAMS : STREAMS + adds]:
        total = total + ref[...].astype(F32)
    refs[-1][...] = total.astype(refs[-1].dtype)


def mixed_part(me, gated, weight, offs, received, kind, after=()):
    length, channels = gated.shape
    tile = 512
    steps = channels // tile

    def column(b):
        return offs[0] + b * (offs[1] - offs[0] if len(offs) > 1 else 0)

    in_specs = [
        pl.BlockSpec((length, channels), lambda b, t, me: (0, 0)),
    ]
    in_specs += [
        pl.BlockSpec(
            (channels // STREAMS, tile),
            lambda b, t, me, stream=stream: (stream, (me[1] ^ column(b)) * steps + t),
        )
        for stream in range(STREAMS)
    ]
    for unused, (start, stride) in received:
        in_specs.append(
            pl.BlockSpec(
                (length, tile), lambda b, t, me, start=start, stride=stride: (0, (start + b * stride) * steps + t)
            )
        )
    in_specs += [pl.BlockSpec(memory_space=pl.ANY)] * len(after)
    return pl.pallas_call(
        ignoring(functools.partial(mixed_kernel, len(received)), len(after), 2 + STREAMS + len(received)),
        grid_spec=pltpu.PrefetchScalarGridSpec(
            num_scalar_prefetch=1,
            grid=(len(offs), steps),
            in_specs=in_specs,
            out_specs=pl.BlockSpec((length, tile), lambda b, t, me: (0, b * steps + t)),
        ),
        out_shape=jax.ShapeDtypeStruct((length, channels * len(offs)), kind),
        compiler_params=pltpu.CompilerParams(vmem_limit_bytes=VMEM_BYTES),
        cost_estimate=estimate(2 * length * channels * channels * len(offs), 2 * channels * channels * len(offs)),
        name="mixed_part",
    )(me, gated, *[weight] * STREAMS, *[array for array, unused in received], *after)


def pieces_kernel(per_chan, me_ref, *refs):
    out_ref = refs[-1]
    length, width = refs[0].shape
    span = width // per_chan
    count = len(refs) - 1
    piece = span // count
    for off in range(count):
        for part in range(per_chan):
            target = (me_ref[1] ^ off) * per_chan + part
            start = pl.multiple_of(part * span + me_ref[1] * piece, 128)
            block = refs[off][:, pl.ds(start, piece)]
            out_ref[target ^ me_ref[0]] = jnp.concatenate(
                [block[:, at : at + 128] for at in range(0, piece, 128)], axis=0
            )


def pieces_of(me, cots, n_ctx):
    length, width = cots[0].shape
    piece = width // n_ctx
    rows = length * piece // 128
    if piece % 128:
        return pieces_by_slices(me, cots, n_ctx)
    return pl.pallas_call(
        functools.partial(pieces_kernel, n_ctx // len(cots)),
        grid_spec=pltpu.PrefetchScalarGridSpec(
            num_scalar_prefetch=1,
            grid=(1,),
            in_specs=[pl.BlockSpec((length, width), lambda i, me: (0, 0))] * len(cots),
            out_specs=pl.BlockSpec((n_ctx, rows, 128), lambda i, me: (0, 0, 0)),
        ),
        out_shape=jax.ShapeDtypeStruct((n_ctx, rows, 128), BF16),
        compiler_params=pltpu.CompilerParams(vmem_limit_bytes=VMEM_BYTES),
        cost_estimate=estimate(10**6, 2**20),
        name="pieces",
    )(me, *cots)


def pieces_by_slices(me, cots, n_ctx):
    length, width = cots[0].shape
    count = len(cots)
    piece = width // n_ctx
    table = jnp.stack(cots).reshape(count, length, n_ctx // count, count, piece)
    mine = lax.dynamic_index_in_dim(table, me[1], 3, False)
    parts = mine.transpose(0, 2, 1, 3).reshape(n_ctx, length * piece // 128, 128)
    order = jnp.arange(n_ctx, dtype=jnp.int32) ^ me[0]
    per_chan = n_ctx // count
    return parts[(order // per_chan ^ me[1]) * per_chan + order % per_chan]


def weight_kernel(slots, parts, half, me_ref, owner_ref, *refs):
    gated_refs = refs[: slots - 1]
    far_low, far_high = refs[slots - 1 : slots + 1]
    cot_refs = refs[slots + 1 : slots + 1 + parts]
    out_ref = refs[-1]
    length = far_low.shape[0]
    far = jnp.where(pl.program_id(0) < half, far_low[...], far_high[...])
    columns = jnp.concatenate([ref[...] for ref in gated_refs] + [far], axis=0)
    for part in range(parts):
        rows = []
        for slot in range(slots):
            block = cot_refs[part][owner_ref[me_ref[0], slot]]
            rows.append(
                jnp.concatenate([block[at : at + length] for at in range(0, block.shape[0], length)], axis=1)
            )
        total = mm(columns, jnp.concatenate(rows, axis=0), TN)
        piece = total.shape[1]
        place = pl.multiple_of((me_ref[1] ^ part) * piece, piece) if parts > 1 else 0
        out_ref[:, pl.ds(place, piece)] = total.astype(BF16)


def grad_weight_of(me, owners, blocks, far_low, far_high, cots):
    length, channels = blocks[0].shape
    rows = cots[0].shape[1]
    piece = rows * 128 // length
    tile = 256
    half = channels // tile // 2
    slots, parts = len(blocks) + 1, len(cots)
    in_specs = [pl.BlockSpec((length, tile), lambda i, *ids: (0, i)) for unused in blocks]
    in_specs.append(pl.BlockSpec((length, tile), lambda i, *ids: (0, jnp.minimum(i, half - 1))))
    in_specs.append(pl.BlockSpec((length, tile), lambda i, *ids: (0, jnp.maximum(i - half, 0))))
    in_specs += [pl.BlockSpec(cot.shape, lambda i, *ids: (0, 0, 0)) for cot in cots]
    return pl.pallas_call(
        functools.partial(weight_kernel, slots, parts, half),
        grid_spec=pltpu.PrefetchScalarGridSpec(
            num_scalar_prefetch=2,
            grid=(channels // tile,),
            in_specs=in_specs,
            out_specs=pl.BlockSpec((tile, piece * parts), lambda i, *ids: (i, 0)),
        ),
        out_shape=jax.ShapeDtypeStruct((channels, piece * parts), BF16),
        compiler_params=pltpu.CompilerParams(vmem_limit_bytes=VMEM_BYTES),
        cost_estimate=estimate(2 * slots * length * channels * piece * parts, 12 * 2**20),
        name="grad_weight",
    )(me, owners, *blocks, far_low, far_high, *cots)


def place_kernel(me_ref, in_ref, out_ref):
    count, rows, unused = in_ref.shape
    for at in range(count):
        out_ref[at * rows : (at + 1) * rows] = in_ref[me_ref[0] ^ at].astype(out_ref.dtype)


def placed_blocks(me, blocks):
    count, rows, width = blocks.shape
    return pl.pallas_call(
        place_kernel,
        grid_spec=pltpu.PrefetchScalarGridSpec(
            num_scalar_prefetch=1,
            grid=(1,),
            in_specs=[pl.BlockSpec(blocks.shape, lambda i, me: (0, 0, 0))],
            out_specs=pl.BlockSpec((count * rows, width), lambda i, me: (0, 0)),
        ),
        out_shape=jax.ShapeDtypeStruct((count * rows, width), F32),
        compiler_params=pltpu.CompilerParams(vmem_limit_bytes=VMEM_BYTES),
        cost_estimate=estimate(10**6, 2 * 2**20),
        name="placed_blocks",
    )(me, blocks)


def in_one_piece(me, columns, length):
    count, rows, unused = columns[0].shape
    table = jnp.stack(columns)[jnp.arange(len(columns), dtype=jnp.int32) ^ me[1]]
    piece = rows * 128 // length
    flat = table.reshape(len(columns), count, length, piece).transpose(1, 2, 0, 3)
    flat = flat.reshape(count, length, piece * len(columns) // 128, 128).transpose(0, 2, 1, 3)
    return [flat.reshape(count, -1, 128)]


def cycle_of(count):
    across = 1 << ((count.bit_length() - 1) // 2)
    order = []
    for column in range(across):
        line = [row * across + column for row in range(count // across)]
        order += line if column % 2 == 0 else line[::-1]
    return order


def swap(block, axis, bit):
    size = lax.axis_size(axis)
    return lax.ppermute(block, axis, [(i, i ^ bit) for i in range(size)])


def bits_of(size):
    return [1 << place for place in range(size.bit_length() - 1)]


def gather_by_swaps(block):
    held = {0: block}
    for bit in reversed(bits_of(lax.axis_size("chan"))):
        held.update({off ^ bit: swap(held[off], "chan", bit) for off in list(held)})
    return held


def summed(partial):
    sums = partial
    for bit in bits_of(partial.shape[0]):
        others = swap(sums[1::2], "ctx", bit)
        sums = (sums[::2].astype(F32) + others.astype(F32)).astype(BF16)
    return sums


def exchanged(pieces):
    held, sources, stages = pieces[None], [0], []
    for bit in bits_of(pieces.shape[0]):
        give = held[:, 1::2].reshape((-1,) + pieces.shape[1:])
        stages.append(swap(give, "ctx", bit))
        came = stages[-1].reshape((len(sources), -1) + pieces.shape[1:])
        held = jnp.concatenate([held[:, ::2], came], axis=0)
        sources += [source ^ bit for source in sources]
    return held[:, 0], sources, stages


def doubled(block, axis):
    held = block
    for bit in reversed(bits_of(lax.axis_size(axis))):
        held = jnp.stack([held, swap(held, axis, bit)], axis=1).reshape((-1,) + block.shape[1:])
    return held


def per_device(query_proj, key_proj, value_proj, filters, out_weight, cotangent):
    length, channels = query_proj.shape
    taps = filters.shape[1]
    n_ctx, n_chan = lax.axis_size("ctx"), lax.axis_size("chan")
    me = jnp.stack([lax.axis_index("ctx"), lax.axis_index("chan")]).astype(jnp.int32)
    forward, late, early, lags = [jnp.asarray(m) for m in transforms(taps)]

    product = (key_proj.astype(F32) * value_proj.astype(F32)).astype(BF16)
    earlier = lax.ppermute(product, "ctx", [(i, i + 1) for i in range(n_ctx - 1)])

    cots = gather_by_swaps(cotangent)
    grad_gated = []
    for off in range(n_chan - 1):
        grad_gated = grad_gated_part("middle" if off else "first", me, cots[off], out_weight, off, grad_gated)
        grad_gated = list(grad_gated)
        if off == 0:
            first = grad_gated

    pieces = pieces_of(me, [cots[off] for off in range(n_chan)], n_ctx)
    held, sources, stages = exchanged(pieces)

    gated, filtered = by_channel(
        forward_kernel,
        [query_proj, key_proj, value_proj, earlier, filters, forward, late],
        "ttttcww",
        [("t", BF16), ("t", F32)],
        "forward_filter",
        after=first,
    )

    order = cycle_of(n_ctx)
    ahead = [(order[i], order[(i + 1) % n_ctx]) for i in range(n_ctx)]
    behind = [(b, a) for a, b in ahead]
    half = channels // 2
    from_behind, from_ahead = gated, gated
    blocks = [gated]
    for step in range(n_ctx // 2 - 1):
        from_behind = lax.ppermute(from_behind, "ctx", ahead)
        from_ahead = lax.ppermute(from_ahead, "ctx", behind)
        blocks += [from_behind, from_ahead]
    far_low = lax.ppermute(from_behind[:, :half], "ctx", ahead)
    far_high = lax.ppermute(from_ahead[:, half:], "ctx", behind)

    grad_query, grad_filtered = grad_gated_part(
        "last", me, cots[n_chan - 1], out_weight, n_chan - 1, grad_gated + [query_proj, filtered], [pieces]
    )
    following = lax.ppermute(grad_filtered, "ctx", [(i + 1, i) for i in range(n_ctx - 1)])

    received = []
    left = list(range(n_chan))
    for bit in bits_of(n_chan):
        give = left[1::2]
        left = left[::2]
        stride = give[1] - give[0] if len(give) > 1 else 1
        sums = [(array, ((give[0] - offs[0]) // step, stride // step)) for array, offs, step in received]
        ring = min(len(received) + 1, n_ctx // 2 - 1)
        part = mixed_part(
            me, gated, out_weight, give, sums, BF16, blocks[2 * ring - 1 : 2 * ring + 1] + stages[ring : ring + 1]
        )
        received.append((swap(part, "chan", bit), [off ^ bit for off in give], stride))
    last = received.pop()[0]
    own = mixed_part(me, gated, out_weight, [0], [(array, (0, 1)) for array, offs, step in received], F32, blocks[-2:])
    mixed = (own + last.astype(F32)).astype(BF16)

    direct = channels // n_ctx == 256
    tap_grad = by_channel(
        tap_grad_kernel,
        [key_proj, value_proj, earlier, grad_filtered, forward, lags],
        "ttttww",
        [("x" if direct else "c", BF16)],
        "tap_grad",
        me,
        blocks[1:3] + stages[:1],
    )[0].reshape(n_ctx, -1, taps)
    if not direct:
        tap_grad = tap_grad[jnp.arange(n_ctx, dtype=jnp.int32) ^ me[0]]
    grad_filters = placed_blocks(me, doubled(summed(tap_grad), "ctx"))
    grad_key, grad_value = by_channel(
        backward_kernel,
        [key_proj, value_proj, grad_filtered, following, filters, forward, early],
        "ttttcww",
        [("t", BF16), ("t", BF16)],
        "backward_filter",
    )

    columns = gather_by_swaps(held)
    columns = [columns[off] for off in range(n_chan)]
    if (channels // n_ctx) % 128:
        columns = in_one_piece(me, columns, length)
    owners = []
    for c in range(n_ctx):
        spot = order.index(c)
        steps = [0] + [sign * step for step in range(1, n_ctx // 2) for sign in (-1, 1)] + [n_ctx // 2]
        owners.append([sources.index(order[(spot + step) % n_ctx] ^ c) for step in steps])
    grad_weight = grad_weight_of(me, jnp.asarray(owners, jnp.int32), blocks, far_low, far_high, columns)
    return (mixed, grad_query, grad_key, grad_value, grad_filters, grad_weight)


def solution(mesh):
    placed = (
        P("ctx", "chan"),
        P("ctx", "chan"),
        P("ctx", "chan"),
        P("chan", None),
        P("chan", None),
        P("ctx", "chan"),
    )
    return jax.shard_map(
        per_device,
        mesh=mesh,
        in_specs=placed,
        out_specs=(
            P("ctx", "chan"),
            P("ctx", "chan"),
            P("ctx", "chan"),
            P("ctx", "chan"),
            P("chan", None),
            P("chan", "ctx"),
        ),
        check_vma=False,
    )
```

```python
import functools

import jax
import jax.numpy as jnp
import numpy as np
from jax import lax
from jax.experimental import pallas as pl
from jax.experimental.pallas import tpu as pltpu
from jax.sharding import PartitionSpec as P

F32 = jnp.float32
BF16 = jnp.bfloat16
VMEM_BYTES = 40 * 2**20
STREAMS = 4
NT = (((1,), (1,)), ((), ()))
TN = (((0,), (0,)), ((), ()))


def halves(matrix):
    high = matrix.astype(BF16)
    low = (matrix - high.astype(np.float64)).astype(BF16)
    return np.stack([high, low])


def transforms(taps):
    points = 2 * taps
    angle = np.pi * (2 * np.arange(taps)[:, None] + 1) * np.arange(points)[None, :] / points
    forward = np.concatenate([np.cos(angle), -np.sin(angle)], axis=0)
    inverse = forward.T * (2.0 / points)
    late = inverse[taps:]
    early = inverse[:taps]
    lags = inverse[taps - np.arange(taps)]
    return halves(forward), halves(late), halves(early), halves(lags)


def mm(a, b, dims=(((1,), (0,)), ((), ()))):
    return lax.dot_general(a, b, dims, preferred_element_type=F32)


def spectrum(f_ref, rows):
    return mm(f_ref[0], rows) + mm(f_ref[1], rows)


def tap_spectrum(f_ref, filters, taps):
    return mm(f_ref[0, :, :taps], filters, NT) + mm(f_ref[1, :, :taps], filters, NT)


def back(g_ref, real, imag):
    both = jnp.concatenate([real, imag], axis=0)
    high = both.astype(BF16)
    low = (both - high.astype(F32)).astype(BF16)
    return mm(g_ref[0], high) + mm(g_ref[0], low) + mm(g_ref[1], high)


def forward_kernel(taps, q_ref, k_ref, v_ref, earlier_ref, filt_ref, f_ref, g_ref, gated_ref, filtered_ref):
    product = (k_ref[...].astype(F32) * v_ref[...].astype(F32)).astype(BF16)
    x = spectrum(f_ref, jnp.concatenate([earlier_ref[...], product], axis=0))
    h = tap_spectrum(f_ref, filt_ref[...], taps)
    xr, xi, hr, hi = x[:taps], x[taps:], h[:taps], h[taps:]
    filtered = back(g_ref, xr * hr - xi * hi, xr * hi + xi * hr)
    filtered_ref[...] = filtered
    gated_ref[...] = (q_ref[...].astype(F32) * filtered).astype(BF16)


def tap_grad_kernel(taps, k_ref, v_ref, earlier_ref, gf_ref, f_ref, g_ref, out_ref):
    product = (k_ref[...].astype(F32) * v_ref[...].astype(F32)).astype(BF16)
    x = spectrum(f_ref, jnp.concatenate([earlier_ref[...], product], axis=0))
    rows = gf_ref[...]
    g = mm(f_ref[0, :, :taps], rows) + mm(f_ref[1, :, :taps], rows)
    xr, xi, gr, gi = x[:taps], x[taps:], g[:taps], g[taps:]
    tap_rows = back(g_ref, xr * gr + xi * gi, xi * gr - xr * gi)
    out_ref[...] = tap_rows.T.astype(BF16)


def backward_kernel(taps, k_ref, v_ref, gf_ref, following_ref, filt_ref, f_ref, g_ref, gk_ref, gv_ref):
    g = spectrum(f_ref, jnp.concatenate([gf_ref[...], following_ref[...]], axis=0))
    h = tap_spectrum(f_ref, filt_ref[...], taps)
    gr, gi, hr, hi = g[:taps], g[taps:], h[:taps], h[taps:]
    grad_product = back(g_ref, hr * gr + hi * gi, hr * gi - hi * gr)
    gk_ref[...] = (grad_product * v_ref[...].astype(F32)).astype(BF16)
    gv_ref[...] = (grad_product * k_ref[...].astype(F32)).astype(BF16)


def estimate(flops, bytes_accessed):
    return pl.CostEstimate(flops=flops // 16, bytes_accessed=bytes_accessed // 16, transcendentals=0)


def ignoring(body, count, skip):
    def kernel(*refs):
        return body(*refs[:skip], *refs[skip + count :])

    return kernel


def product_kernel(k_ref, v_ref, cot_ref, product_ref, held_ref):
    product_ref[...] = (k_ref[...].astype(F32) * v_ref[...].astype(F32)).astype(BF16)
    held_ref[...] = cot_ref[...]


def product_of(key_proj, value_proj, cotangent):
    whole = pl.BlockSpec(key_proj.shape, lambda i: (0, 0))
    return pl.pallas_call(
        product_kernel,
        grid=(1,),
        in_specs=[whole] * 3,
        out_specs=[whole] * 2,
        out_shape=[jax.ShapeDtypeStruct(key_proj.shape, BF16)] * 2,
        compiler_params=pltpu.CompilerParams(vmem_limit_bytes=VMEM_BYTES),
        cost_estimate=estimate(10**6, 2**20),
        name="product",
    )(key_proj, value_proj, cotangent)


def held_back(block, after):
    def nothing(*refs):
        pass

    anywhere = pl.BlockSpec(memory_space=pl.ANY)
    return pl.pallas_call(
        nothing,
        in_specs=[anywhere] * (1 + len(after)),
        out_specs=anywhere,
        out_shape=jax.ShapeDtypeStruct(block.shape, block.dtype),
        input_output_aliases={0: 0},
        cost_estimate=estimate(0, 0),
        name="held_back",
    )(block, *after)


def by_channel(kernel, arrays, kinds, outs, name, me=None, after=()):
    length, channels = arrays[0].shape
    width = min(512, channels) if me is None else 256
    specs = {
        "t": pl.BlockSpec((length, width), lambda i, *ids: (0, i)),
        "c": pl.BlockSpec((width, length), lambda i, *ids: (i, 0)),
        "x": pl.BlockSpec((width, length), lambda i, *ids: (i ^ ids[0][0], 0)),
    }

    def spec_of(kind, shape):
        if kind == "w":
            return pl.BlockSpec(shape, lambda i, *ids: (0,) * len(shape))
        return specs[kind]

    body = ignoring(functools.partial(kernel, length), len(after), len(arrays))
    return pl.pallas_call(
        body if me is None else lambda ids_ref, *refs: body(*refs),
        grid_spec=pltpu.PrefetchScalarGridSpec(
            num_scalar_prefetch=0 if me is None else 1,
            grid=(channels // width,),
            in_specs=[spec_of(kind, a.shape) for kind, a in zip(kinds, arrays)]
            + [pl.BlockSpec(memory_space=pl.ANY)] * len(after),
            out_specs=[specs[kind] for kind, unused in outs],
        ),
        out_shape=[
            jax.ShapeDtypeStruct((length, channels) if kind == "t" else (channels, length), dtype)
            for kind, dtype in outs
        ],
        compiler_params=pltpu.CompilerParams(vmem_limit_bytes=VMEM_BYTES),
        cost_estimate=estimate(10**9, 4 * 2**20),
        name=name,
    )(*([] if me is None else [me]), *arrays, *after)


def grad_gated_kernel(kind, me_ref, cot_ref, w_ref, *refs):
    turned_ref = refs[-1]

    @pl.when(pl.program_id(0) == 0)
    def turn():
        turned_ref[...] = cot_ref[...].T

    total = mm(w_ref[...], turned_ref[...])
    if kind == "first":
        refs[-2][...] = total
        return
    total = total + refs[0][...]
    if kind == "middle":
        refs[-2][...] = total
        return
    total = total.T
    q_ref, filtered_ref, gq_ref, gf_ref = refs[1:-1]
    gq_ref[...] = (total * filtered_ref[...]).astype(BF16)
    gf_ref[...] = (total * q_ref[...].astype(F32)).astype(BF16)


def grad_gated_part(kind, me, cot, weight, off, arrays, after=()):
    length, width = cot.shape
    channels = weight.shape[0]
    tile = 512
    by_token = pl.BlockSpec((length, tile), lambda i, me: (0, i))
    by_channel_rows = pl.BlockSpec((tile, length), lambda i, me: (i, 0))
    if kind == "last":
        out_specs, out_shape = [by_token] * 2, [jax.ShapeDtypeStruct((length, channels), BF16)] * 2
    else:
        out_specs, out_shape = [by_channel_rows], [jax.ShapeDtypeStruct((channels, length), F32)]
    return pl.pallas_call(
        ignoring(functools.partial(grad_gated_kernel, kind), len(after), 3 + len(arrays)),
        grid_spec=pltpu.PrefetchScalarGridSpec(
            num_scalar_prefetch=1,
            grid=(channels // tile,),
            in_specs=[
                pl.BlockSpec((length, width), lambda i, me: (0, 0)),
                pl.BlockSpec((tile, width), lambda i, me: (i, me[1] ^ off)),
            ]
            + [by_channel_rows, by_token, by_token][: len(arrays)]
            + [pl.BlockSpec(memory_space=pl.ANY)] * len(after),
            out_specs=out_specs,
            scratch_shapes=[pltpu.VMEM((width, length), BF16)],
        ),
        out_shape=out_shape,
        compiler_params=pltpu.CompilerParams(vmem_limit_bytes=VMEM_BYTES),
        cost_estimate=estimate(2 * length * width * channels, 2 * width * channels),
        name="grad_gated_" + kind,
    )(me, cot, weight, *arrays, *after)


def mixed_kernel(adds, me_ref, gated_ref, *refs):
    depth = gated_ref.shape[1] // STREAMS
    total = mm(gated_ref[:, :depth], refs[0][...])
    for stream in range(1, STREAMS):
        total = total + mm(gated_ref[:, stream * depth : (stream + 1) * depth], refs[stream][...])
    for ref in refs[STREAMS : STREAMS + adds]:
        total = total + ref[...].astype(F32)
    refs[-1][...] = total.astype(refs[-1].dtype)


def mixed_part(me, gated, weight, offs, received, kind, after=()):
    length, channels = gated.shape
    tile = 512
    steps = channels // tile

    def column(b):
        return offs[0] + b * (offs[1] - offs[0] if len(offs) > 1 else 0)

    in_specs = [
        pl.BlockSpec((length, channels), lambda b, t, me: (0, 0)),
    ]
    in_specs += [
        pl.BlockSpec(
            (channels // STREAMS, tile),
            lambda b, t, me, stream=stream: (stream, (me[1] ^ column(b)) * steps + t),
        )
        for stream in range(STREAMS)
    ]
    for unused, (start, stride) in received:
        in_specs.append(
            pl.BlockSpec(
                (length, tile), lambda b, t, me, start=start, stride=stride: (0, (start + b * stride) * steps + t)
            )
        )
    in_specs += [pl.BlockSpec(memory_space=pl.ANY)] * len(after)
    return pl.pallas_call(
        ignoring(functools.partial(mixed_kernel, len(received)), len(after), 2 + STREAMS + len(received)),
        grid_spec=pltpu.PrefetchScalarGridSpec(
            num_scalar_prefetch=1,
            grid=(len(offs), steps),
            in_specs=in_specs,
            out_specs=pl.BlockSpec((length, tile), lambda b, t, me: (0, b * steps + t)),
        ),
        out_shape=jax.ShapeDtypeStruct((length, channels * len(offs)), kind),
        compiler_params=pltpu.CompilerParams(vmem_limit_bytes=VMEM_BYTES),
        cost_estimate=estimate(2 * length * channels * channels * len(offs), 2 * channels * channels * len(offs)),
        name="mixed_part",
    )(me, gated, *[weight] * STREAMS, *[array for array, unused in received], *after)


def pieces_kernel(per_chan, me_ref, *refs):
    out_ref = refs[-1]
    length, width = refs[0].shape
    span = width // per_chan
    count = len(refs) - 1
    piece = span // count
    for off in range(count):
        for part in range(per_chan):
            target = (me_ref[1] ^ off) * per_chan + part
            start = pl.multiple_of(part * span + me_ref[1] * piece, 128)
            block = refs[off][:, pl.ds(start, piece)]
            out_ref[target ^ me_ref[0]] = jnp.concatenate(
                [block[:, at : at + 128] for at in range(0, piece, 128)], axis=0
            )


def pieces_of(me, cots, n_ctx, after):
    length, width = cots[0].shape
    piece = width // n_ctx
    rows = length * piece // 128
    if piece % 128:
        return pieces_by_slices(me, cots, n_ctx)
    return pl.pallas_call(
        ignoring(functools.partial(pieces_kernel, n_ctx // len(cots)), len(after), 1 + len(cots)),
        grid_spec=pltpu.PrefetchScalarGridSpec(
            num_scalar_prefetch=1,
            grid=(1,),
            in_specs=[pl.BlockSpec((length, width), lambda i, me: (0, 0))] * len(cots)
            + [pl.BlockSpec(memory_space=pl.ANY)] * len(after),
            out_specs=pl.BlockSpec((n_ctx, rows, 128), lambda i, me: (0, 0, 0)),
        ),
        out_shape=jax.ShapeDtypeStruct((n_ctx, rows, 128), BF16),
        compiler_params=pltpu.CompilerParams(vmem_limit_bytes=VMEM_BYTES),
        cost_estimate=estimate(10**6, 2**20),
        name="pieces",
    )(me, *cots, *after)


def pieces_by_slices(me, cots, n_ctx):
    length, width = cots[0].shape
    count = len(cots)
    piece = width // n_ctx
    table = jnp.stack(cots).reshape(count, length, n_ctx // count, count, piece)
    mine = lax.dynamic_index_in_dim(table, me[1], 3, False)
    parts = mine.transpose(0, 2, 1, 3).reshape(n_ctx, length * piece // 128, 128)
    order = jnp.arange(n_ctx, dtype=jnp.int32) ^ me[0]
    per_chan = n_ctx // count
    return parts[(order // per_chan ^ me[1]) * per_chan + order % per_chan]


def weight_kernel(slots, parts, half, me_ref, owner_ref, *refs):
    gated_refs = refs[: slots - 1]
    far_low, far_high = refs[slots - 1 : slots + 1]
    cot_refs = refs[slots + 1 : slots + 1 + parts]
    out_ref = refs[-1]
    length = far_low.shape[0]
    far = jnp.where(pl.program_id(0) < half, far_low[...], far_high[...])
    columns = jnp.concatenate([ref[...] for ref in gated_refs] + [far], axis=0)
    for part in range(parts):
        rows = []
        for slot in range(slots):
            block = cot_refs[part][owner_ref[me_ref[0], slot]]
            rows.append(
                jnp.concatenate([block[at : at + length] for at in range(0, block.shape[0], length)], axis=1)
            )
        total = mm(columns, jnp.concatenate(rows, axis=0), TN)
        piece = total.shape[1]
        place = pl.multiple_of((me_ref[1] ^ part) * piece, piece) if parts > 1 else 0
        out_ref[:, pl.ds(place, piece)] = total.astype(BF16)


def grad_weight_of(me, owners, blocks, far_low, far_high, cots):
    length, channels = blocks[0].shape
    rows = cots[0].shape[1]
    piece = rows * 128 // length
    tile = 256
    half = channels // tile // 2
    slots, parts = len(blocks) + 1, len(cots)
    in_specs = [pl.BlockSpec((length, tile), lambda i, *ids: (0, i)) for unused in blocks]
    in_specs.append(pl.BlockSpec((length, tile), lambda i, *ids: (0, jnp.minimum(i, half - 1))))
    in_specs.append(pl.BlockSpec((length, tile), lambda i, *ids: (0, jnp.maximum(i - half, 0))))
    in_specs += [pl.BlockSpec(cot.shape, lambda i, *ids: (0, 0, 0)) for cot in cots]
    return pl.pallas_call(
        functools.partial(weight_kernel, slots, parts, half),
        grid_spec=pltpu.PrefetchScalarGridSpec(
            num_scalar_prefetch=2,
            grid=(channels // tile,),
            in_specs=in_specs,
            out_specs=pl.BlockSpec((tile, piece * parts), lambda i, *ids: (i, 0)),
        ),
        out_shape=jax.ShapeDtypeStruct((channels, piece * parts), BF16),
        compiler_params=pltpu.CompilerParams(vmem_limit_bytes=VMEM_BYTES),
        cost_estimate=estimate(2 * slots * length * channels * piece * parts, 12 * 2**20),
        name="grad_weight",
    )(me, owners, *blocks, far_low, far_high, *cots)


def place_kernel(me_ref, in_ref, out_ref):
    count, rows, unused = in_ref.shape
    for at in range(count):
        out_ref[at * rows : (at + 1) * rows] = in_ref[me_ref[0] ^ at].astype(out_ref.dtype)


def placed_blocks(me, blocks):
    count, rows, width = blocks.shape
    return pl.pallas_call(
        place_kernel,
        grid_spec=pltpu.PrefetchScalarGridSpec(
            num_scalar_prefetch=1,
            grid=(1,),
            in_specs=[pl.BlockSpec(blocks.shape, lambda i, me: (0, 0, 0))],
            out_specs=pl.BlockSpec((count * rows, width), lambda i, me: (0, 0)),
        ),
        out_shape=jax.ShapeDtypeStruct((count * rows, width), F32),
        compiler_params=pltpu.CompilerParams(vmem_limit_bytes=VMEM_BYTES),
        cost_estimate=estimate(10**6, 2 * 2**20),
        name="placed_blocks",
    )(me, blocks)


def in_one_piece(me, columns, length):
    count, rows, unused = columns[0].shape
    table = jnp.stack(columns)[jnp.arange(len(columns), dtype=jnp.int32) ^ me[1]]
    piece = rows * 128 // length
    flat = table.reshape(len(columns), count, length, piece).transpose(1, 2, 0, 3)
    flat = flat.reshape(count, length, piece * len(columns) // 128, 128).transpose(0, 2, 1, 3)
    return [flat.reshape(count, -1, 128)]


def cycle_of(count):
    across = 1 << ((count.bit_length() - 1) // 2)
    order = []
    for column in range(across):
        line = [row * across + column for row in range(count // across)]
        order += line if column % 2 == 0 else line[::-1]
    return order


def swap(block, axis, bit):
    size = lax.axis_size(axis)
    return lax.ppermute(block, axis, [(i, i ^ bit) for i in range(size)])


def bits_of(size):
    return [1 << place for place in range(size.bit_length() - 1)]


def gather_by_swaps(block):
    held = {0: block}
    for bit in reversed(bits_of(lax.axis_size("chan"))):
        held.update({off ^ bit: swap(held[off], "chan", bit) for off in list(held)})
    return held


def halved_kernel(kept_ref, came_ref, next_ref, left_ref):
    total = (kept_ref[...].astype(F32) + came_ref[...].astype(F32)).astype(BF16)
    count = total.shape[0] // 2
    for at in range(count):
        left_ref[at] = total[2 * at]
        next_ref[at] = total[2 * at + 1]


def added_kernel(kept_ref, came_ref, out_ref):
    out_ref[...] = (kept_ref[...].astype(F32) + came_ref[...].astype(F32)).astype(BF16)


def added(kept, came, after):
    count = kept.shape[0]
    whole = pl.BlockSpec(kept.shape, lambda i: (0, 0, 0))
    half = pl.BlockSpec((max(count // 2, 1),) + kept.shape[1:], lambda i: (0, 0, 0))
    outs = 2 if count > 1 else 1
    return pl.pallas_call(
        ignoring(halved_kernel if count > 1 else added_kernel, len(after), 2),
        grid=(1,),
        in_specs=[whole, whole] + [pl.BlockSpec(memory_space=pl.ANY)] * len(after),
        out_specs=[half] * outs,
        out_shape=[jax.ShapeDtypeStruct(half.block_shape, BF16)] * outs,
        compiler_params=pltpu.CompilerParams(vmem_limit_bytes=VMEM_BYTES),
        cost_estimate=estimate(10**6, 2**20),
        name="added",
    )(kept, came, *after)


def summed(partial, gates):
    give, left = partial[1::2], partial[::2]
    for step, bit in enumerate(bits_of(partial.shape[0])):
        sums = added(left, swap(give, "ctx", bit), gates[step] if step < len(gates) else ())
        if len(sums) == 2:
            give, left = sums
    return sums[0]


def exchanged(pieces):
    held, sources, stages = pieces[None], [0], []
    for bit in bits_of(pieces.shape[0]):
        give = held[:, 1::2].reshape((-1,) + pieces.shape[1:])
        stages.append(swap(give, "ctx", bit))
        came = stages[-1].reshape((len(sources), -1) + pieces.shape[1:])
        held = jnp.concatenate([held[:, ::2], came], axis=0)
        sources += [source ^ bit for source in sources]
    return held[:, 0], sources, stages


def doubled(block, axis):
    held = block
    for bit in reversed(bits_of(lax.axis_size(axis))):
        held = jnp.stack([held, swap(held, axis, bit)], axis=1).reshape((-1,) + block.shape[1:])
    return held


def per_device(query_proj, key_proj, value_proj, filters, out_weight, cotangent):
    length, channels = query_proj.shape
    taps = filters.shape[1]
    n_ctx, n_chan = lax.axis_size("ctx"), lax.axis_size("chan")
    me = jnp.stack([lax.axis_index("ctx"), lax.axis_index("chan")]).astype(jnp.int32)
    forward, late, early, lags = [jnp.asarray(m) for m in transforms(taps)]

    product, cotangent = product_of(key_proj, value_proj, cotangent)
    earlier = lax.ppermute(product, "ctx", [(i, i + 1) for i in range(n_ctx - 1)])

    cots, turns = {0: cotangent, 1: swap(cotangent, "chan", 1)}, [0, 1]
    for bit in reversed(bits_of(n_chan)[1:]):
        cots.update({off ^ bit: swap(cots[off], "chan", bit) for off in list(cots) if off % 2 == 0})
    sums = []
    for off in turns:
        sums = grad_gated_part("middle" if sums else "first", me, cots[off], out_weight, off, list(sums))
    for off in [off for off in cots if off % 2 == 0 and off]:
        cots[off] = held_back(cots[off], sums)
        cots[off + 1] = swap(cots[off], "chan", 1)
        turns += [off, off + 1]

    gated, filtered = by_channel(
        forward_kernel,
        [query_proj, key_proj, value_proj, earlier, filters, forward, late],
        "ttttcww",
        [("t", BF16), ("t", F32)],
        "forward_filter",
        after=sums,
    )
    for off in turns[2:-1]:
        sums = grad_gated_part("middle", me, cots[off], out_weight, off, list(sums), [gated])

    pieces = pieces_of(me, [cots[off] for off in range(n_chan)], n_ctx, sums)
    held, sources, stages = exchanged(pieces)

    order = cycle_of(n_ctx)
    ahead = [(order[i], order[(i + 1) % n_ctx]) for i in range(n_ctx)]
    behind = [(b, a) for a, b in ahead]
    half = channels // 2
    from_behind, from_ahead = gated, gated
    blocks = [gated]
    for step in range(n_ctx // 2 - 1):
        from_behind = lax.ppermute(from_behind, "ctx", ahead)
        from_ahead = lax.ppermute(from_ahead, "ctx", behind)
        blocks += [from_behind, from_ahead]
    far_low = lax.ppermute(from_behind[:, :half], "ctx", ahead)
    far_high = lax.ppermute(from_ahead[:, half:], "ctx", behind)

    grad_query, grad_filtered = grad_gated_part(
        "last", me, cots[turns[-1]], out_weight, turns[-1], list(sums) + [query_proj, filtered], [pieces]
    )
    following = lax.ppermute(grad_filtered, "ctx", [(i + 1, i) for i in range(n_ctx - 1)])

    direct = channels // n_ctx == 256
    tap_grad = by_channel(
        tap_grad_kernel,
        [key_proj, value_proj, earlier, grad_filtered, forward, lags],
        "ttttww",
        [("x" if direct else "c", BF16)],
        "tap_grad",
        me,
    )[0].reshape(n_ctx, -1, taps)
    if not direct:
        tap_grad = tap_grad[jnp.arange(n_ctx, dtype=jnp.int32) ^ me[0]]

    received, parts = [], []
    left = list(range(n_chan))
    for bit in bits_of(n_chan):
        give = left[1::2]
        left = left[::2]
        stride = give[1] - give[0] if len(give) > 1 else 1
        sums = [(array, ((give[0] - offs[0]) // step, stride // step)) for array, offs, step in received]
        step = min(len(received), n_ctx // 2 - 2)
        order_after = blocks[2 * step + 1 : 2 * step + 3] + stages[step : step + 1] + [tap_grad]
        part = mixed_part(me, gated, out_weight, give, sums, BF16, order_after)
        parts.append(part)
        received.append((swap(part, "chan", bit), [off ^ bit for off in give], stride))
    last = received.pop()[0]
    own = mixed_part(me, gated, out_weight, [0], [(array, (0, 1)) for array, offs, step in received], F32, blocks[-2:])
    mixed = (own + last.astype(F32)).astype(BF16)

    grad_filters = placed_blocks(me, doubled(summed(tap_grad, [[part] for part in parts] + [[own]]), "ctx"))
    grad_key, grad_value = by_channel(
        backward_kernel,
        [key_proj, value_proj, grad_filtered, following, filters, forward, early],
        "ttttcww",
        [("t", BF16), ("t", BF16)],
        "backward_filter",
        after=parts[-1:],
    )

    columns = gather_by_swaps(held)
    columns = [columns[off] for off in range(n_chan)]
    if (channels // n_ctx) % 128:
        columns = in_one_piece(me, columns, length)
    owners = []
    for c in range(n_ctx):
        spot = order.index(c)
        steps = [0] + [sign * step for step in range(1, n_ctx // 2) for sign in (-1, 1)] + [n_ctx // 2]
        owners.append([sources.index(order[(spot + step) % n_ctx] ^ c) for step in steps])
    grad_weight = grad_weight_of(me, jnp.asarray(owners, jnp.int32), blocks, far_low, far_high, columns)
    return (mixed, grad_query, grad_key, grad_value, grad_filters, grad_weight)


def solution(mesh):
    placed = (
        P("ctx", "chan"),
        P("ctx", "chan"),
        P("ctx", "chan"),
        P("chan", None),
        P("chan", None),
        P("ctx", "chan"),
    )
    return jax.shard_map(
        per_device,
        mesh=mesh,
        in_specs=placed,
        out_specs=(
            P("ctx", "chan"),
            P("ctx", "chan"),
            P("ctx", "chan"),
            P("ctx", "chan"),
            P("chan", None),
            P("chan", "ctx"),
        ),
        check_vma=False,
    )
```

```python
import functools

import jax
import jax.numpy as jnp
import numpy as np
from jax import lax
from jax.experimental import pallas as pl
from jax.experimental.pallas import tpu as pltpu
from jax.sharding import PartitionSpec as P

F32 = jnp.float32
BF16 = jnp.bfloat16
VMEM_BYTES = 40 * 2**20
NT = (((1,), (1,)), ((), ()))
TN = (((0,), (0,)), ((), ()))


def halves(matrix):
    high = matrix.astype(BF16)
    low = (matrix - high.astype(np.float64)).astype(BF16)
    return np.stack([high, low])


def transforms(taps):
    points = 2 * taps
    angle = np.pi * (2 * np.arange(taps)[:, None] + 1) * np.arange(points)[None, :] / points
    forward = np.concatenate([np.cos(angle), -np.sin(angle)], axis=0)
    inverse = forward.T * (2.0 / points)
    late = inverse[taps:]
    early = inverse[:taps]
    lags = inverse[taps - np.arange(taps)]
    return halves(forward), halves(late), halves(early), halves(lags)


def mm(a, b, dims=(((1,), (0,)), ((), ()))):
    return lax.dot_general(a, b, dims, preferred_element_type=F32)


def spectrum(f_ref, rows):
    return mm(f_ref[0], rows) + mm(f_ref[1], rows)


def tap_spectrum(f_ref, filters, taps):
    return mm(f_ref[0, :, :taps], filters, NT) + mm(f_ref[1, :, :taps], filters, NT)


def back(g_ref, real, imag):
    both = jnp.concatenate([real, imag], axis=0)
    high = both.astype(BF16)
    low = (both - high.astype(F32)).astype(BF16)
    return mm(g_ref[0], high) + mm(g_ref[0], low) + mm(g_ref[1], high)


def forward_kernel(taps, q_ref, k_ref, v_ref, earlier_ref, filt_ref, f_ref, g_ref, gated_ref, filtered_ref):
    product = (k_ref[...].astype(F32) * v_ref[...].astype(F32)).astype(BF16)
    x = spectrum(f_ref, jnp.concatenate([earlier_ref[...], product], axis=0))
    h = tap_spectrum(f_ref, filt_ref[...], taps)
    xr, xi, hr, hi = x[:taps], x[taps:], h[:taps], h[taps:]
    filtered = back(g_ref, xr * hr - xi * hi, xr * hi + xi * hr)
    filtered_ref[...] = filtered
    gated_ref[...] = (q_ref[...].astype(F32) * filtered).astype(BF16)


def tap_grad_kernel(taps, k_ref, v_ref, earlier_ref, gf_ref, f_ref, g_ref, out_ref):
    product = (k_ref[...].astype(F32) * v_ref[...].astype(F32)).astype(BF16)
    x = spectrum(f_ref, jnp.concatenate([earlier_ref[...], product], axis=0))
    rows = gf_ref[...]
    g = mm(f_ref[0, :, :taps], rows) + mm(f_ref[1, :, :taps], rows)
    xr, xi, gr, gi = x[:taps], x[taps:], g[:taps], g[taps:]
    tap_rows = back(g_ref, xr * gr + xi * gi, xi * gr - xr * gi)
    out_ref[...] = tap_rows.T.astype(BF16)


def backward_kernel(taps, k_ref, v_ref, gf_ref, following_ref, filt_ref, f_ref, g_ref, gk_ref, gv_ref):
    g = spectrum(f_ref, jnp.concatenate([gf_ref[...], following_ref[...]], axis=0))
    h = tap_spectrum(f_ref, filt_ref[...], taps)
    gr, gi, hr, hi = g[:taps], g[taps:], h[:taps], h[taps:]
    grad_product = back(g_ref, hr * gr + hi * gi, hr * gi - hi * gr)
    gk_ref[...] = (grad_product * v_ref[...].astype(F32)).astype(BF16)
    gv_ref[...] = (grad_product * k_ref[...].astype(F32)).astype(BF16)


def estimate(micros):
    return pl.CostEstimate(flops=int(micros * 10**9), bytes_accessed=0, transcendentals=0)


def ignoring(body, count, skip):
    def kernel(*refs):
        return body(*refs[:skip], *refs[skip + count :])

    return kernel


def by_channel(kernel, arrays, kinds, outs, name, me=None, after=()):
    length, channels = arrays[0].shape
    width = min(512, channels) if me is None else 256
    specs = {
        "t": pl.BlockSpec((length, width), lambda i, *ids: (0, i)),
        "c": pl.BlockSpec((width, length), lambda i, *ids: (i, 0)),
        "x": pl.BlockSpec((width, length), lambda i, *ids: (i ^ ids[0][0], 0)),
    }

    def spec_of(kind, shape):
        if kind == "w":
            return pl.BlockSpec(shape, lambda i, *ids: (0,) * len(shape))
        return specs[kind]

    body = ignoring(functools.partial(kernel, length), len(after), len(arrays))
    return pl.pallas_call(
        body if me is None else lambda ids_ref, *refs: body(*refs),
        grid_spec=pltpu.PrefetchScalarGridSpec(
            num_scalar_prefetch=0 if me is None else 1,
            grid=(channels // width,),
            in_specs=[spec_of(kind, a.shape) for kind, a in zip(kinds, arrays)]
            + [pl.BlockSpec(memory_space=pl.ANY)] * len(after),
            out_specs=[specs[kind] for kind, unused in outs],
        ),
        out_shape=[
            jax.ShapeDtypeStruct((length, channels) if kind == "t" else (channels, length), dtype)
            for kind, dtype in outs
        ],
        compiler_params=pltpu.CompilerParams(vmem_limit_bytes=VMEM_BYTES),
        cost_estimate=estimate(3),
        name=name,
    )(*([] if me is None else [me]), *arrays, *after)


def grad_gated_kernel(has_sum, me_ref, cot_ref, w_ref, *refs):
    out_ref, turned_ref = refs[-2:]

    @pl.when(pl.program_id(0) == 0)
    def turn():
        turned_ref[...] = cot_ref[...].T

    total = mm(w_ref[...], turned_ref[...])
    out_ref[...] = total + refs[0][...] if has_sum else total


def grad_gated_part(me, cot, weight, off, sums):
    length, width = cot.shape
    channels = weight.shape[0]
    tile = 512
    rows = pl.BlockSpec((tile, length), lambda r, me: (r, 0))
    return pl.pallas_call(
        functools.partial(grad_gated_kernel, bool(sums)),
        grid_spec=pltpu.PrefetchScalarGridSpec(
            num_scalar_prefetch=1,
            grid=(channels // tile,),
            in_specs=[
                pl.BlockSpec((length, width), lambda r, me: (0, 0)),
                pl.BlockSpec((tile, width), lambda r, me: (r, me[1] ^ off)),
            ]
            + [rows] * len(sums),
            out_specs=[rows],
            scratch_shapes=[pltpu.VMEM((width, length), BF16)],
        ),
        out_shape=[jax.ShapeDtypeStruct((channels, length), F32)],
        compiler_params=pltpu.CompilerParams(vmem_limit_bytes=VMEM_BYTES),
        cost_estimate=estimate(4),
        name="grad_gated_part",
    )(me, cot, weight, *sums)


def both_kernel(count, with_grad, me_ref, w_ref, gated_ref, *refs):
    block, step = pl.program_id(0), pl.program_id(1)
    last = pl.num_programs(1) - 1
    mixed_refs, held_ref = refs[-count - 1 : -1], refs[-1]
    if with_grad:
        cot_refs = refs[:count]
        sum_ref, q_ref, filtered_ref, gq_ref, gf_ref = refs[count : count + 5]
        mixed_refs = refs[count + 5 : 2 * count + 5]
        held_ref, turned_ref, total_ref = refs[-3:]
        for at in range(count):

            @pl.when((block == at) & (step == 0))
            def turn():
                turned_ref[...] = cot_refs[at][...].T

        total = mm(w_ref[...], turned_ref[...])
        tile = total.shape[0]
        rows = pl.ds(pl.multiple_of(step * tile, tile), tile)

        @pl.when(block == 0)
        def begin():
            total_ref[rows, :] = sum_ref[...] + total

        @pl.when(block > 0)
        def add():
            total_ref[rows, :] = total_ref[rows, :] + total

        @pl.when(block == count - 1)
        def finish():
            grad = total_ref[rows, :].T
            gq_ref[...] = (grad * filtered_ref[...]).astype(BF16)
            gf_ref[...] = (grad * q_ref[...].astype(F32)).astype(BF16)

    part = mm(gated_ref[...], w_ref[...])

    @pl.when(step == 0)
    def first():
        held_ref[...] = part

    @pl.when(step > 0)
    def more():
        held_ref[...] = held_ref[...] + part

    for at in range(count):

        @pl.when((block == at) & (step == last))
        def give():
            mixed_refs[at][...] = held_ref[...].astype(mixed_refs[at].dtype)


def both_parts(me, gated, weight, offs, grads, after):
    length, channels = gated.shape
    tile, count = 512, len(offs)
    steps = channels // tile
    end = count - 1

    def column(b, me):
        place = me[1] ^ offs[0]
        for at in range(1, count):
            place = jnp.where(b == at, me[1] ^ offs[at], place)
        return place

    whole = pl.BlockSpec((length, channels), lambda b, r, me: (0, 0))
    by_token = pl.BlockSpec((length, tile), lambda b, r, me: (0, jnp.where(b == end, r, 0)))
    in_specs = [
        pl.BlockSpec((tile, channels), lambda b, r, me: (r, column(b, me))),
        pl.BlockSpec((length, tile), lambda b, r, me: (0, r)),
    ]
    out_specs, out_shape = [whole] * count, [
        jax.ShapeDtypeStruct((length, channels), BF16 if off % 2 else F32) for off in offs
    ]
    scratch = [pltpu.VMEM((length, channels), F32)]
    arrays = [weight, gated]
    if grads:
        arrays += grads
        in_specs += [whole] * count
        in_specs += [pl.BlockSpec((tile, length), lambda b, r, me: (jnp.where(b == 0, r, steps - 1), 0))]
        in_specs += [by_token] * 2
        out_specs = [by_token] * 2 + out_specs
        out_shape = [jax.ShapeDtypeStruct((length, channels), BF16)] * 2 + out_shape
        scratch += [pltpu.VMEM((channels, length), BF16), pltpu.VMEM((channels, length), F32)]
    return pl.pallas_call(
        ignoring(functools.partial(both_kernel, count, bool(grads)), len(after), 1 + len(arrays)),
        grid_spec=pltpu.PrefetchScalarGridSpec(
            num_scalar_prefetch=1,
            grid=(count, steps),
            in_specs=in_specs + [pl.BlockSpec(memory_space=pl.ANY)] * len(after),
            out_specs=out_specs,
            scratch_shapes=scratch,
        ),
        out_shape=out_shape,
        compiler_params=pltpu.CompilerParams(vmem_limit_bytes=VMEM_BYTES),
        cost_estimate=estimate(3 * count),
        name="grads_and_mixed" if grads else "mixed_part",
    )(me, *arrays, *after)


def pieces_kernel(per_chan, me_ref, *refs):
    out_ref = refs[-1]
    length, width = refs[0].shape
    span = width // per_chan
    count = len(refs) - 1
    piece = span // count
    for off in range(count):
        for part in range(per_chan):
            target = (me_ref[1] ^ off) * per_chan + part
            start = pl.multiple_of(part * span + me_ref[1] * piece, 128)
            block = refs[off][:, pl.ds(start, piece)]
            out_ref[target ^ me_ref[0]] = jnp.concatenate(
                [block[:, at : at + 128] for at in range(0, piece, 128)], axis=0
            )


def pieces_of(me, cots, n_ctx, after):
    length, width = cots[0].shape
    piece = width // n_ctx
    rows = length * piece // 128
    if piece % 128:
        return pieces_by_slices(me, cots, n_ctx)
    return pl.pallas_call(
        ignoring(functools.partial(pieces_kernel, n_ctx // len(cots)), len(after), 1 + len(cots)),
        grid_spec=pltpu.PrefetchScalarGridSpec(
            num_scalar_prefetch=1,
            grid=(1,),
            in_specs=[pl.BlockSpec((length, width), lambda i, me: (0, 0))] * len(cots)
            + [pl.BlockSpec(memory_space=pl.ANY)] * len(after),
            out_specs=pl.BlockSpec((n_ctx, rows, 128), lambda i, me: (0, 0, 0)),
        ),
        out_shape=jax.ShapeDtypeStruct((n_ctx, rows, 128), BF16),
        compiler_params=pltpu.CompilerParams(vmem_limit_bytes=VMEM_BYTES),
        cost_estimate=estimate(0.5),
        name="pieces",
    )(me, *cots, *after)


def pieces_by_slices(me, cots, n_ctx):
    length, width = cots[0].shape
    count = len(cots)
    piece = width // n_ctx
    table = jnp.stack(cots).reshape(count, length, n_ctx // count, count, piece)
    mine = lax.dynamic_index_in_dim(table, me[1], 3, False)
    parts = mine.transpose(0, 2, 1, 3).reshape(n_ctx, length * piece // 128, 128)
    order = jnp.arange(n_ctx, dtype=jnp.int32) ^ me[0]
    per_chan = n_ctx // count
    return parts[(order // per_chan ^ me[1]) * per_chan + order % per_chan]


def weight_kernel(slots, parts, half, me_ref, owner_ref, *refs):
    gated_refs = refs[: slots - 1]
    far_low, far_high = refs[slots - 1 : slots + 1]
    cot_refs = refs[slots + 1 : slots + 1 + parts]
    out_ref = refs[-1]
    length = far_low.shape[0]
    far = jnp.where(pl.program_id(0) < half, far_low[...], far_high[...])
    columns = jnp.concatenate([ref[...] for ref in gated_refs] + [far], axis=0)
    for part in range(parts):
        rows = []
        for slot in range(slots):
            block = cot_refs[part][owner_ref[me_ref[0], slot]]
            rows.append(
                jnp.concatenate([block[at : at + length] for at in range(0, block.shape[0], length)], axis=1)
            )
        total = mm(columns, jnp.concatenate(rows, axis=0), TN)
        piece = total.shape[1]
        place = pl.multiple_of((me_ref[1] ^ part) * piece, piece) if parts > 1 else 0
        out_ref[:, pl.ds(place, piece)] = total.astype(BF16)


def grad_weight_of(me, owners, blocks, far_low, far_high, cots):
    length, channels = blocks[0].shape
    rows = cots[0].shape[1]
    piece = rows * 128 // length
    tile = 256
    half = channels // tile // 2
    slots, parts = len(blocks) + 1, len(cots)
    in_specs = [pl.BlockSpec((length, tile), lambda i, *ids: (0, i)) for unused in blocks]
    in_specs.append(pl.BlockSpec((length, tile), lambda i, *ids: (0, jnp.minimum(i, half - 1))))
    in_specs.append(pl.BlockSpec((length, tile), lambda i, *ids: (0, jnp.maximum(i - half, 0))))
    in_specs += [pl.BlockSpec(cot.shape, lambda i, *ids: (0, 0, 0)) for cot in cots]
    return pl.pallas_call(
        functools.partial(weight_kernel, slots, parts, half),
        grid_spec=pltpu.PrefetchScalarGridSpec(
            num_scalar_prefetch=2,
            grid=(channels // tile,),
            in_specs=in_specs,
            out_specs=pl.BlockSpec((tile, piece * parts), lambda i, *ids: (i, 0)),
        ),
        out_shape=jax.ShapeDtypeStruct((channels, piece * parts), BF16),
        compiler_params=pltpu.CompilerParams(vmem_limit_bytes=VMEM_BYTES),
        cost_estimate=estimate(6),
        name="grad_weight",
    )(me, owners, *blocks, far_low, far_high, *cots)


def place_kernel(me_ref, in_ref, out_ref):
    count, rows, unused = in_ref.shape
    for at in range(count):
        out_ref[at * rows : (at + 1) * rows] = in_ref[me_ref[0] ^ at].astype(out_ref.dtype)


def placed_blocks(me, blocks):
    count, rows, width = blocks.shape
    return pl.pallas_call(
        place_kernel,
        grid_spec=pltpu.PrefetchScalarGridSpec(
            num_scalar_prefetch=1,
            grid=(1,),
            in_specs=[pl.BlockSpec(blocks.shape, lambda i, me: (0, 0, 0))],
            out_specs=pl.BlockSpec((count * rows, width), lambda i, me: (0, 0)),
        ),
        out_shape=jax.ShapeDtypeStruct((count * rows, width), F32),
        compiler_params=pltpu.CompilerParams(vmem_limit_bytes=VMEM_BYTES),
        cost_estimate=estimate(0.5),
        name="placed_blocks",
    )(me, blocks)


def in_one_piece(me, columns, length):
    count, rows, unused = columns[0].shape
    table = jnp.stack(columns)[jnp.arange(len(columns), dtype=jnp.int32) ^ me[1]]
    piece = rows * 128 // length
    flat = table.reshape(len(columns), count, length, piece).transpose(1, 2, 0, 3)
    flat = flat.reshape(count, length, piece * len(columns) // 128, 128).transpose(0, 2, 1, 3)
    return [flat.reshape(count, -1, 128)]


def cycle_of(count):
    across = 1 << ((count.bit_length() - 1) // 2)
    order = []
    for column in range(across):
        line = [row * across + column for row in range(count // across)]
        order += line if column % 2 == 0 else line[::-1]
    return order


def swap(block, axis, bit):
    size = lax.axis_size(axis)
    return lax.ppermute(block, axis, [(i, i ^ bit) for i in range(size)])


def bits_of(size):
    return [1 << place for place in range(size.bit_length() - 1)]


def gather_by_swaps(block):
    held = {0: block}
    for bit in reversed(bits_of(lax.axis_size("chan"))):
        held.update({off ^ bit: swap(held[off], "chan", bit) for off in list(held)})
    return held


def halved_kernel(kept_ref, came_ref, next_ref, left_ref):
    total = (kept_ref[...].astype(F32) + came_ref[...].astype(F32)).astype(BF16)
    count = total.shape[0] // 2
    for at in range(count):
        left_ref[at] = total[2 * at]
        next_ref[at] = total[2 * at + 1]


def added_kernel(kept_ref, came_ref, out_ref):
    out_ref[...] = (kept_ref[...].astype(F32) + came_ref[...].astype(F32)).astype(BF16)


def added(kept, came, after):
    count = kept.shape[0]
    whole = pl.BlockSpec(kept.shape, lambda i: (0, 0, 0))
    half = pl.BlockSpec((max(count // 2, 1),) + kept.shape[1:], lambda i: (0, 0, 0))
    outs = 2 if count > 1 else 1
    return pl.pallas_call(
        ignoring(halved_kernel if count > 1 else added_kernel, len(after), 2),
        grid=(1,),
        in_specs=[whole, whole] + [pl.BlockSpec(memory_space=pl.ANY)] * len(after),
        out_specs=[half] * outs,
        out_shape=[jax.ShapeDtypeStruct(half.block_shape, BF16)] * outs,
        compiler_params=pltpu.CompilerParams(vmem_limit_bytes=VMEM_BYTES),
        cost_estimate=estimate(0.5),
        name="added",
    )(kept, came, *after)


def summed(partial, gates):
    give, left = partial[1::2], partial[::2]
    for step, bit in enumerate(bits_of(partial.shape[0])):
        sums = added(left, swap(give, "ctx", bit), gates[step] if step < len(gates) else ())
        if len(sums) == 2:
            give, left = sums
    return sums[0]


def exchanged(pieces):
    held, sources, stages = pieces[None], [0], []
    for bit in bits_of(pieces.shape[0]):
        give = held[:, 1::2].reshape((-1,) + pieces.shape[1:])
        stages.append(swap(give, "ctx", bit))
        came = stages[-1].reshape((len(sources), -1) + pieces.shape[1:])
        held = jnp.concatenate([held[:, ::2], came], axis=0)
        sources += [source ^ bit for source in sources]
    return held[:, 0], sources, stages


def doubled(block, axis):
    held = block
    for bit in reversed(bits_of(lax.axis_size(axis))):
        held = jnp.stack([held, swap(held, axis, bit)], axis=1).reshape((-1,) + block.shape[1:])
    return held


def per_device(query_proj, key_proj, value_proj, filters, out_weight, cotangent):
    length, channels = query_proj.shape
    taps = filters.shape[1]
    n_ctx, n_chan = lax.axis_size("ctx"), lax.axis_size("chan")
    me = jnp.stack([lax.axis_index("ctx"), lax.axis_index("chan")]).astype(jnp.int32)
    forward, late, early, lags = [jnp.asarray(m) for m in transforms(taps)]

    product = (key_proj.astype(F32) * value_proj.astype(F32)).astype(BF16)
    earlier = lax.ppermute(product, "ctx", [(i, i + 1) for i in range(n_ctx - 1)])

    cots = {0: cotangent, 1: swap(cotangent, "chan", 1)}
    for bit in reversed(bits_of(n_chan)[1:]):
        cots.update({off ^ bit: swap(cots[off], "chan", bit) for off in list(cots) if off % 2 == 0})
    offs = sorted(off for off in cots if off % 2 == 0 and off)
    for off in offs:
        cots[off + 1] = swap(cots[off], "chan", 1)
    offs = sorted(offs + [off + 1 for off in offs])
    sums = grad_gated_part(me, cots[0], out_weight, 0, [])
    sums = grad_gated_part(me, cots[1], out_weight, 1, sums)

    gated, filtered = by_channel(
        forward_kernel,
        [query_proj, key_proj, value_proj, earlier, filters, forward, late],
        "ttttcww",
        [("t", BF16), ("t", F32)],
        "forward_filter",
        after=sums,
    )

    pieces = pieces_of(me, [cots[off] for off in range(n_chan)], n_ctx, sums)
    held, sources, stages = exchanged(pieces)

    order = cycle_of(n_ctx)
    ahead = [(order[i], order[(i + 1) % n_ctx]) for i in range(n_ctx)]
    behind = [(b, a) for a, b in ahead]
    half = channels // 2
    from_behind, from_ahead = gated, gated
    blocks = [gated]
    for step in range(n_ctx // 2 - 1):
        from_behind = lax.ppermute(from_behind, "ctx", ahead)
        from_ahead = lax.ppermute(from_ahead, "ctx", behind)
        blocks += [from_behind, from_ahead]
    far_low = lax.ppermute(from_behind[:, :half], "ctx", ahead)
    far_high = lax.ppermute(from_ahead[:, half:], "ctx", behind)

    grad_query, grad_filtered, *parts = both_parts(
        me, gated, out_weight, offs, [cots[off] for off in offs] + list(sums) + [query_proj, filtered], [pieces]
    )
    terms = dict(zip(offs, parts))
    following = lax.ppermute(grad_filtered, "ctx", [(i + 1, i) for i in range(n_ctx - 1)])

    direct = channels // n_ctx == 256
    tap_grad = by_channel(
        tap_grad_kernel,
        [key_proj, value_proj, earlier, grad_filtered, forward, lags],
        "ttttww",
        [("x" if direct else "c", BF16)],
        "tap_grad",
        me,
    )[0].reshape(n_ctx, -1, taps)
    if not direct:
        tap_grad = tap_grad[jnp.arange(n_ctx, dtype=jnp.int32) ^ me[0]]

    terms[1], terms[0] = both_parts(me, gated, out_weight, [1, 0], [], blocks[1:3] + stages[:1] + [tap_grad])
    mixed_done = [terms[0]]
    for bit in bits_of(n_chan):
        for off in [off for off in sorted(terms, reverse=True) if off & bit]:
            came = swap(terms.pop(off).astype(BF16), "chan", bit).astype(F32)
            terms[off ^ bit] = terms[off ^ bit] + came
    mixed = terms[0].astype(BF16)

    grad_key, grad_value = by_channel(
        backward_kernel,
        [key_proj, value_proj, grad_filtered, following, filters, forward, early],
        "ttttcww",
        [("t", BF16), ("t", BF16)],
        "backward_filter",
        after=blocks[3:5] + stages[1:2] + mixed_done,
    )
    gates = [mixed_done, [grad_key], blocks[5:7]]
    grad_filters = placed_blocks(me, doubled(summed(tap_grad, gates), "ctx"))

    columns = gather_by_swaps(held)
    columns = [columns[off] for off in range(n_chan)]
    if (channels // n_ctx) % 128:
        columns = in_one_piece(me, columns, length)
    owners = []
    for c in range(n_ctx):
        spot = order.index(c)
        steps = [0] + [sign * step for step in range(1, n_ctx // 2) for sign in (-1, 1)] + [n_ctx // 2]
        owners.append([sources.index(order[(spot + step) % n_ctx] ^ c) for step in steps])
    grad_weight = grad_weight_of(me, jnp.asarray(owners, jnp.int32), blocks, far_low, far_high, columns)
    return (mixed, grad_query, grad_key, grad_value, grad_filters, grad_weight)


def solution(mesh):
    placed = (
        P("ctx", "chan"),
        P("ctx", "chan"),
        P("ctx", "chan"),
        P("chan", None),
        P("chan", None),
        P("ctx", "chan"),
    )
    return jax.shard_map(
        per_device,
        mesh=mesh,
        in_specs=placed,
        out_specs=(
            P("ctx", "chan"),
            P("ctx", "chan"),
            P("ctx", "chan"),
            P("ctx", "chan"),
            P("chan", None),
            P("chan", "ctx"),
        ),
        check_vma=False,
    )
```

```python
import functools

import jax
import jax.numpy as jnp
import numpy as np
from jax import lax
from jax.experimental import pallas as pl
from jax.experimental.pallas import tpu as pltpu
from jax.sharding import PartitionSpec as P

F32 = jnp.float32
BF16 = jnp.bfloat16
VMEM_BYTES = 40 * 2**20
NT = (((1,), (1,)), ((), ()))
TN = (((0,), (0,)), ((), ()))


def halves(matrix):
    high = matrix.astype(BF16)
    low = (matrix - high.astype(np.float64)).astype(BF16)
    return np.stack([high, low])


def transforms(taps):
    points = 2 * taps
    angle = np.pi * (2 * np.arange(taps)[:, None] + 1) * np.arange(points)[None, :] / points
    forward = np.concatenate([np.cos(angle), -np.sin(angle)], axis=0)
    inverse = forward.T * (2.0 / points)
    late = inverse[taps:]
    early = inverse[:taps]
    lags = inverse[taps - np.arange(taps)]
    return halves(forward), halves(late), halves(early), halves(lags)


def mm(a, b, dims=(((1,), (0,)), ((), ()))):
    return lax.dot_general(a, b, dims, preferred_element_type=F32)


def spectrum(f_ref, rows):
    return mm(f_ref[0], rows) + mm(f_ref[1], rows)


def tap_spectrum(f_ref, filters, taps):
    return mm(f_ref[0, :, :taps], filters, NT) + mm(f_ref[1, :, :taps], filters, NT)


def back(g_ref, real, imag):
    both = jnp.concatenate([real, imag], axis=0)
    high = both.astype(BF16)
    low = (both - high.astype(F32)).astype(BF16)
    return mm(g_ref[0], high) + mm(g_ref[0], low) + mm(g_ref[1], high)


def forward_kernel(taps, q_ref, k_ref, v_ref, earlier_ref, filt_ref, f_ref, g_ref, gated_ref, filtered_ref):
    product = (k_ref[...].astype(F32) * v_ref[...].astype(F32)).astype(BF16)
    x = spectrum(f_ref, jnp.concatenate([earlier_ref[...], product], axis=0))
    h = tap_spectrum(f_ref, filt_ref[...], taps)
    xr, xi, hr, hi = x[:taps], x[taps:], h[:taps], h[taps:]
    filtered = back(g_ref, xr * hr - xi * hi, xr * hi + xi * hr)
    filtered_ref[...] = filtered
    gated_ref[...] = (q_ref[...].astype(F32) * filtered).astype(BF16)


def tap_grad_kernel(taps, k_ref, v_ref, earlier_ref, gf_ref, f_ref, g_ref, out_ref):
    product = (k_ref[...].astype(F32) * v_ref[...].astype(F32)).astype(BF16)
    x = spectrum(f_ref, jnp.concatenate([earlier_ref[...], product], axis=0))
    rows = gf_ref[...]
    g = mm(f_ref[0, :, :taps], rows) + mm(f_ref[1, :, :taps], rows)
    xr, xi, gr, gi = x[:taps], x[taps:], g[:taps], g[taps:]
    tap_rows = back(g_ref, xr * gr + xi * gi, xi * gr - xr * gi)
    out_ref[...] = tap_rows.T.astype(BF16)


def backward_kernel(taps, k_ref, v_ref, gf_ref, following_ref, filt_ref, f_ref, g_ref, gk_ref, gv_ref):
    g = spectrum(f_ref, jnp.concatenate([gf_ref[...], following_ref[...]], axis=0))
    h = tap_spectrum(f_ref, filt_ref[...], taps)
    gr, gi, hr, hi = g[:taps], g[taps:], h[:taps], h[taps:]
    grad_product = back(g_ref, hr * gr + hi * gi, hr * gi - hi * gr)
    gk_ref[...] = (grad_product * v_ref[...].astype(F32)).astype(BF16)
    gv_ref[...] = (grad_product * k_ref[...].astype(F32)).astype(BF16)


def estimate(micros):
    return pl.CostEstimate(flops=int(micros * 10**9), bytes_accessed=0, transcendentals=0)


def ignoring(body, count, skip):
    def kernel(*refs):
        return body(*refs[:skip], *refs[skip + count :])

    return kernel


def by_channel(kernel, arrays, kinds, outs, name, after=()):
    length, channels = arrays[0].shape
    width = min(512, channels)
    specs = {
        "t": pl.BlockSpec((length, width), lambda i: (0, i)),
        "c": pl.BlockSpec((width, length), lambda i: (i, 0)),
    }

    def spec_of(kind, shape):
        if kind == "w":
            return pl.BlockSpec(shape, lambda i: (0,) * len(shape))
        return specs[kind]

    return pl.pallas_call(
        ignoring(functools.partial(kernel, length), len(after), len(arrays)),
        grid=(channels // width,),
        in_specs=[spec_of(kind, a.shape) for kind, a in zip(kinds, arrays)]
        + [pl.BlockSpec(memory_space=pl.ANY)] * len(after),
        out_specs=[specs[kind] for kind, unused in outs],
        out_shape=[
            jax.ShapeDtypeStruct((length, channels) if kind == "t" else (channels, length), dtype)
            for kind, dtype in outs
        ],
        compiler_params=pltpu.CompilerParams(vmem_limit_bytes=VMEM_BYTES),
        cost_estimate=estimate(3),
        name=name,
    )(*arrays, *after)


def pass_kernel(with_mixed, with_grad, has_sum, last, me_ref, w_ref, *refs):
    refs = list(refs)
    step = pl.program_id(0)
    if with_mixed:
        gated_ref = refs.pop(0)
    if with_grad:
        cot_ref = refs.pop(0)
        sum_ref = refs.pop(0) if has_sum else None
        turned_ref = refs.pop()

        @pl.when(step == 0)
        def turn():
            turned_ref[...] = cot_ref[...].T

        total = mm(w_ref[...], turned_ref[...])
        if has_sum:
            total = total + sum_ref[...]
        if last:
            q_ref, filtered_ref, gq_ref, gf_ref = refs[:4]
            total = total.T
            gq_ref[...] = (total * filtered_ref[...]).astype(BF16)
            gf_ref[...] = (total * q_ref[...].astype(F32)).astype(BF16)
        else:
            refs[0][...] = total
    if with_mixed:
        held_ref, mixed_ref = refs.pop(), refs.pop()
        part = mm(gated_ref[...], w_ref[...])

        @pl.when(step == 0)
        def first():
            held_ref[...] = part

        @pl.when(step > 0)
        def more():
            held_ref[...] = held_ref[...] + part

        @pl.when(step == pl.num_programs(0) - 1)
        def give():
            mixed_ref[...] = held_ref[...].astype(mixed_ref.dtype)


def weight_pass(me, weight, off, gated=None, cot=None, sums=(), ends=(), after=()):
    length = (cot if gated is None else gated).shape[0]
    channels = weight.shape[0]
    tile = 512
    whole = pl.BlockSpec((length, channels), lambda r, me: (0, 0))
    by_token = pl.BlockSpec((length, tile), lambda r, me: (0, r))
    by_row = pl.BlockSpec((tile, length), lambda r, me: (r, 0))
    arrays, in_specs = [weight], [pl.BlockSpec((tile, channels), lambda r, me: (r, me[1] ^ off))]
    out_specs, out_shape, scratch = [], [], []
    if gated is not None:
        arrays.append(gated)
        in_specs.append(by_token)
    if cot is not None:
        arrays += [cot, *sums, *ends]
        in_specs += [whole] + [by_row] * len(sums) + [by_token] * len(ends)
        out_specs += [by_token] * 2 if ends else [by_row]
        out_shape += [jax.ShapeDtypeStruct((length, channels), BF16)] * 2 if ends else [
            jax.ShapeDtypeStruct((channels, length), F32)
        ]
    if gated is not None:
        out_specs.append(whole)
        out_shape.append(jax.ShapeDtypeStruct((length, channels), BF16 if off % 2 else F32))
        scratch.append(pltpu.VMEM((length, channels), F32))
    if cot is not None:
        scratch.append(pltpu.VMEM((channels, length), BF16))
    body = functools.partial(pass_kernel, gated is not None, cot is not None, bool(sums), bool(ends))
    return pl.pallas_call(
        ignoring(body, len(after), 1 + len(arrays)),
        grid_spec=pltpu.PrefetchScalarGridSpec(
            num_scalar_prefetch=1,
            grid=(channels // tile,),
            in_specs=in_specs + [pl.BlockSpec(memory_space=pl.ANY)] * len(after),
            out_specs=out_specs,
            scratch_shapes=scratch,
        ),
        out_shape=out_shape,
        compiler_params=pltpu.CompilerParams(vmem_limit_bytes=VMEM_BYTES),
        cost_estimate=estimate(3 * ((cot is not None) + (gated is not None))),
        name="grad_gated_part" if gated is None else "mixed_part" if cot is None else "grads_and_mixed",
    )(me, *arrays, *after)


def pieces_kernel(per_chan, me_ref, *refs):
    out_ref = refs[-1]
    length, width = refs[0].shape
    span = width // per_chan
    count = len(refs) - 1
    piece = span // count
    for off in range(count):
        for part in range(per_chan):
            target = (me_ref[1] ^ off) * per_chan + part
            start = pl.multiple_of(part * span + me_ref[1] * piece, 128)
            block = refs[off][:, pl.ds(start, piece)]
            out_ref[target ^ me_ref[0]] = jnp.concatenate(
                [block[:, at : at + 128] for at in range(0, piece, 128)], axis=0
            )


def pieces_of(me, cots, n_ctx, after):
    length, width = cots[0].shape
    piece = width // n_ctx
    rows = length * piece // 128
    if piece % 128:
        return pieces_by_slices(me, cots, n_ctx)
    return pl.pallas_call(
        ignoring(functools.partial(pieces_kernel, n_ctx // len(cots)), len(after), 1 + len(cots)),
        grid_spec=pltpu.PrefetchScalarGridSpec(
            num_scalar_prefetch=1,
            grid=(1,),
            in_specs=[pl.BlockSpec((length, width), lambda i, me: (0, 0))] * len(cots)
            + [pl.BlockSpec(memory_space=pl.ANY)] * len(after),
            out_specs=pl.BlockSpec((n_ctx, rows, 128), lambda i, me: (0, 0, 0)),
        ),
        out_shape=jax.ShapeDtypeStruct((n_ctx, rows, 128), BF16),
        compiler_params=pltpu.CompilerParams(vmem_limit_bytes=VMEM_BYTES),
        cost_estimate=estimate(0.5),
        name="pieces",
    )(me, *cots, *after)


def pieces_by_slices(me, cots, n_ctx):
    length, width = cots[0].shape
    count = len(cots)
    piece = width // n_ctx
    table = jnp.stack(cots).reshape(count, length, n_ctx // count, count, piece)
    mine = lax.dynamic_index_in_dim(table, me[1], 3, False)
    parts = mine.transpose(0, 2, 1, 3).reshape(n_ctx, length * piece // 128, 128)
    order = jnp.arange(n_ctx, dtype=jnp.int32) ^ me[0]
    per_chan = n_ctx // count
    return parts[(order // per_chan ^ me[1]) * per_chan + order % per_chan]


def weight_kernel(slots, parts, half, me_ref, owner_ref, *refs):
    gated_refs = refs[: slots - 1]
    far_low, far_high = refs[slots - 1 : slots + 1]
    cot_refs = refs[slots + 1 : slots + 1 + parts]
    out_ref = refs[-1]
    length = far_low.shape[0]
    far = jnp.where(pl.program_id(0) < half, far_low[...], far_high[...])
    columns = jnp.concatenate([ref[...] for ref in gated_refs] + [far], axis=0)
    for part in range(parts):
        rows = []
        for slot in range(slots):
            block = cot_refs[part][owner_ref[me_ref[0], slot]]
            rows.append(
                jnp.concatenate([block[at : at + length] for at in range(0, block.shape[0], length)], axis=1)
            )
        total = mm(columns, jnp.concatenate(rows, axis=0), TN)
        piece = total.shape[1]
        place = pl.multiple_of((me_ref[1] ^ part) * piece, piece) if parts > 1 else 0
        out_ref[:, pl.ds(place, piece)] = total.astype(BF16)


def grad_weight_of(me, owners, blocks, far_low, far_high, cots):
    length, channels = blocks[0].shape
    rows = cots[0].shape[1]
    piece = rows * 128 // length
    tile = 256
    half = channels // tile // 2
    slots, parts = len(blocks) + 1, len(cots)
    in_specs = [pl.BlockSpec((length, tile), lambda i, *ids: (0, i)) for unused in blocks]
    in_specs.append(pl.BlockSpec((length, tile), lambda i, *ids: (0, jnp.minimum(i, half - 1))))
    in_specs.append(pl.BlockSpec((length, tile), lambda i, *ids: (0, jnp.maximum(i - half, 0))))
    in_specs += [pl.BlockSpec(cot.shape, lambda i, *ids: (0, 0, 0)) for cot in cots]
    return pl.pallas_call(
        functools.partial(weight_kernel, slots, parts, half),
        grid_spec=pltpu.PrefetchScalarGridSpec(
            num_scalar_prefetch=2,
            grid=(channels // tile,),
            in_specs=in_specs,
            out_specs=pl.BlockSpec((tile, piece * parts), lambda i, *ids: (i, 0)),
        ),
        out_shape=jax.ShapeDtypeStruct((channels, piece * parts), BF16),
        compiler_params=pltpu.CompilerParams(vmem_limit_bytes=VMEM_BYTES),
        cost_estimate=estimate(6),
        name="grad_weight",
    )(me, owners, *blocks, far_low, far_high, *cots)


def in_one_piece(me, columns, length):
    count, rows, unused = columns[0].shape
    table = jnp.stack(columns)[jnp.arange(len(columns), dtype=jnp.int32) ^ me[1]]
    piece = rows * 128 // length
    flat = table.reshape(len(columns), count, length, piece).transpose(1, 2, 0, 3)
    flat = flat.reshape(count, length, piece * len(columns) // 128, 128).transpose(0, 2, 1, 3)
    return [flat.reshape(count, -1, 128)]


def cycle_of(count):
    across = 1 << ((count.bit_length() - 1) // 2)
    order = []
    for column in range(across):
        line = [row * across + column for row in range(count // across)]
        order += line if column % 2 == 0 else line[::-1]
    return order


def swap(block, axis, bit):
    size = lax.axis_size(axis)
    return lax.ppermute(block, axis, [(i, i ^ bit) for i in range(size)])


def bits_of(size):
    return [1 << place for place in range(size.bit_length() - 1)]


def gather_by_swaps(block):
    held = {0: block}
    for bit in reversed(bits_of(lax.axis_size("chan"))):
        held.update({off ^ bit: swap(held[off], "chan", bit) for off in list(held)})
    return held


def added_kernel(bit, me_ref, own_ref, came_ref, *outs):
    total = (own_ref[...].astype(F32) + came_ref[...].astype(F32)).astype(BF16)
    if not bit:
        outs[0][...] = total
        return
    rows = outs[0].shape[0]
    mine = (me_ref[0] & bit) != 0
    outs[0][...] = jnp.where(mine, total[rows:], total[:rows])
    outs[1][...] = jnp.where(mine, total[:rows], total[rows:])


def added(me, own, came, bit, after):
    shape = (own.shape[0] // 2, own.shape[1]) if bit else own.shape
    whole = pl.BlockSpec(own.shape, lambda i, me: (0, 0))
    outs = 2 if bit else 1
    return pl.pallas_call(
        ignoring(functools.partial(added_kernel, bit), len(after), 3),
        grid_spec=pltpu.PrefetchScalarGridSpec(
            num_scalar_prefetch=1,
            grid=(1,),
            in_specs=[whole, whole] + [pl.BlockSpec(memory_space=pl.ANY)] * len(after),
            out_specs=[pl.BlockSpec(shape, lambda i, me: (0, 0))] * outs,
        ),
        out_shape=[jax.ShapeDtypeStruct(shape, BF16)] * outs,
        compiler_params=pltpu.CompilerParams(vmem_limit_bytes=VMEM_BYTES),
        cost_estimate=estimate(0.5),
        name="added",
    )(me, own, came, *after)


def summed(me, partial, gates):
    bits = bits_of(lax.axis_size("ctx"))
    inner = bits[min(1, len(bits) - 1)]
    sums = partial
    for step, bit in enumerate(bits):
        came = swap(send if bit == inner else sums, "ctx", bit)
        ahead = inner if bits[step + 1 : step + 2] == [inner] else 0
        sums, *send = added(me, sums, came, ahead, gates[step] if step < len(gates) else ())
        send = send[0] if send else None
    return sums, swap(sums, "ctx", inner), inner


def joined_kernel(bit, me_ref, own_ref, other_ref, out_ref):
    rows = own_ref.shape[0]
    mine = (me_ref[0] & bit) != 0
    out_ref[:rows] = jnp.where(mine, other_ref[...], own_ref[...]).astype(F32)
    out_ref[rows:] = jnp.where(mine, own_ref[...], other_ref[...]).astype(F32)


def joined(me, own, other, bit, after):
    rows, width = own.shape
    whole = pl.BlockSpec(own.shape, lambda i, me: (0, 0))
    return pl.pallas_call(
        ignoring(functools.partial(joined_kernel, bit), len(after), 3),
        grid_spec=pltpu.PrefetchScalarGridSpec(
            num_scalar_prefetch=1,
            grid=(1,),
            in_specs=[whole, whole] + [pl.BlockSpec(memory_space=pl.ANY)] * len(after),
            out_specs=pl.BlockSpec((2 * rows, width), lambda i, me: (0, 0)),
        ),
        out_shape=jax.ShapeDtypeStruct((2 * rows, width), F32),
        compiler_params=pltpu.CompilerParams(vmem_limit_bytes=VMEM_BYTES),
        cost_estimate=estimate(0.5),
        name="joined",
    )(me, own, other, *after)


def exchanged(pieces):
    held, sources, stages = pieces[None], [0], []
    for bit in bits_of(pieces.shape[0]):
        give = held[:, 1::2].reshape((-1,) + pieces.shape[1:])
        stages.append(swap(give, "ctx", bit))
        came = stages[-1].reshape((len(sources), -1) + pieces.shape[1:])
        held = jnp.concatenate([held[:, ::2], came], axis=0)
        sources += [source ^ bit for source in sources]
    return held[:, 0], sources, stages


def per_device(query_proj, key_proj, value_proj, filters, out_weight, cotangent):
    length, channels = query_proj.shape
    taps = filters.shape[1]
    n_ctx, n_chan = lax.axis_size("ctx"), lax.axis_size("chan")
    me = jnp.stack([lax.axis_index("ctx"), lax.axis_index("chan")]).astype(jnp.int32)
    forward, late, early, lags = [jnp.asarray(m) for m in transforms(taps)]

    product = (key_proj.astype(F32) * value_proj.astype(F32)).astype(BF16)
    earlier = lax.ppermute(product, "ctx", [(i, i + 1) for i in range(n_ctx - 1)])

    cots = {0: cotangent, 1: swap(cotangent, "chan", 1)}
    for bit in reversed(bits_of(n_chan)[1:]):
        cots.update({off ^ bit: swap(cots[off], "chan", bit) for off in list(cots) if off % 2 == 0})
    offs = sorted(off for off in cots if off % 2 == 0 and off)
    for off in offs:
        cots[off + 1] = swap(cots[off], "chan", 1)
    offs = sorted(offs + [off + 1 for off in offs])
    sums = weight_pass(me, out_weight, 0, cot=cots[0])
    sums = weight_pass(me, out_weight, 1, cot=cots[1], sums=sums)

    gated, filtered = by_channel(
        forward_kernel,
        [query_proj, key_proj, value_proj, earlier, filters, forward, late],
        "ttttcww",
        [("t", BF16), ("t", F32)],
        "forward_filter",
        after=sums,
    )

    pieces = pieces_of(me, [cots[off] for off in range(n_chan)], n_ctx, sums)
    held, sources, stages = exchanged(pieces)

    order = cycle_of(n_ctx)
    ahead = [(order[i], order[(i + 1) % n_ctx]) for i in range(n_ctx)]
    behind = [(b, a) for a, b in ahead]
    half = channels // 2
    from_behind, from_ahead = gated, gated
    blocks = [gated]
    for step in range(n_ctx // 2 - 1):
        from_behind = lax.ppermute(from_behind, "ctx", ahead)
        from_ahead = lax.ppermute(from_ahead, "ctx", behind)
        blocks += [from_behind, from_ahead]
    far_low = lax.ppermute(from_behind[:, :half], "ctx", ahead)
    far_high = lax.ppermute(from_ahead[:, half:], "ctx", behind)

    terms, gates = {}, [pieces]
    for at, off in enumerate(offs[:-1]):
        *sums, terms[off] = weight_pass(me, out_weight, off, gated, cots[off], sums, after=gates)
        gates = blocks[2 * at + 1 : 2 * at + 3] + stages[at : at + 1]
    grad_query, grad_filtered, terms[offs[-1]] = weight_pass(
        me, out_weight, offs[-1], gated, cots[offs[-1]], sums, [query_proj, filtered], gates
    )
    following = lax.ppermute(grad_filtered, "ctx", [(i + 1, i) for i in range(n_ctx - 1)])

    tap_grad = by_channel(
        tap_grad_kernel,
        [key_proj, value_proj, earlier, grad_filtered, forward, lags],
        "ttttww",
        [("c", BF16)],
        "tap_grad",
        after=blocks[3:5] + stages[1:2],
    )[0]

    terms[1] = weight_pass(me, out_weight, 1, gated, after=[tap_grad])[0]
    terms[0] = weight_pass(me, out_weight, 0, gated, after=blocks[5:7] + stages[2:3] + [terms[1]])[0]
    gates = [[terms[1]], [terms[0]]]
    for bit in bits_of(n_chan):
        for off in [off for off in sorted(terms, reverse=True) if off & bit]:
            came = swap(terms.pop(off).astype(BF16), "chan", bit).astype(F32)
            terms[off ^ bit] = terms[off ^ bit] + came
    mixed = terms[0].astype(BF16)

    grad_key, grad_value = by_channel(
        backward_kernel,
        [key_proj, value_proj, grad_filtered, following, filters, forward, early],
        "ttttcww",
        [("t", BF16), ("t", BF16)],
        "backward_filter",
        after=gates[-1],
    )
    halves_summed = summed(me, tap_grad, gates + [[grad_key, far_low, far_high]])

    columns = gather_by_swaps(held)
    columns = [columns[off] for off in range(n_chan)]
    if (channels // n_ctx) % 128:
        columns = in_one_piece(me, columns, length)
    owners = []
    for c in range(n_ctx):
        spot = order.index(c)
        steps = [0] + [sign * step for step in range(1, n_ctx // 2) for sign in (-1, 1)] + [n_ctx // 2]
        owners.append([sources.index(order[(spot + step) % n_ctx] ^ c) for step in steps])
    grad_weight = grad_weight_of(me, jnp.asarray(owners, jnp.int32), blocks, far_low, far_high, columns)
    grad_filters = joined(me, *halves_summed, [grad_weight])
    return (mixed, grad_query, grad_key, grad_value, grad_filters, grad_weight)


def solution(mesh):
    placed = (
        P("ctx", "chan"),
        P("ctx", "chan"),
        P("ctx", "chan"),
        P("chan", None),
        P("chan", None),
        P("ctx", "chan"),
    )
    return jax.shard_map(
        per_device,
        mesh=mesh,
        in_specs=placed,
        out_specs=(
            P("ctx", "chan"),
            P("ctx", "chan"),
            P("ctx", "chan"),
            P("ctx", "chan"),
            P("chan", None),
            P("chan", "ctx"),
        ),
        check_vma=False,
    )
```

```python
import functools

import jax
import jax.numpy as jnp
import numpy as np
from jax import lax
from jax.experimental import pallas as pl
from jax.experimental.pallas import tpu as pltpu
from jax.sharding import PartitionSpec as P

F32 = jnp.float32
BF16 = jnp.bfloat16
VMEM_BYTES = 40 * 2**20
NT = (((1,), (1,)), ((), ()))
TN = (((0,), (0,)), ((), ()))


def halves(matrix):
    high = matrix.astype(BF16)
    low = (matrix - high.astype(np.float64)).astype(BF16)
    return np.stack([high, low])


def transforms(taps):
    points = 2 * taps
    angle = np.pi * (2 * np.arange(taps)[:, None] + 1) * np.arange(points)[None, :] / points
    forward = np.concatenate([np.cos(angle), -np.sin(angle)], axis=0)
    inverse = forward.T * (2.0 / points)
    late = inverse[taps:]
    early = inverse[:taps]
    lags = inverse[taps - np.arange(taps)]
    return halves(forward), halves(late), halves(early), halves(lags)


def mm(a, b, dims=(((1,), (0,)), ((), ()))):
    return lax.dot_general(a, b, dims, preferred_element_type=F32)


def spectrum(f_ref, rows):
    return mm(f_ref[0], rows) + mm(f_ref[1], rows)


def tap_spectrum(f_ref, filters, taps):
    return mm(f_ref[0, :, :taps], filters, NT) + mm(f_ref[1, :, :taps], filters, NT)


def back(g_ref, real, imag):
    both = jnp.concatenate([real, imag], axis=0)
    high = both.astype(BF16)
    low = (both - high.astype(F32)).astype(BF16)
    return mm(g_ref[0], high) + mm(g_ref[0], low) + mm(g_ref[1], high)


def forward_kernel(taps, q_ref, k_ref, v_ref, earlier_ref, filt_ref, f_ref, g_ref, gated_ref, filtered_ref):
    product = (k_ref[...].astype(F32) * v_ref[...].astype(F32)).astype(BF16)
    x = spectrum(f_ref, jnp.concatenate([earlier_ref[...], product], axis=0))
    h = tap_spectrum(f_ref, filt_ref[...], taps)
    xr, xi, hr, hi = x[:taps], x[taps:], h[:taps], h[taps:]
    filtered = back(g_ref, xr * hr - xi * hi, xr * hi + xi * hr)
    filtered_ref[...] = filtered
    gated_ref[...] = (q_ref[...].astype(F32) * filtered).astype(BF16)


def tap_grad_kernel(taps, k_ref, v_ref, earlier_ref, gf_ref, f_ref, g_ref, out_ref):
    product = (k_ref[...].astype(F32) * v_ref[...].astype(F32)).astype(BF16)
    x = spectrum(f_ref, jnp.concatenate([earlier_ref[...], product], axis=0))
    rows = gf_ref[...]
    g = mm(f_ref[0, :, :taps], rows) + mm(f_ref[1, :, :taps], rows)
    xr, xi, gr, gi = x[:taps], x[taps:], g[:taps], g[taps:]
    tap_rows = back(g_ref, xr * gr + xi * gi, xi * gr - xr * gi)
    out_ref[...] = tap_rows.T.astype(BF16)


def backward_kernel(taps, k_ref, v_ref, gf_ref, following_ref, filt_ref, f_ref, g_ref, gk_ref, gv_ref):
    g = spectrum(f_ref, jnp.concatenate([gf_ref[...], following_ref[...]], axis=0))
    h = tap_spectrum(f_ref, filt_ref[...], taps)
    gr, gi, hr, hi = g[:taps], g[taps:], h[:taps], h[taps:]
    grad_product = back(g_ref, hr * gr + hi * gi, hr * gi - hi * gr)
    gk_ref[...] = (grad_product * v_ref[...].astype(F32)).astype(BF16)
    gv_ref[...] = (grad_product * k_ref[...].astype(F32)).astype(BF16)


def estimate(micros):
    return pl.CostEstimate(flops=int(micros * 10**9), bytes_accessed=0, transcendentals=0)


def ignoring(body, count, skip):
    def kernel(*refs):
        return body(*refs[:skip], *refs[skip + count :])

    return kernel


def by_channel(kernel, arrays, kinds, outs, name, after=()):
    length, channels = arrays[0].shape
    width = min(512, channels)
    specs = {
        "t": pl.BlockSpec((length, width), lambda i: (0, i)),
        "c": pl.BlockSpec((width, length), lambda i: (i, 0)),
    }

    def spec_of(kind, shape):
        if kind == "w":
            return pl.BlockSpec(shape, lambda i: (0,) * len(shape))
        return specs[kind]

    return pl.pallas_call(
        ignoring(functools.partial(kernel, length), len(after), len(arrays)),
        grid=(channels // width,),
        in_specs=[spec_of(kind, a.shape) for kind, a in zip(kinds, arrays)]
        + [pl.BlockSpec(memory_space=pl.ANY)] * len(after),
        out_specs=[specs[kind] for kind, unused in outs],
        out_shape=[
            jax.ShapeDtypeStruct((length, channels) if kind == "t" else (channels, length), dtype)
            for kind, dtype in outs
        ],
        compiler_params=pltpu.CompilerParams(vmem_limit_bytes=VMEM_BYTES),
        cost_estimate=estimate(3),
        name=name,
    )(*arrays, *after)


def pass_kernel(with_mixed, with_grad, has_sum, last, me_ref, w_ref, *refs):
    refs = list(refs)
    step = pl.program_id(0)
    if with_mixed:
        gated_ref = refs.pop(0)
    if with_grad:
        cot_ref = refs.pop(0)
        sum_ref = refs.pop(0) if has_sum else None
        turned_ref = refs.pop()

        @pl.when(step == 0)
        def turn():
            turned_ref[...] = cot_ref[...].T

        total = mm(w_ref[...], turned_ref[...])
        if has_sum:
            total = total + sum_ref[...]
        if last:
            q_ref, filtered_ref, gq_ref, gf_ref = refs[:4]
            total = total.T
            gq_ref[...] = (total * filtered_ref[...]).astype(BF16)
            gf_ref[...] = (total * q_ref[...].astype(F32)).astype(BF16)
        else:
            refs[0][...] = total
    if with_mixed:
        held_ref, mixed_ref = refs.pop(), refs.pop()
        part = mm(gated_ref[...], w_ref[...])

        @pl.when(step == 0)
        def first():
            held_ref[...] = part

        @pl.when(step > 0)
        def more():
            held_ref[...] = held_ref[...] + part

        @pl.when(step == pl.num_programs(0) - 1)
        def give():
            mixed_ref[...] = held_ref[...].astype(mixed_ref.dtype)


def weight_pass(me, weight, off, gated=None, cot=None, sums=(), ends=(), after=()):
    length = (cot if gated is None else gated).shape[0]
    channels = weight.shape[0]
    tile = 512
    whole = pl.BlockSpec((length, channels), lambda r, me: (0, 0))
    by_token = pl.BlockSpec((length, tile), lambda r, me: (0, r))
    by_row = pl.BlockSpec((tile, length), lambda r, me: (r, 0))
    arrays, in_specs = [weight], [pl.BlockSpec((tile, channels), lambda r, me: (r, me[1] ^ off))]
    out_specs, out_shape, scratch = [], [], []
    if gated is not None:
        arrays.append(gated)
        in_specs.append(by_token)
    if cot is not None:
        arrays += [cot, *sums, *ends]
        in_specs += [whole] + [by_row] * len(sums) + [by_token] * len(ends)
        out_specs += [by_token] * 2 if ends else [by_row]
        out_shape += [jax.ShapeDtypeStruct((length, channels), BF16)] * 2 if ends else [
            jax.ShapeDtypeStruct((channels, length), F32)
        ]
    if gated is not None:
        out_specs.append(whole)
        out_shape.append(jax.ShapeDtypeStruct((length, channels), BF16 if off % 2 else F32))
        scratch.append(pltpu.VMEM((length, channels), F32))
    if cot is not None:
        scratch.append(pltpu.VMEM((channels, length), BF16))
    body = functools.partial(pass_kernel, gated is not None, cot is not None, bool(sums), bool(ends))
    return pl.pallas_call(
        ignoring(body, len(after), 1 + len(arrays)),
        grid_spec=pltpu.PrefetchScalarGridSpec(
            num_scalar_prefetch=1,
            grid=(channels // tile,),
            in_specs=in_specs + [pl.BlockSpec(memory_space=pl.ANY)] * len(after),
            out_specs=out_specs,
            scratch_shapes=scratch,
        ),
        out_shape=out_shape,
        compiler_params=pltpu.CompilerParams(vmem_limit_bytes=VMEM_BYTES),
        cost_estimate=estimate(3 * ((cot is not None) + (gated is not None))),
        name="grad_gated_part" if gated is None else "mixed_part" if cot is None else "grads_and_mixed",
    )(me, *arrays, *after)


def pieces_kernel(per_chan, me_ref, *refs):
    out_ref = refs[-1]
    length, width = refs[0].shape
    span = width // per_chan
    count = len(refs) - 1
    piece = span // count
    for off in range(count):
        for part in range(per_chan):
            target = (me_ref[1] ^ off) * per_chan + part
            start = pl.multiple_of(part * span + me_ref[1] * piece, 128)
            block = refs[off][:, pl.ds(start, piece)]
            out_ref[target ^ me_ref[0]] = jnp.concatenate(
                [block[:, at : at + 128] for at in range(0, piece, 128)], axis=0
            )


def pieces_of(me, cots, n_ctx, after):
    length, width = cots[0].shape
    piece = width // n_ctx
    rows = length * piece // 128
    if piece % 128:
        return pieces_by_slices(me, cots, n_ctx)
    return pl.pallas_call(
        ignoring(functools.partial(pieces_kernel, n_ctx // len(cots)), len(after), 1 + len(cots)),
        grid_spec=pltpu.PrefetchScalarGridSpec(
            num_scalar_prefetch=1,
            grid=(1,),
            in_specs=[pl.BlockSpec((length, width), lambda i, me: (0, 0))] * len(cots)
            + [pl.BlockSpec(memory_space=pl.ANY)] * len(after),
            out_specs=pl.BlockSpec((n_ctx, rows, 128), lambda i, me: (0, 0, 0)),
        ),
        out_shape=jax.ShapeDtypeStruct((n_ctx, rows, 128), BF16),
        compiler_params=pltpu.CompilerParams(vmem_limit_bytes=VMEM_BYTES),
        cost_estimate=estimate(0.5),
        name="pieces",
    )(me, *cots, *after)


def pieces_by_slices(me, cots, n_ctx):
    length, width = cots[0].shape
    count = len(cots)
    piece = width // n_ctx
    table = jnp.stack(cots).reshape(count, length, n_ctx // count, count, piece)
    mine = lax.dynamic_index_in_dim(table, me[1], 3, False)
    parts = mine.transpose(0, 2, 1, 3).reshape(n_ctx, length * piece // 128, 128)
    order = jnp.arange(n_ctx, dtype=jnp.int32) ^ me[0]
    per_chan = n_ctx // count
    return parts[(order // per_chan ^ me[1]) * per_chan + order % per_chan]


def weight_kernel(slots, parts, half, me_ref, owner_ref, *refs):
    gated_refs = refs[: slots - 1]
    far_low, far_high = refs[slots - 1 : slots + 1]
    cot_refs = refs[slots + 1 : slots + 1 + parts]
    out_ref = refs[-1]
    length = far_low.shape[0]
    far = jnp.where(pl.program_id(0) < half, far_low[...], far_high[...])
    columns = jnp.concatenate([ref[...] for ref in gated_refs] + [far], axis=0)
    for part in range(parts):
        rows = []
        for slot in range(slots):
            block = cot_refs[part][owner_ref[me_ref[0], slot]]
            rows.append(
                jnp.concatenate([block[at : at + length] for at in range(0, block.shape[0], length)], axis=1)
            )
        total = mm(columns, jnp.concatenate(rows, axis=0), TN)
        piece = total.shape[1]
        place = pl.multiple_of((me_ref[1] ^ part) * piece, piece) if parts > 1 else 0
        out_ref[:, pl.ds(place, piece)] = total.astype(BF16)


def grad_weight_of(me, owners, blocks, far_low, far_high, cots):
    length, channels = blocks[0].shape
    rows = cots[0].shape[1]
    piece = rows * 128 // length
    tile = 256
    half = channels // tile // 2
    slots, parts = len(blocks) + 1, len(cots)
    in_specs = [pl.BlockSpec((length, tile), lambda i, *ids: (0, i)) for unused in blocks]
    in_specs.append(pl.BlockSpec((length, tile), lambda i, *ids: (0, jnp.minimum(i, half - 1))))
    in_specs.append(pl.BlockSpec((length, tile), lambda i, *ids: (0, jnp.maximum(i - half, 0))))
    in_specs += [pl.BlockSpec(cot.shape, lambda i, *ids: (0, 0, 0)) for cot in cots]
    return pl.pallas_call(
        functools.partial(weight_kernel, slots, parts, half),
        grid_spec=pltpu.PrefetchScalarGridSpec(
            num_scalar_prefetch=2,
            grid=(channels // tile,),
            in_specs=in_specs,
            out_specs=pl.BlockSpec((tile, piece * parts), lambda i, *ids: (i, 0)),
        ),
        out_shape=jax.ShapeDtypeStruct((channels, piece * parts), BF16),
        compiler_params=pltpu.CompilerParams(vmem_limit_bytes=VMEM_BYTES),
        cost_estimate=estimate(6),
        name="grad_weight",
    )(me, owners, *blocks, far_low, far_high, *cots)


def in_one_piece(me, columns, length):
    count, rows, unused = columns[0].shape
    table = jnp.stack(columns)[jnp.arange(len(columns), dtype=jnp.int32) ^ me[1]]
    piece = rows * 128 // length
    flat = table.reshape(len(columns), count, length, piece).transpose(1, 2, 0, 3)
    flat = flat.reshape(count, length, piece * len(columns) // 128, 128).transpose(0, 2, 1, 3)
    return [flat.reshape(count, -1, 128)]


def cycle_of(count):
    across = 1 << ((count.bit_length() - 1) // 2)
    order = []
    for column in range(across):
        line = [row * across + column for row in range(count // across)]
        order += line if column % 2 == 0 else line[::-1]
    return order


def swap(block, axis, bit):
    size = lax.axis_size(axis)
    return lax.ppermute(block, axis, [(i, i ^ bit) for i in range(size)])


def bits_of(size):
    return [1 << place for place in range(size.bit_length() - 1)]


def gather_by_swaps(block):
    held = {0: block}
    for bit in reversed(bits_of(lax.axis_size("chan"))):
        held.update({off ^ bit: swap(held[off], "chan", bit) for off in list(held)})
    return held


def added_kernel(bit, me_ref, own_ref, came_ref, *outs):
    total = (own_ref[...].astype(F32) + came_ref[...].astype(F32)).astype(BF16)
    if not bit:
        outs[0][...] = total
        return
    rows = outs[0].shape[0]
    mine = (me_ref[0] & bit) != 0
    outs[0][...] = jnp.where(mine, total[rows:], total[:rows])
    outs[1][...] = jnp.where(mine, total[:rows], total[rows:])


def added(me, own, came, bit, after):
    shape = (own.shape[0] // 2, own.shape[1]) if bit else own.shape
    whole = pl.BlockSpec(own.shape, lambda i, me: (0, 0))
    outs = 2 if bit else 1
    return pl.pallas_call(
        ignoring(functools.partial(added_kernel, bit), len(after), 3),
        grid_spec=pltpu.PrefetchScalarGridSpec(
            num_scalar_prefetch=1,
            grid=(1,),
            in_specs=[whole, whole] + [pl.BlockSpec(memory_space=pl.ANY)] * len(after),
            out_specs=[pl.BlockSpec(shape, lambda i, me: (0, 0))] * outs,
        ),
        out_shape=[jax.ShapeDtypeStruct(shape, BF16)] * outs,
        compiler_params=pltpu.CompilerParams(vmem_limit_bytes=VMEM_BYTES),
        cost_estimate=estimate(0.5),
        name="added",
    )(me, own, came, *after)


def split(me, block, bit):
    rows = block.shape[0] // 2
    mine = (me[0] & bit) != 0
    low, high = block[:rows], block[rows:]
    return jnp.where(mine, high, low), jnp.where(mine, low, high)


def summed(me, partial, gates):
    bits = bits_of(lax.axis_size("ctx"))
    sums, send = split(me, partial, bits[0])
    for step, bit in enumerate(bits):
        came = swap(send if step < 2 else sums, "ctx", bit)
        sums, *send = added(me, sums, came, bits[1] if step == 0 else 0, gates[step] if step < len(gates) else ())
        send = send[0] if send else None
    sums = joined(me, sums, swap(sums, "ctx", bits[1]), bits[1], BF16, ())
    return sums, swap(sums, "ctx", bits[0]), bits[0]


def joined_kernel(bit, me_ref, own_ref, other_ref, out_ref):
    rows = own_ref.shape[0]
    mine = (me_ref[0] & bit) != 0
    out_ref[:rows] = jnp.where(mine, other_ref[...], own_ref[...]).astype(out_ref.dtype)
    out_ref[rows:] = jnp.where(mine, own_ref[...], other_ref[...]).astype(out_ref.dtype)


def joined(me, own, other, bit, dtype, after):
    rows, width = own.shape
    whole = pl.BlockSpec(own.shape, lambda i, me: (0, 0))
    return pl.pallas_call(
        ignoring(functools.partial(joined_kernel, bit), len(after), 3),
        grid_spec=pltpu.PrefetchScalarGridSpec(
            num_scalar_prefetch=1,
            grid=(1,),
            in_specs=[whole, whole] + [pl.BlockSpec(memory_space=pl.ANY)] * len(after),
            out_specs=pl.BlockSpec((2 * rows, width), lambda i, me: (0, 0)),
        ),
        out_shape=jax.ShapeDtypeStruct((2 * rows, width), dtype),
        compiler_params=pltpu.CompilerParams(vmem_limit_bytes=VMEM_BYTES),
        cost_estimate=estimate(0.5),
        name="joined",
    )(me, own, other, *after)


def exchanged(pieces):
    held, sources, stages = pieces[None], [0], []
    for bit in reversed(bits_of(pieces.shape[0])):
        give = held[:, bit:].reshape((-1,) + pieces.shape[1:])
        stages.append(swap(give, "ctx", bit))
        came = stages[-1].reshape((len(sources), bit) + pieces.shape[1:])
        held = jnp.concatenate([held[:, :bit], came], axis=0)
        sources += [source ^ bit for source in sources]
    return held[:, 0], sources, stages


def per_device(query_proj, key_proj, value_proj, filters, out_weight, cotangent):
    length, channels = query_proj.shape
    taps = filters.shape[1]
    n_ctx, n_chan = lax.axis_size("ctx"), lax.axis_size("chan")
    me = jnp.stack([lax.axis_index("ctx"), lax.axis_index("chan")]).astype(jnp.int32)
    forward, late, early, lags = [jnp.asarray(m) for m in transforms(taps)]

    product = (key_proj.astype(F32) * value_proj.astype(F32)).astype(BF16)
    product, cotangent = lax.optimization_barrier((product, cotangent))
    earlier = lax.ppermute(product, "ctx", [(i, i + 1) for i in range(n_ctx - 1)])

    cots = {0: cotangent, 1: swap(cotangent, "chan", 1)}
    for bit in reversed(bits_of(n_chan)[1:]):
        cots.update({off ^ bit: swap(cots[off], "chan", bit) for off in list(cots) if off % 2 == 0})
    offs = sorted(off for off in cots if off % 2 == 0 and off)
    for off in offs:
        cots[off + 1] = swap(cots[off], "chan", 1)
    offs = sorted(offs + [off + 1 for off in offs])
    sums = weight_pass(me, out_weight, 0, cot=cots[0])
    sums = weight_pass(me, out_weight, 1, cot=cots[1], sums=sums)

    gated, filtered = by_channel(
        forward_kernel,
        [query_proj, key_proj, value_proj, earlier, filters, forward, late],
        "ttttcww",
        [("t", BF16), ("t", F32)],
        "forward_filter",
        after=sums,
    )

    pieces = pieces_of(me, [cots[off] for off in range(n_chan)], n_ctx, sums)
    held, sources, stages = exchanged(pieces)

    order = cycle_of(n_ctx)
    ahead = [(order[i], order[(i + 1) % n_ctx]) for i in range(n_ctx)]
    behind = [(b, a) for a, b in ahead]
    half = channels // 2
    from_behind, from_ahead = gated, gated
    blocks = [gated]
    for step in range(n_ctx // 2 - 1):
        from_behind = lax.ppermute(from_behind, "ctx", ahead)
        from_ahead = lax.ppermute(from_ahead, "ctx", behind)
        blocks += [from_behind, from_ahead]
    far_low = lax.ppermute(from_behind[:, :half], "ctx", ahead)
    far_high = lax.ppermute(from_ahead[:, half:], "ctx", behind)

    terms = {}
    for off in offs[:-1]:
        *sums, terms[off] = weight_pass(me, out_weight, off, gated, cots[off], sums, after=[pieces])
    grad_query, grad_filtered, terms[offs[-1]] = weight_pass(
        me, out_weight, offs[-1], gated, cots[offs[-1]], sums, [query_proj, filtered]
    )
    following = lax.ppermute(grad_filtered, "ctx", [(i + 1, i) for i in range(n_ctx - 1)])

    tap_grad = by_channel(
        tap_grad_kernel,
        [key_proj, value_proj, earlier, grad_filtered, forward, lags],
        "ttttww",
        [("c", BF16)],
        "tap_grad",
    )[0]

    terms[1] = weight_pass(me, out_weight, 1, gated, after=blocks[1:3] + stages[:1] + [tap_grad])[0]
    terms[0] = weight_pass(me, out_weight, 0, gated, after=blocks[3:5] + stages[1:2] + [terms[1]])[0]
    gates = [[terms[1]], [terms[0]]]
    for bit in bits_of(n_chan):
        for off in [off for off in sorted(terms, reverse=True) if off & bit]:
            came = swap(terms.pop(off).astype(BF16), "chan", bit).astype(F32)
            terms[off ^ bit] = terms[off ^ bit] + came
    mixed = terms[0].astype(BF16)

    grad_key, grad_value = by_channel(
        backward_kernel,
        [key_proj, value_proj, grad_filtered, following, filters, forward, early],
        "ttttcww",
        [("t", BF16), ("t", BF16)],
        "backward_filter",
        after=gates[-1] + blocks[5:7],
    )
    halves_summed = summed(me, tap_grad, gates + [[grad_key, far_low, far_high]])

    columns = gather_by_swaps(held)
    columns = [columns[off] for off in range(n_chan)]
    if (channels // n_ctx) % 128:
        columns = in_one_piece(me, columns, length)
    owners = []
    for c in range(n_ctx):
        spot = order.index(c)
        steps = [0] + [sign * step for step in range(1, n_ctx // 2) for sign in (-1, 1)] + [n_ctx // 2]
        owners.append([sources.index(order[(spot + step) % n_ctx] ^ c) for step in steps])
    grad_weight = grad_weight_of(me, jnp.asarray(owners, jnp.int32), blocks, far_low, far_high, columns)
    grad_filters = joined(me, *halves_summed, F32, [grad_weight])
    return (mixed, grad_query, grad_key, grad_value, grad_filters, grad_weight)


def solution(mesh):
    placed = (
        P("ctx", "chan"),
        P("ctx", "chan"),
        P("ctx", "chan"),
        P("chan", None),
        P("chan", None),
        P("ctx", "chan"),
    )
    return jax.shard_map(
        per_device,
        mesh=mesh,
        in_specs=placed,
        out_specs=(
            P("ctx", "chan"),
            P("ctx", "chan"),
            P("ctx", "chan"),
            P("ctx", "chan"),
            P("chan", None),
            P("chan", "ctx"),
        ),
        check_vma=False,
    )
```

```python
import functools

import jax
import jax.numpy as jnp
import numpy as np
from jax import lax
from jax.experimental import pallas as pl
from jax.experimental.pallas import tpu as pltpu
from jax.sharding import PartitionSpec as P

F32 = jnp.float32
BF16 = jnp.bfloat16
VMEM_BYTES = 40 * 2**20
NT = (((1,), (1,)), ((), ()))
TN = (((0,), (0,)), ((), ()))


def halves(matrix):
    high = matrix.astype(BF16)
    low = (matrix - high.astype(np.float64)).astype(BF16)
    return np.stack([high, low])


def transforms(taps):
    points = 2 * taps
    angle = np.pi * (2 * np.arange(taps)[:, None] + 1) * np.arange(points)[None, :] / points
    forward = np.concatenate([np.cos(angle), -np.sin(angle)], axis=0)
    inverse = forward.T * (2.0 / points)
    late = inverse[taps:]
    early = inverse[:taps]
    lags = inverse[taps - np.arange(taps)]
    return halves(forward), halves(late), halves(early), halves(lags)


def mm(a, b, dims=(((1,), (0,)), ((), ()))):
    return lax.dot_general(a, b, dims, preferred_element_type=F32)


def spectrum(f_ref, rows):
    return mm(f_ref[0], rows) + mm(f_ref[1], rows)


def tap_spectrum(f_ref, filters, taps):
    return mm(f_ref[0, :, :taps], filters, NT) + mm(f_ref[1, :, :taps], filters, NT)


def back(g_ref, real, imag):
    both = jnp.concatenate([real, imag], axis=0)
    high = both.astype(BF16)
    low = (both - high.astype(F32)).astype(BF16)
    return mm(g_ref[0], high) + mm(g_ref[0], low) + mm(g_ref[1], high)


def forward_kernel(taps, q_ref, k_ref, v_ref, earlier_ref, filt_ref, f_ref, g_ref, gated_ref, filtered_ref):
    product = (k_ref[...].astype(F32) * v_ref[...].astype(F32)).astype(BF16)
    x = spectrum(f_ref, jnp.concatenate([earlier_ref[...], product], axis=0))
    h = tap_spectrum(f_ref, filt_ref[...], taps)
    xr, xi, hr, hi = x[:taps], x[taps:], h[:taps], h[taps:]
    filtered = back(g_ref, xr * hr - xi * hi, xr * hi + xi * hr)
    filtered_ref[...] = filtered
    gated_ref[...] = (q_ref[...].astype(F32) * filtered).astype(BF16)


def tap_grad_kernel(taps, k_ref, v_ref, low_ref, high_ref, gf_ref, f_ref, g_ref, out_ref):
    product = (k_ref[...].astype(F32) * v_ref[...].astype(F32)).astype(BF16)
    x = spectrum(f_ref, jnp.concatenate([of_half(low_ref, high_ref), product], axis=0))
    rows = gf_ref[...]
    g = mm(f_ref[0, :, :taps], rows) + mm(f_ref[1, :, :taps], rows)
    xr, xi, gr, gi = x[:taps], x[taps:], g[:taps], g[taps:]
    tap_rows = back(g_ref, xr * gr + xi * gi, xi * gr - xr * gi)
    out_ref[...] = tap_rows.T.astype(BF16)


def backward_kernel(taps, k_ref, v_ref, gf_ref, following_ref, filt_ref, f_ref, g_ref, gk_ref, gv_ref):
    g = spectrum(f_ref, jnp.concatenate([gf_ref[...], following_ref[...]], axis=0))
    h = tap_spectrum(f_ref, filt_ref[...], taps)
    gr, gi, hr, hi = g[:taps], g[taps:], h[:taps], h[taps:]
    grad_product = back(g_ref, hr * gr + hi * gi, hr * gi - hi * gr)
    gk_ref[...] = (grad_product * v_ref[...].astype(F32)).astype(BF16)
    gv_ref[...] = (grad_product * k_ref[...].astype(F32)).astype(BF16)


def estimate(micros):
    return pl.CostEstimate(flops=int(micros * 10**9), bytes_accessed=0, transcendentals=0)


def ignoring(body, count, skip):
    def kernel(*refs):
        return body(*refs[:skip], *refs[skip + count :])

    return kernel


def half_specs(shape, count):
    middle = count // 2
    return [
        pl.BlockSpec(shape, lambda i, *ids: (0, jnp.minimum(i, middle - 1))),
        pl.BlockSpec(shape, lambda i, *ids: (0, jnp.maximum(i - middle, 0))),
    ]


def of_half(low_ref, high_ref):
    return jnp.where(pl.program_id(0) < pl.num_programs(0) // 2, low_ref[...], high_ref[...])


def by_channel(kernel, arrays, kinds, outs, name, after=(), half=None):
    length, channels = arrays[0].shape
    width = min(512, channels // 2)
    steps = channels // width
    first = 0
    if half is not None:
        channels, steps = channels // 2, steps // 2
        first = half * steps
    specs = {
        "t": pl.BlockSpec((length, width), lambda i: (0, first + i)),
        "c": pl.BlockSpec((width, length), lambda i: (first + i, 0)),
        "n": pl.BlockSpec((length, width), lambda i: (0, i)),
    }
    operands, in_specs = [], []
    for kind, array in zip(kinds, arrays):
        if kind == "h":
            operands += array
            in_specs += half_specs((length, width), steps)
            continue
        operands.append(array)
        in_specs.append(
            pl.BlockSpec(array.shape, lambda i, rank=array.ndim: (0,) * rank) if kind == "w" else specs[kind]
        )
    return pl.pallas_call(
        ignoring(functools.partial(kernel, length), len(after), len(operands)),
        grid=(steps,),
        in_specs=in_specs + [pl.BlockSpec(memory_space=pl.ANY)] * len(after),
        out_specs=[specs[kind] for kind, unused in outs],
        out_shape=[
            jax.ShapeDtypeStruct((channels, length) if kind == "c" else (length, channels), dtype)
            for kind, dtype in outs
        ],
        compiler_params=pltpu.CompilerParams(vmem_limit_bytes=VMEM_BYTES),
        cost_estimate=estimate(0.7),
        name=name,
    )(*operands, *after)


def pass_kernel(with_mixed, with_grad, has_sum, last, me_ref, w_ref, *refs):
    refs = list(refs)
    step = pl.program_id(0)
    if with_mixed:
        gated = of_half(refs.pop(0), refs.pop(0))
    if with_grad:
        cot_ref = refs.pop(0)
        sum_ref = refs.pop(0) if has_sum else None
        turned_ref = refs.pop()

        @pl.when(step == 0)
        def turn():
            turned_ref[...] = cot_ref[...].T

        total = mm(w_ref[...], turned_ref[...])
        if has_sum:
            total = total + sum_ref[...]
        if last:
            q_ref, low_ref, high_ref, gq_ref, gf_ref = refs[:5]
            total = total.T
            gq_ref[...] = (total * of_half(low_ref, high_ref)).astype(BF16)
            gf_ref[...] = (total * q_ref[...].astype(F32)).astype(BF16)
        else:
            refs[0][...] = total
    if with_mixed:
        held_ref, mixed_ref = refs.pop(), refs.pop()
        part = mm(gated, w_ref[...])

        @pl.when(step == 0)
        def first():
            held_ref[...] = part

        @pl.when(step > 0)
        def more():
            held_ref[...] = held_ref[...] + part

        @pl.when(step == pl.num_programs(0) - 1)
        def give():
            mixed_ref[...] = held_ref[...].astype(mixed_ref.dtype)


def weight_pass(me, weight, off, gated=None, cot=None, sums=(), ends=(), after=()):
    length = (cot if gated is None else gated[0]).shape[0]
    channels = weight.shape[0]
    tile = 512
    whole = pl.BlockSpec((length, channels), lambda r, me: (0, 0))
    by_token = pl.BlockSpec((length, tile), lambda r, me: (0, r))
    by_row = pl.BlockSpec((tile, length), lambda r, me: (r, 0))
    arrays, in_specs = [weight], [pl.BlockSpec((tile, channels), lambda r, me: (r, me[1] ^ off))]
    out_specs, out_shape, scratch = [], [], []
    by_half = half_specs((length, tile), channels // tile)
    if gated is not None:
        arrays += gated
        in_specs += by_half
    if cot is not None:
        arrays += [cot, *sums, *ends]
        in_specs += [whole] + [by_row] * len(sums) + ([by_token] + by_half if ends else [])
        out_specs += [by_token] * 2 if ends else [by_row]
        out_shape += [jax.ShapeDtypeStruct((length, channels), BF16)] * 2 if ends else [
            jax.ShapeDtypeStruct((channels, length), F32)
        ]
    if gated is not None:
        out_specs.append(whole)
        out_shape.append(jax.ShapeDtypeStruct((length, channels), BF16 if off % 2 else F32))
        scratch.append(pltpu.VMEM((length, channels), F32))
    if cot is not None:
        scratch.append(pltpu.VMEM((channels, length), BF16))
    body = functools.partial(pass_kernel, gated is not None, cot is not None, bool(sums), bool(ends))
    return pl.pallas_call(
        ignoring(body, len(after), 1 + len(arrays)),
        grid_spec=pltpu.PrefetchScalarGridSpec(
            num_scalar_prefetch=1,
            grid=(channels // tile,),
            in_specs=in_specs + [pl.BlockSpec(memory_space=pl.ANY)] * len(after),
            out_specs=out_specs,
            scratch_shapes=scratch,
        ),
        out_shape=out_shape,
        compiler_params=pltpu.CompilerParams(vmem_limit_bytes=VMEM_BYTES),
        cost_estimate=estimate(0.7 * ((cot is not None) + (gated is not None))),
        name="grad_gated_part" if gated is None else "mixed_part" if cot is None else "grads_and_mixed",
    )(me, *arrays, *after)


def pieces_kernel(per_chan, me_ref, *refs):
    out_ref = refs[-1]
    length, width = refs[0].shape
    span = width // per_chan
    count = len(refs) - 1
    piece = span // count
    for off in range(count):
        for part in range(per_chan):
            target = (me_ref[1] ^ off) * per_chan + part
            start = pl.multiple_of(part * span + me_ref[1] * piece, 128)
            block = refs[off][:, pl.ds(start, piece)]
            out_ref[target ^ me_ref[0]] = jnp.concatenate(
                [block[:, at : at + 128] for at in range(0, piece, 128)], axis=0
            )


def pieces_of(me, cots, n_ctx, after):
    length, width = cots[0].shape
    piece = width // n_ctx
    rows = length * piece // 128
    if piece % 128:
        return pieces_by_slices(me, cots, n_ctx)
    return pl.pallas_call(
        ignoring(functools.partial(pieces_kernel, n_ctx // len(cots)), len(after), 1 + len(cots)),
        grid_spec=pltpu.PrefetchScalarGridSpec(
            num_scalar_prefetch=1,
            grid=(1,),
            in_specs=[pl.BlockSpec((length, width), lambda i, me: (0, 0))] * len(cots)
            + [pl.BlockSpec(memory_space=pl.ANY)] * len(after),
            out_specs=pl.BlockSpec((n_ctx, rows, 128), lambda i, me: (0, 0, 0)),
        ),
        out_shape=jax.ShapeDtypeStruct((n_ctx, rows, 128), BF16),
        compiler_params=pltpu.CompilerParams(vmem_limit_bytes=VMEM_BYTES),
        cost_estimate=estimate(0.5),
        name="pieces",
    )(me, *cots, *after)


def pieces_by_slices(me, cots, n_ctx):
    length, width = cots[0].shape
    count = len(cots)
    piece = width // n_ctx
    table = jnp.stack(cots).reshape(count, length, n_ctx // count, count, piece)
    mine = lax.dynamic_index_in_dim(table, me[1], 3, False)
    parts = mine.transpose(0, 2, 1, 3).reshape(n_ctx, length * piece // 128, 128)
    order = jnp.arange(n_ctx, dtype=jnp.int32) ^ me[0]
    per_chan = n_ctx // count
    return parts[(order // per_chan ^ me[1]) * per_chan + order % per_chan]


def weight_kernel(slots, parts, me_ref, owner_ref, *refs):
    cot_refs = refs[slots : slots + parts]
    out_ref = refs[-1]
    length = refs[0].shape[0]
    columns = jnp.concatenate([ref[...] for ref in refs[:slots]], axis=0)
    for part in range(parts):
        rows = []
        for slot in range(slots):
            block = cot_refs[part][owner_ref[me_ref[0], slot]]
            rows.append(
                jnp.concatenate([block[at : at + length] for at in range(0, block.shape[0], length)], axis=1)
            )
        total = mm(columns, jnp.concatenate(rows, axis=0), TN)
        piece = total.shape[1]
        place = pl.multiple_of((me_ref[1] ^ part) * piece, piece) if parts > 1 else 0
        out_ref[:, pl.ds(place, piece)] = total.astype(BF16)


def grad_weight_of(me, owners, blocks, cots, earlier):
    length, channels = blocks[0].shape
    rows = cots[0].shape[1]
    piece = rows * 128 // length
    tile = 256
    first = len(earlier) * (channels // tile)
    slots, parts = len(blocks), len(cots)
    in_specs = [pl.BlockSpec((length, tile), lambda i, *ids: (0, i)) for unused in blocks]
    in_specs += [pl.BlockSpec(cot.shape, lambda i, *ids: (0, 0, 0)) for cot in cots]
    return pl.pallas_call(
        ignoring(functools.partial(weight_kernel, slots, parts), len(earlier), 2 + slots + parts),
        grid_spec=pltpu.PrefetchScalarGridSpec(
            num_scalar_prefetch=2,
            grid=(channels // tile,),
            in_specs=in_specs + [pl.BlockSpec(memory_space=pl.ANY)] * len(earlier),
            out_specs=pl.BlockSpec((tile, piece * parts), lambda i, *ids: (first + i, 0)),
        ),
        out_shape=jax.ShapeDtypeStruct((2 * channels, piece * parts), BF16),
        input_output_aliases={2 + slots + parts: 0} if earlier else {},
        compiler_params=pltpu.CompilerParams(vmem_limit_bytes=VMEM_BYTES),
        cost_estimate=estimate(2),
        name="grad_weight",
    )(me, owners, *blocks, *cots, *earlier)


def in_one_piece(me, columns, length):
    count, rows, unused = columns[0].shape
    table = jnp.stack(columns)[jnp.arange(len(columns), dtype=jnp.int32) ^ me[1]]
    piece = rows * 128 // length
    flat = table.reshape(len(columns), count, length, piece).transpose(1, 2, 0, 3)
    flat = flat.reshape(count, length, piece * len(columns) // 128, 128).transpose(0, 2, 1, 3)
    return [flat.reshape(count, -1, 128)]


def cycle_of(count):
    across = 1 << ((count.bit_length() - 1) // 2)
    order = []
    for column in range(across):
        line = [row * across + column for row in range(count // across)]
        order += line if column % 2 == 0 else line[::-1]
    return order


def held_until(arrays, kernels):
    return lax.optimization_barrier((*arrays, *kernels))[: len(arrays)]


class Gather:
    def __init__(self, count):
        self.order = cycle_of(count)
        self.ahead = [(self.order[i], self.order[(i + 1) % count]) for i in range(count)]
        self.behind = [(b, a) for a, b in self.ahead]
        self.last = count // 2 - 1
        self.ends = [None, None]
        self.blocks = [[], []]
        self.turns = []

    def start(self, part, block):
        self.ends[part] = (block, block)
        self.blocks[part].append(block)
        self.turns.insert(0, (part, 0))
        self.step(())

    def step(self, kernels):
        if not self.turns:
            return []
        part, step = self.turns.pop(0)
        came = list(self.ends[part]) if step else []
        from_behind, from_ahead = held_until(self.ends[part], kernels) if kernels else self.ends[part]
        if step == self.last:
            far = lax.ppermute(from_ahead, "ctx", self.behind) if part else lax.ppermute(from_behind, "ctx", self.ahead)
            self.blocks[part].append(far)
            return came
        self.ends[part] = (
            lax.ppermute(from_behind, "ctx", self.ahead), lax.ppermute(from_ahead, "ctx", self.behind)
        )
        self.blocks[part] += self.ends[part]
        self.turns.append((part, step + 1))
        return came


def swap(block, axis, bit):
    size = lax.axis_size(axis)
    return lax.ppermute(block, axis, [(i, i ^ bit) for i in range(size)])


def bits_of(size):
    return [1 << place for place in range(size.bit_length() - 1)]


def gather_by_swaps(block):
    held = {0: block}
    for bit in reversed(bits_of(lax.axis_size("chan"))):
        held.update({off ^ bit: swap(held[off], "chan", bit) for off in list(held)})
    return held


def added_kernel(bit, me_ref, own_ref, came_ref, *outs):
    total = (own_ref[...].astype(F32) + came_ref[...].astype(F32)).astype(BF16)
    if not bit:
        outs[0][...] = total
        return
    rows = outs[0].shape[0]
    mine = (me_ref[0] & bit) != 0
    outs[0][...] = jnp.where(mine, total[rows:], total[:rows])
    outs[1][...] = jnp.where(mine, total[:rows], total[rows:])


def added(me, own, came, bit, after):
    shape = (own.shape[0] // 2, own.shape[1]) if bit else own.shape
    whole = pl.BlockSpec(own.shape, lambda i, me: (0, 0))
    outs = 2 if bit else 1
    return pl.pallas_call(
        ignoring(functools.partial(added_kernel, bit), len(after), 3),
        grid_spec=pltpu.PrefetchScalarGridSpec(
            num_scalar_prefetch=1,
            grid=(1,),
            in_specs=[whole, whole] + [pl.BlockSpec(memory_space=pl.ANY)] * len(after),
            out_specs=[pl.BlockSpec(shape, lambda i, me: (0, 0))] * outs,
        ),
        out_shape=[jax.ShapeDtypeStruct(shape, BF16)] * outs,
        compiler_params=pltpu.CompilerParams(vmem_limit_bytes=VMEM_BYTES),
        cost_estimate=estimate(0.5),
        name="added",
    )(me, own, came, *after)


def split(me, block, bit):
    rows = block.shape[0] // 2
    mine = (me[0] & bit) != 0
    low, high = block[:rows], block[rows:]
    return jnp.where(mine, high, low), jnp.where(mine, low, high)


def summed(me, partial, gates):
    bits = bits_of(lax.axis_size("ctx"))
    sums, send = split(me, partial, bits[0])
    for step, bit in enumerate(bits):
        came = swap(send if step < 2 else sums, "ctx", bit)
        sums, *send = added(me, sums, came, bits[1] if step == 0 else 0, gates[step] if step < len(gates) else ())
        send = send[0] if send else None
    sums = joined(me, sums, swap(sums, "ctx", bits[1]), bits[1], BF16, gates[-1])
    return sums, swap(sums, "ctx", bits[0]), bits[0]


def joined_kernel(bit, me_ref, own_ref, other_ref, out_ref):
    rows = own_ref.shape[0]
    mine = (me_ref[0] & bit) != 0
    out_ref[:rows] = jnp.where(mine, other_ref[...], own_ref[...]).astype(out_ref.dtype)
    out_ref[rows:] = jnp.where(mine, own_ref[...], other_ref[...]).astype(out_ref.dtype)


def joined(me, own, other, bit, dtype, after):
    rows, width = own.shape
    whole = pl.BlockSpec(own.shape, lambda i, me: (0, 0))
    return pl.pallas_call(
        ignoring(functools.partial(joined_kernel, bit), len(after), 3),
        grid_spec=pltpu.PrefetchScalarGridSpec(
            num_scalar_prefetch=1,
            grid=(1,),
            in_specs=[whole, whole] + [pl.BlockSpec(memory_space=pl.ANY)] * len(after),
            out_specs=pl.BlockSpec((2 * rows, width), lambda i, me: (0, 0)),
        ),
        out_shape=jax.ShapeDtypeStruct((2 * rows, width), dtype),
        compiler_params=pltpu.CompilerParams(vmem_limit_bytes=VMEM_BYTES),
        cost_estimate=estimate(0.5),
        name="joined",
    )(me, own, other, *after)


class Exchange:
    def __init__(self, pieces):
        self.shape = pieces.shape[1:]
        self.held, self.sources = pieces[None], [0]
        self.bits = bits_of(pieces.shape[0])

    def step(self, kernels):
        if not self.bits:
            return []
        bit = self.bits.pop()
        give = self.held[:, bit:].reshape((-1,) + self.shape)
        came = swap(held_until([give], kernels)[0], "ctx", bit)
        self.held = jnp.concatenate(
            [self.held[:, :bit], came.reshape((len(self.sources), bit) + self.shape)], axis=0
        )
        self.sources += [source ^ bit for source in self.sources]
        return [came]


def per_device(query_proj, key_proj, value_proj, filters, out_weight, cotangent):
    length, channels = query_proj.shape
    taps = filters.shape[1]
    n_ctx, n_chan = lax.axis_size("ctx"), lax.axis_size("chan")
    me = jnp.stack([lax.axis_index("ctx"), lax.axis_index("chan")]).astype(jnp.int32)
    forward, late, early, lags = [jnp.asarray(m) for m in transforms(taps)]

    half = channels // 2
    halves_at = [slice(0, half), slice(half, channels)]
    products = [
        (key_proj[:, at].astype(F32) * value_proj[:, at].astype(F32)).astype(BF16) for at in halves_at
    ]
    *products, cotangent = lax.optimization_barrier((*products, cotangent))
    onward = [(i, i + 1) for i in range(n_ctx - 1)]
    earlier = [lax.ppermute(product, "ctx", onward) for product in products]

    cots = {0: cotangent, 1: swap(cotangent, "chan", 1)}
    for bit in reversed(bits_of(n_chan)[1:]):
        cots.update({off ^ bit: swap(cots[off], "chan", bit) for off in list(cots) if off % 2 == 0})
    offs = sorted(off for off in cots if off % 2 == 0 and off)
    sums = weight_pass(me, out_weight, 0, cot=cots[0])
    for off in offs:
        cots[off + 1] = swap(held_until([cots[off]], sums)[0], "chan", 1)
    offs = sorted(offs + [off + 1 for off in offs])

    gather = Gather(n_ctx)
    gated, filtered = [], []
    for part in (0, 1):
        gated_half, filtered_half = by_channel(
            forward_kernel,
            [query_proj, key_proj, value_proj, earlier[part], filters, forward, late],
            "tttncww",
            [("n", BF16), ("n", F32)],
            "forward_filter",
            [*sums, *gated],
            part,
        )
        gated.append(gated_half)
        filtered.append(filtered_half)
        gather.start(part, gated_half)
    sums = weight_pass(me, out_weight, 1, cot=cots[1], sums=sums, after=gated)
    came = gather.step(sums)

    pieces = pieces_of(me, [cots[off] for off in range(n_chan)], n_ctx, sums)
    exchange = Exchange(pieces)
    brought = exchange.step([pieces])

    terms = {}
    for off in offs[:-1]:
        *sums, terms[off] = weight_pass(me, out_weight, off, gated, cots[off], sums, after=[pieces] + came)
        came = gather.step(sums)
    grad_query, grad_filtered, terms[offs[-1]] = weight_pass(
        me, out_weight, offs[-1], gated, cots[offs[-1]], sums, [query_proj, *filtered], came
    )
    came = gather.step([grad_filtered])

    tap_grad = by_channel(
        tap_grad_kernel,
        [key_proj, value_proj, earlier, grad_filtered, forward, lags],
        "tthtww",
        [("c", BF16)],
        "tap_grad",
        came + brought,
    )[0]
    brought = exchange.step([tap_grad])
    given = held_until([grad_filtered], [tap_grad])[0]
    following = lax.ppermute(given, "ctx", [(b, a) for a, b in onward])
    came = gather.step([tap_grad])

    terms[1] = weight_pass(me, out_weight, 1, gated, after=came + [tap_grad])[0]
    came = gather.step([terms[1]])
    terms[0] = weight_pass(me, out_weight, 0, gated, after=came + brought + [terms[1]])[0]
    came = gather.step([terms[0]])
    while exchange.bits:
        exchange.step([terms[0]])
    gates = [[terms[1]], [terms[0]]]
    for bit in bits_of(n_chan):
        for off in [off for off in sorted(terms, reverse=True) if off & bit]:
            other = swap(terms.pop(off).astype(BF16), "chan", bit).astype(F32)
            terms[off ^ bit] = terms[off ^ bit] + other
    mixed = terms[0].astype(BF16)

    grad_key, grad_value = by_channel(
        backward_kernel,
        [key_proj, value_proj, grad_filtered, following, filters, forward, early],
        "ttttcww",
        [("t", BF16), ("t", BF16)],
        "backward_filter",
        gates[-1] + came,
    )
    while gather.turns:
        gather.step(())
    order, blocks = gather.order, gather.blocks
    gates += [[grad_key, blocks[0][-1]], blocks[1][-1:]]
    halves_summed = summed(me, tap_grad, gates)

    columns = gather_by_swaps(exchange.held[:, 0])
    columns = [columns[off] for off in range(n_chan)]
    if (channels // n_ctx) % 128:
        columns = in_one_piece(me, columns, length)
    owners = []
    for c in range(n_ctx):
        spot = order.index(c)
        turns = [0] + [sign * step for step in range(1, n_ctx // 2) for sign in (-1, 1)] + [n_ctx // 2]
        owners.append([exchange.sources.index(order[(spot + turn) % n_ctx] ^ c) for turn in turns])
    owners = jnp.asarray(owners, jnp.int32)
    grad_weight = grad_weight_of(me, owners, blocks[0], columns, [])
    grad_weight = grad_weight_of(me, owners, blocks[1], columns, [grad_weight])
    grad_filters = joined(me, *halves_summed, F32, [grad_weight])
    return (mixed, grad_query, grad_key, grad_value, grad_filters, grad_weight)


def solution(mesh):
    placed = (
        P("ctx", "chan"),
        P("ctx", "chan"),
        P("ctx", "chan"),
        P("chan", None),
        P("chan", None),
        P("ctx", "chan"),
    )
    return jax.shard_map(
        per_device,
        mesh=mesh,
        in_specs=placed,
        out_specs=(
            P("ctx", "chan"),
            P("ctx", "chan"),
            P("ctx", "chan"),
            P("ctx", "chan"),
            P("chan", None),
            P("chan", "ctx"),
        ),
        check_vma=False,
    )
```

```python
import functools

import jax
import jax.numpy as jnp
import numpy as np
from jax import lax
from jax.experimental import pallas as pl
from jax.experimental.pallas import tpu as pltpu
from jax.sharding import PartitionSpec as P

F32 = jnp.float32
BF16 = jnp.bfloat16
VMEM_BYTES = 40 * 2**20
NT = (((1,), (1,)), ((), ()))
TN = (((0,), (0,)), ((), ()))


def halves(matrix):
    high = matrix.astype(BF16)
    low = (matrix - high.astype(np.float64)).astype(BF16)
    return np.stack([high, low])


def transforms(taps):
    points = 2 * taps
    angle = np.pi * (2 * np.arange(taps)[:, None] + 1) * np.arange(points)[None, :] / points
    forward = np.concatenate([np.cos(angle), -np.sin(angle)], axis=0)
    inverse = forward.T * (2.0 / points)
    late = inverse[taps:]
    early = inverse[:taps]
    lags = inverse[taps - np.arange(taps)]
    return halves(forward), halves(late), halves(early), halves(lags)


def mm(a, b, dims=(((1,), (0,)), ((), ()))):
    return lax.dot_general(a, b, dims, preferred_element_type=F32)


def spectrum(f_ref, rows):
    return mm(f_ref[0], rows) + mm(f_ref[1], rows)


def tap_spectrum(f_ref, filters, taps):
    return mm(f_ref[0, :, :taps], filters, NT) + mm(f_ref[1, :, :taps], filters, NT)


def back(g_ref, real, imag):
    both = jnp.concatenate([real, imag], axis=0)
    high = both.astype(BF16)
    low = (both - high.astype(F32)).astype(BF16)
    return mm(g_ref[0], high) + mm(g_ref[0], low) + mm(g_ref[1], high)


def forward_kernel(taps, q_ref, k_ref, v_ref, earlier_ref, filt_ref, f_ref, g_ref, gated_ref, filtered_ref):
    product = (k_ref[...].astype(F32) * v_ref[...].astype(F32)).astype(BF16)
    x = spectrum(f_ref, jnp.concatenate([earlier_ref[...], product], axis=0))
    h = tap_spectrum(f_ref, filt_ref[...], taps)
    xr, xi, hr, hi = x[:taps], x[taps:], h[:taps], h[taps:]
    filtered = back(g_ref, xr * hr - xi * hi, xr * hi + xi * hr)
    filtered_ref[...] = filtered
    gated_ref[...] = (q_ref[...].astype(F32) * filtered).astype(BF16)


def tap_grad_kernel(taps, k_ref, v_ref, earlier_ref, gf_ref, f_ref, g_ref, out_ref):
    product = (k_ref[...].astype(F32) * v_ref[...].astype(F32)).astype(BF16)
    x = spectrum(f_ref, jnp.concatenate([earlier_ref[...], product], axis=0))
    rows = gf_ref[...]
    g = mm(f_ref[0, :, :taps], rows) + mm(f_ref[1, :, :taps], rows)
    xr, xi, gr, gi = x[:taps], x[taps:], g[:taps], g[taps:]
    tap_rows = back(g_ref, xr * gr + xi * gi, xi * gr - xr * gi)
    out_ref[...] = tap_rows.T.astype(BF16)


def backward_kernel(taps, k_ref, v_ref, gf_ref, following_ref, filt_ref, f_ref, g_ref, gk_ref, gv_ref):
    g = spectrum(f_ref, jnp.concatenate([gf_ref[...], following_ref[...]], axis=0))
    h = tap_spectrum(f_ref, filt_ref[...], taps)
    gr, gi, hr, hi = g[:taps], g[taps:], h[:taps], h[taps:]
    grad_product = back(g_ref, hr * gr + hi * gi, hr * gi - hi * gr)
    gk_ref[...] = (grad_product * v_ref[...].astype(F32)).astype(BF16)
    gv_ref[...] = (grad_product * k_ref[...].astype(F32)).astype(BF16)


def estimate(micros):
    return pl.CostEstimate(flops=int(micros * 10**9), bytes_accessed=0, transcendentals=0)


def ignoring(body, count, skip):
    def kernel(*refs):
        return body(*refs[:skip], *refs[skip + count :])

    return kernel


def by_channel(kernel, arrays, kinds, outs, name, after=()):
    length, channels = arrays[0].shape
    width = min(512, channels)
    specs = {
        "t": pl.BlockSpec((length, width), lambda i: (0, i)),
        "c": pl.BlockSpec((width, length), lambda i: (i, 0)),
    }

    def spec_of(kind, shape):
        if kind == "w":
            return pl.BlockSpec(shape, lambda i: (0,) * len(shape))
        return specs[kind]

    return pl.pallas_call(
        ignoring(functools.partial(kernel, length), len(after), len(arrays)),
        grid=(channels // width,),
        in_specs=[spec_of(kind, a.shape) for kind, a in zip(kinds, arrays)]
        + [pl.BlockSpec(memory_space=pl.ANY)] * len(after),
        out_specs=[specs[kind] for kind, unused in outs],
        out_shape=[
            jax.ShapeDtypeStruct((length, channels) if kind == "t" else (channels, length), dtype)
            for kind, dtype in outs
        ],
        compiler_params=pltpu.CompilerParams(vmem_limit_bytes=VMEM_BYTES),
        cost_estimate=estimate(3),
        name=name,
    )(*arrays, *after)


def pass_kernel(with_mixed, with_grad, has_sum, last, me_ref, w_ref, *refs):
    refs = list(refs)
    step = pl.program_id(0)
    if with_mixed:
        gated_ref = refs.pop(0)
    if with_grad:
        cot_ref = refs.pop(0)
        sum_ref = refs.pop(0) if has_sum else None
        turned_ref = refs.pop()

        @pl.when(step == 0)
        def turn():
            turned_ref[...] = cot_ref[...].T

        total = mm(w_ref[...], turned_ref[...])
        if has_sum:
            total = total + sum_ref[...]
        if last:
            q_ref, filtered_ref, gq_ref, gf_ref = refs[:4]
            total = total.T
            gq_ref[...] = (total * filtered_ref[...]).astype(BF16)
            gf_ref[...] = (total * q_ref[...].astype(F32)).astype(BF16)
        else:
            refs[0][...] = total
    if with_mixed:
        held_ref, mixed_ref = refs.pop(), refs.pop()
        part = mm(gated_ref[...], w_ref[...])

        @pl.when(step == 0)
        def first():
            held_ref[...] = part

        @pl.when(step > 0)
        def more():
            held_ref[...] = held_ref[...] + part

        @pl.when(step == pl.num_programs(0) - 1)
        def give():
            mixed_ref[...] = held_ref[...].astype(mixed_ref.dtype)


def weight_pass(me, weight, off, gated=None, cot=None, sums=(), ends=(), after=()):
    length = (cot if gated is None else gated).shape[0]
    channels = weight.shape[0]
    tile = 512
    whole = pl.BlockSpec((length, channels), lambda r, me: (0, 0))
    by_token = pl.BlockSpec((length, tile), lambda r, me: (0, r))
    by_row = pl.BlockSpec((tile, length), lambda r, me: (r, 0))
    arrays, in_specs = [weight], [pl.BlockSpec((tile, channels), lambda r, me: (r, me[1] ^ off))]
    out_specs, out_shape, scratch = [], [], []
    if gated is not None:
        arrays.append(gated)
        in_specs.append(by_token)
    if cot is not None:
        arrays += [cot, *sums, *ends]
        in_specs += [whole] + [by_row] * len(sums) + [by_token] * len(ends)
        out_specs += [by_token] * 2 if ends else [by_row]
        out_shape += [jax.ShapeDtypeStruct((length, channels), BF16)] * 2 if ends else [
            jax.ShapeDtypeStruct((channels, length), F32)
        ]
    if gated is not None:
        out_specs.append(whole)
        out_shape.append(jax.ShapeDtypeStruct((length, channels), BF16 if off % 2 else F32))
        scratch.append(pltpu.VMEM((length, channels), F32))
    if cot is not None:
        scratch.append(pltpu.VMEM((channels, length), BF16))
    body = functools.partial(pass_kernel, gated is not None, cot is not None, bool(sums), bool(ends))
    return pl.pallas_call(
        ignoring(body, len(after), 1 + len(arrays)),
        grid_spec=pltpu.PrefetchScalarGridSpec(
            num_scalar_prefetch=1,
            grid=(channels // tile,),
            in_specs=in_specs + [pl.BlockSpec(memory_space=pl.ANY)] * len(after),
            out_specs=out_specs,
            scratch_shapes=scratch,
        ),
        out_shape=out_shape,
        compiler_params=pltpu.CompilerParams(vmem_limit_bytes=VMEM_BYTES),
        cost_estimate=estimate(3 * ((cot is not None) + (gated is not None))),
        name="grad_gated_part" if gated is None else "mixed_part" if cot is None else "grads_and_mixed",
    )(me, *arrays, *after)


def pieces_kernel(per_chan, me_ref, *refs):
    out_ref = refs[-1]
    length, width = refs[0].shape
    span = width // per_chan
    count = len(refs) - 1
    piece = span // count
    for off in range(count):
        for part in range(per_chan):
            target = (me_ref[1] ^ off) * per_chan + part
            start = pl.multiple_of(part * span + me_ref[1] * piece, 128)
            block = refs[off][:, pl.ds(start, piece)]
            out_ref[target ^ me_ref[0]] = jnp.concatenate(
                [block[:, at : at + 128] for at in range(0, piece, 128)], axis=0
            )


def pieces_of(me, cots, n_ctx, after):
    length, width = cots[0].shape
    piece = width // n_ctx
    rows = length * piece // 128
    if piece % 128:
        return pieces_by_slices(me, cots, n_ctx)
    return pl.pallas_call(
        ignoring(functools.partial(pieces_kernel, n_ctx // len(cots)), len(after), 1 + len(cots)),
        grid_spec=pltpu.PrefetchScalarGridSpec(
            num_scalar_prefetch=1,
            grid=(1,),
            in_specs=[pl.BlockSpec((length, width), lambda i, me: (0, 0))] * len(cots)
            + [pl.BlockSpec(memory_space=pl.ANY)] * len(after),
            out_specs=pl.BlockSpec((n_ctx, rows, 128), lambda i, me: (0, 0, 0)),
        ),
        out_shape=jax.ShapeDtypeStruct((n_ctx, rows, 128), BF16),
        compiler_params=pltpu.CompilerParams(vmem_limit_bytes=VMEM_BYTES),
        cost_estimate=estimate(0.5),
        name="pieces",
    )(me, *cots, *after)


def pieces_by_slices(me, cots, n_ctx):
    length, width = cots[0].shape
    count = len(cots)
    piece = width // n_ctx
    table = jnp.stack(cots).reshape(count, length, n_ctx // count, count, piece)
    mine = lax.dynamic_index_in_dim(table, me[1], 3, False)
    parts = mine.transpose(0, 2, 1, 3).reshape(n_ctx, length * piece // 128, 128)
    order = jnp.arange(n_ctx, dtype=jnp.int32) ^ me[0]
    per_chan = n_ctx // count
    return parts[(order // per_chan ^ me[1]) * per_chan + order % per_chan]


def weight_kernel(slots, parts, half, me_ref, owner_ref, *refs):
    gated_refs = refs[: slots - 1]
    far_low, far_high = refs[slots - 1 : slots + 1]
    cot_refs = refs[slots + 1 : slots + 1 + parts]
    out_ref = refs[-1]
    length = far_low.shape[0]
    far = jnp.where(pl.program_id(0) < half, far_low[...], far_high[...])
    columns = jnp.concatenate([ref[...] for ref in gated_refs] + [far], axis=0)
    for part in range(parts):
        rows = []
        for slot in range(slots):
            block = cot_refs[part][owner_ref[me_ref[0], slot]]
            rows.append(
                jnp.concatenate([block[at : at + length] for at in range(0, block.shape[0], length)], axis=1)
            )
        total = mm(columns, jnp.concatenate(rows, axis=0), TN)
        piece = total.shape[1]
        place = pl.multiple_of((me_ref[1] ^ part) * piece, piece) if parts > 1 else 0
        out_ref[:, pl.ds(place, piece)] = total.astype(BF16)


def grad_weight_of(me, owners, blocks, far_low, far_high, cots):
    length, channels = blocks[0].shape
    rows = cots[0].shape[1]
    piece = rows * 128 // length
    tile = 256
    half = channels // tile // 2
    slots, parts = len(blocks) + 1, len(cots)
    in_specs = [pl.BlockSpec((length, tile), lambda i, *ids: (0, i)) for unused in blocks]
    in_specs.append(pl.BlockSpec((length, tile), lambda i, *ids: (0, jnp.minimum(i, half - 1))))
    in_specs.append(pl.BlockSpec((length, tile), lambda i, *ids: (0, jnp.maximum(i - half, 0))))
    in_specs += [pl.BlockSpec(cot.shape, lambda i, *ids: (0, 0, 0)) for cot in cots]
    return pl.pallas_call(
        functools.partial(weight_kernel, slots, parts, half),
        grid_spec=pltpu.PrefetchScalarGridSpec(
            num_scalar_prefetch=2,
            grid=(channels // tile,),
            in_specs=in_specs,
            out_specs=pl.BlockSpec((tile, piece * parts), lambda i, *ids: (i, 0)),
        ),
        out_shape=jax.ShapeDtypeStruct((channels, piece * parts), BF16),
        compiler_params=pltpu.CompilerParams(vmem_limit_bytes=VMEM_BYTES),
        cost_estimate=estimate(6),
        name="grad_weight",
    )(me, owners, *blocks, far_low, far_high, *cots)


def in_one_piece(me, columns, length):
    count, rows, unused = columns[0].shape
    table = jnp.stack(columns)[jnp.arange(len(columns), dtype=jnp.int32) ^ me[1]]
    piece = rows * 128 // length
    flat = table.reshape(len(columns), count, length, piece).transpose(1, 2, 0, 3)
    flat = flat.reshape(count, length, piece * len(columns) // 128, 128).transpose(0, 2, 1, 3)
    return [flat.reshape(count, -1, 128)]


def cycle_of(count):
    across = 1 << ((count.bit_length() - 1) // 2)
    order = []
    for column in range(across):
        line = [row * across + column for row in range(count // across)]
        order += line if column % 2 == 0 else line[::-1]
    return order


def held_until(arrays, kernels):
    return lax.optimization_barrier((*arrays, *kernels))[: len(arrays)]


def swap(block, axis, bit):
    size = lax.axis_size(axis)
    return lax.ppermute(block, axis, [(i, i ^ bit) for i in range(size)])


def bits_of(size):
    return [1 << place for place in range(size.bit_length() - 1)]


def gather_by_swaps(block):
    held = {0: block}
    for bit in reversed(bits_of(lax.axis_size("chan"))):
        held.update({off ^ bit: swap(held[off], "chan", bit) for off in list(held)})
    return held


def added_kernel(bit, me_ref, own_ref, came_ref, *outs):
    total = (own_ref[...].astype(F32) + came_ref[...].astype(F32)).astype(BF16)
    if not bit:
        outs[0][...] = total
        return
    rows = outs[0].shape[0]
    mine = (me_ref[0] & bit) != 0
    outs[0][...] = jnp.where(mine, total[rows:], total[:rows])
    outs[1][...] = jnp.where(mine, total[:rows], total[rows:])


def added(me, own, came, bit, after):
    shape = (own.shape[0] // 2, own.shape[1]) if bit else own.shape
    whole = pl.BlockSpec(own.shape, lambda i, me: (0, 0))
    outs = 2 if bit else 1
    return pl.pallas_call(
        ignoring(functools.partial(added_kernel, bit), len(after), 3),
        grid_spec=pltpu.PrefetchScalarGridSpec(
            num_scalar_prefetch=1,
            grid=(1,),
            in_specs=[whole, whole] + [pl.BlockSpec(memory_space=pl.ANY)] * len(after),
            out_specs=[pl.BlockSpec(shape, lambda i, me: (0, 0))] * outs,
        ),
        out_shape=[jax.ShapeDtypeStruct(shape, BF16)] * outs,
        compiler_params=pltpu.CompilerParams(vmem_limit_bytes=VMEM_BYTES),
        cost_estimate=estimate(0.5),
        name="added",
    )(me, own, came, *after)


def split(me, block, bit):
    rows = block.shape[0] // 2
    mine = (me[0] & bit) != 0
    low, high = block[:rows], block[rows:]
    return jnp.where(mine, high, low), jnp.where(mine, low, high)


def summed(me, partial, gates):
    bits = bits_of(lax.axis_size("ctx"))
    sums, send = split(me, partial, bits[0])
    for step, bit in enumerate(bits):
        came = swap(send if step < 2 else sums, "ctx", bit)
        sums, *send = added(me, sums, came, bits[1] if step == 0 else 0, gates[step] if step < len(gates) else ())
        send = send[0] if send else None
    sums = joined(me, sums, swap(sums, "ctx", bits[1]), bits[1], BF16, ())
    return sums, swap(sums, "ctx", bits[0]), bits[0]


def joined_kernel(bit, me_ref, own_ref, other_ref, out_ref):
    rows = own_ref.shape[0]
    mine = (me_ref[0] & bit) != 0
    out_ref[:rows] = jnp.where(mine, other_ref[...], own_ref[...]).astype(out_ref.dtype)
    out_ref[rows:] = jnp.where(mine, own_ref[...], other_ref[...]).astype(out_ref.dtype)


def joined(me, own, other, bit, dtype, after):
    rows, width = own.shape
    whole = pl.BlockSpec(own.shape, lambda i, me: (0, 0))
    return pl.pallas_call(
        ignoring(functools.partial(joined_kernel, bit), len(after), 3),
        grid_spec=pltpu.PrefetchScalarGridSpec(
            num_scalar_prefetch=1,
            grid=(1,),
            in_specs=[whole, whole] + [pl.BlockSpec(memory_space=pl.ANY)] * len(after),
            out_specs=pl.BlockSpec((2 * rows, width), lambda i, me: (0, 0)),
        ),
        out_shape=jax.ShapeDtypeStruct((2 * rows, width), dtype),
        compiler_params=pltpu.CompilerParams(vmem_limit_bytes=VMEM_BYTES),
        cost_estimate=estimate(0.5),
        name="joined",
    )(me, own, other, *after)


def exchanged(pieces):
    held, sources, stages = pieces[None], [0], []
    for bit in reversed(bits_of(pieces.shape[0])):
        give = held[:, bit:].reshape((-1,) + pieces.shape[1:])
        stages.append(swap(give, "ctx", bit))
        came = stages[-1].reshape((len(sources), bit) + pieces.shape[1:])
        held = jnp.concatenate([held[:, :bit], came], axis=0)
        sources += [source ^ bit for source in sources]
    return held[:, 0], sources, stages


def per_device(query_proj, key_proj, value_proj, filters, out_weight, cotangent):
    length, channels = query_proj.shape
    taps = filters.shape[1]
    n_ctx, n_chan = lax.axis_size("ctx"), lax.axis_size("chan")
    me = jnp.stack([lax.axis_index("ctx"), lax.axis_index("chan")]).astype(jnp.int32)
    forward, late, early, lags = [jnp.asarray(m) for m in transforms(taps)]

    product = (key_proj.astype(F32) * value_proj.astype(F32)).astype(BF16)
    product, cotangent = lax.optimization_barrier((product, cotangent))
    earlier = lax.ppermute(product, "ctx", [(i, i + 1) for i in range(n_ctx - 1)])

    cots = {0: cotangent, 1: swap(cotangent, "chan", 1)}
    for bit in reversed(bits_of(n_chan)[1:]):
        cots.update({off ^ bit: swap(cots[off], "chan", bit) for off in list(cots) if off % 2 == 0})
    offs = sorted(off for off in cots if off % 2 == 0 and off)
    sums = weight_pass(me, out_weight, 0, cot=cots[0])
    for off in offs:
        cots[off + 1] = swap(held_until([cots[off]], sums)[0], "chan", 1)
    offs = sorted(offs + [off + 1 for off in offs])
    sums = weight_pass(me, out_weight, 1, cot=cots[1], sums=sums)

    gated, filtered = by_channel(
        forward_kernel,
        [query_proj, key_proj, value_proj, earlier, filters, forward, late],
        "ttttcww",
        [("t", BF16), ("t", F32)],
        "forward_filter",
        after=sums,
    )

    pieces = pieces_of(me, [cots[off] for off in range(n_chan)], n_ctx, sums)
    held, sources, stages = exchanged(pieces)

    order = cycle_of(n_ctx)
    ahead = [(order[i], order[(i + 1) % n_ctx]) for i in range(n_ctx)]
    behind = [(b, a) for a, b in ahead]
    half = channels // 2
    from_behind, from_ahead = gated, gated
    blocks = [gated]
    for step in range(n_ctx // 2 - 1):
        from_behind = lax.ppermute(from_behind, "ctx", ahead)
        from_ahead = lax.ppermute(from_ahead, "ctx", behind)
        blocks += [from_behind, from_ahead]
    far_low = lax.ppermute(from_behind[:, :half], "ctx", ahead)
    far_high = lax.ppermute(from_ahead[:, half:], "ctx", behind)

    terms = {}
    for off in offs[:-1]:
        *sums, terms[off] = weight_pass(me, out_weight, off, gated, cots[off], sums, after=[pieces])
    grad_query, grad_filtered, terms[offs[-1]] = weight_pass(
        me, out_weight, offs[-1], gated, cots[offs[-1]], sums, [query_proj, filtered],
        blocks[1:3] + stages[:1],
    )
    following = lax.ppermute(grad_filtered, "ctx", [(i + 1, i) for i in range(n_ctx - 1)])

    tap_grad = by_channel(
        tap_grad_kernel,
        [key_proj, value_proj, earlier, grad_filtered, forward, lags],
        "ttttww",
        [("c", BF16)],
        "tap_grad",
    )[0]

    terms[1] = weight_pass(me, out_weight, 1, gated, after=[tap_grad])[0]
    terms[0] = weight_pass(me, out_weight, 0, gated, after=blocks[3:5] + stages[1:2] + [terms[1]])[0]
    gates = [[terms[1]], [terms[0]]]
    for bit in bits_of(n_chan):
        for off in [off for off in sorted(terms, reverse=True) if off & bit]:
            came = swap(terms.pop(off).astype(BF16), "chan", bit).astype(F32)
            terms[off ^ bit] = terms[off ^ bit] + came
    mixed = terms[0].astype(BF16)

    grad_key, grad_value = by_channel(
        backward_kernel,
        [key_proj, value_proj, grad_filtered, following, filters, forward, early],
        "ttttcww",
        [("t", BF16), ("t", BF16)],
        "backward_filter",
        after=gates[-1],
    )
    halves_summed = summed(me, held_until([tap_grad], blocks[3:5])[0], [gates[-1], blocks[5:7], [far_low, far_high]])

    columns = gather_by_swaps(held)
    columns = [columns[off] for off in range(n_chan)]
    if (channels // n_ctx) % 128:
        columns = in_one_piece(me, columns, length)
    owners = []
    for c in range(n_ctx):
        spot = order.index(c)
        steps = [0] + [sign * step for step in range(1, n_ctx // 2) for sign in (-1, 1)] + [n_ctx // 2]
        owners.append([sources.index(order[(spot + step) % n_ctx] ^ c) for step in steps])
    grad_weight = grad_weight_of(me, jnp.asarray(owners, jnp.int32), blocks, far_low, far_high, columns)
    own, other, bit = halves_summed
    grad_filters = joined(me, own, held_until([other], [grad_weight])[0], bit, F32, ())
    return (mixed, grad_query, grad_key, grad_value, grad_filters, grad_weight)


def solution(mesh):
    placed = (
        P("ctx", "chan"),
        P("ctx", "chan"),
        P("ctx", "chan"),
        P("chan", None),
        P("chan", None),
        P("ctx", "chan"),
    )
    return jax.shard_map(
        per_device,
        mesh=mesh,
        in_specs=placed,
        out_specs=(
            P("ctx", "chan"),
            P("ctx", "chan"),
            P("ctx", "chan"),
            P("ctx", "chan"),
            P("chan", None),
            P("chan", "ctx"),
        ),
        check_vma=False,
    )
```

```python
import functools

import jax
import jax.numpy as jnp
import numpy as np
from jax import lax
from jax.experimental import pallas as pl
from jax.experimental.pallas import tpu as pltpu
from jax.sharding import PartitionSpec as P

F32 = jnp.float32
BF16 = jnp.bfloat16
VMEM_BYTES = 40 * 2**20
NT = (((1,), (1,)), ((), ()))
TN = (((0,), (0,)), ((), ()))


def halves(matrix):
    high = matrix.astype(BF16)
    low = (matrix - high.astype(np.float64)).astype(BF16)
    return np.stack([high, low])


def transforms(taps):
    points = 2 * taps
    angle = np.pi * (2 * np.arange(taps)[:, None] + 1) * np.arange(points)[None, :] / points
    forward = np.concatenate([np.cos(angle), -np.sin(angle)], axis=0)
    inverse = forward.T * (2.0 / points)
    late = inverse[taps:]
    early = inverse[:taps]
    lags = inverse[taps - np.arange(taps)]
    return halves(forward), halves(late), halves(early), halves(lags)


def mm(a, b, dims=(((1,), (0,)), ((), ()))):
    return lax.dot_general(a, b, dims, preferred_element_type=F32)


def spectrum(f_ref, rows):
    return mm(f_ref[0], rows) + mm(f_ref[1], rows)


def tap_spectrum(f_ref, filters, taps):
    return mm(f_ref[0, :, :taps], filters, NT) + mm(f_ref[1, :, :taps], filters, NT)


def back(g_ref, real, imag):
    both = jnp.concatenate([real, imag], axis=0)
    high = both.astype(BF16)
    low = (both - high.astype(F32)).astype(BF16)
    return mm(g_ref[0], high) + mm(g_ref[0], low) + mm(g_ref[1], high)


def forward_kernel(taps, q_ref, k_ref, v_ref, earlier_ref, filt_ref, f_ref, g_ref, gated_ref, filtered_ref):
    product = (k_ref[...].astype(F32) * v_ref[...].astype(F32)).astype(BF16)
    x = spectrum(f_ref, jnp.concatenate([earlier_ref[...], product], axis=0))
    h = tap_spectrum(f_ref, filt_ref[...], taps)
    xr, xi, hr, hi = x[:taps], x[taps:], h[:taps], h[taps:]
    filtered = back(g_ref, xr * hr - xi * hi, xr * hi + xi * hr)
    filtered_ref[...] = filtered
    gated_ref[...] = (q_ref[...].astype(F32) * filtered).astype(BF16)


def tap_grad_kernel(taps, k_ref, v_ref, earlier_ref, gf_ref, f_ref, g_ref, out_ref):
    product = (k_ref[...].astype(F32) * v_ref[...].astype(F32)).astype(BF16)
    x = spectrum(f_ref, jnp.concatenate([earlier_ref[...], product], axis=0))
    rows = gf_ref[...]
    g = mm(f_ref[0, :, :taps], rows) + mm(f_ref[1, :, :taps], rows)
    xr, xi, gr, gi = x[:taps], x[taps:], g[:taps], g[taps:]
    tap_rows = back(g_ref, xr * gr + xi * gi, xi * gr - xr * gi)
    out_ref[...] = tap_rows.T.astype(BF16)


def backward_kernel(taps, k_ref, v_ref, gf_ref, following_ref, filt_ref, f_ref, g_ref, gk_ref, gv_ref):
    g = spectrum(f_ref, jnp.concatenate([gf_ref[...], following_ref[...]], axis=0))
    h = tap_spectrum(f_ref, filt_ref[...], taps)
    gr, gi, hr, hi = g[:taps], g[taps:], h[:taps], h[taps:]
    grad_product = back(g_ref, hr * gr + hi * gi, hr * gi - hi * gr)
    gk_ref[...] = (grad_product * v_ref[...].astype(F32)).astype(BF16)
    gv_ref[...] = (grad_product * k_ref[...].astype(F32)).astype(BF16)


def estimate(micros):
    return pl.CostEstimate(flops=int(micros * 10**9), bytes_accessed=0, transcendentals=0)


def ignoring(body, count, skip):
    def kernel(*refs):
        return body(*refs[:skip], *refs[skip + count :])

    return kernel


def by_channel(kernel, arrays, kinds, outs, name, after=()):
    length, channels = arrays[0].shape
    width = min(512, channels)
    specs = {
        "t": pl.BlockSpec((length, width), lambda i: (0, i)),
        "c": pl.BlockSpec((width, length), lambda i: (i, 0)),
    }

    def spec_of(kind, shape):
        if kind == "w":
            return pl.BlockSpec(shape, lambda i: (0,) * len(shape))
        return specs[kind]

    return pl.pallas_call(
        ignoring(functools.partial(kernel, length), len(after), len(arrays)),
        grid=(channels // width,),
        in_specs=[spec_of(kind, a.shape) for kind, a in zip(kinds, arrays)]
        + [pl.BlockSpec(memory_space=pl.ANY)] * len(after),
        out_specs=[specs[kind] for kind, unused in outs],
        out_shape=[
            jax.ShapeDtypeStruct((length, channels) if kind == "t" else (channels, length), dtype)
            for kind, dtype in outs
        ],
        compiler_params=pltpu.CompilerParams(vmem_limit_bytes=VMEM_BYTES),
        cost_estimate=estimate(3),
        name=name,
    )(*arrays, *after)


def pass_kernel(with_mixed, with_grad, has_sum, last, adds, me_ref, w_ref, *refs):
    refs = list(refs)
    step = pl.program_id(0)
    if with_mixed:
        gated_ref = refs.pop(0)
    add_refs = [refs.pop(0) for unused in range(adds)]
    if with_grad:
        cot_ref = refs.pop(0)
        sum_ref = refs.pop(0) if has_sum else None
        turned_ref = refs.pop()

        @pl.when(step == 0)
        def turn():
            turned_ref[...] = cot_ref[...].T

        total = mm(w_ref[...], turned_ref[...])
        if has_sum:
            total = total + sum_ref[...]
        if last:
            q_ref, filtered_ref, gq_ref, gf_ref = refs[:4]
            total = total.T
            gq_ref[...] = (total * filtered_ref[...]).astype(BF16)
            gf_ref[...] = (total * q_ref[...].astype(F32)).astype(BF16)
        else:
            refs[0][...] = total
    if with_mixed:
        held_ref, mixed_ref = refs.pop(), refs.pop()
        part = mm(gated_ref[...], w_ref[...])

        @pl.when(step == 0)
        def first():
            held_ref[...] = part

        @pl.when(step > 0)
        def more():
            held_ref[...] = held_ref[...] + part

        @pl.when(step == pl.num_programs(0) - 1)
        def give():
            mixed = held_ref[...]
            for add_ref in add_refs:
                mixed = mixed + add_ref[...].astype(F32)
            mixed_ref[...] = mixed.astype(mixed_ref.dtype)


def weight_pass(me, weight, off, gated=None, cot=None, sums=(), ends=(), adds=(), after=()):
    length = (cot if gated is None else gated).shape[0]
    channels = weight.shape[0]
    tile = 512
    whole = pl.BlockSpec((length, channels), lambda r, me: (0, 0))
    by_token = pl.BlockSpec((length, tile), lambda r, me: (0, r))
    by_row = pl.BlockSpec((tile, length), lambda r, me: (r, 0))
    arrays, in_specs = [weight], [pl.BlockSpec((tile, channels), lambda r, me: (r, me[1] ^ off))]
    out_specs, out_shape, scratch = [], [], []
    if gated is not None:
        arrays.append(gated)
        in_specs.append(by_token)
        arrays += adds
        in_specs += [whole] * len(adds)
    if cot is not None:
        arrays += [cot, *sums, *ends]
        in_specs += [whole] + [by_row] * len(sums) + [by_token] * len(ends)
        out_specs += [by_token] * 2 if ends else [by_row]
        out_shape += [jax.ShapeDtypeStruct((length, channels), BF16)] * 2 if ends else [
            jax.ShapeDtypeStruct((channels, length), F32)
        ]
    if gated is not None:
        out_specs.append(whole)
        out_shape.append(jax.ShapeDtypeStruct((length, channels), BF16 if off % 2 or adds else F32))
        scratch.append(pltpu.VMEM((length, channels), F32))
    if cot is not None:
        scratch.append(pltpu.VMEM((channels, length), BF16))
    body = functools.partial(pass_kernel, gated is not None, cot is not None, bool(sums), bool(ends), len(adds))
    return pl.pallas_call(
        ignoring(body, len(after), 1 + len(arrays)),
        grid_spec=pltpu.PrefetchScalarGridSpec(
            num_scalar_prefetch=1,
            grid=(channels // tile,),
            in_specs=in_specs + [pl.BlockSpec(memory_space=pl.ANY)] * len(after),
            out_specs=out_specs,
            scratch_shapes=scratch,
        ),
        out_shape=out_shape,
        compiler_params=pltpu.CompilerParams(vmem_limit_bytes=VMEM_BYTES),
        cost_estimate=estimate(3 * ((cot is not None) + (gated is not None))),
        name="grad_gated_part" if gated is None else "mixed_part" if cot is None else "grads_and_mixed",
    )(me, *arrays, *after)


def pieces_kernel(per_chan, me_ref, *refs):
    out_ref = refs[-1]
    length, width = refs[0].shape
    span = width // per_chan
    count = len(refs) - 1
    piece = span // count
    for off in range(count):
        for part in range(per_chan):
            target = (me_ref[1] ^ off) * per_chan + part
            start = pl.multiple_of(part * span + me_ref[1] * piece, 128)
            block = refs[off][:, pl.ds(start, piece)]
            out_ref[target ^ me_ref[0]] = jnp.concatenate(
                [block[:, at : at + 128] for at in range(0, piece, 128)], axis=0
            )


def pieces_of(me, cots, n_ctx, after):
    length, width = cots[0].shape
    piece = width // n_ctx
    rows = length * piece // 128
    if piece % 128:
        return pieces_by_slices(me, cots, n_ctx)
    return pl.pallas_call(
        ignoring(functools.partial(pieces_kernel, n_ctx // len(cots)), len(after), 1 + len(cots)),
        grid_spec=pltpu.PrefetchScalarGridSpec(
            num_scalar_prefetch=1,
            grid=(1,),
            in_specs=[pl.BlockSpec((length, width), lambda i, me: (0, 0))] * len(cots)
            + [pl.BlockSpec(memory_space=pl.ANY)] * len(after),
            out_specs=pl.BlockSpec((n_ctx, rows, 128), lambda i, me: (0, 0, 0)),
        ),
        out_shape=jax.ShapeDtypeStruct((n_ctx, rows, 128), BF16),
        compiler_params=pltpu.CompilerParams(vmem_limit_bytes=VMEM_BYTES),
        cost_estimate=estimate(0.5),
        name="pieces",
    )(me, *cots, *after)


def pieces_by_slices(me, cots, n_ctx):
    length, width = cots[0].shape
    count = len(cots)
    piece = width // n_ctx
    table = jnp.stack(cots).reshape(count, length, n_ctx // count, count, piece)
    mine = lax.dynamic_index_in_dim(table, me[1], 3, False)
    parts = mine.transpose(0, 2, 1, 3).reshape(n_ctx, length * piece // 128, 128)
    order = jnp.arange(n_ctx, dtype=jnp.int32) ^ me[0]
    per_chan = n_ctx // count
    return parts[(order // per_chan ^ me[1]) * per_chan + order % per_chan]


def weight_kernel(slots, parts, half, me_ref, owner_ref, *refs):
    gated_refs = refs[: slots - 1]
    far_low, far_high = refs[slots - 1 : slots + 1]
    cot_refs = refs[slots + 1 : slots + 1 + parts]
    out_ref = refs[-1]
    length = far_low.shape[0]
    far = jnp.where(pl.program_id(0) < half, far_low[...], far_high[...])
    columns = jnp.concatenate([ref[...] for ref in gated_refs] + [far], axis=0)
    for part in range(parts):
        rows = []
        for slot in range(slots):
            block = cot_refs[part][owner_ref[me_ref[0], slot]]
            rows.append(
                jnp.concatenate([block[at : at + length] for at in range(0, block.shape[0], length)], axis=1)
            )
        total = mm(columns, jnp.concatenate(rows, axis=0), TN)
        piece = total.shape[1]
        place = pl.multiple_of((me_ref[1] ^ part) * piece, piece) if parts > 1 else 0
        out_ref[:, pl.ds(place, piece)] = total.astype(BF16)


def grad_weight_of(me, owners, blocks, far_low, far_high, cots):
    length, channels = blocks[0].shape
    rows = cots[0].shape[1]
    piece = rows * 128 // length
    tile = 256
    half = channels // tile // 2
    slots, parts = len(blocks) + 1, len(cots)
    in_specs = [pl.BlockSpec((length, tile), lambda i, *ids: (0, i)) for unused in blocks]
    in_specs.append(pl.BlockSpec((length, tile), lambda i, *ids: (0, jnp.minimum(i, half - 1))))
    in_specs.append(pl.BlockSpec((length, tile), lambda i, *ids: (0, jnp.maximum(i - half, 0))))
    in_specs += [pl.BlockSpec(cot.shape, lambda i, *ids: (0, 0, 0)) for cot in cots]
    return pl.pallas_call(
        functools.partial(weight_kernel, slots, parts, half),
        grid_spec=pltpu.PrefetchScalarGridSpec(
            num_scalar_prefetch=2,
            grid=(channels // tile,),
            in_specs=in_specs,
            out_specs=pl.BlockSpec((tile, piece * parts), lambda i, *ids: (i, 0)),
        ),
        out_shape=jax.ShapeDtypeStruct((channels, piece * parts), BF16),
        compiler_params=pltpu.CompilerParams(vmem_limit_bytes=VMEM_BYTES),
        cost_estimate=estimate(6),
        name="grad_weight",
    )(me, owners, *blocks, far_low, far_high, *cots)


def in_one_piece(me, columns, length):
    count, rows, unused = columns[0].shape
    table = jnp.stack(columns)[jnp.arange(len(columns), dtype=jnp.int32) ^ me[1]]
    piece = rows * 128 // length
    flat = table.reshape(len(columns), count, length, piece).transpose(1, 2, 0, 3)
    flat = flat.reshape(count, length, piece * len(columns) // 128, 128).transpose(0, 2, 1, 3)
    return [flat.reshape(count, -1, 128)]


def cycle_of(count):
    across = 1 << ((count.bit_length() - 1) // 2)
    order = []
    for column in range(across):
        line = [row * across + column for row in range(count // across)]
        order += line if column % 2 == 0 else line[::-1]
    return order


def held_until(arrays, kernels):
    return lax.optimization_barrier((*arrays, *kernels))[: len(arrays)]


def swap(block, axis, bit):
    size = lax.axis_size(axis)
    return lax.ppermute(block, axis, [(i, i ^ bit) for i in range(size)])


def bits_of(size):
    return [1 << place for place in range(size.bit_length() - 1)]


def gather_by_swaps(block):
    held = {0: block}
    for bit in reversed(bits_of(lax.axis_size("chan"))):
        held.update({off ^ bit: swap(held[off], "chan", bit) for off in list(held)})
    return held


def added_kernel(bit, me_ref, own_ref, came_ref, *outs):
    total = (own_ref[...].astype(F32) + came_ref[...].astype(F32)).astype(BF16)
    if not bit:
        outs[0][...] = total
        return
    rows = outs[0].shape[0]
    mine = (me_ref[0] & bit) != 0
    outs[0][...] = jnp.where(mine, total[rows:], total[:rows])
    outs[1][...] = jnp.where(mine, total[:rows], total[rows:])


def added(me, own, came, bit, after):
    shape = (own.shape[0] // 2, own.shape[1]) if bit else own.shape
    whole = pl.BlockSpec(own.shape, lambda i, me: (0, 0))
    outs = 2 if bit else 1
    return pl.pallas_call(
        ignoring(functools.partial(added_kernel, bit), len(after), 3),
        grid_spec=pltpu.PrefetchScalarGridSpec(
            num_scalar_prefetch=1,
            grid=(1,),
            in_specs=[whole, whole] + [pl.BlockSpec(memory_space=pl.ANY)] * len(after),
            out_specs=[pl.BlockSpec(shape, lambda i, me: (0, 0))] * outs,
        ),
        out_shape=[jax.ShapeDtypeStruct(shape, BF16)] * outs,
        compiler_params=pltpu.CompilerParams(vmem_limit_bytes=VMEM_BYTES),
        cost_estimate=estimate(0.5),
        name="added",
    )(me, own, came, *after)


def split(me, block, bit):
    rows = block.shape[0] // 2
    mine = (me[0] & bit) != 0
    low, high = block[:rows], block[rows:]
    return jnp.where(mine, high, low), jnp.where(mine, low, high)


def summed(me, partial, gates, join_gate):
    bits = bits_of(lax.axis_size("ctx"))
    sums, send = split(me, partial, bits[0])
    for step, bit in enumerate(bits):
        came = swap(send if step < 2 else sums, "ctx", bit)
        sums, *send = added(me, sums, came, bits[1] if step == 0 else 0, gates[step] if step < len(gates) else ())
        send = send[0] if send else None
    sums = joined(me, sums, swap(sums, "ctx", bits[1]), bits[1], BF16, join_gate)
    return sums, swap(sums, "ctx", bits[0]), bits[0]


def joined_kernel(bit, me_ref, own_ref, other_ref, out_ref):
    rows = own_ref.shape[0]
    mine = (me_ref[0] & bit) != 0
    out_ref[:rows] = jnp.where(mine, other_ref[...], own_ref[...]).astype(out_ref.dtype)
    out_ref[rows:] = jnp.where(mine, own_ref[...], other_ref[...]).astype(out_ref.dtype)


def joined(me, own, other, bit, dtype, after):
    rows, width = own.shape
    whole = pl.BlockSpec(own.shape, lambda i, me: (0, 0))
    return pl.pallas_call(
        ignoring(functools.partial(joined_kernel, bit), len(after), 3),
        grid_spec=pltpu.PrefetchScalarGridSpec(
            num_scalar_prefetch=1,
            grid=(1,),
            in_specs=[whole, whole] + [pl.BlockSpec(memory_space=pl.ANY)] * len(after),
            out_specs=pl.BlockSpec((2 * rows, width), lambda i, me: (0, 0)),
        ),
        out_shape=jax.ShapeDtypeStruct((2 * rows, width), dtype),
        compiler_params=pltpu.CompilerParams(vmem_limit_bytes=VMEM_BYTES),
        cost_estimate=estimate(0.5),
        name="joined",
    )(me, own, other, *after)


class Exchange:
    def __init__(self, pieces):
        self.shape = pieces.shape[1:]
        self.held, self.sources = pieces[None], [0]
        self.bits = bits_of(pieces.shape[0])

    def step(self, kernels):
        if not self.bits:
            return []
        bit = self.bits.pop()
        give = self.held[:, bit:].reshape((-1,) + self.shape)
        came = swap(held_until([give], kernels)[0], "ctx", bit)
        self.held = jnp.concatenate(
            [self.held[:, :bit], came.reshape((len(self.sources), bit) + self.shape)], axis=0
        )
        self.sources += [source ^ bit for source in self.sources]
        return [came]


def per_device(query_proj, key_proj, value_proj, filters, out_weight, cotangent):
    length, channels = query_proj.shape
    taps = filters.shape[1]
    n_ctx, n_chan = lax.axis_size("ctx"), lax.axis_size("chan")
    me = jnp.stack([lax.axis_index("ctx"), lax.axis_index("chan")]).astype(jnp.int32)
    forward, late, early, lags = [jnp.asarray(m) for m in transforms(taps)]

    product = (key_proj.astype(F32) * value_proj.astype(F32)).astype(BF16)
    product, cotangent = lax.optimization_barrier((product, cotangent))
    earlier = lax.ppermute(product, "ctx", [(i, i + 1) for i in range(n_ctx - 1)])

    cots = {0: cotangent, 1: swap(cotangent, "chan", 1)}
    for bit in reversed(bits_of(n_chan)[1:]):
        cots.update({off ^ bit: swap(cots[off], "chan", bit) for off in list(cots) if off % 2 == 0})
    offs = sorted(off for off in cots if off % 2 == 0 and off)
    sums = weight_pass(me, out_weight, 0, cot=cots[0])
    for off in offs:
        cots[off + 1] = swap(held_until([cots[off]], sums)[0], "chan", 1)
    offs = sorted(offs + [off + 1 for off in offs])

    gated, filtered = by_channel(
        forward_kernel,
        [query_proj, key_proj, value_proj, earlier, filters, forward, late],
        "ttttcww",
        [("t", BF16), ("t", F32)],
        "forward_filter",
        after=sums,
    )

    pieces = pieces_of(me, [cots[off] for off in range(n_chan)], n_ctx, [gated])
    exchange = Exchange(pieces)
    stages = exchange.step([pieces])

    order = cycle_of(n_ctx)
    ahead = [(order[i], order[(i + 1) % n_ctx]) for i in range(n_ctx)]
    behind = [(b, a) for a, b in ahead]
    half = channels // 2
    from_behind, from_ahead = gated, gated
    blocks = [gated]
    for step in range(n_ctx // 2 - 1):
        from_behind = lax.ppermute(from_behind, "ctx", ahead)
        from_ahead = lax.ppermute(from_ahead, "ctx", behind)
        blocks += [from_behind, from_ahead]
    far_low = lax.ppermute(from_behind[:, :half], "ctx", ahead)
    far_high = lax.ppermute(from_ahead[:, half:], "ctx", behind)

    sums = weight_pass(me, out_weight, 1, cot=cots[1], sums=sums, after=[pieces])
    terms = {}
    for off in offs[:-1]:
        *sums, terms[off] = weight_pass(me, out_weight, off, gated, cots[off], sums)
    grad_query, grad_filtered, terms[offs[-1]] = weight_pass(
        me, out_weight, offs[-1], gated, cots[offs[-1]], sums, [query_proj, filtered],
        (),
        blocks[1:3] + stages,
    )
    stages = exchange.step(stages)
    following = lax.ppermute(grad_filtered, "ctx", [(i + 1, i) for i in range(n_ctx - 1)])

    tap_grad = by_channel(
        tap_grad_kernel,
        [key_proj, value_proj, earlier, grad_filtered, forward, lags],
        "ttttww",
        [("c", BF16)],
        "tap_grad",
    )[0]

    for off in [off for off in sorted(terms) if off % 2]:
        came = swap(terms.pop(off), "chan", 1)
        terms[off ^ 1] = terms[off ^ 1] + came.astype(F32)
    terms[1] = weight_pass(me, out_weight, 1, gated, after=[tap_grad, came])[0]
    while exchange.bits:
        exchange.step([terms[1]])
    final = [swap(terms.pop(1), "chan", 1)]
    for bit in bits_of(n_chan)[1:]:
        for off in [off for off in sorted(terms, reverse=True) if off & bit]:
            came = swap(terms.pop(off).astype(BF16), "chan", bit)
            if off == bit:
                final.append(came)
            else:
                terms[off ^ bit] = terms[off ^ bit] + came.astype(F32)

    grad_key, grad_value = by_channel(
        backward_kernel,
        [key_proj, value_proj, grad_filtered, following, filters, forward, early],
        "ttttcww",
        [("t", BF16), ("t", BF16)],
        "backward_filter",
        after=blocks[3:5] + stages,
    )
    mixed = weight_pass(me, out_weight, 0, gated, adds=final, after=[grad_key] + blocks[5:7])[0]
    halves_summed = summed(me, held_until([tap_grad], [grad_key])[0], [(), [mixed]], [far_low, far_high])

    columns = gather_by_swaps(exchange.held[:, 0])
    columns = [columns[off] for off in range(n_chan)]
    if (channels // n_ctx) % 128:
        columns = in_one_piece(me, columns, length)
    owners = []
    for c in range(n_ctx):
        spot = order.index(c)
        steps = [0] + [sign * step for step in range(1, n_ctx // 2) for sign in (-1, 1)] + [n_ctx // 2]
        owners.append([exchange.sources.index(order[(spot + step) % n_ctx] ^ c) for step in steps])
    grad_weight = grad_weight_of(me, jnp.asarray(owners, jnp.int32), blocks, far_low, far_high, columns)
    own, other, bit = halves_summed
    grad_filters = joined(me, own, held_until([other], [grad_weight])[0], bit, F32, ())
    return (mixed, grad_query, grad_key, grad_value, grad_filters, grad_weight)


def solution(mesh):
    placed = (
        P("ctx", "chan"),
        P("ctx", "chan"),
        P("ctx", "chan"),
        P("chan", None),
        P("chan", None),
        P("ctx", "chan"),
    )
    return jax.shard_map(
        per_device,
        mesh=mesh,
        in_specs=placed,
        out_specs=(
            P("ctx", "chan"),
            P("ctx", "chan"),
            P("ctx", "chan"),
            P("ctx", "chan"),
            P("chan", None),
            P("chan", "ctx"),
        ),
        check_vma=False,
    )
```

```python
import functools

import jax
import jax.numpy as jnp
import numpy as np
from jax import lax
from jax.experimental import pallas as pl
from jax.experimental.pallas import tpu as pltpu
from jax.sharding import PartitionSpec as P

F32 = jnp.float32
BF16 = jnp.bfloat16
VMEM_BYTES = 40 * 2**20
NT = (((1,), (1,)), ((), ()))
TN = (((0,), (0,)), ((), ()))


def halves(matrix):
    high = matrix.astype(BF16)
    low = (matrix - high.astype(np.float64)).astype(BF16)
    return np.stack([high, low])


def transforms(taps):
    points = 2 * taps
    angle = np.pi * (2 * np.arange(taps)[:, None] + 1) * np.arange(points)[None, :] / points
    forward = np.concatenate([np.cos(angle), -np.sin(angle)], axis=0)
    inverse = forward.T * (2.0 / points)
    late = inverse[taps:]
    early = inverse[:taps]
    lags = inverse[taps - np.arange(taps)]
    return halves(forward), halves(late), halves(early), halves(lags)


def mm(a, b, dims=(((1,), (0,)), ((), ()))):
    return lax.dot_general(a, b, dims, preferred_element_type=F32)


def spectrum(f_ref, rows):
    return mm(f_ref[0], rows) + mm(f_ref[1], rows)


def tap_spectrum(f_ref, filters, taps):
    return mm(f_ref[0, :, :taps], filters, NT) + mm(f_ref[1, :, :taps], filters, NT)


def back(g_ref, real, imag):
    both = jnp.concatenate([real, imag], axis=0)
    high = both.astype(BF16)
    low = (both - high.astype(F32)).astype(BF16)
    return mm(g_ref[0], high) + mm(g_ref[0], low) + mm(g_ref[1], high)


def forward_kernel(taps, q_ref, k_ref, v_ref, earlier_ref, filt_ref, f_ref, g_ref, gated_ref, filtered_ref):
    product = (k_ref[...].astype(F32) * v_ref[...].astype(F32)).astype(BF16)
    x = spectrum(f_ref, jnp.concatenate([earlier_ref[...], product], axis=0))
    h = tap_spectrum(f_ref, filt_ref[...], taps)
    xr, xi, hr, hi = x[:taps], x[taps:], h[:taps], h[taps:]
    filtered = back(g_ref, xr * hr - xi * hi, xr * hi + xi * hr)
    filtered_ref[...] = filtered
    gated_ref[...] = (q_ref[...].astype(F32) * filtered).astype(BF16)


def tap_grad_kernel(taps, k_ref, v_ref, earlier_ref, gf_ref, f_ref, g_ref, out_ref):
    product = (k_ref[...].astype(F32) * v_ref[...].astype(F32)).astype(BF16)
    x = spectrum(f_ref, jnp.concatenate([earlier_ref[...], product], axis=0))
    rows = gf_ref[...]
    g = mm(f_ref[0, :, :taps], rows) + mm(f_ref[1, :, :taps], rows)
    xr, xi, gr, gi = x[:taps], x[taps:], g[:taps], g[taps:]
    tap_rows = back(g_ref, xr * gr + xi * gi, xi * gr - xr * gi)
    out_ref[...] = tap_rows.T.astype(BF16)


def backward_kernel(taps, k_ref, v_ref, gf_ref, following_ref, filt_ref, f_ref, g_ref, gk_ref, gv_ref):
    g = spectrum(f_ref, jnp.concatenate([gf_ref[...], following_ref[...]], axis=0))
    h = tap_spectrum(f_ref, filt_ref[...], taps)
    gr, gi, hr, hi = g[:taps], g[taps:], h[:taps], h[taps:]
    grad_product = back(g_ref, hr * gr + hi * gi, hr * gi - hi * gr)
    gk_ref[...] = (grad_product * v_ref[...].astype(F32)).astype(BF16)
    gv_ref[...] = (grad_product * k_ref[...].astype(F32)).astype(BF16)


def estimate(micros):
    return pl.CostEstimate(flops=int(micros * 10**9), bytes_accessed=0, transcendentals=0)


def ignoring(body, count, skip):
    def kernel(*refs):
        return body(*refs[:skip], *refs[skip + count :])

    return kernel


def by_channel(kernel, arrays, kinds, outs, name, after=()):
    length, channels = arrays[0].shape
    width = min(512, channels)
    specs = {
        "t": pl.BlockSpec((length, width), lambda i: (0, i)),
        "c": pl.BlockSpec((width, length), lambda i: (i, 0)),
    }

    def spec_of(kind, shape):
        if kind == "w":
            return pl.BlockSpec(shape, lambda i: (0,) * len(shape))
        return specs[kind]

    return pl.pallas_call(
        ignoring(functools.partial(kernel, length), len(after), len(arrays)),
        grid=(channels // width,),
        in_specs=[spec_of(kind, a.shape) for kind, a in zip(kinds, arrays)]
        + [pl.BlockSpec(memory_space=pl.ANY)] * len(after),
        out_specs=[specs[kind] for kind, unused in outs],
        out_shape=[
            jax.ShapeDtypeStruct((length, channels) if kind == "t" else (channels, length), dtype)
            for kind, dtype in outs
        ],
        compiler_params=pltpu.CompilerParams(vmem_limit_bytes=VMEM_BYTES),
        cost_estimate=estimate(3),
        name=name,
    )(*arrays, *after)


def pass_kernel(with_mixed, with_grad, has_sum, last, me_ref, w_ref, *refs):
    refs = list(refs)
    step = pl.program_id(0)
    if with_mixed:
        gated_ref = refs.pop(0)
    if with_grad:
        cot_ref = refs.pop(0)
        sum_ref = refs.pop(0) if has_sum else None
        turned_ref = refs.pop()

        @pl.when(step == 0)
        def turn():
            turned_ref[...] = cot_ref[...].T

        total = mm(w_ref[...], turned_ref[...])
        if has_sum:
            total = total + sum_ref[...]
        if last:
            q_ref, filtered_ref, gq_ref, gf_ref = refs[:4]
            total = total.T
            gq_ref[...] = (total * filtered_ref[...]).astype(BF16)
            gf_ref[...] = (total * q_ref[...].astype(F32)).astype(BF16)
        else:
            refs[0][...] = total
    if with_mixed:
        held_ref, mixed_ref = refs.pop(), refs.pop()
        part = mm(gated_ref[...], w_ref[...])

        @pl.when(step == 0)
        def first():
            held_ref[...] = part

        @pl.when(step > 0)
        def more():
            held_ref[...] = held_ref[...] + part

        @pl.when(step == pl.num_programs(0) - 1)
        def give():
            mixed_ref[...] = held_ref[...].astype(mixed_ref.dtype)


def weight_pass(me, weight, off, gated=None, cot=None, sums=(), ends=(), after=()):
    length = (cot if gated is None else gated).shape[0]
    channels = weight.shape[0]
    tile = 512
    whole = pl.BlockSpec((length, channels), lambda r, me: (0, 0))
    by_token = pl.BlockSpec((length, tile), lambda r, me: (0, r))
    by_row = pl.BlockSpec((tile, length), lambda r, me: (r, 0))
    arrays, in_specs = [weight], [pl.BlockSpec((tile, channels), lambda r, me: (r, me[1] ^ off))]
    out_specs, out_shape, scratch = [], [], []
    if gated is not None:
        arrays.append(gated)
        in_specs.append(by_token)
    if cot is not None:
        arrays += [cot, *sums, *ends]
        in_specs += [whole] + [by_row] * len(sums) + [by_token] * len(ends)
        out_specs += [by_token] * 2 if ends else [by_row]
        out_shape += [jax.ShapeDtypeStruct((length, channels), BF16)] * 2 if ends else [
            jax.ShapeDtypeStruct((channels, length), F32)
        ]
    if gated is not None:
        out_specs.append(whole)
        out_shape.append(jax.ShapeDtypeStruct((length, channels), BF16 if off % 2 else F32))
        scratch.append(pltpu.VMEM((length, channels), F32))
    if cot is not None:
        scratch.append(pltpu.VMEM((channels, length), BF16))
    body = functools.partial(pass_kernel, gated is not None, cot is not None, bool(sums), bool(ends))
    return pl.pallas_call(
        ignoring(body, len(after), 1 + len(arrays)),
        grid_spec=pltpu.PrefetchScalarGridSpec(
            num_scalar_prefetch=1,
            grid=(channels // tile,),
            in_specs=in_specs + [pl.BlockSpec(memory_space=pl.ANY)] * len(after),
            out_specs=out_specs,
            scratch_shapes=scratch,
        ),
        out_shape=out_shape,
        compiler_params=pltpu.CompilerParams(vmem_limit_bytes=VMEM_BYTES),
        cost_estimate=estimate(3 if gated is None else 0.5),
        name="grad_gated_part" if gated is None else "mixed_part" if cot is None else "grads_and_mixed",
    )(me, *arrays, *after)


def pieces_kernel(per_chan, me_ref, slot_ref, *refs):
    out_ref = refs[-1]
    length, width = refs[0].shape
    span = width // per_chan
    count = len(refs) - 1
    piece = span // count
    rows = length * piece // width
    for off in range(count):
        for part in range(per_chan):
            target = (me_ref[1] ^ off) * per_chan + part
            start = pl.multiple_of(part * span + me_ref[1] * piece, 128)
            block = refs[off][:, pl.ds(start, piece)]
            place = pl.multiple_of(slot_ref[me_ref[0], target] * rows, rows)
            out_ref[pl.ds(place, rows), :] = jnp.concatenate(
                [block[at : at + rows] for at in range(0, length, rows)], axis=1
            )


def pieces_of(me, slots, cots, after):
    length, width = cots[0].shape
    n_ctx = slots.shape[0]
    piece = width // n_ctx
    if piece % 128:
        return pieces_by_slices(me, slots, cots)
    return pl.pallas_call(
        ignoring(functools.partial(pieces_kernel, n_ctx // len(cots)), len(after), 2 + len(cots)),
        grid_spec=pltpu.PrefetchScalarGridSpec(
            num_scalar_prefetch=2,
            grid=(1,),
            in_specs=[pl.BlockSpec((length, width), lambda i, *ids: (0, 0))] * len(cots)
            + [pl.BlockSpec(memory_space=pl.ANY)] * len(after),
            out_specs=pl.BlockSpec((length, width), lambda i, *ids: (0, 0)),
        ),
        out_shape=jax.ShapeDtypeStruct((length, width), BF16),
        compiler_params=pltpu.CompilerParams(vmem_limit_bytes=VMEM_BYTES),
        cost_estimate=estimate(0.5),
        name="pieces",
    )(me, slots, *cots, *after)


def pieces_by_slices(me, slots, cots):
    length, width = cots[0].shape
    n_ctx, count = slots.shape[0], len(cots)
    piece, per_chan = width // n_ctx, n_ctx // count
    rows = length * piece // width
    table = jnp.stack(cots).reshape(count, length, per_chan, count, piece)
    mine = lax.dynamic_index_in_dim(table, me[1], 3, False)
    parts = mine.transpose(0, 2, 1, 3).reshape(n_ctx, length // rows, rows, piece)
    parts = parts.transpose(0, 2, 1, 3).reshape(n_ctx, rows, width)
    order = jnp.argsort(slots[me[0]])
    return parts[(order // per_chan ^ me[1]) * per_chan + order % per_chan].reshape(length, width)


def weight_kernel(places, parts, me_ref, *refs):
    out_ref = refs[-1]
    length = sum(rows for unused, rows in places[0])
    blocks = []
    at = 0
    for place in places:
        for start, rows in place:
            blocks.append(refs[at][start : start + rows, :])
            at += 1
    columns = jnp.concatenate(blocks, axis=0)
    for part in range(parts):
        packed = jnp.concatenate([ref[...] for ref in refs[at + 2 * part : at + 2 * part + 2]], axis=0)
        rows = packed.shape[0] // len(places)
        piece = packed.shape[1] * rows // length
        wide = [
            packed[slot * rows : (slot + 1) * rows, lane : lane + piece]
            for slot in range(len(places))
            for lane in range(0, packed.shape[1], piece)
        ]
        total = mm(columns, jnp.concatenate(wide, axis=0), TN)
        place = pl.multiple_of((me_ref[1] ^ part) * piece, piece)
        out_ref[:, pl.ds(place, piece)] = total.astype(BF16)


def grad_weight_of(me, arrays, places, cots):
    channels = arrays[0].shape[1]
    slots, parts = len(places), len(cots)
    pieces = [array for pair in cots for array, unused in pair]
    half = cots[0][0][0].shape[0]
    tile = 256
    width = 2 * half * channels // (slots * sum(count for unused, count in places[0])) * parts
    return pl.pallas_call(
        functools.partial(weight_kernel, places, parts),
        grid_spec=pltpu.PrefetchScalarGridSpec(
            num_scalar_prefetch=1,
            grid=(channels // tile,),
            in_specs=[pl.BlockSpec((array.shape[0], tile), lambda i, me: (0, i)) for array in arrays]
            + [pl.BlockSpec((half, channels), lambda i, me, at=at: (at, 0)) for pair in cots for unused, at in pair],
            out_specs=pl.BlockSpec((tile, width), lambda i, me: (i, 0)),
        ),
        out_shape=jax.ShapeDtypeStruct((channels, width), BF16),
        compiler_params=pltpu.CompilerParams(vmem_limit_bytes=VMEM_BYTES),
        cost_estimate=estimate(2),
        name="grad_weight",
    )(me, *arrays, *pieces)


def narrow_grad_weight(me, arrays, places, cots):
    blocks, at = [], 0
    for place in places:
        for start, rows in place:
            blocks.append(arrays[at][start : start + rows])
            at += 1
    columns = jnp.concatenate(blocks, axis=0)
    length = columns.shape[0] // len(places)
    packed = jnp.stack([jnp.concatenate(pair, axis=0) for pair in cots])
    packed = packed[jnp.arange(len(cots), dtype=jnp.int32) ^ me[1]]
    parts, height, width = packed.shape
    rows = height // len(places)
    piece = rows * width // length
    wide = packed.reshape(parts, len(places), rows, length // rows, piece).transpose(1, 3, 2, 0, 4)
    return mm(columns, wide.reshape(columns.shape[0], parts * piece), TN).astype(BF16)


def cycle_of(count):
    across = 1 << ((count.bit_length() - 1) // 2)
    order = []
    for column in range(across):
        line = [row * across + column for row in range(count // across)]
        order += line if column % 2 == 0 else line[::-1]
    return order


def held_until(arrays, kernels):
    return lax.optimization_barrier((*arrays, *kernels))[: len(arrays)]


def swap(block, axis, bit):
    size = lax.axis_size(axis)
    return lax.ppermute(block, axis, [(i, i ^ bit) for i in range(size)])


def bits_of(size):
    return [1 << place for place in range(size.bit_length() - 1)]


def gather_of_chips(block):
    held = {0: block}
    for bit in reversed(bits_of(lax.axis_size("chan"))[1:]):
        held.update({off ^ bit: swap(held[off], "chan", bit) for off in list(held)})
    return held


def added_kernel(bit, me_ref, own_ref, came_ref, *outs):
    total = (own_ref[...].astype(F32) + came_ref[...].astype(F32)).astype(BF16)
    if not bit:
        outs[0][...] = total
        return
    rows = outs[0].shape[0]
    mine = (me_ref[0] & bit) != 0
    outs[0][...] = jnp.where(mine, total[rows:], total[:rows])
    outs[1][...] = jnp.where(mine, total[:rows], total[rows:])


def added(me, own, came, bit, after):
    shape = (own.shape[0] // 2, own.shape[1]) if bit else own.shape
    whole = pl.BlockSpec(own.shape, lambda i, me: (0, 0))
    outs = 2 if bit else 1
    return pl.pallas_call(
        ignoring(functools.partial(added_kernel, bit), len(after), 3),
        grid_spec=pltpu.PrefetchScalarGridSpec(
            num_scalar_prefetch=1,
            grid=(1,),
            in_specs=[whole, whole] + [pl.BlockSpec(memory_space=pl.ANY)] * len(after),
            out_specs=[pl.BlockSpec(shape, lambda i, me: (0, 0))] * outs,
        ),
        out_shape=[jax.ShapeDtypeStruct(shape, BF16)] * outs,
        compiler_params=pltpu.CompilerParams(vmem_limit_bytes=VMEM_BYTES),
        cost_estimate=estimate(0.5),
        name="added",
    )(me, own, came, *after)


def split(me, block, bit):
    rows = block.shape[0] // 2
    mine = (me[0] & bit) != 0
    low, high = block[:rows], block[rows:]
    return jnp.where(mine, high, low), jnp.where(mine, low, high)


def summed(me, partial, gates, join_gate):
    bits = bits_of(lax.axis_size("ctx"))
    sums, send = split(me, partial, bits[0])
    for step, bit in enumerate(bits):
        came = swap(send if step < 2 else sums, "ctx", bit)
        sums, *send = added(me, sums, came, bits[1] if step == 0 else 0, gates[step] if step < len(gates) else ())
        send = send[0] if send else None
    sums = joined(me, sums, swap(sums, "ctx", bits[1]), bits[1], BF16, join_gate)
    return sums, swap(sums, "ctx", bits[0]), bits[0]


def joined_kernel(bit, me_ref, own_ref, other_ref, out_ref):
    rows = own_ref.shape[0]
    mine = (me_ref[0] & bit) != 0
    out_ref[:rows] = jnp.where(mine, other_ref[...], own_ref[...]).astype(out_ref.dtype)
    out_ref[rows:] = jnp.where(mine, own_ref[...], other_ref[...]).astype(out_ref.dtype)


def joined(me, own, other, bit, dtype, after):
    rows, width = own.shape
    whole = pl.BlockSpec(own.shape, lambda i, me: (0, 0))
    return pl.pallas_call(
        ignoring(functools.partial(joined_kernel, bit), len(after), 3),
        grid_spec=pltpu.PrefetchScalarGridSpec(
            num_scalar_prefetch=1,
            grid=(1,),
            in_specs=[whole, whole] + [pl.BlockSpec(memory_space=pl.ANY)] * len(after),
            out_specs=pl.BlockSpec((2 * rows, width), lambda i, me: (0, 0)),
        ),
        out_shape=jax.ShapeDtypeStruct((2 * rows, width), dtype),
        compiler_params=pltpu.CompilerParams(vmem_limit_bytes=VMEM_BYTES),
        cost_estimate=estimate(0.5),
        name="joined",
    )(me, own, other, *after)


def per_device(query_proj, key_proj, value_proj, filters, out_weight, cotangent):
    length, channels = query_proj.shape
    taps = filters.shape[1]
    n_ctx, n_chan = lax.axis_size("ctx"), lax.axis_size("chan")
    me = jnp.stack([lax.axis_index("ctx"), lax.axis_index("chan")]).astype(jnp.int32)
    forward, late, early_rows, lags = [jnp.asarray(m) for m in transforms(taps)]

    product = (key_proj.astype(F32) * value_proj.astype(F32)).astype(BF16)
    product, cotangent = lax.optimization_barrier((product, cotangent))
    earlier = lax.ppermute(product, "ctx", [(i, i + 1) for i in range(n_ctx - 1)])

    cots = {0: cotangent, 1: swap(cotangent, "chan", 1)}
    for bit in reversed(bits_of(n_chan)[1:]):
        cots.update({off ^ bit: swap(cots[off], "chan", bit) for off in list(cots) if off % 2 == 0})
    offs = sorted(off for off in cots if off % 2 == 0 and off)
    sums = weight_pass(me, out_weight, 0, cot=cots[0])
    for off in offs:
        cots[off + 1] = swap(held_until([cots[off]], sums)[0], "chan", 1)
    offs = sorted(offs + [off + 1 for off in offs])

    sums = weight_pass(me, out_weight, 1, cot=cots[1], sums=sums)

    order = cycle_of(n_ctx)
    slots = []
    for c in range(n_ctx):
        spot = order.index(c)
        turn = [0, n_ctx // 2] + list(range(1, n_ctx // 2)) + list(range(1 - n_ctx // 2, 0))
        targets = [order[(spot + step) % n_ctx] for step in turn]
        slots.append([targets.index(target) for target in range(n_ctx)])
    pieces = pieces_of(me, jnp.asarray(slots, jnp.int32), [cots[off] for off in range(n_chan)], sums)

    gated, filtered = by_channel(
        forward_kernel,
        [query_proj, key_proj, value_proj, earlier, filters, forward, late],
        "ttttcww",
        [("t", BF16), ("t", F32)],
        "forward_filter",
        after=sums,
    )

    ahead = [(order[i], order[(i + 1) % n_ctx]) for i in range(n_ctx)]
    behind = [(b, a) for a, b in ahead]
    turns = n_ctx // 2
    rows, piece = length // n_ctx, channels // n_ctx
    span = (turns - 1) * rows
    across = lax.ppermute(
        pieces[rows : 2 * rows], "ctx", [(order[i], order[(i + turns) % n_ctx]) for i in range(n_ctx)]
    )
    onto = jnp.concatenate([pieces[2 * rows : 2 * rows + span], gated], axis=0)
    back = jnp.concatenate([gated, pieces[2 * rows + span :]], axis=0)
    arrays, places = [gated], [[(0, length)]]
    brought, arrived = [pieces[:rows], across], []
    for step in range(1, turns):
        onto, back = lax.ppermute(onto, "ctx", ahead), lax.ppermute(back, "ctx", behind)
        arrived.append([onto, back])
        arrays += [onto, back]
        places += [[(onto.shape[0] - length, length)], [(0, length)]]
        brought += [onto[:rows], back[-rows:]]
        onto, back = onto[rows:], back[:-rows]
    half = length // 2
    far = [lax.ppermute(onto[:half], "ctx", ahead), lax.ppermute(back[half:], "ctx", behind)]
    arrays = arrays[:1] + far + arrays[1:]
    places.insert(1, [(0, half), (0, half)])

    early = 2 + 2 * min(1, turns - 1)
    cols = [gather_of_chips(jnp.concatenate(part, axis=0)) for part in (brought[:early], brought[early:])]

    terms = {}
    for off in offs[:-1]:
        *sums, terms[off] = weight_pass(me, out_weight, off, gated, cots[off], sums)
    terms[1] = weight_pass(me, out_weight, 1, gated, after=sums)[0]
    grad_query, grad_filtered, terms[offs[-1]] = weight_pass(
        me, out_weight, offs[-1], gated, cots[offs[-1]], sums, [query_proj, filtered],
        arrived[0] + [terms[1]],
    )
    following = lax.ppermute(grad_filtered, "ctx", [(i + 1, i) for i in range(n_ctx - 1)])

    tap_grad = by_channel(
        tap_grad_kernel,
        [key_proj, value_proj, earlier, grad_filtered, forward, lags],
        "ttttww",
        [("c", BF16)],
        "tap_grad",
    )[0]

    for off in [off for off in sorted(terms) if off > 1 and off % 2]:
        terms[off ^ 1] = terms[off ^ 1] + swap(terms.pop(off), "chan", 1).astype(F32)
    terms[0] = weight_pass(me, out_weight, 0, gated, after=arrived[1] + [tap_grad])[0]
    last_part = terms[0]
    terms[0] = terms[0] + swap(terms.pop(1), "chan", 1).astype(F32)
    for bit in bits_of(n_chan)[1:]:
        for off in [off for off in sorted(terms, reverse=True) if off & bit]:
            terms[off ^ bit] = terms[off ^ bit] + swap(terms.pop(off).astype(BF16), "chan", bit).astype(F32)
    mixed = terms[0].astype(BF16)

    grad_key, grad_value = by_channel(
        backward_kernel,
        [key_proj, value_proj, grad_filtered, following, filters, forward, early_rows],
        "ttttcww",
        [("t", BF16), ("t", BF16)],
        "backward_filter",
        after=[last_part],
    )
    own, other, bit = summed(me, tap_grad, [[], arrived[2]], far)

    evens = [off for off in range(n_chan) if off % 2 == 0]
    wide = piece % 128 == 0 and 2 * early == n_ctx
    columns = {off: [(part[off], 0) for part in cols] for off in evens}
    crossed = swap(jnp.concatenate([part[off] for off in evens for part in cols], axis=0), "chan", 1)
    if wide:
        for at, off in enumerate(evens):
            columns[off + 1] = [(crossed, 2 * at), (crossed, 2 * at + 1)]
        grad_weight = grad_weight_of(me, arrays, places, [columns[off] for off in range(n_chan)])
    else:
        for at, off in enumerate(evens):
            columns[off + 1] = [(crossed[at * length : (at + 1) * length], 0)]
        pairs = [[array for array, unused in columns[off]] for off in range(n_chan)]
        grad_weight = narrow_grad_weight(me, arrays, places, pairs)
    grad_filters = joined(me, own, held_until([other], [grad_weight])[0], bit, F32, ())
    return (mixed, grad_query, grad_key, grad_value, grad_filters, grad_weight)


def solution(mesh):
    placed = (
        P("ctx", "chan"),
        P("ctx", "chan"),
        P("ctx", "chan"),
        P("chan", None),
        P("chan", None),
        P("ctx", "chan"),
    )
    return jax.shard_map(
        per_device,
        mesh=mesh,
        in_specs=placed,
        out_specs=(
            P("ctx", "chan"),
            P("ctx", "chan"),
            P("ctx", "chan"),
            P("ctx", "chan"),
            P("chan", None),
            P("chan", "ctx"),
        ),
        check_vma=False,
    )
```

```python
import functools

import jax
import jax.numpy as jnp
import numpy as np
from jax import lax
from jax.experimental import pallas as pl
from jax.experimental.pallas import tpu as pltpu
from jax.sharding import PartitionSpec as P

F32 = jnp.float32
BF16 = jnp.bfloat16
VMEM_BYTES = 40 * 2**20
NT = (((1,), (1,)), ((), ()))
TN = (((0,), (0,)), ((), ()))


def halves(matrix):
    high = matrix.astype(BF16)
    low = (matrix - high.astype(np.float64)).astype(BF16)
    return np.stack([high, low])


def transforms(taps):
    points = 2 * taps
    angle = np.pi * (2 * np.arange(taps)[:, None] + 1) * np.arange(points)[None, :] / points
    forward = np.concatenate([np.cos(angle), -np.sin(angle)], axis=0)
    inverse = forward.T * (2.0 / points)
    late = inverse[taps:]
    early = inverse[:taps]
    lags = inverse[taps - np.arange(taps)]
    return halves(forward), halves(late), halves(early), halves(lags)


def mm(a, b, dims=(((1,), (0,)), ((), ()))):
    return lax.dot_general(a, b, dims, preferred_element_type=F32)


def spectrum(f_ref, rows):
    return mm(f_ref[0], rows) + mm(f_ref[1], rows)


def tap_spectrum(f_ref, filters, taps):
    return mm(f_ref[0, :, :taps], filters, NT) + mm(f_ref[1, :, :taps], filters, NT)


def back(g_ref, real, imag):
    both = jnp.concatenate([real, imag], axis=0)
    high = both.astype(BF16)
    low = (both - high.astype(F32)).astype(BF16)
    return mm(g_ref[0], high) + mm(g_ref[0], low) + mm(g_ref[1], high)


def forward_kernel(taps, q_ref, k_ref, v_ref, earlier_ref, filt_ref, f_ref, g_ref, gated_ref, filtered_ref):
    product = (k_ref[...].astype(F32) * v_ref[...].astype(F32)).astype(BF16)
    x = spectrum(f_ref, jnp.concatenate([earlier_ref[...], product], axis=0))
    h = tap_spectrum(f_ref, filt_ref[...], taps)
    xr, xi, hr, hi = x[:taps], x[taps:], h[:taps], h[taps:]
    filtered = back(g_ref, xr * hr - xi * hi, xr * hi + xi * hr)
    filtered_ref[...] = filtered
    gated_ref[...] = (q_ref[...].astype(F32) * filtered).astype(BF16)


def tap_grad_kernel(taps, k_ref, v_ref, earlier_ref, gf_ref, f_ref, g_ref, out_ref):
    product = (k_ref[...].astype(F32) * v_ref[...].astype(F32)).astype(BF16)
    x = spectrum(f_ref, jnp.concatenate([earlier_ref[...], product], axis=0))
    rows = gf_ref[...]
    g = mm(f_ref[0, :, :taps], rows) + mm(f_ref[1, :, :taps], rows)
    xr, xi, gr, gi = x[:taps], x[taps:], g[:taps], g[taps:]
    tap_rows = back(g_ref, xr * gr + xi * gi, xi * gr - xr * gi)
    out_ref[...] = tap_rows.T.astype(BF16)


def backward_kernel(taps, k_ref, v_ref, gf_ref, following_ref, filt_ref, f_ref, g_ref, gk_ref, gv_ref):
    g = spectrum(f_ref, jnp.concatenate([gf_ref[...], following_ref[...]], axis=0))
    h = tap_spectrum(f_ref, filt_ref[...], taps)
    gr, gi, hr, hi = g[:taps], g[taps:], h[:taps], h[taps:]
    grad_product = back(g_ref, hr * gr + hi * gi, hr * gi - hi * gr)
    gk_ref[...] = (grad_product * v_ref[...].astype(F32)).astype(BF16)
    gv_ref[...] = (grad_product * k_ref[...].astype(F32)).astype(BF16)


def estimate(micros):
    return pl.CostEstimate(flops=int(micros * 10**9), bytes_accessed=0, transcendentals=0)


def ignoring(body, count, skip):
    def kernel(*refs):
        return body(*refs[:skip], *refs[skip + count :])

    return kernel


def by_channel(kernel, arrays, kinds, outs, name, after=()):
    length, channels = arrays[0].shape
    width = min(512, channels)
    specs = {
        "t": pl.BlockSpec((length, width), lambda i: (0, i)),
        "c": pl.BlockSpec((width, length), lambda i: (i, 0)),
    }

    def spec_of(kind, shape):
        if kind == "w":
            return pl.BlockSpec(shape, lambda i: (0,) * len(shape))
        return specs[kind]

    return pl.pallas_call(
        ignoring(functools.partial(kernel, length), len(after), len(arrays)),
        grid=(channels // width,),
        in_specs=[spec_of(kind, a.shape) for kind, a in zip(kinds, arrays)]
        + [pl.BlockSpec(memory_space=pl.ANY)] * len(after),
        out_specs=[specs[kind] for kind, unused in outs],
        out_shape=[
            jax.ShapeDtypeStruct((length, channels) if kind == "t" else (channels, length), dtype)
            for kind, dtype in outs
        ],
        compiler_params=pltpu.CompilerParams(vmem_limit_bytes=VMEM_BYTES),
        cost_estimate=estimate(3),
        name=name,
    )(*arrays, *after)


def pass_kernel(with_mixed, with_grad, has_sum, last, me_ref, w_ref, *refs):
    refs = list(refs)
    step = pl.program_id(0)
    if with_mixed:
        gated_ref = refs.pop(0)
    if with_grad:
        cot_ref = refs.pop(0)
        sum_ref = refs.pop(0) if has_sum else None
        turned_ref = refs.pop()

        @pl.when(step == 0)
        def turn():
            turned_ref[...] = cot_ref[...].T

        total = mm(w_ref[...], turned_ref[...])
        if has_sum:
            total = total + sum_ref[...]
        if last:
            q_ref, filtered_ref, gq_ref, gf_ref = refs[:4]
            total = total.T
            gq_ref[...] = (total * filtered_ref[...]).astype(BF16)
            gf_ref[...] = (total * q_ref[...].astype(F32)).astype(BF16)
        else:
            refs[0][...] = total
    if with_mixed:
        held_ref, mixed_ref = refs.pop(), refs.pop()
        part = mm(gated_ref[...], w_ref[...])

        @pl.when(step == 0)
        def first():
            held_ref[...] = part

        @pl.when(step > 0)
        def more():
            held_ref[...] = held_ref[...] + part

        @pl.when(step == pl.num_programs(0) - 1)
        def give():
            mixed_ref[...] = held_ref[...].astype(mixed_ref.dtype)


def weight_pass(me, weight, off, gated=None, cot=None, sums=(), ends=(), after=()):
    length = (cot if gated is None else gated).shape[0]
    channels = weight.shape[0]
    tile = 512
    whole = pl.BlockSpec((length, channels), lambda r, me: (0, 0))
    by_token = pl.BlockSpec((length, tile), lambda r, me: (0, r))
    by_row = pl.BlockSpec((tile, length), lambda r, me: (r, 0))
    arrays, in_specs = [weight], [pl.BlockSpec((tile, channels), lambda r, me: (r, me[1] ^ off))]
    out_specs, out_shape, scratch = [], [], []
    if gated is not None:
        arrays.append(gated)
        in_specs.append(by_token)
    if cot is not None:
        arrays += [cot, *sums, *ends]
        in_specs += [whole] + [by_row] * len(sums) + [by_token] * len(ends)
        out_specs += [by_token] * 2 if ends else [by_row]
        out_shape += [jax.ShapeDtypeStruct((length, channels), BF16)] * 2 if ends else [
            jax.ShapeDtypeStruct((channels, length), F32)
        ]
    if gated is not None:
        out_specs.append(whole)
        out_shape.append(jax.ShapeDtypeStruct((length, channels), BF16 if off % 2 else F32))
        scratch.append(pltpu.VMEM((length, channels), F32))
    if cot is not None:
        scratch.append(pltpu.VMEM((channels, length), BF16))
    body = functools.partial(pass_kernel, gated is not None, cot is not None, bool(sums), bool(ends))
    return pl.pallas_call(
        ignoring(body, len(after), 1 + len(arrays)),
        grid_spec=pltpu.PrefetchScalarGridSpec(
            num_scalar_prefetch=1,
            grid=(channels // tile,),
            in_specs=in_specs + [pl.BlockSpec(memory_space=pl.ANY)] * len(after),
            out_specs=out_specs,
            scratch_shapes=scratch,
        ),
        out_shape=out_shape,
        compiler_params=pltpu.CompilerParams(vmem_limit_bytes=VMEM_BYTES),
        cost_estimate=estimate(3 if gated is None else 0.5),
        name="grad_gated_part" if gated is None else "mixed_part" if cot is None else "grads_and_mixed",
    )(me, *arrays, *after)


def pieces_kernel(per_chan, me_ref, slot_ref, *refs):
    out_ref = refs[-1]
    length, width = refs[0].shape
    span = width // per_chan
    count = len(refs) - 1
    piece = span // count
    rows = length * piece // width
    for off in range(count):
        for part in range(per_chan):
            target = (me_ref[1] ^ off) * per_chan + part
            start = pl.multiple_of(part * span + me_ref[1] * piece, 128)
            block = refs[off][:, pl.ds(start, piece)]
            place = pl.multiple_of(slot_ref[me_ref[0], target] * rows, rows)
            out_ref[pl.ds(place, rows), :] = jnp.concatenate(
                [block[at : at + rows] for at in range(0, length, rows)], axis=1
            )


def pieces_of(me, slots, cots, after):
    length, width = cots[0].shape
    n_ctx = slots.shape[0]
    piece = width // n_ctx
    if piece % 128:
        return pieces_by_slices(me, slots, cots)
    return pl.pallas_call(
        ignoring(functools.partial(pieces_kernel, n_ctx // len(cots)), len(after), 2 + len(cots)),
        grid_spec=pltpu.PrefetchScalarGridSpec(
            num_scalar_prefetch=2,
            grid=(1,),
            in_specs=[pl.BlockSpec((length, width), lambda i, *ids: (0, 0))] * len(cots)
            + [pl.BlockSpec(memory_space=pl.ANY)] * len(after),
            out_specs=pl.BlockSpec((length, width), lambda i, *ids: (0, 0)),
        ),
        out_shape=jax.ShapeDtypeStruct((length, width), BF16),
        compiler_params=pltpu.CompilerParams(vmem_limit_bytes=VMEM_BYTES),
        cost_estimate=estimate(0.5),
        name="pieces",
    )(me, slots, *cots, *after)


def pieces_by_slices(me, slots, cots):
    length, width = cots[0].shape
    n_ctx, count = slots.shape[0], len(cots)
    piece, per_chan = width // n_ctx, n_ctx // count
    rows = length * piece // width
    table = jnp.stack(cots).reshape(count, length, per_chan, count, piece)
    mine = lax.dynamic_index_in_dim(table, me[1], 3, False)
    parts = mine.transpose(0, 2, 1, 3).reshape(n_ctx, length // rows, rows, piece)
    parts = parts.transpose(0, 2, 1, 3).reshape(n_ctx, rows, width)
    order = jnp.argsort(slots[me[0]])
    return parts[(order // per_chan ^ me[1]) * per_chan + order % per_chan].reshape(length, width)


def weight_kernel(places, parts, me_ref, *refs):
    out_ref = refs[-1]
    length = sum(rows for unused, rows in places[0])
    blocks = []
    at = 0
    for place in places:
        for start, rows in place:
            blocks.append(refs[at][start : start + rows, :])
            at += 1
    columns = jnp.concatenate(blocks, axis=0)
    for part in range(parts):
        packed = jnp.concatenate([ref[...] for ref in refs[at + 2 * part : at + 2 * part + 2]], axis=0)
        rows = packed.shape[0] // len(places)
        piece = packed.shape[1] * rows // length
        wide = [
            packed[slot * rows : (slot + 1) * rows, lane : lane + piece]
            for slot in range(len(places))
            for lane in range(0, packed.shape[1], piece)
        ]
        total = mm(columns, jnp.concatenate(wide, axis=0), TN)
        place = pl.multiple_of((me_ref[1] ^ part) * piece, piece)
        out_ref[:, pl.ds(place, piece)] = total.astype(BF16)


def grad_weight_of(me, arrays, places, cots, earlier):
    channels = arrays[0].shape[1]
    slots, parts = len(places), len(cots)
    pieces = [array for pair in cots for array, unused in pair]
    half = cots[0][0][0].shape[0]
    tile = 256
    width = 2 * half * channels // (slots * sum(count for unused, count in places[0])) * parts
    steps = channels // tile // 2
    first = steps * len(earlier)
    count = 1 + len(arrays) + len(pieces)
    return pl.pallas_call(
        ignoring(functools.partial(weight_kernel, places, parts), len(earlier), count),
        grid_spec=pltpu.PrefetchScalarGridSpec(
            num_scalar_prefetch=1,
            grid=(steps,),
            in_specs=[pl.BlockSpec((array.shape[0], tile), lambda i, me: (0, first + i)) for array in arrays]
            + [pl.BlockSpec((half, channels), lambda i, me, at=at: (at, 0)) for pair in cots for unused, at in pair]
            + [pl.BlockSpec(memory_space=pl.ANY)] * len(earlier),
            out_specs=pl.BlockSpec((tile, width), lambda i, me: (first + i, 0)),
        ),
        out_shape=jax.ShapeDtypeStruct((channels, width), BF16),
        input_output_aliases={count: 0} if earlier else {},
        compiler_params=pltpu.CompilerParams(vmem_limit_bytes=VMEM_BYTES),
        cost_estimate=estimate(2),
        name="grad_weight",
    )(me, *arrays, *pieces, *earlier)


def narrow_grad_weight(me, arrays, places, cots):
    blocks, at = [], 0
    for place in places:
        for start, rows in place:
            blocks.append(arrays[at][start : start + rows])
            at += 1
    columns = jnp.concatenate(blocks, axis=0)
    length = columns.shape[0] // len(places)
    packed = jnp.stack([jnp.concatenate(pair, axis=0) for pair in cots])
    packed = packed[jnp.arange(len(cots), dtype=jnp.int32) ^ me[1]]
    parts, height, width = packed.shape
    rows = height // len(places)
    piece = rows * width // length
    wide = packed.reshape(parts, len(places), rows, length // rows, piece).transpose(1, 3, 2, 0, 4)
    return mm(columns, wide.reshape(columns.shape[0], parts * piece), TN).astype(BF16)


def cycle_of(count):
    across = 1 << ((count.bit_length() - 1) // 2)
    order = []
    for column in range(across):
        line = [row * across + column for row in range(count // across)]
        order += line if column % 2 == 0 else line[::-1]
    return order


def held_until(arrays, kernels):
    return lax.optimization_barrier((*arrays, *kernels))[: len(arrays)]


def swap(block, axis, bit):
    size = lax.axis_size(axis)
    return lax.ppermute(block, axis, [(i, i ^ bit) for i in range(size)])


def bits_of(size):
    return [1 << place for place in range(size.bit_length() - 1)]


def gather_of_chips(block):
    held = {0: block}
    for bit in reversed(bits_of(lax.axis_size("chan"))[1:]):
        held.update({off ^ bit: swap(held[off], "chan", bit) for off in list(held)})
    return held


def added_kernel(bit, me_ref, own_ref, came_ref, *outs):
    total = (own_ref[...].astype(F32) + came_ref[...].astype(F32)).astype(BF16)
    if not bit:
        outs[0][...] = total
        return
    rows = outs[0].shape[0]
    mine = (me_ref[0] & bit) != 0
    outs[0][...] = jnp.where(mine, total[rows:], total[:rows])
    outs[1][...] = jnp.where(mine, total[:rows], total[rows:])


def added(me, own, came, bit, after):
    shape = (own.shape[0] // 2, own.shape[1]) if bit else own.shape
    whole = pl.BlockSpec(own.shape, lambda i, me: (0, 0))
    outs = 2 if bit else 1
    return pl.pallas_call(
        ignoring(functools.partial(added_kernel, bit), len(after), 3),
        grid_spec=pltpu.PrefetchScalarGridSpec(
            num_scalar_prefetch=1,
            grid=(1,),
            in_specs=[whole, whole] + [pl.BlockSpec(memory_space=pl.ANY)] * len(after),
            out_specs=[pl.BlockSpec(shape, lambda i, me: (0, 0))] * outs,
        ),
        out_shape=[jax.ShapeDtypeStruct(shape, BF16)] * outs,
        compiler_params=pltpu.CompilerParams(vmem_limit_bytes=VMEM_BYTES),
        cost_estimate=estimate(0.5),
        name="added",
    )(me, own, came, *after)


def split(me, block, bit):
    rows = block.shape[0] // 2
    mine = (me[0] & bit) != 0
    low, high = block[:rows], block[rows:]
    return jnp.where(mine, high, low), jnp.where(mine, low, high)


def summed(me, partial, gates):
    bits = bits_of(lax.axis_size("ctx"))
    sums, send = split(me, partial, bits[0])
    for step, bit in enumerate(bits):
        came = swap(send if step < 2 else sums, "ctx", bit)
        sums, *send = added(me, sums, came, bits[1] if step == 0 else 0, gates[step] if step < len(gates) else ())
        send = send[0] if send else None
    return sums, swap(sums, "ctx", bits[1]), bits[:2]


def joined_kernel(bit, me_ref, own_ref, other_ref, out_ref):
    rows = own_ref.shape[0]
    mine = (me_ref[0] & bit) != 0
    out_ref[:rows] = jnp.where(mine, other_ref[...], own_ref[...]).astype(out_ref.dtype)
    out_ref[rows:] = jnp.where(mine, own_ref[...], other_ref[...]).astype(out_ref.dtype)


def joined(me, own, other, bit, dtype, after):
    rows, width = own.shape
    whole = pl.BlockSpec(own.shape, lambda i, me: (0, 0))
    return pl.pallas_call(
        ignoring(functools.partial(joined_kernel, bit), len(after), 3),
        grid_spec=pltpu.PrefetchScalarGridSpec(
            num_scalar_prefetch=1,
            grid=(1,),
            in_specs=[whole, whole] + [pl.BlockSpec(memory_space=pl.ANY)] * len(after),
            out_specs=pl.BlockSpec((2 * rows, width), lambda i, me: (0, 0)),
        ),
        out_shape=jax.ShapeDtypeStruct((2 * rows, width), dtype),
        compiler_params=pltpu.CompilerParams(vmem_limit_bytes=VMEM_BYTES),
        cost_estimate=estimate(0.5),
        name="joined",
    )(me, own, other, *after)


def per_device(query_proj, key_proj, value_proj, filters, out_weight, cotangent):
    length, channels = query_proj.shape
    taps = filters.shape[1]
    n_ctx, n_chan = lax.axis_size("ctx"), lax.axis_size("chan")
    me = jnp.stack([lax.axis_index("ctx"), lax.axis_index("chan")]).astype(jnp.int32)
    forward, late, early_rows, lags = [jnp.asarray(m) for m in transforms(taps)]

    product = (key_proj.astype(F32) * value_proj.astype(F32)).astype(BF16)
    product, cotangent = lax.optimization_barrier((product, cotangent))
    earlier = lax.ppermute(product, "ctx", [(i, i + 1) for i in range(n_ctx - 1)])

    cots = {0: cotangent, 1: swap(cotangent, "chan", 1)}
    for bit in reversed(bits_of(n_chan)[1:]):
        cots.update({off ^ bit: swap(cots[off], "chan", bit) for off in list(cots) if off % 2 == 0})
    offs = sorted(off for off in cots if off % 2 == 0 and off)
    sums = weight_pass(me, out_weight, 0, cot=cots[0])
    for off in offs:
        cots[off + 1] = swap(held_until([cots[off]], sums)[0], "chan", 1)
    offs = sorted(offs + [off + 1 for off in offs])

    sums = weight_pass(me, out_weight, 1, cot=cots[1], sums=sums)

    order = cycle_of(n_ctx)
    slots = []
    for c in range(n_ctx):
        spot = order.index(c)
        turn = [0, n_ctx // 2] + list(range(1, n_ctx // 2)) + list(range(1 - n_ctx // 2, 0))
        targets = [order[(spot + step) % n_ctx] for step in turn]
        slots.append([targets.index(target) for target in range(n_ctx)])
    pieces = pieces_of(me, jnp.asarray(slots, jnp.int32), [cots[off] for off in range(n_chan)], sums)

    gated, filtered = by_channel(
        forward_kernel,
        [query_proj, key_proj, value_proj, earlier, filters, forward, late],
        "ttttcww",
        [("t", BF16), ("t", F32)],
        "forward_filter",
        after=sums,
    )

    ahead = [(order[i], order[(i + 1) % n_ctx]) for i in range(n_ctx)]
    behind = [(b, a) for a, b in ahead]
    turns = n_ctx // 2
    rows, piece = length // n_ctx, channels // n_ctx
    span = (turns - 1) * rows
    across = lax.ppermute(
        pieces[rows : 2 * rows], "ctx", [(order[i], order[(i + turns) % n_ctx]) for i in range(n_ctx)]
    )
    onto = jnp.concatenate([pieces[2 * rows : 2 * rows + span], gated], axis=0)
    back = jnp.concatenate([gated, pieces[2 * rows + span :]], axis=0)
    arrays, places = [gated], [[(0, length)]]
    brought, arrived = [pieces[:rows], across], []
    for step in range(1, turns):
        onto, back = lax.ppermute(onto, "ctx", ahead), lax.ppermute(back, "ctx", behind)
        arrived.append([onto, back])
        arrays += [onto, back]
        places += [[(onto.shape[0] - length, length)], [(0, length)]]
        brought += [onto[:rows], back[-rows:]]
        onto, back = onto[rows:], back[:-rows]
    half = length // 2
    far = [lax.ppermute(onto[:half], "ctx", ahead), lax.ppermute(back[half:], "ctx", behind)]
    arrays = arrays[:1] + far + arrays[1:]
    places.insert(1, [(0, half), (0, half)])

    early = 2 + 2 * min(1, turns - 1)
    first = held_until([jnp.concatenate(brought[:early], axis=0)], arrived[1])[0]
    cols = [gather_of_chips(part) for part in (first, jnp.concatenate(brought[early:], axis=0))]

    terms = {}
    for off in offs[:-1]:
        *sums, terms[off] = weight_pass(me, out_weight, off, gated, cots[off], sums)
    from_core = [swap(weight_pass(me, out_weight, 1, gated, after=sums)[0], "chan", 1)]
    grad_query, grad_filtered, terms[offs[-1]] = weight_pass(
        me, out_weight, offs[-1], gated, cots[offs[-1]], sums, [query_proj, filtered],
        arrived[0] + from_core,
    )
    following = lax.ppermute(grad_filtered, "ctx", [(i + 1, i) for i in range(n_ctx - 1)])

    tap_grad = by_channel(
        tap_grad_kernel,
        [key_proj, value_proj, earlier, grad_filtered, forward, lags],
        "ttttww",
        [("c", BF16)],
        "tap_grad",
    )[0]

    for off in [off for off in sorted(terms) if off % 2]:
        from_core.append(swap(terms.pop(off), "chan", 1))
        terms[off ^ 1] = terms[off ^ 1] + from_core[-1].astype(F32)
    terms = dict(zip(terms, held_until(terms.values(), arrived[1])))

    grad_key, grad_value = by_channel(
        backward_kernel,
        [key_proj, value_proj, grad_filtered, following, filters, forward, early_rows],
        "ttttcww",
        [("t", BF16), ("t", BF16)],
        "backward_filter",
        after=far,
    )
    terms[0] = weight_pass(me, out_weight, 0, gated, after=from_core[1:] + [cols[0][off] for off in cols[0] if off])[0] + from_core[0].astype(F32)
    for bit in bits_of(n_chan)[1:]:
        for off in [off for off in sorted(terms, reverse=True) if off & bit]:
            terms[off ^ bit] = terms[off ^ bit] + swap(terms.pop(off).astype(BF16), "chan", bit).astype(F32)
    mixed = terms[0].astype(BF16)

    own, other, bits = summed(me, held_until([tap_grad], arrived[1])[0], [[], far])

    evens = [off for off in range(n_chan) if off % 2 == 0]
    wide = piece % 128 == 0 and 2 * early == n_ctx
    columns = {off: [(part[off], 0) for part in cols] for off in evens}
    crossed = jnp.concatenate([part[off] for off in evens for part in cols], axis=0)
    crossed = swap(held_until([crossed], far)[0], "chan", 1)
    if wide:
        for at, off in enumerate(evens):
            columns[off + 1] = [(crossed, 2 * at), (crossed, 2 * at + 1)]
        columns = [columns[off] for off in range(n_chan)]
        low_half = grad_weight_of(me, arrays, places, columns, [])
        grad_weight = grad_weight_of(me, arrays, places, columns, [low_half])
    else:
        for at, off in enumerate(evens):
            columns[off + 1] = [(crossed[at * length : (at + 1) * length], 0)]
        pairs = [[array for array, unused in columns[off]] for off in range(n_chan)]
        low_half = grad_weight = narrow_grad_weight(me, arrays, places, pairs)
    own = joined(me, own, held_until([other], [low_half])[0], bits[1], BF16, ())
    other = swap(own, "ctx", bits[0])
    grad_filters = joined(me, own, held_until([other], [grad_weight])[0], bits[0], F32, ())
    return (mixed, grad_query, grad_key, grad_value, grad_filters, grad_weight)


def solution(mesh):
    placed = (
        P("ctx", "chan"),
        P("ctx", "chan"),
        P("ctx", "chan"),
        P("chan", None),
        P("chan", None),
        P("ctx", "chan"),
    )
    return jax.shard_map(
        per_device,
        mesh=mesh,
        in_specs=placed,
        out_specs=(
            P("ctx", "chan"),
            P("ctx", "chan"),
            P("ctx", "chan"),
            P("ctx", "chan"),
            P("chan", None),
            P("chan", "ctx"),
        ),
        check_vma=False,
    )
```

```python
import functools

import jax
import jax.numpy as jnp
import numpy as np
from jax import lax
from jax.experimental import pallas as pl
from jax.experimental.pallas import tpu as pltpu
from jax.sharding import PartitionSpec as P

F32 = jnp.float32
BF16 = jnp.bfloat16
VMEM_BYTES = 40 * 2**20
NT = (((1,), (1,)), ((), ()))
TN = (((0,), (0,)), ((), ()))


def halves(matrix):
    high = matrix.astype(BF16)
    low = (matrix - high.astype(np.float64)).astype(BF16)
    return np.stack([high, low])


def transforms(taps):
    points = 2 * taps
    angle = np.pi * (2 * np.arange(taps)[:, None] + 1) * np.arange(points)[None, :] / points
    forward = np.concatenate([np.cos(angle), -np.sin(angle)], axis=0)
    inverse = forward.T * (2.0 / points)
    late = inverse[taps:]
    early = inverse[:taps]
    lags = inverse[taps - np.arange(taps)]
    return halves(forward), halves(late), halves(early), halves(lags)


def mm(a, b, dims=(((1,), (0,)), ((), ()))):
    return lax.dot_general(a, b, dims, preferred_element_type=F32)


def spectrum(f_ref, rows):
    return mm(f_ref[0], rows) + mm(f_ref[1], rows)


def tap_spectrum(f_ref, filters, taps):
    return mm(f_ref[0, :, :taps], filters, NT) + mm(f_ref[1, :, :taps], filters, NT)


def back(g_ref, real, imag):
    both = jnp.concatenate([real, imag], axis=0)
    high = both.astype(BF16)
    low = (both - high.astype(F32)).astype(BF16)
    return mm(g_ref[0], high) + mm(g_ref[0], low) + mm(g_ref[1], high)


def forward_kernel(taps, q_ref, k_ref, v_ref, earlier_ref, filt_ref, f_ref, g_ref, gated_ref, filtered_ref):
    product = (k_ref[...].astype(F32) * v_ref[...].astype(F32)).astype(BF16)
    x = spectrum(f_ref, jnp.concatenate([earlier_ref[...], product], axis=0))
    h = tap_spectrum(f_ref, filt_ref[...], taps)
    xr, xi, hr, hi = x[:taps], x[taps:], h[:taps], h[taps:]
    filtered = back(g_ref, xr * hr - xi * hi, xr * hi + xi * hr)
    filtered_ref[...] = filtered
    gated_ref[...] = (q_ref[...].astype(F32) * filtered).astype(BF16)


def tap_grad_kernel(taps, k_ref, v_ref, earlier_ref, gf_ref, f_ref, g_ref, out_ref):
    product = (k_ref[...].astype(F32) * v_ref[...].astype(F32)).astype(BF16)
    x = spectrum(f_ref, jnp.concatenate([earlier_ref[...], product], axis=0))
    rows = gf_ref[...]
    g = mm(f_ref[0, :, :taps], rows) + mm(f_ref[1, :, :taps], rows)
    xr, xi, gr, gi = x[:taps], x[taps:], g[:taps], g[taps:]
    tap_rows = back(g_ref, xr * gr + xi * gi, xi * gr - xr * gi)
    out_ref[...] = tap_rows.T.astype(BF16)


def backward_kernel(taps, k_ref, v_ref, gf_ref, following_ref, filt_ref, f_ref, g_ref, gk_ref, gv_ref):
    g = spectrum(f_ref, jnp.concatenate([gf_ref[...], following_ref[...]], axis=0))
    h = tap_spectrum(f_ref, filt_ref[...], taps)
    gr, gi, hr, hi = g[:taps], g[taps:], h[:taps], h[taps:]
    grad_product = back(g_ref, hr * gr + hi * gi, hr * gi - hi * gr)
    gk_ref[...] = (grad_product * v_ref[...].astype(F32)).astype(BF16)
    gv_ref[...] = (grad_product * k_ref[...].astype(F32)).astype(BF16)


def estimate(micros):
    return pl.CostEstimate(flops=int(micros * 10**9), bytes_accessed=0, transcendentals=0)


def ignoring(body, count, skip):
    def kernel(*refs):
        return body(*refs[:skip], *refs[skip + count :])

    return kernel


def by_channel(kernel, arrays, kinds, outs, name, after=()):
    length, channels = arrays[0].shape
    width = min(512, channels)
    specs = {
        "t": pl.BlockSpec((length, width), lambda i: (0, i)),
        "c": pl.BlockSpec((width, length), lambda i: (i, 0)),
    }

    def spec_of(kind, shape):
        if kind == "w":
            return pl.BlockSpec(shape, lambda i: (0,) * len(shape))
        return specs[kind]

    return pl.pallas_call(
        ignoring(functools.partial(kernel, length), len(after), len(arrays)),
        grid=(channels // width,),
        in_specs=[spec_of(kind, a.shape) for kind, a in zip(kinds, arrays)]
        + [pl.BlockSpec(memory_space=pl.ANY)] * len(after),
        out_specs=[specs[kind] for kind, unused in outs],
        out_shape=[
            jax.ShapeDtypeStruct((length, channels) if kind == "t" else (channels, length), dtype)
            for kind, dtype in outs
        ],
        compiler_params=pltpu.CompilerParams(vmem_limit_bytes=VMEM_BYTES),
        cost_estimate=estimate(3),
        name=name,
    )(*arrays, *after)


def pass_kernel(with_mixed, with_grad, has_sum, last, me_ref, w_ref, *refs):
    refs = list(refs)
    step = pl.program_id(0)
    if with_mixed:
        gated_ref = refs.pop(0)
    if with_grad:
        cot_ref = refs.pop(0)
        sum_ref = refs.pop(0) if has_sum else None
        turned_ref = refs.pop()

        @pl.when(step == 0)
        def turn():
            turned_ref[...] = cot_ref[...].T

        total = mm(w_ref[...], turned_ref[...])
        if has_sum:
            total = total + sum_ref[...]
        if last:
            q_ref, filtered_ref, gq_ref, gf_ref = refs[:4]
            total = total.T
            gq_ref[...] = (total * filtered_ref[...]).astype(BF16)
            gf_ref[...] = (total * q_ref[...].astype(F32)).astype(BF16)
        else:
            refs[0][...] = total
    if with_mixed:
        held_ref, mixed_ref = refs.pop(), refs.pop()
        part = mm(gated_ref[...], w_ref[...])

        @pl.when(step == 0)
        def first():
            held_ref[...] = part

        @pl.when(step > 0)
        def more():
            held_ref[...] = held_ref[...] + part

        @pl.when(step == pl.num_programs(0) - 1)
        def give():
            mixed_ref[...] = held_ref[...].astype(mixed_ref.dtype)


def weight_pass(me, weight, off, gated=None, cot=None, sums=(), ends=(), after=()):
    length = (cot if gated is None else gated).shape[0]
    channels = weight.shape[0]
    tile = 512
    whole = pl.BlockSpec((length, channels), lambda r, me: (0, 0))
    by_token = pl.BlockSpec((length, tile), lambda r, me: (0, r))
    by_row = pl.BlockSpec((tile, length), lambda r, me: (r, 0))
    arrays, in_specs = [weight], [pl.BlockSpec((tile, channels), lambda r, me: (r, me[1] ^ off))]
    out_specs, out_shape, scratch = [], [], []
    if gated is not None:
        arrays.append(gated)
        in_specs.append(by_token)
    if cot is not None:
        arrays += [cot, *sums, *ends]
        in_specs += [whole] + [by_row] * len(sums) + [by_token] * len(ends)
        out_specs += [by_token] * 2 if ends else [by_row]
        out_shape += [jax.ShapeDtypeStruct((length, channels), BF16)] * 2 if ends else [
            jax.ShapeDtypeStruct((channels, length), F32)
        ]
    if gated is not None:
        out_specs.append(whole)
        out_shape.append(jax.ShapeDtypeStruct((length, channels), BF16 if off % 2 else F32))
        scratch.append(pltpu.VMEM((length, channels), F32))
    if cot is not None:
        scratch.append(pltpu.VMEM((channels, length), BF16))
    body = functools.partial(pass_kernel, gated is not None, cot is not None, bool(sums), bool(ends))
    return pl.pallas_call(
        ignoring(body, len(after), 1 + len(arrays)),
        grid_spec=pltpu.PrefetchScalarGridSpec(
            num_scalar_prefetch=1,
            grid=(channels // tile,),
            in_specs=in_specs + [pl.BlockSpec(memory_space=pl.ANY)] * len(after),
            out_specs=out_specs,
            scratch_shapes=scratch,
        ),
        out_shape=out_shape,
        compiler_params=pltpu.CompilerParams(vmem_limit_bytes=VMEM_BYTES),
        cost_estimate=estimate(3 if gated is None else 0.5),
        name="grad_gated_part" if gated is None else "mixed_part" if cot is None else "grads_and_mixed",
    )(me, *arrays, *after)


def pieces_kernel(per_chan, me_ref, slot_ref, *refs):
    out_ref = refs[-1]
    length, width = refs[0].shape
    span = width // per_chan
    count = len(refs) - 1
    piece = span // count
    rows = length * piece // width
    for off in range(count):
        for part in range(per_chan):
            target = (me_ref[1] ^ off) * per_chan + part
            start = pl.multiple_of(part * span + me_ref[1] * piece, 128)
            block = refs[off][:, pl.ds(start, piece)]
            place = pl.multiple_of(slot_ref[me_ref[0], target] * rows, rows)
            out_ref[pl.ds(place, rows), :] = jnp.concatenate(
                [block[at : at + rows] for at in range(0, length, rows)], axis=1
            )


def pieces_of(me, slots, cots, after):
    length, width = cots[0].shape
    n_ctx = slots.shape[0]
    piece = width // n_ctx
    if piece % 128:
        return pieces_by_slices(me, slots, cots)
    return pl.pallas_call(
        ignoring(functools.partial(pieces_kernel, n_ctx // len(cots)), len(after), 2 + len(cots)),
        grid_spec=pltpu.PrefetchScalarGridSpec(
            num_scalar_prefetch=2,
            grid=(1,),
            in_specs=[pl.BlockSpec((length, width), lambda i, *ids: (0, 0))] * len(cots)
            + [pl.BlockSpec(memory_space=pl.ANY)] * len(after),
            out_specs=pl.BlockSpec((length, width), lambda i, *ids: (0, 0)),
        ),
        out_shape=jax.ShapeDtypeStruct((length, width), BF16),
        compiler_params=pltpu.CompilerParams(vmem_limit_bytes=VMEM_BYTES),
        cost_estimate=estimate(0.5),
        name="pieces",
    )(me, slots, *cots, *after)


def pieces_by_slices(me, slots, cots):
    length, width = cots[0].shape
    n_ctx, count = slots.shape[0], len(cots)
    piece, per_chan = width // n_ctx, n_ctx // count
    rows = length * piece // width
    table = jnp.stack(cots).reshape(count, length, per_chan, count, piece)
    mine = lax.dynamic_index_in_dim(table, me[1], 3, False)
    parts = mine.transpose(0, 2, 1, 3).reshape(n_ctx, length // rows, rows, piece)
    parts = parts.transpose(0, 2, 1, 3).reshape(n_ctx, rows, width)
    order = jnp.argsort(slots[me[0]])
    return parts[(order // per_chan ^ me[1]) * per_chan + order % per_chan].reshape(length, width)


def weight_kernel(places, parts, me_ref, *refs):
    out_ref = refs[-1]
    length = sum(rows for unused, rows in places[0])
    blocks = []
    at = 0
    for place in places:
        for start, rows in place:
            blocks.append(refs[at][start : start + rows, :])
            at += 1
    columns = jnp.concatenate(blocks, axis=0)
    for part in range(parts):
        packed = jnp.concatenate([ref[...] for ref in refs[at + 2 * part : at + 2 * part + 2]], axis=0)
        rows = packed.shape[0] // len(places)
        piece = packed.shape[1] * rows // length
        wide = [
            packed[slot * rows : (slot + 1) * rows, lane : lane + piece]
            for slot in range(len(places))
            for lane in range(0, packed.shape[1], piece)
        ]
        total = mm(columns, jnp.concatenate(wide, axis=0), TN)
        place = pl.multiple_of((me_ref[1] ^ part) * piece, piece)
        out_ref[:, pl.ds(place, piece)] = total.astype(BF16)


def grad_weight_of(me, arrays, places, cots, earlier):
    channels = arrays[0].shape[1]
    slots, parts = len(places), len(cots)
    pieces = [array for pair in cots for array, unused in pair]
    half = cots[0][0][0].shape[0]
    tile = 256
    width = 2 * half * channels // (slots * sum(count for unused, count in places[0])) * parts
    steps = channels // tile // 2
    first = steps * len(earlier)
    count = 1 + len(arrays) + len(pieces)
    return pl.pallas_call(
        ignoring(functools.partial(weight_kernel, places, parts), len(earlier), count),
        grid_spec=pltpu.PrefetchScalarGridSpec(
            num_scalar_prefetch=1,
            grid=(steps,),
            in_specs=[pl.BlockSpec((array.shape[0], tile), lambda i, me: (0, first + i)) for array in arrays]
            + [pl.BlockSpec((half, channels), lambda i, me, at=at: (at, 0)) for pair in cots for unused, at in pair]
            + [pl.BlockSpec(memory_space=pl.ANY)] * len(earlier),
            out_specs=pl.BlockSpec((tile, width), lambda i, me: (first + i, 0)),
        ),
        out_shape=jax.ShapeDtypeStruct((channels, width), BF16),
        input_output_aliases={count: 0} if earlier else {},
        compiler_params=pltpu.CompilerParams(vmem_limit_bytes=VMEM_BYTES),
        cost_estimate=estimate(2),
        name="grad_weight",
    )(me, *arrays, *pieces, *earlier)


def narrow_grad_weight(me, arrays, places, cots):
    blocks, at = [], 0
    for place in places:
        for start, rows in place:
            blocks.append(arrays[at][start : start + rows])
            at += 1
    columns = jnp.concatenate(blocks, axis=0)
    length = columns.shape[0] // len(places)
    packed = jnp.stack([jnp.concatenate(pair, axis=0) for pair in cots])
    packed = packed[jnp.arange(len(cots), dtype=jnp.int32) ^ me[1]]
    parts, height, width = packed.shape
    rows = height // len(places)
    piece = rows * width // length
    wide = packed.reshape(parts, len(places), rows, length // rows, piece).transpose(1, 3, 2, 0, 4)
    return mm(columns, wide.reshape(columns.shape[0], parts * piece), TN).astype(BF16)


def cycle_of(count):
    across = 1 << ((count.bit_length() - 1) // 2)
    order = []
    for column in range(across):
        line = [row * across + column for row in range(count // across)]
        order += line if column % 2 == 0 else line[::-1]
    return order


def held_until(arrays, kernels):
    return lax.optimization_barrier((*arrays, *kernels))[: len(arrays)]


def swap(block, axis, bit):
    size = lax.axis_size(axis)
    return lax.ppermute(block, axis, [(i, i ^ bit) for i in range(size)])


def bits_of(size):
    return [1 << place for place in range(size.bit_length() - 1)]


def gather_of_chips(block):
    held = {0: block}
    for bit in reversed(bits_of(lax.axis_size("chan"))[1:]):
        held.update({off ^ bit: swap(held[off], "chan", bit) for off in list(held)})
    return held


def added_kernel(bit, me_ref, own_ref, came_ref, *outs):
    total = (own_ref[...].astype(F32) + came_ref[...].astype(F32)).astype(BF16)
    if not bit:
        outs[0][...] = total
        return
    rows = outs[0].shape[0]
    mine = (me_ref[0] & bit) != 0
    outs[0][...] = jnp.where(mine, total[rows:], total[:rows])
    outs[1][...] = jnp.where(mine, total[:rows], total[rows:])


def added(me, own, came, bit, after):
    shape = (own.shape[0] // 2, own.shape[1]) if bit else own.shape
    whole = pl.BlockSpec(own.shape, lambda i, me: (0, 0))
    outs = 2 if bit else 1
    return pl.pallas_call(
        ignoring(functools.partial(added_kernel, bit), len(after), 3),
        grid_spec=pltpu.PrefetchScalarGridSpec(
            num_scalar_prefetch=1,
            grid=(1,),
            in_specs=[whole, whole] + [pl.BlockSpec(memory_space=pl.ANY)] * len(after),
            out_specs=[pl.BlockSpec(shape, lambda i, me: (0, 0))] * outs,
        ),
        out_shape=[jax.ShapeDtypeStruct(shape, BF16)] * outs,
        compiler_params=pltpu.CompilerParams(vmem_limit_bytes=VMEM_BYTES),
        cost_estimate=estimate(0.5),
        name="added",
    )(me, own, came, *after)


def split(me, block, bit):
    rows = block.shape[0] // 2
    mine = (me[0] & bit) != 0
    low, high = block[:rows], block[rows:]
    return jnp.where(mine, high, low), jnp.where(mine, low, high)


class Sum:
    def __init__(self, me, partial):
        self.me = me
        self.bits = bits_of(lax.axis_size("ctx"))
        self.step = 0
        self.sums, self.send = split(me, partial, self.bits[0])

    def add(self, after):
        if self.step == len(self.bits):
            return []
        came = swap(self.send if self.step < 2 else self.sums, "ctx", self.bits[self.step])
        self.sums, *send = added(self.me, self.sums, came, 0 if self.step else self.bits[1], after)
        self.send = send[0] if send else None
        self.step += 1
        return [self.sums]


def joined_kernel(bit, me_ref, own_ref, other_ref, out_ref):
    rows = own_ref.shape[0]
    mine = (me_ref[0] & bit) != 0
    out_ref[:rows] = jnp.where(mine, other_ref[...], own_ref[...]).astype(out_ref.dtype)
    out_ref[rows:] = jnp.where(mine, own_ref[...], other_ref[...]).astype(out_ref.dtype)


def joined(me, own, other, bit, dtype, after):
    rows, width = own.shape
    whole = pl.BlockSpec(own.shape, lambda i, me: (0, 0))
    return pl.pallas_call(
        ignoring(functools.partial(joined_kernel, bit), len(after), 3),
        grid_spec=pltpu.PrefetchScalarGridSpec(
            num_scalar_prefetch=1,
            grid=(1,),
            in_specs=[whole, whole] + [pl.BlockSpec(memory_space=pl.ANY)] * len(after),
            out_specs=pl.BlockSpec((2 * rows, width), lambda i, me: (0, 0)),
        ),
        out_shape=jax.ShapeDtypeStruct((2 * rows, width), dtype),
        compiler_params=pltpu.CompilerParams(vmem_limit_bytes=VMEM_BYTES),
        cost_estimate=estimate(0.5),
        name="joined",
    )(me, own, other, *after)


def per_device(query_proj, key_proj, value_proj, filters, out_weight, cotangent):
    length, channels = query_proj.shape
    taps = filters.shape[1]
    n_ctx, n_chan = lax.axis_size("ctx"), lax.axis_size("chan")
    me = jnp.stack([lax.axis_index("ctx"), lax.axis_index("chan")]).astype(jnp.int32)
    forward, late, early_rows, lags = [jnp.asarray(m) for m in transforms(taps)]

    product = (key_proj.astype(F32) * value_proj.astype(F32)).astype(BF16)
    product, cotangent = lax.optimization_barrier((product, cotangent))
    earlier = lax.ppermute(product, "ctx", [(i, i + 1) for i in range(n_ctx - 1)])

    cots = {0: cotangent, 1: swap(cotangent, "chan", 1)}
    for bit in reversed(bits_of(n_chan)[1:]):
        cots.update({off ^ bit: swap(cots[off], "chan", bit) for off in list(cots) if off % 2 == 0})
    offs = sorted(off for off in cots if off % 2 == 0 and off)
    sums = weight_pass(me, out_weight, 0, cot=cots[0])
    for off in offs:
        cots[off + 1] = swap(held_until([cots[off]], sums)[0], "chan", 1)
    offs = sorted(offs + [off + 1 for off in offs])

    sums = weight_pass(me, out_weight, 1, cot=cots[1], sums=sums)

    order = cycle_of(n_ctx)
    slots = []
    for c in range(n_ctx):
        spot = order.index(c)
        turn = [0, n_ctx // 2] + list(range(1, n_ctx // 2)) + list(range(1 - n_ctx // 2, 0))
        targets = [order[(spot + step) % n_ctx] for step in turn]
        slots.append([targets.index(target) for target in range(n_ctx)])
    pieces = pieces_of(me, jnp.asarray(slots, jnp.int32), [cots[off] for off in range(n_chan)], sums)

    gated, filtered = by_channel(
        forward_kernel,
        [query_proj, key_proj, value_proj, earlier, filters, forward, late],
        "ttttcww",
        [("t", BF16), ("t", F32)],
        "forward_filter",
        after=sums,
    )

    ahead = [(order[i], order[(i + 1) % n_ctx]) for i in range(n_ctx)]
    behind = [(b, a) for a, b in ahead]
    turns = n_ctx // 2
    rows, piece = length // n_ctx, channels // n_ctx
    span = (turns - 1) * rows
    ends = [
        jnp.concatenate([pieces[2 * rows : 2 * rows + span], gated], axis=0),
        jnp.concatenate([gated, pieces[2 * rows + span :]], axis=0),
    ]
    arrays, places, brought = [gated], [[(0, length)]], [pieces[:rows]]

    def passed_on(kernels):
        onto, back = held_until(ends, kernels)
        came = [lax.ppermute(onto, "ctx", ahead), lax.ppermute(back, "ctx", behind)]
        arrays.extend(came)
        places.extend([[(came[0].shape[0] - length, length)], [(0, length)]])
        brought.extend([came[0][:rows], came[1][-rows:]])
        ends[:] = [came[0][rows:], came[1][:-rows]]
        return came

    landed = passed_on([])
    across = lax.ppermute(
        held_until([pieces[rows : 2 * rows]], [gated])[0],
        "ctx",
        [(order[i], order[(i + turns) % n_ctx]) for i in range(n_ctx)],
    )
    brought.insert(1, across)

    terms = {}
    for off in offs[:-1]:
        *sums, terms[off] = weight_pass(me, out_weight, off, gated, cots[off], sums)
    grad_query, grad_filtered, terms[offs[-1]] = weight_pass(
        me, out_weight, offs[-1], gated, cots[offs[-1]], sums, [query_proj, filtered]
    )
    previous, landed = landed, passed_on([grad_filtered])

    following = lax.ppermute(grad_filtered, "ctx", [(i + 1, i) for i in range(n_ctx - 1)])
    tap_grad = by_channel(
        tap_grad_kernel,
        [key_proj, value_proj, earlier, grad_filtered, forward, lags],
        "ttttww",
        [("c", BF16)],
        "tap_grad",
        after=previous,
    )[0]
    from_core = []
    for off in [off for off in sorted(terms) if off % 2]:
        from_core.append(swap(terms.pop(off), "chan", 1))
        terms[off ^ 1] = terms[off ^ 1] + from_core[-1].astype(F32)
    mixed_one = weight_pass(me, out_weight, 1, gated, after=[tap_grad])[0]
    last_part = weight_pass(me, out_weight, 0, gated, after=[mixed_one])[0]
    tap_sum = Sum(me, held_until([tap_grad], [mixed_one])[0])
    previous, landed = landed, passed_on([last_part] + tap_sum.add(()))

    grad_key, grad_value = by_channel(
        backward_kernel,
        [key_proj, value_proj, grad_filtered, following, filters, forward, early_rows],
        "ttttcww",
        [("t", BF16), ("t", BF16)],
        "backward_filter",
        after=previous + from_core,
    )
    terms = dict(zip(terms, held_until(terms.values(), previous)))
    terms[0] = last_part + swap(mixed_one, "chan", 1).astype(F32)
    for bit in bits_of(n_chan)[1:]:
        for off in [off for off in sorted(terms, reverse=True) if off & bit]:
            terms[off ^ bit] = terms[off ^ bit] + swap(terms.pop(off).astype(BF16), "chan", bit).astype(F32)
    mixed = terms[0].astype(BF16)
    early = 2 + 2 * min(1, turns - 1)
    first = jnp.concatenate(held_until(brought[:early], previous), axis=0)

    for unused in range(turns - 4):
        landed = passed_on([grad_key])
    half = length // 2
    onto, back = held_until(ends, [following] + tap_sum.add(()))
    far = [lax.ppermute(onto[:half], "ctx", ahead), lax.ppermute(back[half:], "ctx", behind)]
    arrays = arrays[:1] + far + arrays[1:]
    places.insert(1, [(0, half), (0, half)])

    cols = [gather_of_chips(part) for part in (first, jnp.concatenate(brought[early:], axis=0))]

    while tap_sum.add(far):
        pass
    own, bits = tap_sum.sums, tap_sum.bits
    other = swap(own, "ctx", bits[1])

    evens = [off for off in range(n_chan) if off % 2 == 0]
    wide = piece % 128 == 0 and 2 * early == n_ctx
    columns = {off: [(part[off], 0) for part in cols] for off in evens}
    crossed = jnp.concatenate([part[off] for off in evens for part in cols], axis=0)
    crossed = swap(held_until([crossed], far)[0], "chan", 1)
    if wide:
        for at, off in enumerate(evens):
            columns[off + 1] = [(crossed, 2 * at), (crossed, 2 * at + 1)]
        columns = [columns[off] for off in range(n_chan)]
        low_half = grad_weight_of(me, arrays, places, columns, [])
        grad_weight = grad_weight_of(me, arrays, places, columns, [low_half])
    else:
        for at, off in enumerate(evens):
            columns[off + 1] = [(crossed[at * length : (at + 1) * length], 0)]
        pairs = [[array for array, unused in columns[off]] for off in range(n_chan)]
        low_half = grad_weight = narrow_grad_weight(me, arrays, places, pairs)
    own = joined(me, own, held_until([other], [low_half])[0], bits[1], BF16, ())
    other = swap(own, "ctx", bits[0])
    grad_filters = joined(me, own, held_until([other], [grad_weight])[0], bits[0], F32, ())
    return (mixed, grad_query, grad_key, grad_value, grad_filters, grad_weight)


def solution(mesh):
    placed = (
        P("ctx", "chan"),
        P("ctx", "chan"),
        P("ctx", "chan"),
        P("chan", None),
        P("chan", None),
        P("ctx", "chan"),
    )
    return jax.shard_map(
        per_device,
        mesh=mesh,
        in_specs=placed,
        out_specs=(
            P("ctx", "chan"),
            P("ctx", "chan"),
            P("ctx", "chan"),
            P("ctx", "chan"),
            P("chan", None),
            P("chan", "ctx"),
        ),
        check_vma=False,
    )
```

```python
import functools

import jax
import jax.numpy as jnp
import numpy as np
from jax import lax
from jax.experimental import pallas as pl
from jax.experimental.pallas import tpu as pltpu
from jax.sharding import PartitionSpec as P

F32 = jnp.float32
BF16 = jnp.bfloat16
VMEM_BYTES = 40 * 2**20
NT = (((1,), (1,)), ((), ()))
TN = (((0,), (0,)), ((), ()))


def halves(matrix):
    high = matrix.astype(BF16)
    low = (matrix - high.astype(np.float64)).astype(BF16)
    return np.stack([high, low])


def transforms(taps):
    points = 2 * taps
    angle = np.pi * (2 * np.arange(taps)[:, None] + 1) * np.arange(points)[None, :] / points
    forward = np.concatenate([np.cos(angle), -np.sin(angle)], axis=0)
    inverse = forward.T * (2.0 / points)
    late = inverse[taps:]
    early = inverse[:taps]
    lags = inverse[taps - np.arange(taps)]
    return halves(forward), halves(late), halves(early), halves(lags)


def mm(a, b, dims=(((1,), (0,)), ((), ()))):
    return lax.dot_general(a, b, dims, preferred_element_type=F32)


def spectrum(f_ref, rows):
    return mm(f_ref[0], rows) + mm(f_ref[1], rows)


def tap_spectrum(f_ref, filters, taps):
    return mm(f_ref[0, :, :taps], filters, NT) + mm(f_ref[1, :, :taps], filters, NT)


def back(g_ref, real, imag):
    both = jnp.concatenate([real, imag], axis=0)
    high = both.astype(BF16)
    low = (both - high.astype(F32)).astype(BF16)
    return mm(g_ref[0], high) + mm(g_ref[0], low) + mm(g_ref[1], high)


def forward_kernel(taps, q_ref, k_ref, v_ref, earlier_ref, filt_ref, f_ref, g_ref, gated_ref, filtered_ref):
    product = (k_ref[...].astype(F32) * v_ref[...].astype(F32)).astype(BF16)
    x = spectrum(f_ref, jnp.concatenate([earlier_ref[...], product], axis=0))
    h = tap_spectrum(f_ref, filt_ref[...], taps)
    xr, xi, hr, hi = x[:taps], x[taps:], h[:taps], h[taps:]
    filtered = back(g_ref, xr * hr - xi * hi, xr * hi + xi * hr)
    filtered_ref[...] = filtered
    gated_ref[...] = (q_ref[...].astype(F32) * filtered).astype(BF16)


def tap_grad_kernel(taps, k_ref, v_ref, earlier_ref, gf_ref, f_ref, g_ref, out_ref):
    product = (k_ref[...].astype(F32) * v_ref[...].astype(F32)).astype(BF16)
    x = spectrum(f_ref, jnp.concatenate([earlier_ref[...], product], axis=0))
    rows = gf_ref[...]
    g = mm(f_ref[0, :, :taps], rows) + mm(f_ref[1, :, :taps], rows)
    xr, xi, gr, gi = x[:taps], x[taps:], g[:taps], g[taps:]
    tap_rows = back(g_ref, xr * gr + xi * gi, xi * gr - xr * gi)
    out_ref[...] = tap_rows.T.astype(BF16)


def backward_kernel(taps, k_ref, v_ref, gf_ref, following_ref, filt_ref, f_ref, g_ref, gk_ref, gv_ref):
    g = spectrum(f_ref, jnp.concatenate([gf_ref[...], following_ref[...]], axis=0))
    h = tap_spectrum(f_ref, filt_ref[...], taps)
    gr, gi, hr, hi = g[:taps], g[taps:], h[:taps], h[taps:]
    grad_product = back(g_ref, hr * gr + hi * gi, hr * gi - hi * gr)
    gk_ref[...] = (grad_product * v_ref[...].astype(F32)).astype(BF16)
    gv_ref[...] = (grad_product * k_ref[...].astype(F32)).astype(BF16)


def estimate(micros):
    return pl.CostEstimate(flops=int(micros * 10**9), bytes_accessed=0, transcendentals=0)


def ignoring(body, count, skip):
    def kernel(*refs):
        return body(*refs[:skip], *refs[skip + count :])

    return kernel


def by_channel(kernel, arrays, kinds, outs, name, after=()):
    length, channels = arrays[0].shape
    width = min(512, channels)
    specs = {
        "t": pl.BlockSpec((length, width), lambda i: (0, i)),
        "c": pl.BlockSpec((width, length), lambda i: (i, 0)),
    }

    def spec_of(kind, shape):
        if kind == "w":
            return pl.BlockSpec(shape, lambda i: (0,) * len(shape))
        return specs[kind]

    return pl.pallas_call(
        ignoring(functools.partial(kernel, length), len(after), len(arrays)),
        grid=(channels // width,),
        in_specs=[spec_of(kind, a.shape) for kind, a in zip(kinds, arrays)]
        + [pl.BlockSpec(memory_space=pl.ANY)] * len(after),
        out_specs=[specs[kind] for kind, unused in outs],
        out_shape=[
            jax.ShapeDtypeStruct((length, channels) if kind == "t" else (channels, length), dtype)
            for kind, dtype in outs
        ],
        compiler_params=pltpu.CompilerParams(vmem_limit_bytes=VMEM_BYTES),
        cost_estimate=estimate(3),
        name=name,
    )(*arrays, *after)


def pass_kernel(with_mixed, with_grad, has_sum, last, me_ref, w_ref, *refs):
    refs = list(refs)
    step = pl.program_id(0)
    if with_mixed:
        gated_ref = refs.pop(0)
    if with_grad:
        cot_ref = refs.pop(0)
        sum_ref = refs.pop(0) if has_sum else None
        turned_ref = refs.pop()

        @pl.when(step == 0)
        def turn():
            turned_ref[...] = cot_ref[...].T

        total = mm(w_ref[...], turned_ref[...])
        if has_sum:
            total = total + sum_ref[...]
        if last:
            q_ref, filtered_ref, gq_ref, gf_ref = refs[:4]
            total = total.T
            gq_ref[...] = (total * filtered_ref[...]).astype(BF16)
            gf_ref[...] = (total * q_ref[...].astype(F32)).astype(BF16)
        else:
            refs[0][...] = total
    if with_mixed:
        held_ref, mixed_ref = refs.pop(), refs.pop()
        part = mm(gated_ref[...], w_ref[...])

        @pl.when(step == 0)
        def first():
            held_ref[...] = part

        @pl.when(step > 0)
        def more():
            held_ref[...] = held_ref[...] + part

        @pl.when(step == pl.num_programs(0) - 1)
        def give():
            mixed_ref[...] = held_ref[...].astype(mixed_ref.dtype)


def weight_pass(me, weight, off, gated=None, cot=None, sums=(), ends=(), after=()):
    length = (cot if gated is None else gated).shape[0]
    channels = weight.shape[0]
    tile = 512
    whole = pl.BlockSpec((length, channels), lambda r, me: (0, 0))
    by_token = pl.BlockSpec((length, tile), lambda r, me: (0, r))
    by_row = pl.BlockSpec((tile, length), lambda r, me: (r, 0))
    arrays, in_specs = [weight], [pl.BlockSpec((tile, channels), lambda r, me: (r, me[1] ^ off))]
    out_specs, out_shape, scratch = [], [], []
    if gated is not None:
        arrays.append(gated)
        in_specs.append(by_token)
    if cot is not None:
        arrays += [cot, *sums, *ends]
        in_specs += [whole] + [by_row] * len(sums) + [by_token] * len(ends)
        out_specs += [by_token] * 2 if ends else [by_row]
        out_shape += [jax.ShapeDtypeStruct((length, channels), BF16)] * 2 if ends else [
            jax.ShapeDtypeStruct((channels, length), F32)
        ]
    if gated is not None:
        out_specs.append(whole)
        out_shape.append(jax.ShapeDtypeStruct((length, channels), BF16 if off % 2 else F32))
        scratch.append(pltpu.VMEM((length, channels), F32))
    if cot is not None:
        scratch.append(pltpu.VMEM((channels, length), BF16))
    body = functools.partial(pass_kernel, gated is not None, cot is not None, bool(sums), bool(ends))
    return pl.pallas_call(
        ignoring(body, len(after), 1 + len(arrays)),
        grid_spec=pltpu.PrefetchScalarGridSpec(
            num_scalar_prefetch=1,
            grid=(channels // tile,),
            in_specs=in_specs + [pl.BlockSpec(memory_space=pl.ANY)] * len(after),
            out_specs=out_specs,
            scratch_shapes=scratch,
        ),
        out_shape=out_shape,
        compiler_params=pltpu.CompilerParams(vmem_limit_bytes=VMEM_BYTES),
        cost_estimate=estimate(3 if gated is None else 0.5),
        name="grad_gated_part" if gated is None else "mixed_part" if cot is None else "grads_and_mixed",
    )(me, *arrays, *after)


def pieces_kernel(per_chan, me_ref, slot_ref, *refs):
    out_ref = refs[-1]
    length, width = refs[0].shape
    span = width // per_chan
    count = len(refs) - 1
    piece = span // count
    rows = length * piece // width
    for off in range(count):
        for part in range(per_chan):
            target = (me_ref[1] ^ off) * per_chan + part
            start = pl.multiple_of(part * span + me_ref[1] * piece, 128)
            block = refs[off][:, pl.ds(start, piece)]
            place = pl.multiple_of(slot_ref[me_ref[0], target] * rows, rows)
            out_ref[pl.ds(place, rows), :] = jnp.concatenate(
                [block[at : at + rows] for at in range(0, length, rows)], axis=1
            )


def pieces_of(me, slots, cots, after):
    length, width = cots[0].shape
    n_ctx = slots.shape[0]
    piece = width // n_ctx
    if piece % 128:
        return pieces_by_slices(me, slots, cots)
    return pl.pallas_call(
        ignoring(functools.partial(pieces_kernel, n_ctx // len(cots)), len(after), 2 + len(cots)),
        grid_spec=pltpu.PrefetchScalarGridSpec(
            num_scalar_prefetch=2,
            grid=(1,),
            in_specs=[pl.BlockSpec((length, width), lambda i, *ids: (0, 0))] * len(cots)
            + [pl.BlockSpec(memory_space=pl.ANY)] * len(after),
            out_specs=pl.BlockSpec((length, width), lambda i, *ids: (0, 0)),
        ),
        out_shape=jax.ShapeDtypeStruct((length, width), BF16),
        compiler_params=pltpu.CompilerParams(vmem_limit_bytes=VMEM_BYTES),
        cost_estimate=estimate(0.5),
        name="pieces",
    )(me, slots, *cots, *after)


def pieces_by_slices(me, slots, cots):
    length, width = cots[0].shape
    n_ctx, count = slots.shape[0], len(cots)
    piece, per_chan = width // n_ctx, n_ctx // count
    rows = length * piece // width
    table = jnp.stack(cots).reshape(count, length, per_chan, count, piece)
    mine = lax.dynamic_index_in_dim(table, me[1], 3, False)
    parts = mine.transpose(0, 2, 1, 3).reshape(n_ctx, length // rows, rows, piece)
    parts = parts.transpose(0, 2, 1, 3).reshape(n_ctx, rows, width)
    order = jnp.argsort(slots[me[0]])
    return parts[(order // per_chan ^ me[1]) * per_chan + order % per_chan].reshape(length, width)


def weight_kernel(places, parts, me_ref, *refs):
    out_ref = refs[-1]
    length = sum(rows for unused, rows in places[0])
    blocks = []
    at = 0
    for place in places:
        for start, rows in place:
            blocks.append(refs[at][start : start + rows, :])
            at += 1
    columns = jnp.concatenate(blocks, axis=0)
    for part in range(parts):
        packed = jnp.concatenate([ref[...] for ref in refs[at + 2 * part : at + 2 * part + 2]], axis=0)
        rows = packed.shape[0] // len(places)
        piece = packed.shape[1] * rows // length
        wide = [
            packed[slot * rows : (slot + 1) * rows, lane : lane + piece]
            for slot in range(len(places))
            for lane in range(0, packed.shape[1], piece)
        ]
        total = mm(columns, jnp.concatenate(wide, axis=0), TN)
        place = pl.multiple_of((me_ref[1] ^ part) * piece, piece)
        out_ref[:, pl.ds(place, piece)] = total.astype(BF16)


def grad_weight_of(me, arrays, places, cots, earlier):
    channels = arrays[0].shape[1]
    slots, parts = len(places), len(cots)
    pieces = [array for pair in cots for array, unused in pair]
    half = cots[0][0][0].shape[0]
    tile = 256
    width = 2 * half * channels // (slots * sum(count for unused, count in places[0])) * parts
    steps = channels // tile // 2
    first = steps * len(earlier)
    count = 1 + len(arrays) + len(pieces)
    return pl.pallas_call(
        ignoring(functools.partial(weight_kernel, places, parts), len(earlier), count),
        grid_spec=pltpu.PrefetchScalarGridSpec(
            num_scalar_prefetch=1,
            grid=(steps,),
            in_specs=[pl.BlockSpec((array.shape[0], tile), lambda i, me: (0, first + i)) for array in arrays]
            + [pl.BlockSpec((half, channels), lambda i, me, at=at: (at, 0)) for pair in cots for unused, at in pair]
            + [pl.BlockSpec(memory_space=pl.ANY)] * len(earlier),
            out_specs=pl.BlockSpec((tile, width), lambda i, me: (first + i, 0)),
        ),
        out_shape=jax.ShapeDtypeStruct((channels, width), BF16),
        input_output_aliases={count: 0} if earlier else {},
        compiler_params=pltpu.CompilerParams(vmem_limit_bytes=VMEM_BYTES),
        cost_estimate=estimate(2),
        name="grad_weight",
    )(me, *arrays, *pieces, *earlier)


def narrow_grad_weight(me, arrays, places, cots):
    blocks, at = [], 0
    for place in places:
        for start, rows in place:
            blocks.append(arrays[at][start : start + rows])
            at += 1
    columns = jnp.concatenate(blocks, axis=0)
    length = columns.shape[0] // len(places)
    packed = jnp.stack([jnp.concatenate(pair, axis=0) for pair in cots])
    packed = packed[jnp.arange(len(cots), dtype=jnp.int32) ^ me[1]]
    parts, height, width = packed.shape
    rows = height // len(places)
    piece = rows * width // length
    wide = packed.reshape(parts, len(places), rows, length // rows, piece).transpose(1, 3, 2, 0, 4)
    return mm(columns, wide.reshape(columns.shape[0], parts * piece), TN).astype(BF16)


def cycle_of(count):
    across = 1 << ((count.bit_length() - 1) // 2)
    order = []
    for column in range(across):
        line = [row * across + column for row in range(count // across)]
        order += line if column % 2 == 0 else line[::-1]
    return order


def held_until(arrays, kernels):
    return lax.optimization_barrier((*arrays, *kernels))[: len(arrays)]


def swap(block, axis, bit):
    size = lax.axis_size(axis)
    return lax.ppermute(block, axis, [(i, i ^ bit) for i in range(size)])


def bits_of(size):
    return [1 << place for place in range(size.bit_length() - 1)]


def gather_of_chips(block):
    held = {0: block}
    for bit in reversed(bits_of(lax.axis_size("chan"))[1:]):
        held.update({off ^ bit: swap(held[off], "chan", bit) for off in list(held)})
    return held


def added_kernel(bit, me_ref, own_ref, came_ref, *outs):
    total = (own_ref[...].astype(F32) + came_ref[...].astype(F32)).astype(BF16)
    if not bit:
        outs[0][...] = total
        return
    rows = outs[0].shape[0]
    mine = (me_ref[0] & bit) != 0
    outs[0][...] = jnp.where(mine, total[rows:], total[:rows])
    outs[1][...] = jnp.where(mine, total[:rows], total[rows:])


def added(me, own, came, bit, after):
    shape = (own.shape[0] // 2, own.shape[1]) if bit else own.shape
    whole = pl.BlockSpec(own.shape, lambda i, me: (0, 0))
    outs = 2 if bit else 1
    return pl.pallas_call(
        ignoring(functools.partial(added_kernel, bit), len(after), 3),
        grid_spec=pltpu.PrefetchScalarGridSpec(
            num_scalar_prefetch=1,
            grid=(1,),
            in_specs=[whole, whole] + [pl.BlockSpec(memory_space=pl.ANY)] * len(after),
            out_specs=[pl.BlockSpec(shape, lambda i, me: (0, 0))] * outs,
        ),
        out_shape=[jax.ShapeDtypeStruct(shape, BF16)] * outs,
        compiler_params=pltpu.CompilerParams(vmem_limit_bytes=VMEM_BYTES),
        cost_estimate=estimate(0.5),
        name="added",
    )(me, own, came, *after)


def split(me, block, bit):
    rows = block.shape[0] // 2
    mine = (me[0] & bit) != 0
    low, high = block[:rows], block[rows:]
    return jnp.where(mine, high, low), jnp.where(mine, low, high)


class Sum:
    def __init__(self, me, partial):
        self.me = me
        self.bits = bits_of(lax.axis_size("ctx"))
        self.step = 0
        self.sums, self.send = split(me, partial, self.bits[0])

    def add(self, after):
        if self.step == len(self.bits):
            return []
        came = swap(self.send if self.step < 2 else self.sums, "ctx", self.bits[self.step])
        self.sums, *send = added(self.me, self.sums, came, 0 if self.step else self.bits[1], after)
        self.send = send[0] if send else None
        self.step += 1
        return [self.sums]


def joined_kernel(bit, me_ref, own_ref, other_ref, out_ref):
    rows = own_ref.shape[0]
    mine = (me_ref[0] & bit) != 0
    out_ref[:rows] = jnp.where(mine, other_ref[...], own_ref[...]).astype(out_ref.dtype)
    out_ref[rows:] = jnp.where(mine, own_ref[...], other_ref[...]).astype(out_ref.dtype)


def joined(me, own, other, bit, dtype, after):
    rows, width = own.shape
    whole = pl.BlockSpec(own.shape, lambda i, me: (0, 0))
    return pl.pallas_call(
        ignoring(functools.partial(joined_kernel, bit), len(after), 3),
        grid_spec=pltpu.PrefetchScalarGridSpec(
            num_scalar_prefetch=1,
            grid=(1,),
            in_specs=[whole, whole] + [pl.BlockSpec(memory_space=pl.ANY)] * len(after),
            out_specs=pl.BlockSpec((2 * rows, width), lambda i, me: (0, 0)),
        ),
        out_shape=jax.ShapeDtypeStruct((2 * rows, width), dtype),
        compiler_params=pltpu.CompilerParams(vmem_limit_bytes=VMEM_BYTES),
        cost_estimate=estimate(0.5),
        name="joined",
    )(me, own, other, *after)


def per_device(query_proj, key_proj, value_proj, filters, out_weight, cotangent):
    length, channels = query_proj.shape
    taps = filters.shape[1]
    n_ctx, n_chan = lax.axis_size("ctx"), lax.axis_size("chan")
    me = jnp.stack([lax.axis_index("ctx"), lax.axis_index("chan")]).astype(jnp.int32)
    forward, late, early_rows, lags = [jnp.asarray(m) for m in transforms(taps)]

    product = (key_proj.astype(F32) * value_proj.astype(F32)).astype(BF16)
    product, cotangent = lax.optimization_barrier((product, cotangent))
    earlier = lax.ppermute(product, "ctx", [(i, i + 1) for i in range(n_ctx - 1)])

    cots = {0: cotangent, 1: swap(cotangent, "chan", 1)}
    for bit in reversed(bits_of(n_chan)[1:]):
        cots.update({off ^ bit: swap(cots[off], "chan", bit) for off in list(cots) if off % 2 == 0})
    offs = sorted(off for off in cots if off % 2 == 0 and off)
    sums = weight_pass(me, out_weight, 0, cot=cots[0])
    for off in offs:
        cots[off + 1] = swap(held_until([cots[off]], sums)[0], "chan", 1)
    offs = sorted(offs + [off + 1 for off in offs])

    sums = weight_pass(me, out_weight, 1, cot=cots[1], sums=sums)

    order = cycle_of(n_ctx)
    slots = []
    for c in range(n_ctx):
        spot = order.index(c)
        turn = [0, n_ctx // 2] + list(range(1, n_ctx // 2)) + list(range(1 - n_ctx // 2, 0))
        targets = [order[(spot + step) % n_ctx] for step in turn]
        slots.append([targets.index(target) for target in range(n_ctx)])
    pieces = pieces_of(me, jnp.asarray(slots, jnp.int32), [cots[off] for off in range(n_chan)], sums)

    gated, filtered = by_channel(
        forward_kernel,
        [query_proj, key_proj, value_proj, earlier, filters, forward, late],
        "ttttcww",
        [("t", BF16), ("t", F32)],
        "forward_filter",
        after=sums,
    )

    ahead = [(order[i], order[(i + 1) % n_ctx]) for i in range(n_ctx)]
    behind = [(b, a) for a, b in ahead]
    turns = n_ctx // 2
    rows, piece = length // n_ctx, channels // n_ctx
    span = (turns - 1) * rows
    ends = [
        jnp.concatenate([pieces[2 * rows : 2 * rows + span], gated], axis=0),
        jnp.concatenate([gated, pieces[2 * rows + span :]], axis=0),
    ]
    arrays, places, brought = [gated], [[(0, length)]], [pieces[:rows]]

    def passed_on(kernels):
        onto, back = held_until(ends, kernels)
        came = [lax.ppermute(onto, "ctx", ahead), lax.ppermute(back, "ctx", behind)]
        arrays.extend(came)
        places.extend([[(came[0].shape[0] - length, length)], [(0, length)]])
        brought.extend([came[0][:rows], came[1][-rows:]])
        ends[:] = [came[0][rows:], came[1][:-rows]]
        return came

    landed = passed_on([])
    across = lax.ppermute(
        held_until([pieces[rows : 2 * rows]], [gated])[0],
        "ctx",
        [(order[i], order[(i + turns) % n_ctx]) for i in range(n_ctx)],
    )
    brought.insert(1, across)

    terms = {}
    for off in offs[:-1]:
        *sums, terms[off] = weight_pass(me, out_weight, off, gated, cots[off], sums)
    grad_query, grad_filtered, terms[offs[-1]] = weight_pass(
        me, out_weight, offs[-1], gated, cots[offs[-1]], sums, [query_proj, filtered]
    )
    previous, landed = landed, passed_on([grad_filtered])

    tap_grad = by_channel(
        tap_grad_kernel,
        [key_proj, value_proj, earlier, grad_filtered, forward, lags],
        "ttttww",
        [("c", BF16)],
        "tap_grad",
        after=previous,
    )[0]
    from_core = []
    for off in [off for off in sorted(terms) if off % 2]:
        from_core.append(swap(terms.pop(off), "chan", 1))
        terms[off ^ 1] = terms[off ^ 1] + from_core[-1].astype(F32)
    mixed_one = weight_pass(me, out_weight, 1, gated, after=[tap_grad])[0]
    last_part = weight_pass(me, out_weight, 0, gated, after=[mixed_one])[0]
    previous, landed = landed, passed_on([last_part])

    terms = dict(zip(terms, held_until(terms.values(), previous)))
    terms[0] = last_part + swap(mixed_one, "chan", 1).astype(F32)
    for bit in bits_of(n_chan)[1:]:
        for off in [off for off in sorted(terms, reverse=True) if off & bit]:
            terms[off ^ bit] = terms[off ^ bit] + swap(terms.pop(off).astype(BF16), "chan", bit).astype(F32)
    mixed = terms[0].astype(BF16)
    early = 2 + 2 * min(1, turns - 1)
    first = jnp.concatenate(held_until(brought[:early], previous), axis=0)

    for unused in range(turns - 4):
        landed = passed_on([last_part])
    half = length // 2
    tap_sum = Sum(me, held_until([tap_grad], previous)[0])
    onto, back = held_until(ends, tap_sum.add(()))
    far = [lax.ppermute(onto[:half], "ctx", ahead), lax.ppermute(back[half:], "ctx", behind)]
    arrays = arrays[:1] + far + arrays[1:]
    places.insert(1, [(0, half), (0, half)])

    cols = [gather_of_chips(part) for part in (first, jnp.concatenate(brought[early:], axis=0))]

    given = held_until([grad_filtered], far)[0]
    following = lax.ppermute(given, "ctx", [(i + 1, i) for i in range(n_ctx - 1)])
    grad_key, grad_value = by_channel(
        backward_kernel,
        [key_proj, value_proj, grad_filtered, following, filters, forward, early_rows],
        "ttttcww",
        [("t", BF16), ("t", BF16)],
        "backward_filter",
    )

    while tap_sum.add(far):
        pass
    own, bits = tap_sum.sums, tap_sum.bits
    other = swap(own, "ctx", bits[1])

    evens = [off for off in range(n_chan) if off % 2 == 0]
    wide = piece % 128 == 0 and 2 * early == n_ctx
    columns = {off: [(part[off], 0) for part in cols] for off in evens}
    crossed = jnp.concatenate([part[off] for off in evens for part in cols], axis=0)
    crossed = swap(held_until([crossed], far)[0], "chan", 1)
    if wide:
        for at, off in enumerate(evens):
            columns[off + 1] = [(crossed, 2 * at), (crossed, 2 * at + 1)]
        columns = [columns[off] for off in range(n_chan)]
        low_half = grad_weight_of(me, arrays, places, columns, [])
        grad_weight = grad_weight_of(me, arrays, places, columns, [low_half])
    else:
        for at, off in enumerate(evens):
            columns[off + 1] = [(crossed[at * length : (at + 1) * length], 0)]
        pairs = [[array for array, unused in columns[off]] for off in range(n_chan)]
        low_half = grad_weight = narrow_grad_weight(me, arrays, places, pairs)
    own = joined(me, own, held_until([other], [low_half])[0], bits[1], BF16, ())
    other = swap(own, "ctx", bits[0])
    grad_filters = joined(me, own, held_until([other], [grad_weight])[0], bits[0], F32, ())
    return (mixed, grad_query, grad_key, grad_value, grad_filters, grad_weight)


def solution(mesh):
    placed = (
        P("ctx", "chan"),
        P("ctx", "chan"),
        P("ctx", "chan"),
        P("chan", None),
        P("chan", None),
        P("ctx", "chan"),
    )
    return jax.shard_map(
        per_device,
        mesh=mesh,
        in_specs=placed,
        out_specs=(
            P("ctx", "chan"),
            P("ctx", "chan"),
            P("ctx", "chan"),
            P("ctx", "chan"),
            P("chan", None),
            P("chan", "ctx"),
        ),
        check_vma=False,
    )
```

```python
import functools

import jax
import jax.numpy as jnp
import numpy as np
from jax import lax
from jax.experimental import pallas as pl
from jax.experimental.pallas import tpu as pltpu
from jax.sharding import PartitionSpec as P

F32 = jnp.float32
BF16 = jnp.bfloat16
VMEM_BYTES = 40 * 2**20
NT = (((1,), (1,)), ((), ()))
TN = (((0,), (0,)), ((), ()))


def halves(matrix):
    high = matrix.astype(BF16)
    low = (matrix - high.astype(np.float64)).astype(BF16)
    return np.stack([high, low])


def transforms(taps):
    points = 2 * taps
    angle = np.pi * (2 * np.arange(taps)[:, None] + 1) * np.arange(points)[None, :] / points
    forward = np.concatenate([np.cos(angle), -np.sin(angle)], axis=0)
    inverse = forward.T * (2.0 / points)
    late = inverse[taps:]
    early = inverse[:taps]
    lags = inverse[taps - np.arange(taps)]
    return halves(forward), halves(late), halves(early), halves(lags)


def mm(a, b, dims=(((1,), (0,)), ((), ()))):
    return lax.dot_general(a, b, dims, preferred_element_type=F32)


def spectrum(f_ref, rows):
    return mm(f_ref[0], rows) + mm(f_ref[1], rows)


def tap_spectrum(f_ref, filters, taps):
    return mm(f_ref[0, :, :taps], filters, NT) + mm(f_ref[1, :, :taps], filters, NT)


def back(g_ref, real, imag):
    both = jnp.concatenate([real, imag], axis=0)
    high = both.astype(BF16)
    low = (both - high.astype(F32)).astype(BF16)
    return mm(g_ref[0], high) + mm(g_ref[0], low) + mm(g_ref[1], high)


def forward_kernel(taps, q_ref, k_ref, v_ref, earlier_ref, filt_ref, f_ref, g_ref, gated_ref, filtered_ref):
    product = (k_ref[...].astype(F32) * v_ref[...].astype(F32)).astype(BF16)
    x = spectrum(f_ref, jnp.concatenate([earlier_ref[...], product], axis=0))
    h = tap_spectrum(f_ref, filt_ref[...], taps)
    xr, xi, hr, hi = x[:taps], x[taps:], h[:taps], h[taps:]
    filtered = back(g_ref, xr * hr - xi * hi, xr * hi + xi * hr)
    filtered_ref[...] = filtered
    gated_ref[...] = (q_ref[...].astype(F32) * filtered).astype(BF16)


def tap_grad_kernel(taps, k_ref, v_ref, earlier_ref, gf_ref, f_ref, g_ref, out_ref):
    product = (k_ref[...].astype(F32) * v_ref[...].astype(F32)).astype(BF16)
    x = spectrum(f_ref, jnp.concatenate([earlier_ref[...], product], axis=0))
    rows = gf_ref[...]
    g = mm(f_ref[0, :, :taps], rows) + mm(f_ref[1, :, :taps], rows)
    xr, xi, gr, gi = x[:taps], x[taps:], g[:taps], g[taps:]
    tap_rows = back(g_ref, xr * gr + xi * gi, xi * gr - xr * gi)
    out_ref[...] = tap_rows.T.astype(BF16)


def backward_kernel(taps, k_ref, v_ref, gf_ref, following_ref, filt_ref, f_ref, g_ref, gk_ref, gv_ref):
    g = spectrum(f_ref, jnp.concatenate([gf_ref[...], following_ref[...]], axis=0))
    h = tap_spectrum(f_ref, filt_ref[...], taps)
    gr, gi, hr, hi = g[:taps], g[taps:], h[:taps], h[taps:]
    grad_product = back(g_ref, hr * gr + hi * gi, hr * gi - hi * gr)
    gk_ref[...] = (grad_product * v_ref[...].astype(F32)).astype(BF16)
    gv_ref[...] = (grad_product * k_ref[...].astype(F32)).astype(BF16)


def estimate(micros):
    return pl.CostEstimate(flops=int(micros * 10**9), bytes_accessed=0, transcendentals=0)


def ignoring(body, count, skip):
    def kernel(*refs):
        return body(*refs[:skip], *refs[skip + count :])

    return kernel


def by_channel(kernel, arrays, kinds, outs, name, after=()):
    length, channels = arrays[0].shape
    width = min(512, channels)
    specs = {
        "t": pl.BlockSpec((length, width), lambda i: (0, i)),
        "c": pl.BlockSpec((width, length), lambda i: (i, 0)),
    }

    def spec_of(kind, shape):
        if kind == "w":
            return pl.BlockSpec(shape, lambda i: (0,) * len(shape))
        return specs[kind]

    return pl.pallas_call(
        ignoring(functools.partial(kernel, length), len(after), len(arrays)),
        grid=(channels // width,),
        in_specs=[spec_of(kind, a.shape) for kind, a in zip(kinds, arrays)]
        + [pl.BlockSpec(memory_space=pl.ANY)] * len(after),
        out_specs=[specs[kind] for kind, unused in outs],
        out_shape=[
            jax.ShapeDtypeStruct((length, channels) if kind == "t" else (channels, length), dtype)
            for kind, dtype in outs
        ],
        compiler_params=pltpu.CompilerParams(vmem_limit_bytes=VMEM_BYTES),
        cost_estimate=estimate(3),
        name=name,
    )(*arrays, *after)


def pass_kernel(with_mixed, with_grad, has_sum, last, me_ref, w_ref, *refs):
    refs = list(refs)
    step = pl.program_id(0)
    if with_mixed:
        gated_ref = refs.pop(0)
    if with_grad:
        cot_ref = refs.pop(0)
        sum_ref = refs.pop(0) if has_sum else None
        turned_ref = refs.pop()

        @pl.when(step == 0)
        def turn():
            turned_ref[...] = cot_ref[...].T

        total = mm(w_ref[...], turned_ref[...])
        if has_sum:
            total = total + sum_ref[...]
        if last:
            q_ref, filtered_ref, gq_ref, gf_ref = refs[:4]
            total = total.T
            gq_ref[...] = (total * filtered_ref[...]).astype(BF16)
            gf_ref[...] = (total * q_ref[...].astype(F32)).astype(BF16)
        else:
            refs[0][...] = total
    if with_mixed:
        held_ref, mixed_ref = refs.pop(), refs.pop()
        part = mm(gated_ref[...], w_ref[...])

        @pl.when(step == 0)
        def first():
            held_ref[...] = part

        @pl.when(step > 0)
        def more():
            held_ref[...] = held_ref[...] + part

        @pl.when(step == pl.num_programs(0) - 1)
        def give():
            mixed_ref[...] = held_ref[...].astype(mixed_ref.dtype)


def weight_pass(me, weight, off, gated=None, cot=None, sums=(), ends=(), after=()):
    length = (cot if gated is None else gated).shape[0]
    channels = weight.shape[0]
    tile = 512
    whole = pl.BlockSpec((length, channels), lambda r, me: (0, 0))
    by_token = pl.BlockSpec((length, tile), lambda r, me: (0, r))
    by_row = pl.BlockSpec((tile, length), lambda r, me: (r, 0))
    arrays, in_specs = [weight], [pl.BlockSpec((tile, channels), lambda r, me: (r, me[1] ^ off))]
    out_specs, out_shape, scratch = [], [], []
    if gated is not None:
        arrays.append(gated)
        in_specs.append(by_token)
    if cot is not None:
        arrays += [cot, *sums, *ends]
        in_specs += [whole] + [by_row] * len(sums) + [by_token] * len(ends)
        out_specs += [by_token] * 2 if ends else [by_row]
        out_shape += [jax.ShapeDtypeStruct((length, channels), BF16)] * 2 if ends else [
            jax.ShapeDtypeStruct((channels, length), F32)
        ]
    if gated is not None:
        out_specs.append(whole)
        out_shape.append(jax.ShapeDtypeStruct((length, channels), BF16 if off % 2 else F32))
        scratch.append(pltpu.VMEM((length, channels), F32))
    if cot is not None:
        scratch.append(pltpu.VMEM((channels, length), BF16))
    body = functools.partial(pass_kernel, gated is not None, cot is not None, bool(sums), bool(ends))
    return pl.pallas_call(
        ignoring(body, len(after), 1 + len(arrays)),
        grid_spec=pltpu.PrefetchScalarGridSpec(
            num_scalar_prefetch=1,
            grid=(channels // tile,),
            in_specs=in_specs + [pl.BlockSpec(memory_space=pl.ANY)] * len(after),
            out_specs=out_specs,
            scratch_shapes=scratch,
        ),
        out_shape=out_shape,
        compiler_params=pltpu.CompilerParams(vmem_limit_bytes=VMEM_BYTES),
        cost_estimate=estimate(3 if gated is None else 0.5),
        name="grad_gated_part" if gated is None else "mixed_part" if cot is None else "grads_and_mixed",
    )(me, *arrays, *after)


def pieces_kernel(per_chan, me_ref, slot_ref, *refs):
    out_ref = refs[-1]
    length, width = refs[0].shape
    span = width // per_chan
    count = len(refs) - 1
    piece = span // count
    rows = length * piece // width
    for off in range(count):
        for part in range(per_chan):
            target = (me_ref[1] ^ off) * per_chan + part
            start = pl.multiple_of(part * span + me_ref[1] * piece, 128)
            block = refs[off][:, pl.ds(start, piece)]
            place = pl.multiple_of(slot_ref[me_ref[0], target] * rows, rows)
            out_ref[pl.ds(place, rows), :] = jnp.concatenate(
                [block[at : at + rows] for at in range(0, length, rows)], axis=1
            )


def pieces_of(me, slots, cots, after):
    length, width = cots[0].shape
    n_ctx = slots.shape[0]
    piece = width // n_ctx
    if piece % 128:
        return pieces_by_slices(me, slots, cots)
    return pl.pallas_call(
        ignoring(functools.partial(pieces_kernel, n_ctx // len(cots)), len(after), 2 + len(cots)),
        grid_spec=pltpu.PrefetchScalarGridSpec(
            num_scalar_prefetch=2,
            grid=(1,),
            in_specs=[pl.BlockSpec((length, width), lambda i, *ids: (0, 0))] * len(cots)
            + [pl.BlockSpec(memory_space=pl.ANY)] * len(after),
            out_specs=pl.BlockSpec((length, width), lambda i, *ids: (0, 0)),
        ),
        out_shape=jax.ShapeDtypeStruct((length, width), BF16),
        compiler_params=pltpu.CompilerParams(vmem_limit_bytes=VMEM_BYTES),
        cost_estimate=estimate(0.5),
        name="pieces",
    )(me, slots, *cots, *after)


def pieces_by_slices(me, slots, cots):
    length, width = cots[0].shape
    n_ctx, count = slots.shape[0], len(cots)
    piece, per_chan = width // n_ctx, n_ctx // count
    rows = length * piece // width
    table = jnp.stack(cots).reshape(count, length, per_chan, count, piece)
    mine = lax.dynamic_index_in_dim(table, me[1], 3, False)
    parts = mine.transpose(0, 2, 1, 3).reshape(n_ctx, length // rows, rows, piece)
    parts = parts.transpose(0, 2, 1, 3).reshape(n_ctx, rows, width)
    order = jnp.argsort(slots[me[0]])
    return parts[(order // per_chan ^ me[1]) * per_chan + order % per_chan].reshape(length, width)


def weight_kernel(places, parts, me_ref, *refs):
    out_ref = refs[-1]
    length = sum(rows for unused, rows in places[0])
    blocks = []
    at = 0
    for place in places:
        for start, rows in place:
            blocks.append(refs[at][start : start + rows, :])
            at += 1
    columns = jnp.concatenate(blocks, axis=0)
    for part in range(parts):
        packed = jnp.concatenate([ref[...] for ref in refs[at + 2 * part : at + 2 * part + 2]], axis=0)
        rows = packed.shape[0] // len(places)
        piece = packed.shape[1] * rows // length
        wide = [
            packed[slot * rows : (slot + 1) * rows, lane : lane + piece]
            for slot in range(len(places))
            for lane in range(0, packed.shape[1], piece)
        ]
        total = mm(columns, jnp.concatenate(wide, axis=0), TN)
        place = pl.multiple_of((me_ref[1] ^ part) * piece, piece)
        out_ref[:, pl.ds(place, piece)] = total.astype(BF16)


def grad_weight_of(me, arrays, places, cots, earlier):
    channels = arrays[0].shape[1]
    slots, parts = len(places), len(cots)
    pieces = [array for pair in cots for array, unused in pair]
    half = cots[0][0][0].shape[0]
    tile = 256
    width = 2 * half * channels // (slots * sum(count for unused, count in places[0])) * parts
    steps = channels // tile // 2
    first = steps * len(earlier)
    count = 1 + len(arrays) + len(pieces)
    return pl.pallas_call(
        ignoring(functools.partial(weight_kernel, places, parts), len(earlier), count),
        grid_spec=pltpu.PrefetchScalarGridSpec(
            num_scalar_prefetch=1,
            grid=(steps,),
            in_specs=[pl.BlockSpec((array.shape[0], tile), lambda i, me: (0, first + i)) for array in arrays]
            + [pl.BlockSpec((half, channels), lambda i, me, at=at: (at, 0)) for pair in cots for unused, at in pair]
            + [pl.BlockSpec(memory_space=pl.ANY)] * len(earlier),
            out_specs=pl.BlockSpec((tile, width), lambda i, me: (first + i, 0)),
        ),
        out_shape=jax.ShapeDtypeStruct((channels, width), BF16),
        input_output_aliases={count: 0} if earlier else {},
        compiler_params=pltpu.CompilerParams(vmem_limit_bytes=VMEM_BYTES),
        cost_estimate=estimate(2),
        name="grad_weight",
    )(me, *arrays, *pieces, *earlier)


def narrow_grad_weight(me, arrays, places, cots):
    blocks, at = [], 0
    for place in places:
        for start, rows in place:
            blocks.append(arrays[at][start : start + rows])
            at += 1
    columns = jnp.concatenate(blocks, axis=0)
    length = columns.shape[0] // len(places)
    packed = jnp.stack([jnp.concatenate(pair, axis=0) for pair in cots])
    packed = packed[jnp.arange(len(cots), dtype=jnp.int32) ^ me[1]]
    parts, height, width = packed.shape
    rows = height // len(places)
    piece = rows * width // length
    wide = packed.reshape(parts, len(places), rows, length // rows, piece).transpose(1, 3, 2, 0, 4)
    return mm(columns, wide.reshape(columns.shape[0], parts * piece), TN).astype(BF16)


def cycle_of(count):
    across = 1 << ((count.bit_length() - 1) // 2)
    order = []
    for column in range(across):
        line = [row * across + column for row in range(count // across)]
        order += line if column % 2 == 0 else line[::-1]
    return order


def held_until(arrays, kernels):
    return lax.optimization_barrier((*arrays, *kernels))[: len(arrays)]


def swap(block, axis, bit):
    size = lax.axis_size(axis)
    return lax.ppermute(block, axis, [(i, i ^ bit) for i in range(size)])


def bits_of(size):
    return [1 << place for place in range(size.bit_length() - 1)]


def gather_of_chips(block):
    held = {0: block}
    for bit in reversed(bits_of(lax.axis_size("chan"))[1:]):
        held.update({off ^ bit: swap(held[off], "chan", bit) for off in list(held)})
    return held


def added_kernel(bit, me_ref, own_ref, came_ref, *outs):
    total = (own_ref[...].astype(F32) + came_ref[...].astype(F32)).astype(BF16)
    if not bit:
        outs[0][...] = total
        return
    rows = outs[0].shape[0]
    mine = (me_ref[0] & bit) != 0
    outs[0][...] = jnp.where(mine, total[rows:], total[:rows])
    outs[1][...] = jnp.where(mine, total[:rows], total[rows:])


def added(me, own, came, bit, after):
    shape = (own.shape[0] // 2, own.shape[1]) if bit else own.shape
    whole = pl.BlockSpec(own.shape, lambda i, me: (0, 0))
    outs = 2 if bit else 1
    return pl.pallas_call(
        ignoring(functools.partial(added_kernel, bit), len(after), 3),
        grid_spec=pltpu.PrefetchScalarGridSpec(
            num_scalar_prefetch=1,
            grid=(1,),
            in_specs=[whole, whole] + [pl.BlockSpec(memory_space=pl.ANY)] * len(after),
            out_specs=[pl.BlockSpec(shape, lambda i, me: (0, 0))] * outs,
        ),
        out_shape=[jax.ShapeDtypeStruct(shape, BF16)] * outs,
        compiler_params=pltpu.CompilerParams(vmem_limit_bytes=VMEM_BYTES),
        cost_estimate=estimate(0.5),
        name="added",
    )(me, own, came, *after)


def split(me, block, bit):
    rows = block.shape[0] // 2
    mine = (me[0] & bit) != 0
    low, high = block[:rows], block[rows:]
    return jnp.where(mine, high, low), jnp.where(mine, low, high)


class Sum:
    def __init__(self, me, partial):
        self.me = me
        self.bits = bits_of(lax.axis_size("ctx"))
        self.step = 0
        self.sums, self.send = split(me, partial, self.bits[0])

    def add(self, after):
        if self.step == len(self.bits):
            return []
        came = swap(self.send if self.step < 2 else self.sums, "ctx", self.bits[self.step])
        self.sums, *send = added(self.me, self.sums, came, 0 if self.step else self.bits[1], after)
        self.send = send[0] if send else None
        self.step += 1
        return [self.sums]


def joined_kernel(bit, me_ref, own_ref, other_ref, out_ref):
    rows = own_ref.shape[0]
    mine = (me_ref[0] & bit) != 0
    out_ref[:rows] = jnp.where(mine, other_ref[...], own_ref[...]).astype(out_ref.dtype)
    out_ref[rows:] = jnp.where(mine, own_ref[...], other_ref[...]).astype(out_ref.dtype)


def joined(me, own, other, bit, dtype, after):
    rows, width = own.shape
    whole = pl.BlockSpec(own.shape, lambda i, me: (0, 0))
    return pl.pallas_call(
        ignoring(functools.partial(joined_kernel, bit), len(after), 3),
        grid_spec=pltpu.PrefetchScalarGridSpec(
            num_scalar_prefetch=1,
            grid=(1,),
            in_specs=[whole, whole] + [pl.BlockSpec(memory_space=pl.ANY)] * len(after),
            out_specs=pl.BlockSpec((2 * rows, width), lambda i, me: (0, 0)),
        ),
        out_shape=jax.ShapeDtypeStruct((2 * rows, width), dtype),
        compiler_params=pltpu.CompilerParams(vmem_limit_bytes=VMEM_BYTES),
        cost_estimate=estimate(0.5),
        name="joined",
    )(me, own, other, *after)


def per_device(query_proj, key_proj, value_proj, filters, out_weight, cotangent):
    length, channels = query_proj.shape
    taps = filters.shape[1]
    n_ctx, n_chan = lax.axis_size("ctx"), lax.axis_size("chan")
    me = jnp.stack([lax.axis_index("ctx"), lax.axis_index("chan")]).astype(jnp.int32)
    forward, late, early_rows, lags = [jnp.asarray(m) for m in transforms(taps)]

    product = (key_proj.astype(F32) * value_proj.astype(F32)).astype(BF16)
    product, cotangent = lax.optimization_barrier((product, cotangent))
    earlier = lax.ppermute(product, "ctx", [(i, i + 1) for i in range(n_ctx - 1)])

    cots = {0: cotangent, 1: swap(cotangent, "chan", 1)}
    for bit in reversed(bits_of(n_chan)[1:]):
        cots.update({off ^ bit: swap(cots[off], "chan", bit) for off in list(cots) if off % 2 == 0})
    offs = sorted(off for off in cots if off % 2 == 0 and off)
    sums = weight_pass(me, out_weight, 0, cot=cots[0])
    for off in offs:
        cots[off + 1] = swap(held_until([cots[off]], sums)[0], "chan", 1)
    offs = sorted(offs + [off + 1 for off in offs])

    sums = weight_pass(me, out_weight, 1, cot=cots[1], sums=sums)

    order = cycle_of(n_ctx)
    slots = []
    for c in range(n_ctx):
        spot = order.index(c)
        turn = [0, n_ctx // 2] + list(range(1, n_ctx // 2)) + list(range(1 - n_ctx // 2, 0))
        targets = [order[(spot + step) % n_ctx] for step in turn]
        slots.append([targets.index(target) for target in range(n_ctx)])
    pieces = pieces_of(me, jnp.asarray(slots, jnp.int32), [cots[off] for off in range(n_chan)], sums)

    gated, filtered = by_channel(
        forward_kernel,
        [query_proj, key_proj, value_proj, earlier, filters, forward, late],
        "ttttcww",
        [("t", BF16), ("t", F32)],
        "forward_filter",
        after=sums,
    )

    ahead = [(order[i], order[(i + 1) % n_ctx]) for i in range(n_ctx)]
    behind = [(b, a) for a, b in ahead]
    turns = n_ctx // 2
    rows, piece = length // n_ctx, channels // n_ctx
    span = (turns - 1) * rows
    ends = [
        jnp.concatenate([pieces[2 * rows : 2 * rows + span], gated], axis=0),
        jnp.concatenate([gated, pieces[2 * rows + span :]], axis=0),
    ]
    arrays, places, brought = [gated], [[(0, length)]], [pieces[:rows]]

    def passed_on(kernels):
        onto, back = held_until(ends, kernels)
        came = [lax.ppermute(onto, "ctx", ahead), lax.ppermute(back, "ctx", behind)]
        arrays.extend(came)
        places.extend([[(came[0].shape[0] - length, length)], [(0, length)]])
        brought.extend([came[0][:rows], came[1][-rows:]])
        ends[:] = [came[0][rows:], came[1][:-rows]]
        return came

    landed = passed_on([])
    terms = {}
    for off in offs[:-1]:
        *sums, terms[off] = weight_pass(me, out_weight, off, gated, cots[off], sums)
    grad_query, grad_filtered, terms[offs[-1]] = weight_pass(
        me, out_weight, offs[-1], gated, cots[offs[-1]], sums, [query_proj, filtered]
    )
    previous, landed = landed, passed_on([grad_filtered])

    tap_grad = by_channel(
        tap_grad_kernel,
        [key_proj, value_proj, earlier, grad_filtered, forward, lags],
        "ttttww",
        [("c", BF16)],
        "tap_grad",
        after=previous,
    )[0]
    from_core = []
    for off in [off for off in sorted(terms) if off % 2]:
        from_core.append(swap(terms.pop(off), "chan", 1))
        terms[off ^ 1] = terms[off ^ 1] + from_core[-1].astype(F32)
    mixed_one = weight_pass(me, out_weight, 1, gated, after=[tap_grad])[0]
    across = lax.ppermute(
        held_until([pieces[rows : 2 * rows]], [mixed_one])[0],
        "ctx",
        [(order[i], order[(i + turns) % n_ctx]) for i in range(n_ctx)],
    )
    brought.insert(1, across)
    last_part = weight_pass(me, out_weight, 0, gated, after=[mixed_one])[0]
    tap_sum = Sum(me, held_until([tap_grad], [mixed_one])[0])
    previous, landed = landed, passed_on([last_part])

    terms = dict(zip(terms, held_until(terms.values(), previous)))
    terms[0] = last_part + swap(mixed_one, "chan", 1).astype(F32)
    for bit in bits_of(n_chan)[1:]:
        for off in [off for off in sorted(terms, reverse=True) if off & bit]:
            terms[off ^ bit] = terms[off ^ bit] + swap(terms.pop(off).astype(BF16), "chan", bit).astype(F32)
    mixed = terms[0].astype(BF16)
    early = 2 + 2 * min(1, turns - 1)
    first = jnp.concatenate(held_until(brought[:early], previous), axis=0)

    for unused in range(turns - 4):
        landed = passed_on([last_part])
    half = length // 2
    cols = [gather_of_chips(first)]
    onto, back = held_until(ends, tap_sum.add([last_part]) + [cols[0][off] for off in cols[0] if off])
    tap_sum.add(landed)
    far = [lax.ppermute(onto[:half], "ctx", ahead), lax.ppermute(back[half:], "ctx", behind)]
    arrays = arrays[:1] + far + arrays[1:]
    places.insert(1, [(0, half), (0, half)])

    cols.append(gather_of_chips(jnp.concatenate(brought[early:], axis=0)))

    given = held_until([grad_filtered], far)[0]
    following = lax.ppermute(given, "ctx", [(i + 1, i) for i in range(n_ctx - 1)])
    grad_key, grad_value = by_channel(
        backward_kernel,
        [key_proj, value_proj, grad_filtered, following, filters, forward, early_rows],
        "ttttcww",
        [("t", BF16), ("t", BF16)],
        "backward_filter",
    )

    while tap_sum.add(far):
        pass
    own, bits = tap_sum.sums, tap_sum.bits
    other = swap(own, "ctx", bits[1])

    evens = [off for off in range(n_chan) if off % 2 == 0]
    wide = piece % 128 == 0 and 2 * early == n_ctx
    columns = {off: [(part[off], 0) for part in cols] for off in evens}
    crossed = jnp.concatenate([part[off] for off in evens for part in cols], axis=0)
    crossed = swap(held_until([crossed], far)[0], "chan", 1)
    if wide:
        for at, off in enumerate(evens):
            columns[off + 1] = [(crossed, 2 * at), (crossed, 2 * at + 1)]
        columns = [columns[off] for off in range(n_chan)]
        low_half = grad_weight_of(me, arrays, places, columns, [])
        grad_weight = grad_weight_of(me, arrays, places, columns, [low_half])
    else:
        for at, off in enumerate(evens):
            columns[off + 1] = [(crossed[at * length : (at + 1) * length], 0)]
        pairs = [[array for array, unused in columns[off]] for off in range(n_chan)]
        low_half = grad_weight = narrow_grad_weight(me, arrays, places, pairs)
    own = joined(me, own, held_until([other], [low_half])[0], bits[1], BF16, ())
    other = swap(own, "ctx", bits[0])
    grad_filters = joined(me, own, held_until([other], [grad_weight])[0], bits[0], F32, ())
    return (mixed, grad_query, grad_key, grad_value, grad_filters, grad_weight)


def solution(mesh):
    placed = (
        P("ctx", "chan"),
        P("ctx", "chan"),
        P("ctx", "chan"),
        P("chan", None),
        P("chan", None),
        P("ctx", "chan"),
    )
    return jax.shard_map(
        per_device,
        mesh=mesh,
        in_specs=placed,
        out_specs=(
            P("ctx", "chan"),
            P("ctx", "chan"),
            P("ctx", "chan"),
            P("ctx", "chan"),
            P("chan", None),
            P("chan", "ctx"),
        ),
        check_vma=False,
    )
```

```python
import functools

import jax
import jax.numpy as jnp
import numpy as np
from jax import lax
from jax.experimental import pallas as pl
from jax.experimental.pallas import tpu as pltpu
from jax.sharding import PartitionSpec as P

F32 = jnp.float32
BF16 = jnp.bfloat16
VMEM_BYTES = 40 * 2**20
NT = (((1,), (1,)), ((), ()))
TN = (((0,), (0,)), ((), ()))


def halves(matrix):
    high = matrix.astype(BF16)
    low = (matrix - high.astype(np.float64)).astype(BF16)
    return np.stack([high, low])


def transforms(taps):
    points = 2 * taps
    angle = np.pi * (2 * np.arange(taps)[:, None] + 1) * np.arange(points)[None, :] / points
    forward = np.concatenate([np.cos(angle), -np.sin(angle)], axis=0)
    inverse = forward.T * (2.0 / points)
    late = inverse[taps:]
    early = inverse[:taps]
    lags = inverse[taps - np.arange(taps)]
    return halves(forward), halves(late), halves(early), halves(lags)


def mm(a, b, dims=(((1,), (0,)), ((), ()))):
    return lax.dot_general(a, b, dims, preferred_element_type=F32)


def spectrum(f_ref, rows):
    return mm(f_ref[0], rows) + mm(f_ref[1], rows)


def tap_spectrum(f_ref, filters, taps):
    return mm(f_ref[0, :, :taps], filters, NT) + mm(f_ref[1, :, :taps], filters, NT)


def back(g_ref, real, imag):
    both = jnp.concatenate([real, imag], axis=0)
    high = both.astype(BF16)
    low = (both - high.astype(F32)).astype(BF16)
    return mm(g_ref[0], high) + mm(g_ref[0], low) + mm(g_ref[1], high)


def forward_kernel(taps, q_ref, k_ref, v_ref, earlier_ref, filt_ref, f_ref, g_ref, gated_ref, filtered_ref):
    product = (k_ref[...].astype(F32) * v_ref[...].astype(F32)).astype(BF16)
    x = spectrum(f_ref, jnp.concatenate([earlier_ref[...], product], axis=0))
    h = tap_spectrum(f_ref, filt_ref[...], taps)
    xr, xi, hr, hi = x[:taps], x[taps:], h[:taps], h[taps:]
    filtered = back(g_ref, xr * hr - xi * hi, xr * hi + xi * hr)
    filtered_ref[...] = filtered
    gated_ref[...] = (q_ref[...].astype(F32) * filtered).astype(BF16)


def tap_grad_kernel(taps, k_ref, v_ref, earlier_ref, gf_ref, f_ref, g_ref, out_ref):
    product = (k_ref[...].astype(F32) * v_ref[...].astype(F32)).astype(BF16)
    x = spectrum(f_ref, jnp.concatenate([earlier_ref[...], product], axis=0))
    rows = gf_ref[...]
    g = mm(f_ref[0, :, :taps], rows) + mm(f_ref[1, :, :taps], rows)
    xr, xi, gr, gi = x[:taps], x[taps:], g[:taps], g[taps:]
    tap_rows = back(g_ref, xr * gr + xi * gi, xi * gr - xr * gi)
    out_ref[...] = tap_rows.T.astype(BF16)


def backward_kernel(taps, k_ref, v_ref, gf_ref, following_ref, filt_ref, f_ref, g_ref, gk_ref, gv_ref):
    g = spectrum(f_ref, jnp.concatenate([gf_ref[...], following_ref[...]], axis=0))
    h = tap_spectrum(f_ref, filt_ref[...], taps)
    gr, gi, hr, hi = g[:taps], g[taps:], h[:taps], h[taps:]
    grad_product = back(g_ref, hr * gr + hi * gi, hr * gi - hi * gr)
    gk_ref[...] = (grad_product * v_ref[...].astype(F32)).astype(BF16)
    gv_ref[...] = (grad_product * k_ref[...].astype(F32)).astype(BF16)


def estimate(micros):
    return pl.CostEstimate(flops=int(micros * 10**9), bytes_accessed=0, transcendentals=0)


def ignoring(body, count, skip):
    def kernel(*refs):
        return body(*refs[:skip], *refs[skip + count :])

    return kernel


def by_channel(kernel, arrays, kinds, outs, name, after=()):
    length, channels = arrays[0].shape
    width = min(512, channels)
    specs = {
        "t": pl.BlockSpec((length, width), lambda i: (0, i)),
        "c": pl.BlockSpec((width, length), lambda i: (i, 0)),
    }

    def spec_of(kind, shape):
        if kind == "w":
            return pl.BlockSpec(shape, lambda i: (0,) * len(shape))
        return specs[kind]

    return pl.pallas_call(
        ignoring(functools.partial(kernel, length), len(after), len(arrays)),
        grid=(channels // width,),
        in_specs=[spec_of(kind, a.shape) for kind, a in zip(kinds, arrays)]
        + [pl.BlockSpec(memory_space=pl.ANY)] * len(after),
        out_specs=[specs[kind] for kind, unused in outs],
        out_shape=[
            jax.ShapeDtypeStruct((length, channels) if kind == "t" else (channels, length), dtype)
            for kind, dtype in outs
        ],
        compiler_params=pltpu.CompilerParams(vmem_limit_bytes=VMEM_BYTES),
        cost_estimate=estimate(3),
        name=name,
    )(*arrays, *after)


def pass_kernel(with_mixed, with_grad, has_sum, last, me_ref, w_ref, *refs):
    refs = list(refs)
    step = pl.program_id(0)
    if with_mixed:
        gated_ref = refs.pop(0)
    if with_grad:
        cot_ref = refs.pop(0)
        sum_ref = refs.pop(0) if has_sum else None
        turned_ref = refs.pop()

        @pl.when(step == 0)
        def turn():
            turned_ref[...] = cot_ref[...].T

        total = mm(w_ref[...], turned_ref[...])
        if has_sum:
            total = total + sum_ref[...]
        if last:
            q_ref, filtered_ref, gq_ref, gf_ref = refs[:4]
            total = total.T
            gq_ref[...] = (total * filtered_ref[...]).astype(BF16)
            gf_ref[...] = (total * q_ref[...].astype(F32)).astype(BF16)
        else:
            refs[0][...] = total
    if with_mixed:
        held_ref, mixed_ref = refs.pop(), refs.pop()
        part = mm(gated_ref[...], w_ref[...])

        @pl.when(step == 0)
        def first():
            held_ref[...] = part

        @pl.when(step > 0)
        def more():
            held_ref[...] = held_ref[...] + part

        @pl.when(step == pl.num_programs(0) - 1)
        def give():
            mixed_ref[...] = held_ref[...].astype(mixed_ref.dtype)


def weight_pass(me, weight, off, gated=None, cot=None, sums=(), ends=(), after=()):
    length = (cot if gated is None else gated).shape[0]
    channels = weight.shape[0]
    tile = 512
    whole = pl.BlockSpec((length, channels), lambda r, me: (0, 0))
    by_token = pl.BlockSpec((length, tile), lambda r, me: (0, r))
    by_row = pl.BlockSpec((tile, length), lambda r, me: (r, 0))
    arrays, in_specs = [weight], [pl.BlockSpec((tile, channels), lambda r, me: (r, me[1] ^ off))]
    out_specs, out_shape, scratch = [], [], []
    if gated is not None:
        arrays.append(gated)
        in_specs.append(by_token)
    if cot is not None:
        arrays += [cot, *sums, *ends]
        in_specs += [whole] + [by_row] * len(sums) + [by_token] * len(ends)
        out_specs += [by_token] * 2 if ends else [by_row]
        out_shape += [jax.ShapeDtypeStruct((length, channels), BF16)] * 2 if ends else [
            jax.ShapeDtypeStruct((channels, length), F32)
        ]
    if gated is not None:
        out_specs.append(whole)
        out_shape.append(jax.ShapeDtypeStruct((length, channels), BF16 if off % 2 else F32))
        scratch.append(pltpu.VMEM((length, channels), F32))
    if cot is not None:
        scratch.append(pltpu.VMEM((channels, length), BF16))
    body = functools.partial(pass_kernel, gated is not None, cot is not None, bool(sums), bool(ends))
    return pl.pallas_call(
        ignoring(body, len(after), 1 + len(arrays)),
        grid_spec=pltpu.PrefetchScalarGridSpec(
            num_scalar_prefetch=1,
            grid=(channels // tile,),
            in_specs=in_specs + [pl.BlockSpec(memory_space=pl.ANY)] * len(after),
            out_specs=out_specs,
            scratch_shapes=scratch,
        ),
        out_shape=out_shape,
        compiler_params=pltpu.CompilerParams(vmem_limit_bytes=VMEM_BYTES),
        cost_estimate=estimate(3 if gated is None else 0.5),
        name="grad_gated_part" if gated is None else "mixed_part" if cot is None else "grads_and_mixed",
    )(me, *arrays, *after)


def pieces_kernel(per_chan, me_ref, slot_ref, *refs):
    out_ref = refs[-1]
    length, width = refs[0].shape
    span = width // per_chan
    count = len(refs) - 1
    piece = span // count
    rows = length * piece // width
    for off in range(count):
        for part in range(per_chan):
            target = (me_ref[1] ^ off) * per_chan + part
            start = pl.multiple_of(part * span + me_ref[1] * piece, 128)
            block = refs[off][:, pl.ds(start, piece)]
            place = pl.multiple_of(slot_ref[me_ref[0], target] * rows, rows)
            out_ref[pl.ds(place, rows), :] = jnp.concatenate(
                [block[at : at + rows] for at in range(0, length, rows)], axis=1
            )


def pieces_of(me, slots, cots, after):
    length, width = cots[0].shape
    n_ctx = slots.shape[0]
    piece = width // n_ctx
    if piece % 128:
        return pieces_by_slices(me, slots, cots)
    return pl.pallas_call(
        ignoring(functools.partial(pieces_kernel, n_ctx // len(cots)), len(after), 2 + len(cots)),
        grid_spec=pltpu.PrefetchScalarGridSpec(
            num_scalar_prefetch=2,
            grid=(1,),
            in_specs=[pl.BlockSpec((length, width), lambda i, *ids: (0, 0))] * len(cots)
            + [pl.BlockSpec(memory_space=pl.ANY)] * len(after),
            out_specs=pl.BlockSpec((length, width), lambda i, *ids: (0, 0)),
        ),
        out_shape=jax.ShapeDtypeStruct((length, width), BF16),
        compiler_params=pltpu.CompilerParams(vmem_limit_bytes=VMEM_BYTES),
        cost_estimate=estimate(0.5),
        name="pieces",
    )(me, slots, *cots, *after)


def pieces_by_slices(me, slots, cots):
    length, width = cots[0].shape
    n_ctx, count = slots.shape[0], len(cots)
    piece, per_chan = width // n_ctx, n_ctx // count
    rows = length * piece // width
    table = jnp.stack(cots).reshape(count, length, per_chan, count, piece)
    mine = lax.dynamic_index_in_dim(table, me[1], 3, False)
    parts = mine.transpose(0, 2, 1, 3).reshape(n_ctx, length // rows, rows, piece)
    parts = parts.transpose(0, 2, 1, 3).reshape(n_ctx, rows, width)
    order = jnp.argsort(slots[me[0]])
    return parts[(order // per_chan ^ me[1]) * per_chan + order % per_chan].reshape(length, width)


def weight_kernel(places, parts, me_ref, *refs):
    out_ref = refs[-1]
    length = sum(rows for unused, rows in places[0])
    blocks = []
    at = 0
    for place in places:
        for start, rows in place:
            blocks.append(refs[at][start : start + rows, :])
            at += 1
    columns = jnp.concatenate(blocks, axis=0)
    for part in range(parts):
        packed = jnp.concatenate([ref[...] for ref in refs[at + 2 * part : at + 2 * part + 2]], axis=0)
        rows = packed.shape[0] // len(places)
        piece = packed.shape[1] * rows // length
        wide = [
            packed[slot * rows : (slot + 1) * rows, lane : lane + piece]
            for slot in range(len(places))
            for lane in range(0, packed.shape[1], piece)
        ]
        total = mm(columns, jnp.concatenate(wide, axis=0), TN)
        place = pl.multiple_of((me_ref[1] ^ part) * piece, piece)
        out_ref[:, pl.ds(place, piece)] = total.astype(BF16)


def grad_weight_of(me, arrays, places, cots, earlier):
    channels = arrays[0].shape[1]
    slots, parts = len(places), len(cots)
    pieces = [array for pair in cots for array, unused in pair]
    half = cots[0][0][0].shape[0]
    tile = 256
    width = 2 * half * channels // (slots * sum(count for unused, count in places[0])) * parts
    steps = channels // tile // 2
    first = steps * len(earlier)
    count = 1 + len(arrays) + len(pieces)
    return pl.pallas_call(
        ignoring(functools.partial(weight_kernel, places, parts), len(earlier), count),
        grid_spec=pltpu.PrefetchScalarGridSpec(
            num_scalar_prefetch=1,
            grid=(steps,),
            in_specs=[pl.BlockSpec((array.shape[0], tile), lambda i, me: (0, first + i)) for array in arrays]
            + [pl.BlockSpec((half, channels), lambda i, me, at=at: (at, 0)) for pair in cots for unused, at in pair]
            + [pl.BlockSpec(memory_space=pl.ANY)] * len(earlier),
            out_specs=pl.BlockSpec((tile, width), lambda i, me: (first + i, 0)),
        ),
        out_shape=jax.ShapeDtypeStruct((channels, width), BF16),
        input_output_aliases={count: 0} if earlier else {},
        compiler_params=pltpu.CompilerParams(vmem_limit_bytes=VMEM_BYTES),
        cost_estimate=estimate(2),
        name="grad_weight",
    )(me, *arrays, *pieces, *earlier)


def narrow_grad_weight(me, arrays, places, cots):
    blocks, at = [], 0
    for place in places:
        for start, rows in place:
            blocks.append(arrays[at][start : start + rows])
            at += 1
    columns = jnp.concatenate(blocks, axis=0)
    length = columns.shape[0] // len(places)
    packed = jnp.stack([jnp.concatenate(pair, axis=0) for pair in cots])
    packed = packed[jnp.arange(len(cots), dtype=jnp.int32) ^ me[1]]
    parts, height, width = packed.shape
    rows = height // len(places)
    piece = rows * width // length
    wide = packed.reshape(parts, len(places), rows, length // rows, piece).transpose(1, 3, 2, 0, 4)
    return mm(columns, wide.reshape(columns.shape[0], parts * piece), TN).astype(BF16)


def cycle_of(count):
    across = 1 << ((count.bit_length() - 1) // 2)
    order = []
    for column in range(across):
        line = [row * across + column for row in range(count // across)]
        order += line if column % 2 == 0 else line[::-1]
    return order


def held_until(arrays, kernels):
    return lax.optimization_barrier((*arrays, *kernels))[: len(arrays)]


def swap(block, axis, bit):
    size = lax.axis_size(axis)
    return lax.ppermute(block, axis, [(i, i ^ bit) for i in range(size)])


def bits_of(size):
    return [1 << place for place in range(size.bit_length() - 1)]


def gather_of_chips(block):
    held = {0: block}
    for bit in reversed(bits_of(lax.axis_size("chan"))[1:]):
        held.update({off ^ bit: swap(held[off], "chan", bit) for off in list(held)})
    return held


def added_kernel(bit, me_ref, own_ref, came_ref, *outs):
    total = (own_ref[...].astype(F32) + came_ref[...].astype(F32)).astype(BF16)
    if not bit:
        outs[0][...] = total
        return
    rows = outs[0].shape[0]
    mine = (me_ref[0] & bit) != 0
    outs[0][...] = jnp.where(mine, total[rows:], total[:rows])
    outs[1][...] = jnp.where(mine, total[:rows], total[rows:])


def added(me, own, came, bit, after):
    shape = (own.shape[0] // 2, own.shape[1]) if bit else own.shape
    whole = pl.BlockSpec(own.shape, lambda i, me: (0, 0))
    outs = 2 if bit else 1
    return pl.pallas_call(
        ignoring(functools.partial(added_kernel, bit), len(after), 3),
        grid_spec=pltpu.PrefetchScalarGridSpec(
            num_scalar_prefetch=1,
            grid=(1,),
            in_specs=[whole, whole] + [pl.BlockSpec(memory_space=pl.ANY)] * len(after),
            out_specs=[pl.BlockSpec(shape, lambda i, me: (0, 0))] * outs,
        ),
        out_shape=[jax.ShapeDtypeStruct(shape, BF16)] * outs,
        compiler_params=pltpu.CompilerParams(vmem_limit_bytes=VMEM_BYTES),
        cost_estimate=estimate(0.5),
        name="added",
    )(me, own, came, *after)


def split(me, block, bit):
    rows = block.shape[0] // 2
    mine = (me[0] & bit) != 0
    low, high = block[:rows], block[rows:]
    return jnp.where(mine, high, low), jnp.where(mine, low, high)


class Sum:
    def __init__(self, me, partial):
        self.me = me
        self.bits = bits_of(lax.axis_size("ctx"))
        self.step = 0
        self.sums, self.send = split(me, partial, self.bits[0])

    def add(self, after, kernels=()):
        if self.step == len(self.bits):
            return []
        came = swap(self.send if self.step < 2 else self.sums, "ctx", self.bits[self.step])
        came = held_until([came], kernels)[0]
        self.sums, *send = added(self.me, self.sums, came, 0 if self.step else self.bits[1], after)
        self.send = send[0] if send else None
        self.step += 1
        return [self.sums]


def joined_kernel(bit, me_ref, own_ref, other_ref, out_ref):
    rows = own_ref.shape[0]
    mine = (me_ref[0] & bit) != 0
    out_ref[:rows] = jnp.where(mine, other_ref[...], own_ref[...]).astype(out_ref.dtype)
    out_ref[rows:] = jnp.where(mine, own_ref[...], other_ref[...]).astype(out_ref.dtype)


def joined(me, own, other, bit, dtype, after):
    rows, width = own.shape
    whole = pl.BlockSpec(own.shape, lambda i, me: (0, 0))
    return pl.pallas_call(
        ignoring(functools.partial(joined_kernel, bit), len(after), 3),
        grid_spec=pltpu.PrefetchScalarGridSpec(
            num_scalar_prefetch=1,
            grid=(1,),
            in_specs=[whole, whole] + [pl.BlockSpec(memory_space=pl.ANY)] * len(after),
            out_specs=pl.BlockSpec((2 * rows, width), lambda i, me: (0, 0)),
        ),
        out_shape=jax.ShapeDtypeStruct((2 * rows, width), dtype),
        compiler_params=pltpu.CompilerParams(vmem_limit_bytes=VMEM_BYTES),
        cost_estimate=estimate(0.5),
        name="joined",
    )(me, own, other, *after)


def per_device(query_proj, key_proj, value_proj, filters, out_weight, cotangent):
    length, channels = query_proj.shape
    taps = filters.shape[1]
    n_ctx, n_chan = lax.axis_size("ctx"), lax.axis_size("chan")
    me = jnp.stack([lax.axis_index("ctx"), lax.axis_index("chan")]).astype(jnp.int32)
    forward, late, early_rows, lags = [jnp.asarray(m) for m in transforms(taps)]

    product = (key_proj.astype(F32) * value_proj.astype(F32)).astype(BF16)
    product, cotangent = lax.optimization_barrier((product, cotangent))
    earlier = lax.ppermute(product, "ctx", [(i, i + 1) for i in range(n_ctx - 1)])

    cots = {0: cotangent, 1: swap(cotangent, "chan", 1)}
    for bit in reversed(bits_of(n_chan)[1:]):
        cots.update({off ^ bit: swap(cots[off], "chan", bit) for off in list(cots) if off % 2 == 0})
    offs = sorted(off for off in cots if off % 2 == 0 and off)
    sums = weight_pass(me, out_weight, 0, cot=cots[0])
    for off in offs:
        cots[off + 1] = swap(held_until([cots[off]], sums)[0], "chan", 1)
    offs = sorted(offs + [off + 1 for off in offs])

    sums = weight_pass(me, out_weight, 1, cot=cots[1], sums=sums)

    order = cycle_of(n_ctx)
    slots = []
    for c in range(n_ctx):
        spot = order.index(c)
        turn = [0, n_ctx // 2] + list(range(1, n_ctx // 2)) + list(range(1 - n_ctx // 2, 0))
        targets = [order[(spot + step) % n_ctx] for step in turn]
        slots.append([targets.index(target) for target in range(n_ctx)])
    pieces = pieces_of(me, jnp.asarray(slots, jnp.int32), [cots[off] for off in range(n_chan)], sums)

    gated, filtered = by_channel(
        forward_kernel,
        [query_proj, key_proj, value_proj, earlier, filters, forward, late],
        "ttttcww",
        [("t", BF16), ("t", F32)],
        "forward_filter",
        after=sums,
    )

    ahead = [(order[i], order[(i + 1) % n_ctx]) for i in range(n_ctx)]
    behind = [(b, a) for a, b in ahead]
    turns = n_ctx // 2
    rows, piece = length // n_ctx, channels // n_ctx
    span = (turns - 1) * rows
    ends = [
        jnp.concatenate([pieces[2 * rows : 2 * rows + span], gated], axis=0),
        jnp.concatenate([gated, pieces[2 * rows + span :]], axis=0),
    ]
    arrays, places, brought = [gated], [[(0, length)]], [pieces[:rows]]

    def passed_on(kernels):
        onto, back = held_until(ends, kernels)
        came = [lax.ppermute(onto, "ctx", ahead), lax.ppermute(back, "ctx", behind)]
        arrays.extend(came)
        places.extend([[(came[0].shape[0] - length, length)], [(0, length)]])
        brought.extend([came[0][:rows], came[1][-rows:]])
        ends[:] = [came[0][rows:], came[1][:-rows]]
        return came

    landed = passed_on([])
    terms = {}
    for off in offs[:-1]:
        *sums, terms[off] = weight_pass(me, out_weight, off, gated, cots[off], sums)
    grad_query, grad_filtered, terms[offs[-1]] = weight_pass(
        me, out_weight, offs[-1], gated, cots[offs[-1]], sums, [query_proj, filtered]
    )
    previous, landed = landed, passed_on([grad_filtered])

    tap_grad = by_channel(
        tap_grad_kernel,
        [key_proj, value_proj, earlier, grad_filtered, forward, lags],
        "ttttww",
        [("c", BF16)],
        "tap_grad",
        after=previous,
    )[0]
    from_core = []
    for off in [off for off in sorted(terms) if off % 2]:
        from_core.append(swap(terms.pop(off), "chan", 1))
        terms[off ^ 1] = terms[off ^ 1] + from_core[-1].astype(F32)
    mixed_one = weight_pass(me, out_weight, 1, gated, after=[tap_grad])[0]
    across = lax.ppermute(
        held_until([pieces[rows : 2 * rows]], [mixed_one])[0],
        "ctx",
        [(order[i], order[(i + turns) % n_ctx]) for i in range(n_ctx)],
    )
    brought.insert(1, across)
    tap_sum = Sum(me, held_until([tap_grad], [mixed_one])[0])
    previous, landed = landed, passed_on([mixed_one])
    last_part = weight_pass(me, out_weight, 0, gated, after=landed + [mixed_one])[0]

    terms = dict(zip(terms, held_until(terms.values(), previous)))
    terms[0] = last_part + swap(mixed_one, "chan", 1).astype(F32)
    to_chips = []
    for bit in bits_of(n_chan)[1:]:
        for off in [off for off in sorted(terms, reverse=True) if off & bit]:
            to_chips.append(terms.pop(off).astype(BF16))
            terms[off ^ bit] = terms[off ^ bit] + swap(to_chips[-1], "chan", bit).astype(F32)
    mixed = terms[0].astype(BF16)
    early = 2 + 2 * min(1, turns - 1)
    first = jnp.concatenate(held_until(brought[:early], previous), axis=0)

    for unused in range(turns - 4):
        landed = passed_on([last_part])
    half = length // 2
    cols = [gather_of_chips(first)]
    onto, back = held_until(ends, tap_sum.add((), landed) + [cols[0][off] for off in cols[0] if off] + to_chips[:1])
    far = [lax.ppermute(onto[:half], "ctx", ahead), lax.ppermute(back[half:], "ctx", behind)]
    arrays = arrays[:1] + far + arrays[1:]
    places.insert(1, [(0, half), (0, half)])

    cols.append(gather_of_chips(jnp.concatenate(brought[early:], axis=0)))

    given = held_until([grad_filtered], far)[0]
    following = lax.ppermute(given, "ctx", [(i + 1, i) for i in range(n_ctx - 1)])

    evens = [off for off in range(n_chan) if off % 2 == 0]
    wide = piece % 128 == 0 and 2 * early == n_ctx
    columns = {off: [(part[off], 0) for part in cols] for off in evens}
    crossed = jnp.concatenate([part[off] for off in evens for part in cols], axis=0)
    crossed = swap(held_until([crossed], far + [last_part])[0], "chan", 1)
    if wide:
        for at, off in enumerate(evens):
            columns[off + 1] = [(crossed, 2 * at), (crossed, 2 * at + 1)]
        columns = [columns[off] for off in range(n_chan)]
        low_half = grad_weight_of(me, arrays, places, columns, [])
        grad_weight = grad_weight_of(me, arrays, places, columns, [low_half])
    else:
        for at, off in enumerate(evens):
            columns[off + 1] = [(crossed[at * length : (at + 1) * length], 0)]
        pairs = [[array for array, unused in columns[off]] for off in range(n_chan)]
        low_half = grad_weight = narrow_grad_weight(me, arrays, places, pairs)

    tap_sum.add((), [low_half])
    while tap_sum.add((), [grad_weight]):
        pass
    own, bits = tap_sum.sums, tap_sum.bits
    grad_key, grad_value = by_channel(
        backward_kernel,
        [
            key_proj, value_proj, grad_filtered, held_until([following], [grad_weight])[0],
            filters, forward, early_rows,
        ],
        "ttttcww",
        [("t", BF16), ("t", BF16)],
        "backward_filter",
    )
    other = held_until([swap(own, "ctx", bits[1])], [grad_key])[0]
    own = joined(me, own, other, bits[1], BF16, ())
    grad_filters = joined(me, own, swap(own, "ctx", bits[0]), bits[0], F32, ())
    return (mixed, grad_query, grad_key, grad_value, grad_filters, grad_weight)


def solution(mesh):
    placed = (
        P("ctx", "chan"),
        P("ctx", "chan"),
        P("ctx", "chan"),
        P("chan", None),
        P("chan", None),
        P("ctx", "chan"),
    )
    return jax.shard_map(
        per_device,
        mesh=mesh,
        in_specs=placed,
        out_specs=(
            P("ctx", "chan"),
            P("ctx", "chan"),
            P("ctx", "chan"),
            P("ctx", "chan"),
            P("chan", None),
            P("chan", "ctx"),
        ),
        check_vma=False,
    )
```

```python
import functools

import jax
import jax.numpy as jnp
import numpy as np
from jax import lax
from jax.experimental import pallas as pl
from jax.experimental.pallas import tpu as pltpu
from jax.sharding import PartitionSpec as P

F32 = jnp.float32
BF16 = jnp.bfloat16
VMEM_BYTES = 40 * 2**20
NT = (((1,), (1,)), ((), ()))
TN = (((0,), (0,)), ((), ()))


def halves(matrix):
    high = matrix.astype(BF16)
    low = (matrix - high.astype(np.float64)).astype(BF16)
    return np.stack([high, low])


def transforms(taps):
    points = 2 * taps
    angle = np.pi * (2 * np.arange(taps)[:, None] + 1) * np.arange(points)[None, :] / points
    forward = np.concatenate([np.cos(angle), -np.sin(angle)], axis=0)
    inverse = forward.T * (2.0 / points)
    late = inverse[taps:]
    early = inverse[:taps]
    lags = inverse[taps - np.arange(taps)]
    return halves(forward), halves(late), halves(early), halves(lags)


def mm(a, b, dims=(((1,), (0,)), ((), ()))):
    return lax.dot_general(a, b, dims, preferred_element_type=F32)


def spectrum(f_ref, rows):
    return mm(f_ref[0], rows) + mm(f_ref[1], rows)


def tap_spectrum(f_ref, filters, taps):
    return mm(f_ref[0, :, :taps], filters, NT) + mm(f_ref[1, :, :taps], filters, NT)


def back(g_ref, real, imag):
    both = jnp.concatenate([real, imag], axis=0)
    high = both.astype(BF16)
    low = (both - high.astype(F32)).astype(BF16)
    return mm(g_ref[0], high) + mm(g_ref[0], low) + mm(g_ref[1], high)


def forward_kernel(taps, q_ref, k_ref, v_ref, earlier_ref, filt_ref, f_ref, g_ref, gated_ref, filtered_ref):
    product = (k_ref[...].astype(F32) * v_ref[...].astype(F32)).astype(BF16)
    x = spectrum(f_ref, jnp.concatenate([earlier_ref[...], product], axis=0))
    h = tap_spectrum(f_ref, filt_ref[...], taps)
    xr, xi, hr, hi = x[:taps], x[taps:], h[:taps], h[taps:]
    filtered = back(g_ref, xr * hr - xi * hi, xr * hi + xi * hr)
    filtered_ref[...] = filtered
    gated_ref[...] = (q_ref[...].astype(F32) * filtered).astype(BF16)


def tap_grad_kernel(taps, k_ref, v_ref, earlier_ref, gf_ref, f_ref, g_ref, out_ref):
    product = (k_ref[...].astype(F32) * v_ref[...].astype(F32)).astype(BF16)
    x = spectrum(f_ref, jnp.concatenate([earlier_ref[...], product], axis=0))
    rows = gf_ref[...]
    g = mm(f_ref[0, :, :taps], rows) + mm(f_ref[1, :, :taps], rows)
    xr, xi, gr, gi = x[:taps], x[taps:], g[:taps], g[taps:]
    tap_rows = back(g_ref, xr * gr + xi * gi, xi * gr - xr * gi)
    out_ref[...] = tap_rows.T.astype(BF16)


def backward_kernel(taps, k_ref, v_ref, gf_ref, following_ref, filt_ref, f_ref, g_ref, gk_ref, gv_ref):
    g = spectrum(f_ref, jnp.concatenate([gf_ref[...], following_ref[...]], axis=0))
    h = tap_spectrum(f_ref, filt_ref[...], taps)
    gr, gi, hr, hi = g[:taps], g[taps:], h[:taps], h[taps:]
    grad_product = back(g_ref, hr * gr + hi * gi, hr * gi - hi * gr)
    gk_ref[...] = (grad_product * v_ref[...].astype(F32)).astype(BF16)
    gv_ref[...] = (grad_product * k_ref[...].astype(F32)).astype(BF16)


def estimate(micros):
    return pl.CostEstimate(flops=int(micros * 10**9), bytes_accessed=0, transcendentals=0)


def ignoring(body, count, skip):
    def kernel(*refs):
        return body(*refs[:skip], *refs[skip + count :])

    return kernel


def by_channel(kernel, arrays, kinds, outs, name, after=()):
    length, channels = arrays[0].shape
    width = min(512, channels)
    specs = {
        "t": pl.BlockSpec((length, width), lambda i: (0, i)),
        "c": pl.BlockSpec((width, length), lambda i: (i, 0)),
    }

    def spec_of(kind, shape):
        if kind == "w":
            return pl.BlockSpec(shape, lambda i: (0,) * len(shape))
        return specs[kind]

    return pl.pallas_call(
        ignoring(functools.partial(kernel, length), len(after), len(arrays)),
        grid=(channels // width,),
        in_specs=[spec_of(kind, a.shape) for kind, a in zip(kinds, arrays)]
        + [pl.BlockSpec(memory_space=pl.ANY)] * len(after),
        out_specs=[specs[kind] for kind, unused in outs],
        out_shape=[
            jax.ShapeDtypeStruct((length, channels) if kind == "t" else (channels, length), dtype)
            for kind, dtype in outs
        ],
        compiler_params=pltpu.CompilerParams(vmem_limit_bytes=VMEM_BYTES),
        cost_estimate=estimate(3),
        name=name,
    )(*arrays, *after)


def pass_kernel(with_mixed, with_grad, has_sum, last, me_ref, w_ref, *refs):
    refs = list(refs)
    step = pl.program_id(0)
    if with_mixed:
        gated_ref = refs.pop(0)
    if with_grad:
        cot_ref = refs.pop(0)
        sum_ref = refs.pop(0) if has_sum else None
        turned_ref = refs.pop()

        @pl.when(step == 0)
        def turn():
            turned_ref[...] = cot_ref[...].T

        total = mm(w_ref[...], turned_ref[...])
        if has_sum:
            total = total + sum_ref[...]
        if last:
            q_ref, filtered_ref, gq_ref, gf_ref = refs[:4]
            total = total.T
            gq_ref[...] = (total * filtered_ref[...]).astype(BF16)
            gf_ref[...] = (total * q_ref[...].astype(F32)).astype(BF16)
        else:
            refs[0][...] = total
    if with_mixed:
        held_ref, mixed_ref = refs.pop(), refs.pop()
        part = mm(gated_ref[...], w_ref[...])

        @pl.when(step == 0)
        def first():
            held_ref[...] = part

        @pl.when(step > 0)
        def more():
            held_ref[...] = held_ref[...] + part

        @pl.when(step == pl.num_programs(0) - 1)
        def give():
            mixed_ref[...] = held_ref[...].astype(mixed_ref.dtype)


def weight_pass(me, weight, off, gated=None, cot=None, sums=(), ends=(), after=()):
    length = (cot if gated is None else gated).shape[0]
    channels = weight.shape[0]
    tile = 512
    whole = pl.BlockSpec((length, channels), lambda r, me: (0, 0))
    by_token = pl.BlockSpec((length, tile), lambda r, me: (0, r))
    by_row = pl.BlockSpec((tile, length), lambda r, me: (r, 0))
    arrays, in_specs = [weight], [pl.BlockSpec((tile, channels), lambda r, me: (r, me[1] ^ off))]
    out_specs, out_shape, scratch = [], [], []
    if gated is not None:
        arrays.append(gated)
        in_specs.append(by_token)
    if cot is not None:
        arrays += [cot, *sums, *ends]
        in_specs += [whole] + [by_row] * len(sums) + [by_token] * len(ends)
        out_specs += [by_token] * 2 if ends else [by_row]
        out_shape += [jax.ShapeDtypeStruct((length, channels), BF16)] * 2 if ends else [
            jax.ShapeDtypeStruct((channels, length), F32)
        ]
    if gated is not None:
        out_specs.append(whole)
        out_shape.append(jax.ShapeDtypeStruct((length, channels), BF16 if off % 2 else F32))
        scratch.append(pltpu.VMEM((length, channels), F32))
    if cot is not None:
        scratch.append(pltpu.VMEM((channels, length), BF16))
    body = functools.partial(pass_kernel, gated is not None, cot is not None, bool(sums), bool(ends))
    return pl.pallas_call(
        ignoring(body, len(after), 1 + len(arrays)),
        grid_spec=pltpu.PrefetchScalarGridSpec(
            num_scalar_prefetch=1,
            grid=(channels // tile,),
            in_specs=in_specs + [pl.BlockSpec(memory_space=pl.ANY)] * len(after),
            out_specs=out_specs,
            scratch_shapes=scratch,
        ),
        out_shape=out_shape,
        compiler_params=pltpu.CompilerParams(vmem_limit_bytes=VMEM_BYTES),
        cost_estimate=estimate(3 if gated is None else 0.5),
        name="grad_gated_part" if gated is None else "mixed_part" if cot is None else "grads_and_mixed",
    )(me, *arrays, *after)


def pieces_kernel(per_chan, me_ref, slot_ref, *refs):
    out_ref = refs[-1]
    length, width = refs[0].shape
    span = width // per_chan
    count = len(refs) - 1
    piece = span // count
    rows = length * piece // width
    for off in range(count):
        for part in range(per_chan):
            target = (me_ref[1] ^ off) * per_chan + part
            start = pl.multiple_of(part * span + me_ref[1] * piece, 128)
            block = refs[off][:, pl.ds(start, piece)]
            place = pl.multiple_of(slot_ref[me_ref[0], target] * rows, rows)
            out_ref[pl.ds(place, rows), :] = jnp.concatenate(
                [block[at : at + rows] for at in range(0, length, rows)], axis=1
            )


def pieces_of(me, slots, cots, after):
    length, width = cots[0].shape
    n_ctx = slots.shape[0]
    piece = width // n_ctx
    if piece % 128:
        return pieces_by_slices(me, slots, cots)
    return pl.pallas_call(
        ignoring(functools.partial(pieces_kernel, n_ctx // len(cots)), len(after), 2 + len(cots)),
        grid_spec=pltpu.PrefetchScalarGridSpec(
            num_scalar_prefetch=2,
            grid=(1,),
            in_specs=[pl.BlockSpec((length, width), lambda i, *ids: (0, 0))] * len(cots)
            + [pl.BlockSpec(memory_space=pl.ANY)] * len(after),
            out_specs=pl.BlockSpec((length, width), lambda i, *ids: (0, 0)),
        ),
        out_shape=jax.ShapeDtypeStruct((length, width), BF16),
        compiler_params=pltpu.CompilerParams(vmem_limit_bytes=VMEM_BYTES),
        cost_estimate=estimate(0.5),
        name="pieces",
    )(me, slots, *cots, *after)


def pieces_by_slices(me, slots, cots):
    length, width = cots[0].shape
    n_ctx, count = slots.shape[0], len(cots)
    piece, per_chan = width // n_ctx, n_ctx // count
    rows = length * piece // width
    table = jnp.stack(cots).reshape(count, length, per_chan, count, piece)
    mine = lax.dynamic_index_in_dim(table, me[1], 3, False)
    parts = mine.transpose(0, 2, 1, 3).reshape(n_ctx, length // rows, rows, piece)
    parts = parts.transpose(0, 2, 1, 3).reshape(n_ctx, rows, width)
    order = jnp.argsort(slots[me[0]])
    return parts[(order // per_chan ^ me[1]) * per_chan + order % per_chan].reshape(length, width)


def weight_kernel(places, parts, me_ref, *refs):
    out_ref = refs[-1]
    length = sum(rows for unused, rows in places[0])
    blocks = []
    at = 0
    for place in places:
        for start, rows in place:
            blocks.append(refs[at][start : start + rows, :])
            at += 1
    columns = jnp.concatenate(blocks, axis=0)
    for part in range(parts):
        packed = jnp.concatenate([ref[...] for ref in refs[at + 2 * part : at + 2 * part + 2]], axis=0)
        rows = packed.shape[0] // len(places)
        piece = packed.shape[1] * rows // length
        wide = [
            packed[slot * rows : (slot + 1) * rows, lane : lane + piece]
            for slot in range(len(places))
            for lane in range(0, packed.shape[1], piece)
        ]
        total = mm(columns, jnp.concatenate(wide, axis=0), TN)
        place = pl.multiple_of((me_ref[1] ^ part) * piece, piece)
        out_ref[:, pl.ds(place, piece)] = total.astype(BF16)


def grad_weight_of(me, arrays, places, cots, earlier):
    channels = arrays[0].shape[1]
    slots, parts = len(places), len(cots)
    pieces = [array for pair in cots for array, unused in pair]
    half = cots[0][0][0].shape[0]
    tile = 256
    width = 2 * half * channels // (slots * sum(count for unused, count in places[0])) * parts
    steps = channels // tile // 2
    first = steps * len(earlier)
    count = 1 + len(arrays) + len(pieces)
    return pl.pallas_call(
        ignoring(functools.partial(weight_kernel, places, parts), len(earlier), count),
        grid_spec=pltpu.PrefetchScalarGridSpec(
            num_scalar_prefetch=1,
            grid=(steps,),
            in_specs=[pl.BlockSpec((array.shape[0], tile), lambda i, me: (0, first + i)) for array in arrays]
            + [pl.BlockSpec((half, channels), lambda i, me, at=at: (at, 0)) for pair in cots for unused, at in pair]
            + [pl.BlockSpec(memory_space=pl.ANY)] * len(earlier),
            out_specs=pl.BlockSpec((tile, width), lambda i, me: (first + i, 0)),
        ),
        out_shape=jax.ShapeDtypeStruct((channels, width), BF16),
        input_output_aliases={count: 0} if earlier else {},
        compiler_params=pltpu.CompilerParams(vmem_limit_bytes=VMEM_BYTES),
        cost_estimate=estimate(2),
        name="grad_weight",
    )(me, *arrays, *pieces, *earlier)


def narrow_grad_weight(me, arrays, places, cots):
    blocks, at = [], 0
    for place in places:
        for start, rows in place:
            blocks.append(arrays[at][start : start + rows])
            at += 1
    columns = jnp.concatenate(blocks, axis=0)
    length = columns.shape[0] // len(places)
    packed = jnp.stack([jnp.concatenate(pair, axis=0) for pair in cots])
    packed = packed[jnp.arange(len(cots), dtype=jnp.int32) ^ me[1]]
    parts, height, width = packed.shape
    rows = height // len(places)
    piece = rows * width // length
    wide = packed.reshape(parts, len(places), rows, length // rows, piece).transpose(1, 3, 2, 0, 4)
    return mm(columns, wide.reshape(columns.shape[0], parts * piece), TN).astype(BF16)


def cycle_of(count):
    across = 1 << ((count.bit_length() - 1) // 2)
    order = []
    for column in range(across):
        line = [row * across + column for row in range(count // across)]
        order += line if column % 2 == 0 else line[::-1]
    return order


def held_until(arrays, kernels):
    return lax.optimization_barrier((*arrays, *kernels))[: len(arrays)]


def swap(block, axis, bit):
    size = lax.axis_size(axis)
    return lax.ppermute(block, axis, [(i, i ^ bit) for i in range(size)])


def bits_of(size):
    return [1 << place for place in range(size.bit_length() - 1)]


def gather_of_chips(block):
    held = {0: block}
    for bit in reversed(bits_of(lax.axis_size("chan"))[1:]):
        held.update({off ^ bit: swap(held[off], "chan", bit) for off in list(held)})
    return held


def added_kernel(bit, me_ref, own_ref, came_ref, *outs):
    total = (own_ref[...].astype(F32) + came_ref[...].astype(F32)).astype(BF16)
    if not bit:
        outs[0][...] = total
        return
    rows = outs[0].shape[0]
    mine = (me_ref[0] & bit) != 0
    outs[0][...] = jnp.where(mine, total[rows:], total[:rows])
    outs[1][...] = jnp.where(mine, total[:rows], total[rows:])


def added(me, own, came, bit, after):
    shape = (own.shape[0] // 2, own.shape[1]) if bit else own.shape
    whole = pl.BlockSpec(own.shape, lambda i, me: (0, 0))
    outs = 2 if bit else 1
    return pl.pallas_call(
        ignoring(functools.partial(added_kernel, bit), len(after), 3),
        grid_spec=pltpu.PrefetchScalarGridSpec(
            num_scalar_prefetch=1,
            grid=(1,),
            in_specs=[whole, whole] + [pl.BlockSpec(memory_space=pl.ANY)] * len(after),
            out_specs=[pl.BlockSpec(shape, lambda i, me: (0, 0))] * outs,
        ),
        out_shape=[jax.ShapeDtypeStruct(shape, BF16)] * outs,
        compiler_params=pltpu.CompilerParams(vmem_limit_bytes=VMEM_BYTES),
        cost_estimate=estimate(0.5),
        name="added",
    )(me, own, came, *after)


def split(me, block, bit):
    rows = block.shape[0] // 2
    mine = (me[0] & bit) != 0
    low, high = block[:rows], block[rows:]
    return jnp.where(mine, high, low), jnp.where(mine, low, high)


class Sum:
    def __init__(self, me, partial):
        self.me = me
        self.bits = bits_of(lax.axis_size("ctx"))
        self.step = 0
        self.sums, self.send = split(me, partial, self.bits[0])

    def add(self, after, kernels=()):
        if self.step == len(self.bits):
            return []
        came = swap(self.send if self.step < 2 else self.sums, "ctx", self.bits[self.step])
        came = held_until([came], kernels)[0]
        self.sums, *send = added(self.me, self.sums, came, 0 if self.step else self.bits[1], after)
        self.send = send[0] if send else None
        self.step += 1
        return [self.sums]


def joined_kernel(bit, me_ref, own_ref, other_ref, out_ref):
    rows = own_ref.shape[0]
    mine = (me_ref[0] & bit) != 0
    out_ref[:rows] = jnp.where(mine, other_ref[...], own_ref[...]).astype(out_ref.dtype)
    out_ref[rows:] = jnp.where(mine, own_ref[...], other_ref[...]).astype(out_ref.dtype)


def joined(me, own, other, bit, dtype, after):
    rows, width = own.shape
    whole = pl.BlockSpec(own.shape, lambda i, me: (0, 0))
    return pl.pallas_call(
        ignoring(functools.partial(joined_kernel, bit), len(after), 3),
        grid_spec=pltpu.PrefetchScalarGridSpec(
            num_scalar_prefetch=1,
            grid=(1,),
            in_specs=[whole, whole] + [pl.BlockSpec(memory_space=pl.ANY)] * len(after),
            out_specs=pl.BlockSpec((2 * rows, width), lambda i, me: (0, 0)),
        ),
        out_shape=jax.ShapeDtypeStruct((2 * rows, width), dtype),
        compiler_params=pltpu.CompilerParams(vmem_limit_bytes=VMEM_BYTES),
        cost_estimate=estimate(0.5),
        name="joined",
    )(me, own, other, *after)


def per_device(query_proj, key_proj, value_proj, filters, out_weight, cotangent):
    length, channels = query_proj.shape
    taps = filters.shape[1]
    n_ctx, n_chan = lax.axis_size("ctx"), lax.axis_size("chan")
    me = jnp.stack([lax.axis_index("ctx"), lax.axis_index("chan")]).astype(jnp.int32)
    forward, late, early_rows, lags = [jnp.asarray(m) for m in transforms(taps)]

    product = (key_proj.astype(F32) * value_proj.astype(F32)).astype(BF16)
    product, cotangent = lax.optimization_barrier((product, cotangent))
    earlier = lax.ppermute(product, "ctx", [(i, i + 1) for i in range(n_ctx - 1)])

    cots = {0: cotangent, 1: swap(cotangent, "chan", 1)}
    for bit in reversed(bits_of(n_chan)[1:]):
        cots.update({off ^ bit: swap(cots[off], "chan", bit) for off in list(cots) if off % 2 == 0})
    offs = sorted(off for off in cots if off % 2 == 0 and off)
    sums = weight_pass(me, out_weight, 0, cot=cots[0])
    for off in offs:
        cots[off + 1] = swap(held_until([cots[off]], sums)[0], "chan", 1)
    offs = sorted(offs + [off + 1 for off in offs])

    sums = weight_pass(me, out_weight, 1, cot=cots[1], sums=sums)

    order = cycle_of(n_ctx)
    slots = []
    for c in range(n_ctx):
        spot = order.index(c)
        turn = [0, n_ctx // 2] + list(range(1, n_ctx // 2)) + list(range(1 - n_ctx // 2, 0))
        targets = [order[(spot + step) % n_ctx] for step in turn]
        slots.append([targets.index(target) for target in range(n_ctx)])
    pieces = pieces_of(me, jnp.asarray(slots, jnp.int32), [cots[off] for off in range(n_chan)], sums)

    gated, filtered = by_channel(
        forward_kernel,
        [query_proj, key_proj, value_proj, earlier, filters, forward, late],
        "ttttcww",
        [("t", BF16), ("t", F32)],
        "forward_filter",
        after=sums,
    )

    ahead = [(order[i], order[(i + 1) % n_ctx]) for i in range(n_ctx)]
    behind = [(b, a) for a, b in ahead]
    turns = n_ctx // 2
    rows, piece = length // n_ctx, channels // n_ctx
    span = (turns - 1) * rows
    ends = [
        jnp.concatenate([pieces[2 * rows : 2 * rows + span], gated], axis=0),
        jnp.concatenate([gated, pieces[2 * rows + span :]], axis=0),
    ]
    arrays, places, brought = [gated], [[(0, length)]], [pieces[:rows]]

    def passed_on(kernels):
        onto, back = held_until(ends, kernels)
        came = [lax.ppermute(onto, "ctx", ahead), lax.ppermute(back, "ctx", behind)]
        arrays.extend(came)
        places.extend([[(came[0].shape[0] - length, length)], [(0, length)]])
        brought.extend([came[0][:rows], came[1][-rows:]])
        ends[:] = [came[0][rows:], came[1][:-rows]]
        return came

    landed = passed_on([])
    terms = {}
    for off in offs[:-1]:
        *sums, terms[off] = weight_pass(me, out_weight, off, gated, cots[off], sums)
    grad_query, grad_filtered, terms[offs[-1]] = weight_pass(
        me, out_weight, offs[-1], gated, cots[offs[-1]], sums, [query_proj, filtered]
    )
    previous, landed = landed, passed_on([grad_filtered])

    tap_grad = by_channel(
        tap_grad_kernel,
        [key_proj, value_proj, earlier, grad_filtered, forward, lags],
        "ttttww",
        [("c", BF16)],
        "tap_grad",
        after=previous,
    )[0]
    from_core = []
    for off in [off for off in sorted(terms) if off % 2]:
        from_core.append(swap(terms.pop(off), "chan", 1))
        terms[off ^ 1] = terms[off ^ 1] + from_core[-1].astype(F32)
    mixed_one = weight_pass(me, out_weight, 1, gated, after=[tap_grad])[0]
    across = lax.ppermute(
        held_until([pieces[rows : 2 * rows]], [mixed_one])[0],
        "ctx",
        [(order[i], order[(i + turns) % n_ctx]) for i in range(n_ctx)],
    )
    brought.insert(1, across)
    tap_sum = Sum(me, held_until([tap_grad], [mixed_one])[0])
    previous, landed = landed, passed_on([mixed_one])
    given = held_until([grad_filtered], previous)[0]
    following = lax.ppermute(given, "ctx", [(i + 1, i) for i in range(n_ctx - 1)])
    last_part = weight_pass(me, out_weight, 0, gated, after=landed + [mixed_one, following])[0]

    terms = dict(zip(terms, held_until(terms.values(), previous)))
    terms[0] = last_part + swap(mixed_one, "chan", 1).astype(F32)
    to_chips = []
    for bit in bits_of(n_chan)[1:]:
        for off in [off for off in sorted(terms, reverse=True) if off & bit]:
            to_chips.append(terms.pop(off).astype(BF16))
            terms[off ^ bit] = terms[off ^ bit] + swap(to_chips[-1], "chan", bit).astype(F32)
    mixed = terms[0].astype(BF16)
    early = 2 + 2 * min(1, turns - 1)
    first = jnp.concatenate(held_until(brought[:early], previous), axis=0)

    for unused in range(turns - 4):
        landed = passed_on([last_part])
    half = length // 2
    cols = [gather_of_chips(first)]
    onto, back = held_until(ends, tap_sum.add((), landed) + [cols[0][off] for off in cols[0] if off] + to_chips[:1])
    far = [lax.ppermute(onto[:half], "ctx", ahead), lax.ppermute(back[half:], "ctx", behind)]
    arrays = arrays[:1] + far + arrays[1:]
    places.insert(1, [(0, half), (0, half)])

    cols.append(gather_of_chips(jnp.concatenate(brought[early:], axis=0)))

    evens = [off for off in range(n_chan) if off % 2 == 0]
    wide = piece % 128 == 0 and 2 * early == n_ctx
    columns = {off: [(part[off], 0) for part in cols] for off in evens}
    crossed = jnp.concatenate([part[off] for off in evens for part in cols], axis=0)
    crossed = swap(held_until([crossed], far + [last_part])[0], "chan", 1)
    if wide:
        for at, off in enumerate(evens):
            columns[off + 1] = [(crossed, 2 * at), (crossed, 2 * at + 1)]
        columns = [columns[off] for off in range(n_chan)]
        low_half = grad_weight_of(me, arrays, places, columns, [])
        grad_weight = grad_weight_of(me, arrays, places, columns, [low_half])
    else:
        for at, off in enumerate(evens):
            columns[off + 1] = [(crossed[at * length : (at + 1) * length], 0)]
        pairs = [[array for array, unused in columns[off]] for off in range(n_chan)]
        low_half = grad_weight = narrow_grad_weight(me, arrays, places, pairs)

    tap_sum.add((), [low_half])
    while tap_sum.add((), [grad_weight]):
        pass
    own, bits = tap_sum.sums, tap_sum.bits
    grad_key, grad_value = by_channel(
        backward_kernel,
        [
            key_proj, value_proj, grad_filtered, held_until([following], [grad_weight])[0],
            filters, forward, early_rows,
        ],
        "ttttcww",
        [("t", BF16), ("t", BF16)],
        "backward_filter",
    )
    other = held_until([swap(own, "ctx", bits[1])], [grad_key])[0]
    own = joined(me, own, other, bits[1], BF16, ())
    grad_filters = joined(me, own, swap(own, "ctx", bits[0]), bits[0], F32, ())
    return (mixed, grad_query, grad_key, grad_value, grad_filters, grad_weight)


def solution(mesh):
    placed = (
        P("ctx", "chan"),
        P("ctx", "chan"),
        P("ctx", "chan"),
        P("chan", None),
        P("chan", None),
        P("ctx", "chan"),
    )
    return jax.shard_map(
        per_device,
        mesh=mesh,
        in_specs=placed,
        out_specs=(
            P("ctx", "chan"),
            P("ctx", "chan"),
            P("ctx", "chan"),
            P("ctx", "chan"),
            P("chan", None),
            P("chan", "ctx"),
        ),
        check_vma=False,
    )
```

```python
import functools

import jax
import jax.numpy as jnp
import numpy as np
from jax import lax
from jax.experimental import pallas as pl
from jax.experimental.pallas import tpu as pltpu
from jax.sharding import PartitionSpec as P

F32 = jnp.float32
BF16 = jnp.bfloat16
VMEM_BYTES = 20 * 2**20
NT = (((1,), (1,)), ((), ()))
TN = (((0,), (0,)), ((), ()))


def halves(matrix):
    high = matrix.astype(BF16)
    low = (matrix - high.astype(np.float64)).astype(BF16)
    return np.stack([high, low])


def transforms(taps):
    points = 2 * taps
    angle = np.pi * (2 * np.arange(taps)[:, None] + 1) * np.arange(points)[None, :] / points
    forward = np.concatenate([np.cos(angle), -np.sin(angle)], axis=0)
    inverse = forward.T * (2.0 / points)
    late = inverse[taps:]
    early = inverse[:taps]
    lags = inverse[taps - np.arange(taps)]
    return halves(forward), halves(late), halves(early), halves(lags)


def mm(a, b, dims=(((1,), (0,)), ((), ()))):
    return lax.dot_general(a, b, dims, preferred_element_type=F32)


def spectrum(f_ref, rows):
    return mm(f_ref[0], rows) + mm(f_ref[1], rows)


def tap_spectrum(f_ref, filters, taps):
    return mm(f_ref[0, :, :taps], filters, NT) + mm(f_ref[1, :, :taps], filters, NT)


def back(g_ref, real, imag):
    both = jnp.concatenate([real, imag], axis=0)
    high = both.astype(BF16)
    low = (both - high.astype(F32)).astype(BF16)
    return mm(g_ref[0], high) + mm(g_ref[0], low) + mm(g_ref[1], high)


def forward_kernel(taps, q_ref, k_ref, v_ref, earlier_ref, filt_ref, f_ref, g_ref, gated_ref, filtered_ref):
    product = (k_ref[...].astype(F32) * v_ref[...].astype(F32)).astype(BF16)
    x = spectrum(f_ref, jnp.concatenate([earlier_ref[...], product], axis=0))
    h = tap_spectrum(f_ref, filt_ref[...], taps)
    xr, xi, hr, hi = x[:taps], x[taps:], h[:taps], h[taps:]
    filtered = back(g_ref, xr * hr - xi * hi, xr * hi + xi * hr)
    filtered_ref[...] = filtered
    gated_ref[...] = (q_ref[...].astype(F32) * filtered).astype(BF16)


def tap_grad_kernel(taps, k_ref, v_ref, earlier_ref, gf_ref, f_ref, g_ref, out_ref):
    product = (k_ref[...].astype(F32) * v_ref[...].astype(F32)).astype(BF16)
    x = spectrum(f_ref, jnp.concatenate([earlier_ref[...], product], axis=0))
    rows = gf_ref[...]
    g = mm(f_ref[0, :, :taps], rows) + mm(f_ref[1, :, :taps], rows)
    xr, xi, gr, gi = x[:taps], x[taps:], g[:taps], g[taps:]
    tap_rows = back(g_ref, xr * gr + xi * gi, xi * gr - xr * gi)
    out_ref[...] = tap_rows.T.astype(BF16)


def backward_kernel(taps, k_ref, v_ref, gf_ref, following_ref, filt_ref, f_ref, g_ref, gk_ref, gv_ref):
    g = spectrum(f_ref, jnp.concatenate([gf_ref[...], following_ref[...]], axis=0))
    h = tap_spectrum(f_ref, filt_ref[...], taps)
    gr, gi, hr, hi = g[:taps], g[taps:], h[:taps], h[taps:]
    grad_product = back(g_ref, hr * gr + hi * gi, hr * gi - hi * gr)
    gk_ref[...] = (grad_product * v_ref[...].astype(F32)).astype(BF16)
    gv_ref[...] = (grad_product * k_ref[...].astype(F32)).astype(BF16)


def estimate(micros):
    return pl.CostEstimate(flops=int(micros * 10**9), bytes_accessed=0, transcendentals=0)


def ignoring(body, count, skip):
    def kernel(*refs):
        return body(*refs[:skip], *refs[skip + count :])

    return kernel


def by_channel(kernel, arrays, kinds, outs, name, after=()):
    length, channels = arrays[0].shape
    width = min(512, channels)
    specs = {
        "t": pl.BlockSpec((length, width), lambda i: (0, i)),
        "c": pl.BlockSpec((width, length), lambda i: (i, 0)),
    }

    def spec_of(kind, shape):
        if kind == "w":
            return pl.BlockSpec(shape, lambda i: (0,) * len(shape))
        return specs[kind]

    return pl.pallas_call(
        ignoring(functools.partial(kernel, length), len(after), len(arrays)),
        grid=(channels // width,),
        in_specs=[spec_of(kind, a.shape) for kind, a in zip(kinds, arrays)]
        + [pl.BlockSpec(memory_space=pl.ANY)] * len(after),
        out_specs=[specs[kind] for kind, unused in outs],
        out_shape=[
            jax.ShapeDtypeStruct((length, channels) if kind == "t" else (channels, length), dtype)
            for kind, dtype in outs
        ],
        compiler_params=pltpu.CompilerParams(vmem_limit_bytes=VMEM_BYTES),
        cost_estimate=estimate(3),
        name=name,
    )(*arrays, *after)


def pass_kernel(with_mixed, with_grad, has_sum, last, me_ref, w_ref, *refs):
    refs = list(refs)
    step = pl.program_id(0)
    if with_mixed:
        gated_ref = refs.pop(0)
    if with_grad:
        cot_ref = refs.pop(0)
        sum_ref = refs.pop(0) if has_sum else None
        turned_ref = refs.pop()

        @pl.when(step == 0)
        def turn():
            turned_ref[...] = cot_ref[...].T

        total = mm(w_ref[...], turned_ref[...])
        if has_sum:
            total = total + sum_ref[...]
        if last:
            q_ref, filtered_ref, gq_ref, gf_ref = refs[:4]
            total = total.T
            gq_ref[...] = (total * filtered_ref[...]).astype(BF16)
            gf_ref[...] = (total * q_ref[...].astype(F32)).astype(BF16)
        else:
            refs[0][...] = total
    if with_mixed:
        held_ref, mixed_ref = refs.pop(), refs.pop()
        part = mm(gated_ref[...], w_ref[...])

        @pl.when(step == 0)
        def first():
            held_ref[...] = part

        @pl.when(step > 0)
        def more():
            held_ref[...] = held_ref[...] + part

        @pl.when(step == pl.num_programs(0) - 1)
        def give():
            mixed_ref[...] = held_ref[...].astype(mixed_ref.dtype)


def weight_pass(me, weight, off, gated=None, cot=None, sums=(), ends=(), after=()):
    length = (cot if gated is None else gated).shape[0]
    channels = weight.shape[0]
    tile = 512
    whole = pl.BlockSpec((length, channels), lambda r, me: (0, 0))
    by_token = pl.BlockSpec((length, tile), lambda r, me: (0, r))
    by_row = pl.BlockSpec((tile, length), lambda r, me: (r, 0))
    arrays, in_specs = [weight], [pl.BlockSpec((tile, channels), lambda r, me: (r, me[1] ^ off))]
    out_specs, out_shape, scratch = [], [], []
    if gated is not None:
        arrays.append(gated)
        in_specs.append(by_token)
    if cot is not None:
        arrays += [cot, *sums, *ends]
        in_specs += [whole] + [by_row] * len(sums) + [by_token] * len(ends)
        out_specs += [by_token] * 2 if ends else [by_row]
        out_shape += [jax.ShapeDtypeStruct((length, channels), BF16)] * 2 if ends else [
            jax.ShapeDtypeStruct((channels, length), F32)
        ]
    if gated is not None:
        out_specs.append(whole)
        out_shape.append(jax.ShapeDtypeStruct((length, channels), BF16 if off % 2 else F32))
        scratch.append(pltpu.VMEM((length, channels), F32))
    if cot is not None:
        scratch.append(pltpu.VMEM((channels, length), BF16))
    body = functools.partial(pass_kernel, gated is not None, cot is not None, bool(sums), bool(ends))
    return pl.pallas_call(
        ignoring(body, len(after), 1 + len(arrays)),
        grid_spec=pltpu.PrefetchScalarGridSpec(
            num_scalar_prefetch=1,
            grid=(channels // tile,),
            in_specs=in_specs + [pl.BlockSpec(memory_space=pl.ANY)] * len(after),
            out_specs=out_specs,
            scratch_shapes=scratch,
        ),
        out_shape=out_shape,
        compiler_params=pltpu.CompilerParams(vmem_limit_bytes=VMEM_BYTES),
        cost_estimate=estimate(3 if gated is None else 0.5),
        name="grad_gated_part" if gated is None else "mixed_part" if cot is None else "grads_and_mixed",
    )(me, *arrays, *after)


def pieces_kernel(per_chan, me_ref, slot_ref, *refs):
    out_ref = refs[-1]
    length, width = refs[0].shape
    span = width // per_chan
    count = len(refs) - 1
    piece = span // count
    rows = length * piece // width
    for off in range(count):
        for part in range(per_chan):
            target = (me_ref[1] ^ off) * per_chan + part
            start = pl.multiple_of(part * span + me_ref[1] * piece, 128)
            block = refs[off][:, pl.ds(start, piece)]
            place = pl.multiple_of(slot_ref[me_ref[0], target] * rows, rows)
            out_ref[pl.ds(place, rows), :] = jnp.concatenate(
                [block[at : at + rows] for at in range(0, length, rows)], axis=1
            )


def pieces_of(me, slots, cots, after):
    length, width = cots[0].shape
    n_ctx = slots.shape[0]
    piece = width // n_ctx
    if piece % 128:
        return pieces_by_slices(me, slots, cots)
    return pl.pallas_call(
        ignoring(functools.partial(pieces_kernel, n_ctx // len(cots)), len(after), 2 + len(cots)),
        grid_spec=pltpu.PrefetchScalarGridSpec(
            num_scalar_prefetch=2,
            grid=(1,),
            in_specs=[pl.BlockSpec((length, width), lambda i, *ids: (0, 0))] * len(cots)
            + [pl.BlockSpec(memory_space=pl.ANY)] * len(after),
            out_specs=pl.BlockSpec((length, width), lambda i, *ids: (0, 0)),
        ),
        out_shape=jax.ShapeDtypeStruct((length, width), BF16),
        compiler_params=pltpu.CompilerParams(vmem_limit_bytes=VMEM_BYTES),
        cost_estimate=estimate(0.5),
        name="pieces",
    )(me, slots, *cots, *after)


def pieces_by_slices(me, slots, cots):
    length, width = cots[0].shape
    n_ctx, count = slots.shape[0], len(cots)
    piece, per_chan = width // n_ctx, n_ctx // count
    rows = length * piece // width
    table = jnp.stack(cots).reshape(count, length, per_chan, count, piece)
    mine = lax.dynamic_index_in_dim(table, me[1], 3, False)
    parts = mine.transpose(0, 2, 1, 3).reshape(n_ctx, length // rows, rows, piece)
    parts = parts.transpose(0, 2, 1, 3).reshape(n_ctx, rows, width)
    order = jnp.argsort(slots[me[0]])
    return parts[(order // per_chan ^ me[1]) * per_chan + order % per_chan].reshape(length, width)


def weight_kernel(places, parts, me_ref, *refs):
    out_ref = refs[-1]
    length = sum(rows for unused, rows in places[0])
    blocks = []
    at = 0
    for place in places:
        for start, rows in place:
            blocks.append(refs[at][start : start + rows, :])
            at += 1
    columns = jnp.concatenate(blocks, axis=0)
    for part in range(parts):
        packed = jnp.concatenate([ref[...] for ref in refs[at + 2 * part : at + 2 * part + 2]], axis=0)
        rows = packed.shape[0] // len(places)
        piece = packed.shape[1] * rows // length
        wide = [
            packed[slot * rows : (slot + 1) * rows, lane : lane + piece]
            for slot in range(len(places))
            for lane in range(0, packed.shape[1], piece)
        ]
        total = mm(columns, jnp.concatenate(wide, axis=0), TN)
        place = pl.multiple_of((me_ref[1] ^ part) * piece, piece)
        out_ref[:, pl.ds(place, piece)] = total.astype(BF16)


def grad_weight_of(me, arrays, places, cots, earlier):
    channels = arrays[0].shape[1]
    slots, parts = len(places), len(cots)
    pieces = [array for pair in cots for array, unused in pair]
    half = cots[0][0][0].shape[0]
    tile = 256
    width = 2 * half * channels // (slots * sum(count for unused, count in places[0])) * parts
    steps = channels // tile // 2
    first = steps * len(earlier)
    count = 1 + len(arrays) + len(pieces)
    return pl.pallas_call(
        ignoring(functools.partial(weight_kernel, places, parts), len(earlier), count),
        grid_spec=pltpu.PrefetchScalarGridSpec(
            num_scalar_prefetch=1,
            grid=(steps,),
            in_specs=[pl.BlockSpec((array.shape[0], tile), lambda i, me: (0, first + i)) for array in arrays]
            + [pl.BlockSpec((half, channels), lambda i, me, at=at: (at, 0)) for pair in cots for unused, at in pair]
            + [pl.BlockSpec(memory_space=pl.ANY)] * len(earlier),
            out_specs=pl.BlockSpec((tile, width), lambda i, me: (first + i, 0)),
        ),
        out_shape=jax.ShapeDtypeStruct((channels, width), BF16),
        input_output_aliases={count: 0} if earlier else {},
        compiler_params=pltpu.CompilerParams(vmem_limit_bytes=VMEM_BYTES),
        cost_estimate=estimate(2),
        name="grad_weight",
    )(me, *arrays, *pieces, *earlier)


def narrow_grad_weight(me, arrays, places, cots):
    blocks, at = [], 0
    for place in places:
        for start, rows in place:
            blocks.append(arrays[at][start : start + rows])
            at += 1
    columns = jnp.concatenate(blocks, axis=0)
    length = columns.shape[0] // len(places)
    packed = jnp.stack([jnp.concatenate(pair, axis=0) for pair in cots])
    packed = packed[jnp.arange(len(cots), dtype=jnp.int32) ^ me[1]]
    parts, height, width = packed.shape
    rows = height // len(places)
    piece = rows * width // length
    wide = packed.reshape(parts, len(places), rows, length // rows, piece).transpose(1, 3, 2, 0, 4)
    return mm(columns, wide.reshape(columns.shape[0], parts * piece), TN).astype(BF16)


def cycle_of(count):
    across = 1 << ((count.bit_length() - 1) // 2)
    order = []
    for column in range(across):
        line = [row * across + column for row in range(count // across)]
        order += line if column % 2 == 0 else line[::-1]
    return order


def held_until(arrays, kernels):
    return lax.optimization_barrier((*arrays, *kernels))[: len(arrays)]


def swap(block, axis, bit):
    size = lax.axis_size(axis)
    return lax.ppermute(block, axis, [(i, i ^ bit) for i in range(size)])


def bits_of(size):
    return [1 << place for place in range(size.bit_length() - 1)]


def gather_of_chips(block):
    held = {0: block}
    for bit in reversed(bits_of(lax.axis_size("chan"))[1:]):
        held.update({off ^ bit: swap(held[off], "chan", bit) for off in list(held)})
    return held


def added_kernel(bit, me_ref, own_ref, came_ref, *outs):
    total = (own_ref[...].astype(F32) + came_ref[...].astype(F32)).astype(BF16)
    if not bit:
        outs[0][...] = total
        return
    rows = outs[0].shape[0]
    mine = (me_ref[0] & bit) != 0
    outs[0][...] = jnp.where(mine, total[rows:], total[:rows])
    outs[1][...] = jnp.where(mine, total[:rows], total[rows:])


def added(me, own, came, bit, after):
    shape = (own.shape[0] // 2, own.shape[1]) if bit else own.shape
    whole = pl.BlockSpec(own.shape, lambda i, me: (0, 0))
    outs = 2 if bit else 1
    return pl.pallas_call(
        ignoring(functools.partial(added_kernel, bit), len(after), 3),
        grid_spec=pltpu.PrefetchScalarGridSpec(
            num_scalar_prefetch=1,
            grid=(1,),
            in_specs=[whole, whole] + [pl.BlockSpec(memory_space=pl.ANY)] * len(after),
            out_specs=[pl.BlockSpec(shape, lambda i, me: (0, 0))] * outs,
        ),
        out_shape=[jax.ShapeDtypeStruct(shape, BF16)] * outs,
        compiler_params=pltpu.CompilerParams(vmem_limit_bytes=VMEM_BYTES),
        cost_estimate=estimate(0.5),
        name="added",
    )(me, own, came, *after)


def split(me, block, bit):
    rows = block.shape[0] // 2
    mine = (me[0] & bit) != 0
    low, high = block[:rows], block[rows:]
    return jnp.where(mine, high, low), jnp.where(mine, low, high)


class Sum:
    def __init__(self, me, partial):
        self.me = me
        self.bits = bits_of(lax.axis_size("ctx"))
        self.step = 0
        self.sums, self.send = split(me, partial, self.bits[0])

    def add(self, after, kernels=()):
        if self.step == len(self.bits):
            return []
        came = swap(self.send if self.step < 2 else self.sums, "ctx", self.bits[self.step])
        came = held_until([came], kernels)[0]
        self.sums, *send = added(self.me, self.sums, came, 0 if self.step else self.bits[1], after)
        self.send = send[0] if send else None
        self.step += 1
        return [self.sums]


def joined_kernel(bit, me_ref, own_ref, other_ref, out_ref):
    rows = own_ref.shape[0]
    mine = (me_ref[0] & bit) != 0
    out_ref[:rows] = jnp.where(mine, other_ref[...], own_ref[...]).astype(out_ref.dtype)
    out_ref[rows:] = jnp.where(mine, own_ref[...], other_ref[...]).astype(out_ref.dtype)


def joined(me, own, other, bit, dtype, after):
    rows, width = own.shape
    whole = pl.BlockSpec(own.shape, lambda i, me: (0, 0))
    return pl.pallas_call(
        ignoring(functools.partial(joined_kernel, bit), len(after), 3),
        grid_spec=pltpu.PrefetchScalarGridSpec(
            num_scalar_prefetch=1,
            grid=(1,),
            in_specs=[whole, whole] + [pl.BlockSpec(memory_space=pl.ANY)] * len(after),
            out_specs=pl.BlockSpec((2 * rows, width), lambda i, me: (0, 0)),
        ),
        out_shape=jax.ShapeDtypeStruct((2 * rows, width), dtype),
        compiler_params=pltpu.CompilerParams(vmem_limit_bytes=VMEM_BYTES),
        cost_estimate=estimate(0.5),
        name="joined",
    )(me, own, other, *after)


def per_device(query_proj, key_proj, value_proj, filters, out_weight, cotangent):
    length, channels = query_proj.shape
    taps = filters.shape[1]
    n_ctx, n_chan = lax.axis_size("ctx"), lax.axis_size("chan")
    me = jnp.stack([lax.axis_index("ctx"), lax.axis_index("chan")]).astype(jnp.int32)
    forward, late, early_rows, lags = [jnp.asarray(m) for m in transforms(taps)]

    product = (key_proj.astype(F32) * value_proj.astype(F32)).astype(BF16)
    product, cotangent = lax.optimization_barrier((product, cotangent))
    earlier = lax.ppermute(product, "ctx", [(i, i + 1) for i in range(n_ctx - 1)])

    cots = {0: cotangent, 1: swap(cotangent, "chan", 1)}
    for bit in reversed(bits_of(n_chan)[1:]):
        cots.update({off ^ bit: swap(cots[off], "chan", bit) for off in list(cots) if off % 2 == 0})
    offs = sorted(off for off in cots if off % 2 == 0 and off)
    sums = weight_pass(me, out_weight, 0, cot=cots[0])
    for off in offs:
        cots[off + 1] = swap(held_until([cots[off]], sums)[0], "chan", 1)
    offs = sorted(offs + [off + 1 for off in offs])

    sums = weight_pass(me, out_weight, 1, cot=cots[1], sums=sums)

    order = cycle_of(n_ctx)
    slots = []
    for c in range(n_ctx):
        spot = order.index(c)
        turn = [0, n_ctx // 2] + list(range(1, n_ctx // 2)) + list(range(1 - n_ctx // 2, 0))
        targets = [order[(spot + step) % n_ctx] for step in turn]
        slots.append([targets.index(target) for target in range(n_ctx)])
    pieces = pieces_of(me, jnp.asarray(slots, jnp.int32), [cots[off] for off in range(n_chan)], sums)

    gated, filtered = by_channel(
        forward_kernel,
        [query_proj, key_proj, value_proj, earlier, filters, forward, late],
        "ttttcww",
        [("t", BF16), ("t", F32)],
        "forward_filter",
        after=sums,
    )

    ahead = [(order[i], order[(i + 1) % n_ctx]) for i in range(n_ctx)]
    behind = [(b, a) for a, b in ahead]
    turns = n_ctx // 2
    rows, piece = length // n_ctx, channels // n_ctx
    span = (turns - 1) * rows
    ends = [
        jnp.concatenate([pieces[2 * rows : 2 * rows + span], gated], axis=0),
        jnp.concatenate([gated, pieces[2 * rows + span :]], axis=0),
    ]
    arrays, places, brought = [gated], [[(0, length)]], [pieces[:rows]]

    def passed_on(kernels):
        onto, back = held_until(ends, kernels)
        came = [lax.ppermute(onto, "ctx", ahead), lax.ppermute(back, "ctx", behind)]
        arrays.extend(came)
        places.extend([[(came[0].shape[0] - length, length)], [(0, length)]])
        brought.extend([came[0][:rows], came[1][-rows:]])
        ends[:] = [came[0][rows:], came[1][:-rows]]
        return came

    landed = passed_on([])
    terms = {}
    for off in offs[:-1]:
        *sums, terms[off] = weight_pass(me, out_weight, off, gated, cots[off], sums)
    grad_query, grad_filtered, terms[offs[-1]] = weight_pass(
        me, out_weight, offs[-1], gated, cots[offs[-1]], sums, [query_proj, filtered]
    )
    previous, landed = landed, passed_on([grad_filtered])

    tap_grad = by_channel(
        tap_grad_kernel,
        [key_proj, value_proj, earlier, grad_filtered, forward, lags],
        "ttttww",
        [("c", BF16)],
        "tap_grad",
        after=previous,
    )[0]
    from_core = []
    for off in [off for off in sorted(terms) if off % 2]:
        from_core.append(swap(terms.pop(off), "chan", 1))
        terms[off ^ 1] = terms[off ^ 1] + from_core[-1].astype(F32)
    mixed_one = weight_pass(me, out_weight, 1, gated, after=[tap_grad])[0]
    across = lax.ppermute(
        held_until([pieces[rows : 2 * rows]], [mixed_one])[0],
        "ctx",
        [(order[i], order[(i + turns) % n_ctx]) for i in range(n_ctx)],
    )
    brought.insert(1, across)
    tap_sum = Sum(me, held_until([tap_grad], [mixed_one])[0])
    previous, landed = landed, passed_on([mixed_one])
    given = held_until([grad_filtered], landed)[0]
    following = lax.ppermute(given, "ctx", [(i + 1, i) for i in range(n_ctx - 1)])
    last_part = weight_pass(me, out_weight, 0, gated, after=landed + [mixed_one])[0]

    terms = dict(zip(terms, held_until(terms.values(), previous)))
    terms[0] = last_part + swap(mixed_one, "chan", 1).astype(F32)
    to_chips = []
    for bit in bits_of(n_chan)[1:]:
        for off in [off for off in sorted(terms, reverse=True) if off & bit]:
            to_chips.append(terms.pop(off).astype(BF16))
            terms[off ^ bit] = terms[off ^ bit] + swap(to_chips[-1], "chan", bit).astype(F32)
    mixed = terms[0].astype(BF16)
    early = 2 + 2 * min(1, turns - 1)
    first = jnp.concatenate(held_until(brought[:early], previous), axis=0)

    for unused in range(turns - 4):
        landed = passed_on([last_part])
    half = length // 2
    cols = [gather_of_chips(first)]
    onto, back = held_until(ends, tap_sum.add((), landed) + [cols[0][off] for off in cols[0] if off] + to_chips[:1])
    far = [lax.ppermute(onto[:half], "ctx", ahead), lax.ppermute(back[half:], "ctx", behind)]
    arrays = arrays[:1] + far + arrays[1:]
    places.insert(1, [(0, half), (0, half)])

    cols.append(gather_of_chips(jnp.concatenate(brought[early:], axis=0)))

    evens = [off for off in range(n_chan) if off % 2 == 0]
    wide = piece % 128 == 0 and 2 * early == n_ctx
    columns = {off: [(part[off], 0) for part in cols] for off in evens}
    crossed = jnp.concatenate([part[off] for off in evens for part in cols], axis=0)
    crossed = swap(held_until([crossed], far + [last_part, following])[0], "chan", 1)
    if wide:
        for at, off in enumerate(evens):
            columns[off + 1] = [(crossed, 2 * at), (crossed, 2 * at + 1)]
        columns = [columns[off] for off in range(n_chan)]
        low_half = grad_weight_of(me, arrays, places, columns, [])
        grad_weight = grad_weight_of(me, arrays, places, columns, [low_half])
    else:
        for at, off in enumerate(evens):
            columns[off + 1] = [(crossed[at * length : (at + 1) * length], 0)]
        pairs = [[array for array, unused in columns[off]] for off in range(n_chan)]
        low_half = grad_weight = narrow_grad_weight(me, arrays, places, pairs)

    tap_sum.add((), [low_half])
    while tap_sum.add((), [grad_weight]):
        pass
    own, bits = tap_sum.sums, tap_sum.bits
    grad_key, grad_value = by_channel(
        backward_kernel,
        [
            key_proj, value_proj, grad_filtered, held_until([following], [grad_weight])[0],
            filters, forward, early_rows,
        ],
        "ttttcww",
        [("t", BF16), ("t", BF16)],
        "backward_filter",
    )
    other = held_until([swap(own, "ctx", bits[1])], [grad_key])[0]
    own = joined(me, own, other, bits[1], BF16, ())
    grad_filters = joined(me, own, swap(own, "ctx", bits[0]), bits[0], F32, ())
    return (mixed, grad_query, grad_key, grad_value, grad_filters, grad_weight)


def solution(mesh):
    placed = (
        P("ctx", "chan"),
        P("ctx", "chan"),
        P("ctx", "chan"),
        P("chan", None),
        P("chan", None),
        P("ctx", "chan"),
    )
    return jax.shard_map(
        per_device,
        mesh=mesh,
        in_specs=placed,
        out_specs=(
            P("ctx", "chan"),
            P("ctx", "chan"),
            P("ctx", "chan"),
            P("ctx", "chan"),
            P("chan", None),
            P("chan", "ctx"),
        ),
        check_vma=False,
    )
```

```python
import functools

import jax
import jax.numpy as jnp
import numpy as np
from jax import lax
from jax.experimental import pallas as pl
from jax.experimental.pallas import tpu as pltpu
from jax.sharding import PartitionSpec as P

F32 = jnp.float32
BF16 = jnp.bfloat16
VMEM_BYTES = 40 * 2**20
NT = (((1,), (1,)), ((), ()))
TN = (((0,), (0,)), ((), ()))


def halves(matrix):
    high = matrix.astype(BF16)
    low = (matrix - high.astype(np.float64)).astype(BF16)
    return np.stack([high, low])


def transforms(taps):
    points = 2 * taps
    angle = np.pi * (2 * np.arange(taps)[:, None] + 1) * np.arange(points)[None, :] / points
    forward = np.concatenate([np.cos(angle), -np.sin(angle)], axis=0)
    inverse = forward.T * (2.0 / points)
    late = inverse[taps:]
    early = inverse[:taps]
    lags = inverse[taps - np.arange(taps)]
    return halves(forward), halves(late), halves(early), halves(lags)


def mm(a, b, dims=(((1,), (0,)), ((), ()))):
    return lax.dot_general(a, b, dims, preferred_element_type=F32)


def spectrum(f_ref, rows):
    return mm(f_ref[0], rows) + mm(f_ref[1], rows)


def tap_spectrum(f_ref, filters, taps):
    return mm(f_ref[0, :, :taps], filters, NT) + mm(f_ref[1, :, :taps], filters, NT)


def back(g_ref, real, imag):
    both = jnp.concatenate([real, imag], axis=0)
    high = both.astype(BF16)
    low = (both - high.astype(F32)).astype(BF16)
    return mm(g_ref[0], high) + mm(g_ref[0], low) + mm(g_ref[1], high)


def forward_kernel(taps, q_ref, k_ref, v_ref, earlier_ref, filt_ref, f_ref, g_ref, gated_ref, filtered_ref):
    product = (k_ref[...].astype(F32) * v_ref[...].astype(F32)).astype(BF16)
    x = spectrum(f_ref, jnp.concatenate([earlier_ref[...], product], axis=0))
    h = tap_spectrum(f_ref, filt_ref[...], taps)
    xr, xi, hr, hi = x[:taps], x[taps:], h[:taps], h[taps:]
    filtered = back(g_ref, xr * hr - xi * hi, xr * hi + xi * hr)
    filtered_ref[...] = filtered
    gated_ref[...] = (q_ref[...].astype(F32) * filtered).astype(BF16)


def tap_grad_kernel(taps, k_ref, v_ref, earlier_ref, gf_ref, f_ref, g_ref, out_ref):
    product = (k_ref[...].astype(F32) * v_ref[...].astype(F32)).astype(BF16)
    x = spectrum(f_ref, jnp.concatenate([earlier_ref[...], product], axis=0))
    rows = gf_ref[...]
    g = mm(f_ref[0, :, :taps], rows) + mm(f_ref[1, :, :taps], rows)
    xr, xi, gr, gi = x[:taps], x[taps:], g[:taps], g[taps:]
    tap_rows = back(g_ref, xr * gr + xi * gi, xi * gr - xr * gi)
    out_ref[...] = tap_rows.T.astype(BF16)


def backward_kernel(taps, k_ref, v_ref, gf_ref, following_ref, filt_ref, f_ref, g_ref, gk_ref, gv_ref):
    g = spectrum(f_ref, jnp.concatenate([gf_ref[...], following_ref[...]], axis=0))
    h = tap_spectrum(f_ref, filt_ref[...], taps)
    gr, gi, hr, hi = g[:taps], g[taps:], h[:taps], h[taps:]
    grad_product = back(g_ref, hr * gr + hi * gi, hr * gi - hi * gr)
    gk_ref[...] = (grad_product * v_ref[...].astype(F32)).astype(BF16)
    gv_ref[...] = (grad_product * k_ref[...].astype(F32)).astype(BF16)


def estimate(micros):
    return pl.CostEstimate(flops=int(micros * 10**9), bytes_accessed=0, transcendentals=0)


def ignoring(body, count, skip):
    def kernel(*refs):
        return body(*refs[:skip], *refs[skip + count :])

    return kernel


def by_channel(kernel, arrays, kinds, outs, name, after=()):
    length, channels = arrays[0].shape
    width = min(512, channels)
    specs = {
        "t": pl.BlockSpec((length, width), lambda i: (0, i)),
        "c": pl.BlockSpec((width, length), lambda i: (i, 0)),
    }

    def spec_of(kind, shape):
        if kind == "w":
            return pl.BlockSpec(shape, lambda i: (0,) * len(shape))
        return specs[kind]

    return pl.pallas_call(
        ignoring(functools.partial(kernel, length), len(after), len(arrays)),
        grid=(channels // width,),
        in_specs=[spec_of(kind, a.shape) for kind, a in zip(kinds, arrays)]
        + [pl.BlockSpec(memory_space=pl.ANY)] * len(after),
        out_specs=[specs[kind] for kind, unused in outs],
        out_shape=[
            jax.ShapeDtypeStruct((length, channels) if kind == "t" else (channels, length), dtype)
            for kind, dtype in outs
        ],
        compiler_params=pltpu.CompilerParams(vmem_limit_bytes=VMEM_BYTES),
        cost_estimate=estimate(3),
        name=name,
    )(*arrays, *after)


def pass_kernel(with_mixed, with_grad, has_sum, last, me_ref, w_ref, *refs):
    refs = list(refs)
    step = pl.program_id(0)
    if with_mixed:
        gated_ref = refs.pop(0)
    if with_grad:
        cot_ref = refs.pop(0)
        sum_ref = refs.pop(0) if has_sum else None
        turned_ref = refs.pop()

        @pl.when(step == 0)
        def turn():
            turned_ref[...] = cot_ref[...].T

        total = mm(w_ref[...], turned_ref[...])
        if has_sum:
            total = total + sum_ref[...]
        if last:
            q_ref, filtered_ref, gq_ref, gf_ref = refs[:4]
            total = total.T
            gq_ref[...] = (total * filtered_ref[...]).astype(BF16)
            gf_ref[...] = (total * q_ref[...].astype(F32)).astype(BF16)
        else:
            refs[0][...] = total
    if with_mixed:
        held_ref, mixed_ref = refs.pop(), refs.pop()
        part = mm(gated_ref[...], w_ref[...])

        @pl.when(step == 0)
        def first():
            held_ref[...] = part

        @pl.when(step > 0)
        def more():
            held_ref[...] = held_ref[...] + part

        @pl.when(step == pl.num_programs(0) - 1)
        def give():
            mixed_ref[...] = held_ref[...].astype(mixed_ref.dtype)


def weight_pass(me, weight, off, gated=None, cot=None, sums=(), ends=(), after=()):
    length = (cot if gated is None else gated).shape[0]
    channels = weight.shape[0]
    tile = 512
    whole = pl.BlockSpec((length, channels), lambda r, me: (0, 0))
    by_token = pl.BlockSpec((length, tile), lambda r, me: (0, r))
    by_row = pl.BlockSpec((tile, length), lambda r, me: (r, 0))
    arrays, in_specs = [weight], [pl.BlockSpec((tile, channels), lambda r, me: (r, me[1] ^ off))]
    out_specs, out_shape, scratch = [], [], []
    if gated is not None:
        arrays.append(gated)
        in_specs.append(by_token)
    if cot is not None:
        arrays += [cot, *sums, *ends]
        in_specs += [whole] + [by_row] * len(sums) + [by_token] * len(ends)
        out_specs += [by_token] * 2 if ends else [by_row]
        out_shape += [jax.ShapeDtypeStruct((length, channels), BF16)] * 2 if ends else [
            jax.ShapeDtypeStruct((channels, length), F32)
        ]
    if gated is not None:
        out_specs.append(whole)
        out_shape.append(jax.ShapeDtypeStruct((length, channels), BF16 if off % 2 else F32))
        scratch.append(pltpu.VMEM((length, channels), F32))
    if cot is not None:
        scratch.append(pltpu.VMEM((channels, length), BF16))
    body = functools.partial(pass_kernel, gated is not None, cot is not None, bool(sums), bool(ends))
    return pl.pallas_call(
        ignoring(body, len(after), 1 + len(arrays)),
        grid_spec=pltpu.PrefetchScalarGridSpec(
            num_scalar_prefetch=1,
            grid=(channels // tile,),
            in_specs=in_specs + [pl.BlockSpec(memory_space=pl.ANY)] * len(after),
            out_specs=out_specs,
            scratch_shapes=scratch,
        ),
        out_shape=out_shape,
        compiler_params=pltpu.CompilerParams(vmem_limit_bytes=VMEM_BYTES),
        cost_estimate=estimate(3 if gated is None else 0.5),
        name="grad_gated_part" if gated is None else "mixed_part" if cot is None else "grads_and_mixed",
    )(me, *arrays, *after)


def pieces_kernel(per_chan, me_ref, slot_ref, *refs):
    out_ref = refs[-1]
    length, width = refs[0].shape
    span = width // per_chan
    count = len(refs) - 1
    piece = span // count
    rows = length * piece // width
    for off in range(count):
        for part in range(per_chan):
            target = (me_ref[1] ^ off) * per_chan + part
            start = pl.multiple_of(part * span + me_ref[1] * piece, 128)
            block = refs[off][:, pl.ds(start, piece)]
            place = pl.multiple_of(slot_ref[me_ref[0], target] * rows, rows)
            out_ref[pl.ds(place, rows), :] = jnp.concatenate(
                [block[at : at + rows] for at in range(0, length, rows)], axis=1
            )


def pieces_of(me, slots, cots, after):
    length, width = cots[0].shape
    n_ctx = slots.shape[0]
    piece = width // n_ctx
    if piece % 128:
        return pieces_by_slices(me, slots, cots)
    return pl.pallas_call(
        ignoring(functools.partial(pieces_kernel, n_ctx // len(cots)), len(after), 2 + len(cots)),
        grid_spec=pltpu.PrefetchScalarGridSpec(
            num_scalar_prefetch=2,
            grid=(1,),
            in_specs=[pl.BlockSpec((length, width), lambda i, *ids: (0, 0))] * len(cots)
            + [pl.BlockSpec(memory_space=pl.ANY)] * len(after),
            out_specs=pl.BlockSpec((length, width), lambda i, *ids: (0, 0)),
        ),
        out_shape=jax.ShapeDtypeStruct((length, width), BF16),
        compiler_params=pltpu.CompilerParams(vmem_limit_bytes=VMEM_BYTES),
        cost_estimate=estimate(0.5),
        name="pieces",
    )(me, slots, *cots, *after)


def pieces_by_slices(me, slots, cots):
    length, width = cots[0].shape
    n_ctx, count = slots.shape[0], len(cots)
    piece, per_chan = width // n_ctx, n_ctx // count
    rows = length * piece // width
    table = jnp.stack(cots).reshape(count, length, per_chan, count, piece)
    mine = lax.dynamic_index_in_dim(table, me[1], 3, False)
    parts = mine.transpose(0, 2, 1, 3).reshape(n_ctx, length // rows, rows, piece)
    parts = parts.transpose(0, 2, 1, 3).reshape(n_ctx, rows, width)
    order = jnp.argsort(slots[me[0]])
    return parts[(order // per_chan ^ me[1]) * per_chan + order % per_chan].reshape(length, width)


def weight_kernel(places, parts, me_ref, *refs):
    out_ref = refs[-1]
    length = sum(rows for unused, rows in places[0])
    blocks = []
    at = 0
    for place in places:
        for start, rows in place:
            blocks.append(refs[at][start : start + rows, :])
            at += 1
    columns = jnp.concatenate(blocks, axis=0)
    for part in range(parts):
        packed = jnp.concatenate([ref[...] for ref in refs[at + 2 * part : at + 2 * part + 2]], axis=0)
        rows = packed.shape[0] // len(places)
        piece = packed.shape[1] * rows // length
        wide = [
            packed[slot * rows : (slot + 1) * rows, lane : lane + piece]
            for slot in range(len(places))
            for lane in range(0, packed.shape[1], piece)
        ]
        total = mm(columns, jnp.concatenate(wide, axis=0), TN)
        place = pl.multiple_of((me_ref[1] ^ part) * piece, piece)
        out_ref[:, pl.ds(place, piece)] = total.astype(BF16)


def grad_weight_of(me, arrays, places, cots, earlier):
    channels = arrays[0].shape[1]
    slots, parts = len(places), len(cots)
    pieces = [array for pair in cots for array, unused in pair]
    half = cots[0][0][0].shape[0]
    tile = 256
    width = 2 * half * channels // (slots * sum(count for unused, count in places[0])) * parts
    steps = channels // tile // 2
    first = steps * len(earlier)
    count = 1 + len(arrays) + len(pieces)
    return pl.pallas_call(
        ignoring(functools.partial(weight_kernel, places, parts), len(earlier), count),
        grid_spec=pltpu.PrefetchScalarGridSpec(
            num_scalar_prefetch=1,
            grid=(steps,),
            in_specs=[pl.BlockSpec((array.shape[0], tile), lambda i, me: (0, first + i)) for array in arrays]
            + [pl.BlockSpec((half, channels), lambda i, me, at=at: (at, 0)) for pair in cots for unused, at in pair]
            + [pl.BlockSpec(memory_space=pl.ANY)] * len(earlier),
            out_specs=pl.BlockSpec((tile, width), lambda i, me: (first + i, 0)),
        ),
        out_shape=jax.ShapeDtypeStruct((channels, width), BF16),
        input_output_aliases={count: 0} if earlier else {},
        compiler_params=pltpu.CompilerParams(vmem_limit_bytes=VMEM_BYTES),
        cost_estimate=estimate(2),
        name="grad_weight",
    )(me, *arrays, *pieces, *earlier)


def narrow_grad_weight(me, arrays, places, cots):
    blocks, at = [], 0
    for place in places:
        for start, rows in place:
            blocks.append(arrays[at][start : start + rows])
            at += 1
    columns = jnp.concatenate(blocks, axis=0)
    length = columns.shape[0] // len(places)
    packed = jnp.stack([jnp.concatenate(pair, axis=0) for pair in cots])
    packed = packed[jnp.arange(len(cots), dtype=jnp.int32) ^ me[1]]
    parts, height, width = packed.shape
    rows = height // len(places)
    piece = rows * width // length
    wide = packed.reshape(parts, len(places), rows, length // rows, piece).transpose(1, 3, 2, 0, 4)
    return mm(columns, wide.reshape(columns.shape[0], parts * piece), TN).astype(BF16)


def cycle_of(count):
    across = 1 << ((count.bit_length() - 1) // 2)
    order = []
    for column in range(across):
        line = [row * across + column for row in range(count // across)]
        order += line if column % 2 == 0 else line[::-1]
    return order


def held_until(arrays, kernels):
    return lax.optimization_barrier((*arrays, *kernels))[: len(arrays)]


def swap(block, axis, bit):
    size = lax.axis_size(axis)
    return lax.ppermute(block, axis, [(i, i ^ bit) for i in range(size)])


def bits_of(size):
    return [1 << place for place in range(size.bit_length() - 1)]


def gather_of_chips(block):
    held = {0: block}
    for bit in reversed(bits_of(lax.axis_size("chan"))[1:]):
        held.update({off ^ bit: swap(held[off], "chan", bit) for off in list(held)})
    return held


def added_kernel(bit, me_ref, own_ref, came_ref, *outs):
    total = (own_ref[...].astype(F32) + came_ref[...].astype(F32)).astype(BF16)
    if not bit:
        outs[0][...] = total
        return
    rows = outs[0].shape[0]
    mine = (me_ref[0] & bit) != 0
    outs[0][...] = jnp.where(mine, total[rows:], total[:rows])
    outs[1][...] = jnp.where(mine, total[:rows], total[rows:])


def added(me, own, came, bit, after):
    shape = (own.shape[0] // 2, own.shape[1]) if bit else own.shape
    whole = pl.BlockSpec(own.shape, lambda i, me: (0, 0))
    outs = 2 if bit else 1
    return pl.pallas_call(
        ignoring(functools.partial(added_kernel, bit), len(after), 3),
        grid_spec=pltpu.PrefetchScalarGridSpec(
            num_scalar_prefetch=1,
            grid=(1,),
            in_specs=[whole, whole] + [pl.BlockSpec(memory_space=pl.ANY)] * len(after),
            out_specs=[pl.BlockSpec(shape, lambda i, me: (0, 0))] * outs,
        ),
        out_shape=[jax.ShapeDtypeStruct(shape, BF16)] * outs,
        compiler_params=pltpu.CompilerParams(vmem_limit_bytes=VMEM_BYTES),
        cost_estimate=estimate(0.5),
        name="added",
    )(me, own, came, *after)


def split(me, block, bit):
    rows = block.shape[0] // 2
    mine = (me[0] & bit) != 0
    low, high = block[:rows], block[rows:]
    return jnp.where(mine, high, low), jnp.where(mine, low, high)


class Sum:
    def __init__(self, me, partial):
        self.me = me
        self.bits = bits_of(lax.axis_size("ctx"))
        self.step = 0
        self.sums, self.send = split(me, partial, self.bits[0])

    def add(self, after, kernels=()):
        if self.step == len(self.bits):
            return []
        came = swap(self.send if self.step < 2 else self.sums, "ctx", self.bits[self.step])
        came = held_until([came], kernels)[0]
        self.sums, *send = added(self.me, self.sums, came, 0 if self.step else self.bits[1], after)
        self.send = send[0] if send else None
        self.step += 1
        return [self.sums]


def joined_kernel(bit, me_ref, own_ref, other_ref, out_ref):
    rows = own_ref.shape[0]
    mine = (me_ref[0] & bit) != 0
    out_ref[:rows] = jnp.where(mine, other_ref[...], own_ref[...]).astype(out_ref.dtype)
    out_ref[rows:] = jnp.where(mine, own_ref[...], other_ref[...]).astype(out_ref.dtype)


def joined(me, own, other, bit, dtype, after):
    rows, width = own.shape
    whole = pl.BlockSpec(own.shape, lambda i, me: (0, 0))
    return pl.pallas_call(
        ignoring(functools.partial(joined_kernel, bit), len(after), 3),
        grid_spec=pltpu.PrefetchScalarGridSpec(
            num_scalar_prefetch=1,
            grid=(1,),
            in_specs=[whole, whole] + [pl.BlockSpec(memory_space=pl.ANY)] * len(after),
            out_specs=pl.BlockSpec((2 * rows, width), lambda i, me: (0, 0)),
        ),
        out_shape=jax.ShapeDtypeStruct((2 * rows, width), dtype),
        compiler_params=pltpu.CompilerParams(vmem_limit_bytes=VMEM_BYTES),
        cost_estimate=estimate(0.5),
        name="joined",
    )(me, own, other, *after)


def per_device(query_proj, key_proj, value_proj, filters, out_weight, cotangent):
    length, channels = query_proj.shape
    taps = filters.shape[1]
    n_ctx, n_chan = lax.axis_size("ctx"), lax.axis_size("chan")
    me = jnp.stack([lax.axis_index("ctx"), lax.axis_index("chan")]).astype(jnp.int32)
    forward, late, early_rows, lags = [jnp.asarray(m) for m in transforms(taps)]

    product = (key_proj.astype(F32) * value_proj.astype(F32)).astype(BF16)
    product, cotangent = lax.optimization_barrier((product, cotangent))
    earlier = lax.ppermute(product, "ctx", [(i, i + 1) for i in range(n_ctx - 1)])

    cots = {0: cotangent, 1: swap(cotangent, "chan", 1)}
    for bit in reversed(bits_of(n_chan)[1:]):
        cots.update({off ^ bit: swap(cots[off], "chan", bit) for off in list(cots) if off % 2 == 0})
    offs = sorted(off for off in cots if off % 2 == 0 and off)
    sums = weight_pass(me, out_weight, 0, cot=cots[0])
    for off in offs:
        cots[off + 1] = swap(held_until([cots[off]], sums)[0], "chan", 1)
    offs = sorted(offs + [off + 1 for off in offs])

    sums = weight_pass(me, out_weight, 1, cot=cots[1], sums=sums)

    order = cycle_of(n_ctx)
    slots = []
    for c in range(n_ctx):
        spot = order.index(c)
        turn = [0, n_ctx // 2] + list(range(1, n_ctx // 2)) + list(range(1 - n_ctx // 2, 0))
        targets = [order[(spot + step) % n_ctx] for step in turn]
        slots.append([targets.index(target) for target in range(n_ctx)])
    pieces = pieces_of(me, jnp.asarray(slots, jnp.int32), [cots[off] for off in range(n_chan)], sums)

    gated, filtered = by_channel(
        forward_kernel,
        [query_proj, key_proj, value_proj, earlier, filters, forward, late],
        "ttttcww",
        [("t", BF16), ("t", F32)],
        "forward_filter",
        after=sums,
    )

    ahead = [(order[i], order[(i + 1) % n_ctx]) for i in range(n_ctx)]
    behind = [(b, a) for a, b in ahead]
    turns = n_ctx // 2
    rows, piece = length // n_ctx, channels // n_ctx
    span = (turns - 1) * rows
    ends = [
        jnp.concatenate([pieces[2 * rows : 2 * rows + span], gated], axis=0),
        jnp.concatenate([gated, pieces[2 * rows + span :]], axis=0),
    ]
    arrays, places, brought = [gated], [[(0, length)]], [pieces[:rows]]

    def passed_on(kernels):
        onto, back = held_until(ends, kernels)
        came = [lax.ppermute(onto, "ctx", ahead), lax.ppermute(back, "ctx", behind)]
        arrays.extend(came)
        places.extend([[(came[0].shape[0] - length, length)], [(0, length)]])
        brought.extend([came[0][:rows], came[1][-rows:]])
        ends[:] = [came[0][rows:], came[1][:-rows]]
        return came

    landed = passed_on([])
    terms = {}
    for off in offs[:-1]:
        *sums, terms[off] = weight_pass(me, out_weight, off, gated, cots[off], sums)
    grad_query, grad_filtered, terms[offs[-1]] = weight_pass(
        me, out_weight, offs[-1], gated, cots[offs[-1]], sums, [query_proj, filtered]
    )
    previous, landed = landed, passed_on([grad_filtered])

    tap_grad = by_channel(
        tap_grad_kernel,
        [key_proj, value_proj, earlier, grad_filtered, forward, lags],
        "ttttww",
        [("c", BF16)],
        "tap_grad",
        after=previous,
    )[0]
    from_core = []
    for off in [off for off in sorted(terms) if off % 2]:
        from_core.append(swap(terms.pop(off), "chan", 1))
        terms[off ^ 1] = terms[off ^ 1] + from_core[-1].astype(F32)
    mixed_one = weight_pass(me, out_weight, 1, gated, after=[tap_grad])[0]
    across = lax.ppermute(
        held_until([pieces[rows : 2 * rows]], [mixed_one])[0],
        "ctx",
        [(order[i], order[(i + turns) % n_ctx]) for i in range(n_ctx)],
    )
    brought.insert(1, across)
    tap_sum = Sum(me, held_until([tap_grad], [mixed_one])[0])
    previous, landed = landed, passed_on([mixed_one])
    given = held_until([grad_filtered], landed)[0]
    following = lax.ppermute(given, "ctx", [(i + 1, i) for i in range(n_ctx - 1)])
    last_part = weight_pass(me, out_weight, 0, gated, after=landed + [mixed_one])[0]

    terms = dict(zip(terms, held_until(terms.values(), previous)))
    terms[0] = last_part + swap(mixed_one, "chan", 1).astype(F32)
    to_chips = []
    for bit in bits_of(n_chan)[1:]:
        for off in [off for off in sorted(terms, reverse=True) if off & bit]:
            to_chips.append(terms.pop(off).astype(BF16))
            terms[off ^ bit] = terms[off ^ bit] + swap(to_chips[-1], "chan", bit).astype(F32)
    mixed = terms[0].astype(BF16)
    early = 2 + 2 * min(1, turns - 1)
    first = jnp.concatenate(held_until(brought[:early], previous), axis=0)

    for unused in range(turns - 4):
        landed = passed_on([last_part])
    half = length // 2
    cols = [gather_of_chips(first)]
    onto, back = held_until(ends, tap_sum.add((), landed) + [cols[0][off] for off in cols[0] if off] + to_chips[:1])
    far = [lax.ppermute(onto[:half], "ctx", ahead), lax.ppermute(back[half:], "ctx", behind)]
    arrays = arrays[:1] + far + arrays[1:]
    places.insert(1, [(0, half), (0, half)])

    cols.append(gather_of_chips(jnp.concatenate(brought[early:], axis=0)))

    evens = [off for off in range(n_chan) if off % 2 == 0]
    wide = piece % 128 == 0 and 2 * early == n_ctx
    columns = {off: [(part[off], 0) for part in cols] for off in evens}
    crossed = jnp.concatenate([part[off] for off in evens for part in cols], axis=0)
    crossed = swap(held_until([crossed], far + [last_part, following])[0], "chan", 1)
    if wide:
        for at, off in enumerate(evens):
            columns[off + 1] = [(crossed, 2 * at), (crossed, 2 * at + 1)]
        columns = [columns[off] for off in range(n_chan)]
        low_half = grad_weight_of(me, arrays, places, columns, [])
        grad_weight = grad_weight_of(me, arrays, places, columns, [low_half])
    else:
        for at, off in enumerate(evens):
            columns[off + 1] = [(crossed[at * length : (at + 1) * length], 0)]
        pairs = [[array for array, unused in columns[off]] for off in range(n_chan)]
        low_half = grad_weight = narrow_grad_weight(me, arrays, places, pairs)

    tap_sum.add((), [low_half])
    while tap_sum.add((), [grad_weight]):
        pass
    own, bits = tap_sum.sums, tap_sum.bits
    grad_key, grad_value = by_channel(
        backward_kernel,
        [
            key_proj, value_proj, grad_filtered, held_until([following], [grad_weight])[0],
            filters, forward, early_rows,
        ],
        "ttttcww",
        [("t", BF16), ("t", BF16)],
        "backward_filter",
    )
    other = held_until([swap(own, "ctx", bits[1])], [grad_key])[0]
    own = joined(me, own, other, bits[1], BF16, ())
    grad_filters = joined(me, own, swap(own, "ctx", bits[0]), bits[0], F32, ())
    return (mixed, grad_query, grad_key, grad_value, grad_filters, grad_weight)


def solution(mesh):
    placed = (
        P("ctx", "chan"),
        P("ctx", "chan"),
        P("ctx", "chan"),
        P("chan", None),
        P("chan", None),
        P("ctx", "chan"),
    )
    return jax.shard_map(
        per_device,
        mesh=mesh,
        in_specs=placed,
        out_specs=(
            P("ctx", "chan"),
            P("ctx", "chan"),
            P("ctx", "chan"),
            P("ctx", "chan"),
            P("chan", None),
            P("chan", "ctx"),
        ),
        check_vma=False,
    )
```

```python
import functools

import jax
import jax.numpy as jnp
import numpy as np
from jax import lax
from jax.experimental import pallas as pl
from jax.experimental.pallas import tpu as pltpu
from jax.sharding import PartitionSpec as P

F32 = jnp.float32
BF16 = jnp.bfloat16
VMEM_BYTES = 40 * 2**20
NT = (((1,), (1,)), ((), ()))
TN = (((0,), (0,)), ((), ()))


def halves(matrix):
    high = matrix.astype(BF16)
    low = (matrix - high.astype(np.float64)).astype(BF16)
    return np.stack([high, low])


def transforms(taps):
    points = 2 * taps
    angle = np.pi * (2 * np.arange(taps)[:, None] + 1) * np.arange(points)[None, :] / points
    forward = np.concatenate([np.cos(angle), -np.sin(angle)], axis=0)
    inverse = forward.T * (2.0 / points)
    late = inverse[taps:]
    early = inverse[:taps]
    lags = inverse[taps - np.arange(taps)]
    return halves(forward), halves(late), halves(early), halves(lags)


def mm(a, b, dims=(((1,), (0,)), ((), ()))):
    return lax.dot_general(a, b, dims, preferred_element_type=F32)


def spectrum(f_ref, rows):
    return mm(f_ref[0], rows) + mm(f_ref[1], rows)


def tap_spectrum(f_ref, filters, taps):
    return mm(f_ref[0, :, :taps], filters, NT) + mm(f_ref[1, :, :taps], filters, NT)


def back(g_ref, real, imag):
    both = jnp.concatenate([real, imag], axis=0)
    high = both.astype(BF16)
    low = (both - high.astype(F32)).astype(BF16)
    return mm(g_ref[0], high) + mm(g_ref[0], low) + mm(g_ref[1], high)


def forward_kernel(taps, q_ref, k_ref, v_ref, earlier_ref, filt_ref, f_ref, g_ref, gated_ref, filtered_ref):
    product = (k_ref[...].astype(F32) * v_ref[...].astype(F32)).astype(BF16)
    x = spectrum(f_ref, jnp.concatenate([earlier_ref[...], product], axis=0))
    h = tap_spectrum(f_ref, filt_ref[...], taps)
    xr, xi, hr, hi = x[:taps], x[taps:], h[:taps], h[taps:]
    filtered = back(g_ref, xr * hr - xi * hi, xr * hi + xi * hr)
    filtered_ref[...] = filtered
    gated_ref[...] = (q_ref[...].astype(F32) * filtered).astype(BF16)


def tap_grad_kernel(taps, k_ref, v_ref, earlier_ref, gf_ref, f_ref, g_ref, out_ref):
    product = (k_ref[...].astype(F32) * v_ref[...].astype(F32)).astype(BF16)
    x = spectrum(f_ref, jnp.concatenate([earlier_ref[...], product], axis=0))
    rows = gf_ref[...]
    g = mm(f_ref[0, :, :taps], rows) + mm(f_ref[1, :, :taps], rows)
    xr, xi, gr, gi = x[:taps], x[taps:], g[:taps], g[taps:]
    tap_rows = back(g_ref, xr * gr + xi * gi, xi * gr - xr * gi)
    out_ref[...] = tap_rows.T.astype(BF16)


def backward_kernel(taps, k_ref, v_ref, gf_ref, following_ref, filt_ref, f_ref, g_ref, gk_ref, gv_ref):
    g = spectrum(f_ref, jnp.concatenate([gf_ref[...], following_ref[...]], axis=0))
    h = tap_spectrum(f_ref, filt_ref[...], taps)
    gr, gi, hr, hi = g[:taps], g[taps:], h[:taps], h[taps:]
    grad_product = back(g_ref, hr * gr + hi * gi, hr * gi - hi * gr)
    gk_ref[...] = (grad_product * v_ref[...].astype(F32)).astype(BF16)
    gv_ref[...] = (grad_product * k_ref[...].astype(F32)).astype(BF16)


def estimate(micros):
    return pl.CostEstimate(flops=int(micros * 10**9), bytes_accessed=0, transcendentals=0)


def ignoring(body, count, skip):
    def kernel(*refs):
        return body(*refs[:skip], *refs[skip + count :])

    return kernel


def by_channel(kernel, arrays, kinds, outs, name, after=()):
    length, channels = arrays[0].shape
    width = min(512, channels)
    specs = {
        "t": pl.BlockSpec((length, width), lambda i: (0, i)),
        "c": pl.BlockSpec((width, length), lambda i: (i, 0)),
    }

    def spec_of(kind, shape):
        if kind == "w":
            return pl.BlockSpec(shape, lambda i: (0,) * len(shape))
        return specs[kind]

    return pl.pallas_call(
        ignoring(functools.partial(kernel, length), len(after), len(arrays)),
        grid=(channels // width,),
        in_specs=[spec_of(kind, a.shape) for kind, a in zip(kinds, arrays)]
        + [pl.BlockSpec(memory_space=pl.ANY)] * len(after),
        out_specs=[specs[kind] for kind, unused in outs],
        out_shape=[
            jax.ShapeDtypeStruct((length, channels) if kind == "t" else (channels, length), dtype)
            for kind, dtype in outs
        ],
        compiler_params=pltpu.CompilerParams(vmem_limit_bytes=VMEM_BYTES),
        cost_estimate=estimate(3),
        name=name,
    )(*arrays, *after)


def pass_kernel(with_mixed, with_grad, has_sum, last, me_ref, w_ref, *refs):
    refs = list(refs)
    step = pl.program_id(0)
    if with_mixed:
        gated_ref = refs.pop(0)
    if with_grad:
        cot_ref = refs.pop(0)
        sum_ref = refs.pop(0) if has_sum else None
        turned_ref = refs.pop()

        @pl.when(step == 0)
        def turn():
            turned_ref[...] = cot_ref[...].T

        total = mm(w_ref[...], turned_ref[...])
        if has_sum:
            total = total + sum_ref[...]
        if last:
            q_ref, filtered_ref, gq_ref, gf_ref = refs[:4]
            total = total.T
            gq_ref[...] = (total * filtered_ref[...]).astype(BF16)
            gf_ref[...] = (total * q_ref[...].astype(F32)).astype(BF16)
        else:
            refs[0][...] = total
    if with_mixed:
        held_ref, mixed_ref = refs.pop(), refs.pop()
        part = mm(gated_ref[...], w_ref[...])

        @pl.when(step == 0)
        def first():
            held_ref[...] = part

        @pl.when(step > 0)
        def more():
            held_ref[...] = held_ref[...] + part

        @pl.when(step == pl.num_programs(0) - 1)
        def give():
            mixed_ref[...] = held_ref[...].astype(mixed_ref.dtype)


def weight_pass(me, weight, off, gated=None, cot=None, sums=(), ends=(), after=()):
    length = (cot if gated is None else gated).shape[0]
    channels = weight.shape[0]
    tile = 512
    whole = pl.BlockSpec((length, channels), lambda r, me: (0, 0))
    by_token = pl.BlockSpec((length, tile), lambda r, me: (0, r))
    by_row = pl.BlockSpec((tile, length), lambda r, me: (r, 0))
    arrays, in_specs = [weight], [pl.BlockSpec((tile, channels), lambda r, me: (r, me[1] ^ off))]
    out_specs, out_shape, scratch = [], [], []
    if gated is not None:
        arrays.append(gated)
        in_specs.append(by_token)
    if cot is not None:
        arrays += [cot, *sums, *ends]
        in_specs += [whole] + [by_row] * len(sums) + [by_token] * len(ends)
        out_specs += [by_token] * 2 if ends else [by_row]
        out_shape += [jax.ShapeDtypeStruct((length, channels), BF16)] * 2 if ends else [
            jax.ShapeDtypeStruct((channels, length), F32)
        ]
    if gated is not None:
        out_specs.append(whole)
        out_shape.append(jax.ShapeDtypeStruct((length, channels), BF16 if off % 2 else F32))
        scratch.append(pltpu.VMEM((length, channels), F32))
    if cot is not None:
        scratch.append(pltpu.VMEM((channels, length), BF16))
    body = functools.partial(pass_kernel, gated is not None, cot is not None, bool(sums), bool(ends))
    return pl.pallas_call(
        ignoring(body, len(after), 1 + len(arrays)),
        grid_spec=pltpu.PrefetchScalarGridSpec(
            num_scalar_prefetch=1,
            grid=(channels // tile,),
            in_specs=in_specs + [pl.BlockSpec(memory_space=pl.ANY)] * len(after),
            out_specs=out_specs,
            scratch_shapes=scratch,
        ),
        out_shape=out_shape,
        compiler_params=pltpu.CompilerParams(vmem_limit_bytes=VMEM_BYTES),
        cost_estimate=estimate(3 if gated is None else 0.5),
        name="grad_gated_part" if gated is None else "mixed_part" if cot is None else "grads_and_mixed",
    )(me, *arrays, *after)


def pieces_kernel(per_chan, me_ref, slot_ref, *refs):
    out_ref = refs[-1]
    length, width = refs[0].shape
    span = width // per_chan
    count = len(refs) - 1
    piece = span // count
    rows = length * piece // width
    for off in range(count):
        for part in range(per_chan):
            target = (me_ref[1] ^ off) * per_chan + part
            start = pl.multiple_of(part * span + me_ref[1] * piece, 128)
            block = refs[off][:, pl.ds(start, piece)]
            place = pl.multiple_of(slot_ref[me_ref[0], target] * rows, rows)
            out_ref[pl.ds(place, rows), :] = jnp.concatenate(
                [block[at : at + rows] for at in range(0, length, rows)], axis=1
            )


def pieces_of(me, slots, cots, after):
    length, width = cots[0].shape
    n_ctx = slots.shape[0]
    piece = width // n_ctx
    if piece % 128:
        return pieces_by_slices(me, slots, cots)
    return pl.pallas_call(
        ignoring(functools.partial(pieces_kernel, n_ctx // len(cots)), len(after), 2 + len(cots)),
        grid_spec=pltpu.PrefetchScalarGridSpec(
            num_scalar_prefetch=2,
            grid=(1,),
            in_specs=[pl.BlockSpec((length, width), lambda i, *ids: (0, 0))] * len(cots)
            + [pl.BlockSpec(memory_space=pl.ANY)] * len(after),
            out_specs=pl.BlockSpec((length, width), lambda i, *ids: (0, 0)),
        ),
        out_shape=jax.ShapeDtypeStruct((length, width), BF16),
        compiler_params=pltpu.CompilerParams(vmem_limit_bytes=VMEM_BYTES),
        cost_estimate=estimate(0.5),
        name="pieces",
    )(me, slots, *cots, *after)


def pieces_by_slices(me, slots, cots):
    length, width = cots[0].shape
    n_ctx, count = slots.shape[0], len(cots)
    piece, per_chan = width // n_ctx, n_ctx // count
    rows = length * piece // width
    table = jnp.stack(cots).reshape(count, length, per_chan, count, piece)
    mine = lax.dynamic_index_in_dim(table, me[1], 3, False)
    parts = mine.transpose(0, 2, 1, 3).reshape(n_ctx, length // rows, rows, piece)
    parts = parts.transpose(0, 2, 1, 3).reshape(n_ctx, rows, width)
    order = jnp.argsort(slots[me[0]])
    return parts[(order // per_chan ^ me[1]) * per_chan + order % per_chan].reshape(length, width)


def weight_kernel(places, parts, me_ref, *refs):
    out_ref = refs[-1]
    length = sum(rows for unused, rows in places[0])
    blocks = []
    at = 0
    for place in places:
        for start, rows in place:
            blocks.append(refs[at][start : start + rows, :])
            at += 1
    columns = jnp.concatenate(blocks, axis=0)
    for part in range(parts):
        packed = jnp.concatenate([ref[...] for ref in refs[at + 2 * part : at + 2 * part + 2]], axis=0)
        rows = packed.shape[0] // len(places)
        piece = packed.shape[1] * rows // length
        wide = [
            packed[slot * rows : (slot + 1) * rows, lane : lane + piece]
            for slot in range(len(places))
            for lane in range(0, packed.shape[1], piece)
        ]
        total = mm(columns, jnp.concatenate(wide, axis=0), TN)
        place = pl.multiple_of((me_ref[1] ^ part) * piece, piece)
        out_ref[:, pl.ds(place, piece)] = total.astype(BF16)


def grad_weight_of(me, arrays, places, cots, earlier):
    channels = arrays[0].shape[1]
    slots, parts = len(places), len(cots)
    pieces = [array for pair in cots for array, unused in pair]
    half = cots[0][0][0].shape[0]
    tile = 256
    width = 2 * half * channels // (slots * sum(count for unused, count in places[0])) * parts
    steps = channels // tile // 2
    first = steps * len(earlier)
    count = 1 + len(arrays) + len(pieces)
    return pl.pallas_call(
        ignoring(functools.partial(weight_kernel, places, parts), len(earlier), count),
        grid_spec=pltpu.PrefetchScalarGridSpec(
            num_scalar_prefetch=1,
            grid=(steps,),
            in_specs=[pl.BlockSpec((array.shape[0], tile), lambda i, me: (0, first + i)) for array in arrays]
            + [pl.BlockSpec((half, channels), lambda i, me, at=at: (at, 0)) for pair in cots for unused, at in pair]
            + [pl.BlockSpec(memory_space=pl.ANY)] * len(earlier),
            out_specs=pl.BlockSpec((tile, width), lambda i, me: (first + i, 0)),
        ),
        out_shape=jax.ShapeDtypeStruct((channels, width), BF16),
        input_output_aliases={count: 0} if earlier else {},
        compiler_params=pltpu.CompilerParams(vmem_limit_bytes=VMEM_BYTES),
        cost_estimate=estimate(2),
        name="grad_weight",
    )(me, *arrays, *pieces, *earlier)


def narrow_grad_weight(me, arrays, places, cots):
    blocks, at = [], 0
    for place in places:
        for start, rows in place:
            blocks.append(arrays[at][start : start + rows])
            at += 1
    columns = jnp.concatenate(blocks, axis=0)
    length = columns.shape[0] // len(places)
    packed = jnp.stack([jnp.concatenate(pair, axis=0) for pair in cots])
    packed = packed[jnp.arange(len(cots), dtype=jnp.int32) ^ me[1]]
    parts, height, width = packed.shape
    rows = height // len(places)
    piece = rows * width // length
    wide = packed.reshape(parts, len(places), rows, length // rows, piece).transpose(1, 3, 2, 0, 4)
    return mm(columns, wide.reshape(columns.shape[0], parts * piece), TN).astype(BF16)


def cycle_of(count):
    across = 1 << ((count.bit_length() - 1) // 2)
    order = []
    for column in range(across):
        line = [row * across + column for row in range(count // across)]
        order += line if column % 2 == 0 else line[::-1]
    return order


def held_until(arrays, kernels):
    return lax.optimization_barrier((*arrays, *kernels))[: len(arrays)]


def swap(block, axis, bit):
    size = lax.axis_size(axis)
    return lax.ppermute(block, axis, [(i, i ^ bit) for i in range(size)])


def bits_of(size):
    return [1 << place for place in range(size.bit_length() - 1)]


def gather_of_chips(block):
    held = {0: block}
    for bit in reversed(bits_of(lax.axis_size("chan"))[1:]):
        held.update({off ^ bit: swap(held[off], "chan", bit) for off in list(held)})
    return held


def added_kernel(bit, me_ref, own_ref, came_ref, *outs):
    total = (own_ref[...].astype(F32) + came_ref[...].astype(F32)).astype(BF16)
    if not bit:
        outs[0][...] = total
        return
    rows = outs[0].shape[0]
    mine = (me_ref[0] & bit) != 0
    outs[0][...] = jnp.where(mine, total[rows:], total[:rows])
    outs[1][...] = jnp.where(mine, total[:rows], total[rows:])


def added(me, own, came, bit, after):
    shape = (own.shape[0] // 2, own.shape[1]) if bit else own.shape
    whole = pl.BlockSpec(own.shape, lambda i, me: (0, 0))
    outs = 2 if bit else 1
    return pl.pallas_call(
        ignoring(functools.partial(added_kernel, bit), len(after), 3),
        grid_spec=pltpu.PrefetchScalarGridSpec(
            num_scalar_prefetch=1,
            grid=(1,),
            in_specs=[whole, whole] + [pl.BlockSpec(memory_space=pl.ANY)] * len(after),
            out_specs=[pl.BlockSpec(shape, lambda i, me: (0, 0))] * outs,
        ),
        out_shape=[jax.ShapeDtypeStruct(shape, BF16)] * outs,
        compiler_params=pltpu.CompilerParams(vmem_limit_bytes=VMEM_BYTES),
        cost_estimate=estimate(0.5),
        name="added",
    )(me, own, came, *after)


def split(me, block, bit):
    rows = block.shape[0] // 2
    mine = (me[0] & bit) != 0
    low, high = block[:rows], block[rows:]
    return jnp.where(mine, high, low), jnp.where(mine, low, high)


class Sum:
    def __init__(self, me, partial):
        self.me = me
        self.bits = bits_of(lax.axis_size("ctx"))
        self.step = 0
        self.sums, self.send = split(me, partial, self.bits[0])

    def add(self, after, kernels=()):
        if self.step == len(self.bits):
            return []
        came = swap(self.send if self.step < 2 else self.sums, "ctx", self.bits[self.step])
        came = held_until([came], kernels)[0]
        self.sums, *send = added(self.me, self.sums, came, 0 if self.step else self.bits[1], after)
        self.send = send[0] if send else None
        self.step += 1
        return [self.sums]


def joined_kernel(bit, me_ref, own_ref, other_ref, out_ref):
    rows = own_ref.shape[0]
    mine = (me_ref[0] & bit) != 0
    out_ref[:rows] = jnp.where(mine, other_ref[...], own_ref[...]).astype(out_ref.dtype)
    out_ref[rows:] = jnp.where(mine, own_ref[...], other_ref[...]).astype(out_ref.dtype)


def joined(me, own, other, bit, dtype, after):
    rows, width = own.shape
    whole = pl.BlockSpec(own.shape, lambda i, me: (0, 0))
    return pl.pallas_call(
        ignoring(functools.partial(joined_kernel, bit), len(after), 3),
        grid_spec=pltpu.PrefetchScalarGridSpec(
            num_scalar_prefetch=1,
            grid=(1,),
            in_specs=[whole, whole] + [pl.BlockSpec(memory_space=pl.ANY)] * len(after),
            out_specs=pl.BlockSpec((2 * rows, width), lambda i, me: (0, 0)),
        ),
        out_shape=jax.ShapeDtypeStruct((2 * rows, width), dtype),
        compiler_params=pltpu.CompilerParams(vmem_limit_bytes=VMEM_BYTES),
        cost_estimate=estimate(0.5),
        name="joined",
    )(me, own, other, *after)


def per_device(query_proj, key_proj, value_proj, filters, out_weight, cotangent):
    length, channels = query_proj.shape
    taps = filters.shape[1]
    n_ctx, n_chan = lax.axis_size("ctx"), lax.axis_size("chan")
    me = jnp.stack([lax.axis_index("ctx"), lax.axis_index("chan")]).astype(jnp.int32)
    forward, late, early_rows, lags = [jnp.asarray(m) for m in transforms(taps)]

    product = (key_proj.astype(F32) * value_proj.astype(F32)).astype(BF16)
    product, cotangent = lax.optimization_barrier((product, cotangent))
    earlier = lax.ppermute(product, "ctx", [(i, i + 1) for i in range(n_ctx - 1)])

    cots = {0: cotangent, 1: swap(cotangent, "chan", 1)}
    for bit in reversed(bits_of(n_chan)[1:]):
        cots.update({off ^ bit: swap(cots[off], "chan", bit) for off in list(cots) if off % 2 == 0})
    offs = sorted(off for off in cots if off % 2 == 0 and off)
    sums = weight_pass(me, out_weight, 0, cot=cots[0])
    for off in offs:
        cots[off + 1] = swap(held_until([cots[off]], sums)[0], "chan", 1)
    offs = sorted(offs + [off + 1 for off in offs])

    sums = weight_pass(me, out_weight, 1, cot=cots[1], sums=sums)

    order = cycle_of(n_ctx)
    slots = []
    for c in range(n_ctx):
        spot = order.index(c)
        turn = [0, n_ctx // 2] + list(range(1, n_ctx // 2)) + list(range(1 - n_ctx // 2, 0))
        targets = [order[(spot + step) % n_ctx] for step in turn]
        slots.append([targets.index(target) for target in range(n_ctx)])
    pieces = pieces_of(me, jnp.asarray(slots, jnp.int32), [cots[off] for off in range(n_chan)], sums)

    gated, filtered = by_channel(
        forward_kernel,
        [query_proj, key_proj, value_proj, earlier, filters, forward, late],
        "ttttcww",
        [("t", BF16), ("t", F32)],
        "forward_filter",
        after=sums,
    )

    ahead = [(order[i], order[(i + 1) % n_ctx]) for i in range(n_ctx)]
    behind = [(b, a) for a, b in ahead]
    turns = n_ctx // 2
    rows, piece = length // n_ctx, channels // n_ctx
    span = (turns - 1) * rows
    ends = [
        jnp.concatenate([pieces[2 * rows : 2 * rows + span], gated], axis=0),
        jnp.concatenate([gated, pieces[2 * rows + span :]], axis=0),
    ]
    arrays, places, brought = [gated], [[(0, length)]], [pieces[:rows]]

    def passed_on(kernels):
        onto, back = held_until(ends, kernels)
        came = [lax.ppermute(onto, "ctx", ahead), lax.ppermute(back, "ctx", behind)]
        arrays.extend(came)
        places.extend([[(came[0].shape[0] - length, length)], [(0, length)]])
        brought.extend([came[0][:rows], came[1][-rows:]])
        ends[:] = [came[0][rows:], came[1][:-rows]]
        return came

    landed = passed_on([])
    terms = {}
    for off in offs[:-1]:
        *sums, terms[off] = weight_pass(me, out_weight, off, gated, cots[off], sums)
    grad_query, grad_filtered, terms[offs[-1]] = weight_pass(
        me, out_weight, offs[-1], gated, cots[offs[-1]], sums, [query_proj, filtered]
    )
    previous, landed = landed, passed_on([grad_filtered])

    tap_grad = by_channel(
        tap_grad_kernel,
        [key_proj, value_proj, earlier, grad_filtered, forward, lags],
        "ttttww",
        [("c", BF16)],
        "tap_grad",
        after=previous,
    )[0]
    from_core = []
    for off in [off for off in sorted(terms) if off % 2]:
        from_core.append(swap(terms.pop(off), "chan", 1))
        terms[off ^ 1] = terms[off ^ 1] + from_core[-1].astype(F32)
    mixed_one = weight_pass(me, out_weight, 1, gated, after=[tap_grad])[0]
    across = lax.ppermute(
        held_until([pieces[rows : 2 * rows]], [mixed_one])[0],
        "ctx",
        [(order[i], order[(i + turns) % n_ctx]) for i in range(n_ctx)],
    )
    brought.insert(1, across)
    tap_sum = Sum(me, held_until([tap_grad], [mixed_one])[0])
    previous, landed = landed, passed_on([mixed_one])
    last_part = weight_pass(me, out_weight, 0, gated, after=landed + [mixed_one])[0]

    terms = dict(zip(terms, held_until(terms.values(), previous)))
    terms[0] = last_part + swap(mixed_one, "chan", 1).astype(F32)
    to_chips = []
    for bit in bits_of(n_chan)[1:]:
        for off in [off for off in sorted(terms, reverse=True) if off & bit]:
            to_chips.append(terms.pop(off).astype(BF16))
            terms[off ^ bit] = terms[off ^ bit] + swap(to_chips[-1], "chan", bit).astype(F32)
    mixed = terms[0].astype(BF16)
    early = 2 + 2 * min(1, turns - 1)
    first = jnp.concatenate(held_until(brought[:early], previous), axis=0)

    for unused in range(turns - 4):
        landed = passed_on([last_part])
    half = length // 2
    cols = [gather_of_chips(first)]
    onto, back = held_until(ends, tap_sum.add((), landed) + [cols[0][off] for off in cols[0] if off] + to_chips[:1])
    far = [lax.ppermute(onto[:half], "ctx", ahead), lax.ppermute(back[half:], "ctx", behind)]
    arrays = arrays[:1] + far + arrays[1:]
    places.insert(1, [(0, half), (0, half)])

    cols.append(gather_of_chips(jnp.concatenate(brought[early:], axis=0)))

    evens = [off for off in range(n_chan) if off % 2 == 0]
    wide = piece % 128 == 0 and 2 * early == n_ctx
    columns = {off: [(part[off], 0) for part in cols] for off in evens}
    crossed = jnp.concatenate([part[off] for off in evens for part in cols], axis=0)
    crossed = swap(held_until([crossed], far + [last_part])[0], "chan", 1)
    if wide:
        for at, off in enumerate(evens):
            columns[off + 1] = [(crossed, 2 * at), (crossed, 2 * at + 1)]
        columns = [columns[off] for off in range(n_chan)]
        low_half = grad_weight_of(me, arrays, places, columns, [])
        grad_weight = grad_weight_of(me, arrays, places, columns, [low_half])
    else:
        for at, off in enumerate(evens):
            columns[off + 1] = [(crossed[at * length : (at + 1) * length], 0)]
        pairs = [[array for array, unused in columns[off]] for off in range(n_chan)]
        low_half = grad_weight = narrow_grad_weight(me, arrays, places, pairs)

    given = held_until([grad_filtered], tap_sum.add((), [low_half]))[0]
    following = lax.ppermute(given, "ctx", [(i + 1, i) for i in range(n_ctx - 1)])
    while tap_sum.add((), [grad_weight]):
        pass
    own, bits = tap_sum.sums, tap_sum.bits
    grad_key, grad_value = by_channel(
        backward_kernel,
        [
            key_proj, value_proj, grad_filtered, held_until([following], [grad_weight])[0],
            filters, forward, early_rows,
        ],
        "ttttcww",
        [("t", BF16), ("t", BF16)],
        "backward_filter",
    )
    other = held_until([swap(own, "ctx", bits[1])], [grad_key])[0]
    own = joined(me, own, other, bits[1], BF16, ())
    grad_filters = joined(me, own, swap(own, "ctx", bits[0]), bits[0], F32, ())
    return (mixed, grad_query, grad_key, grad_value, grad_filters, grad_weight)


def solution(mesh):
    placed = (
        P("ctx", "chan"),
        P("ctx", "chan"),
        P("ctx", "chan"),
        P("chan", None),
        P("chan", None),
        P("ctx", "chan"),
    )
    return jax.shard_map(
        per_device,
        mesh=mesh,
        in_specs=placed,
        out_specs=(
            P("ctx", "chan"),
            P("ctx", "chan"),
            P("ctx", "chan"),
            P("ctx", "chan"),
            P("chan", None),
            P("chan", "ctx"),
        ),
        check_vma=False,
    )
```
